32 devices in a mesh: dp: 8 (over z, x), mp: 4 (over y, core).
Axes of the slice: x: 2, y: 2, z: 4, core: 2. Of those that a mesh axis runs over, the one named last changes fastest.
Arguments:
- inputs: bfloat16 [8192, 768], P('dp'), may hold values from -6 to 6
- page_feat: bfloat16 [8, 8, 768], P('dp'), may hold values from -6 to 6
- page_onehot: int32 [8192, 8], P('dp'), may hold values from 0 to 1, as said below
- lengths: int32 [8], P('dp'), may hold values from 256 to 1024, as said below
- hor_pos: int32 [8192], P('dp'), may hold values from 0 to 999
- ver_pos: int32 [8192], P('dp'), may hold values from 0 to 999
- norm1_gain: bfloat16 [768], replicated, may hold values from 0.099609375 to 1.8984375
- w_query: bfloat16 [768, 768], P(None, 'mp'), may hold values from -0.21875 to 0.21875
- w_key: bfloat16 [768, 768], P(None, 'mp'), may hold values from -0.21875 to 0.21875
- w_value: bfloat16 [768, 768], P(None, 'mp'), may hold values from -0.21875 to 0.21875
- rel_table: bfloat16 [12, 32], P('mp'), may hold values from -4 to 4
- hor_table: bfloat16 [12, 32], P('mp'), may hold values from -4 to 4
- ver_table: bfloat16 [12, 32], P('mp'), may hold values from -4 to 4
- w_output: bfloat16 [768, 768], P('mp'), may hold values from -0.875 to 0.875
- norm2_gain: bfloat16 [768], replicated, may hold values from 0.099609375 to 1.8984375
- w_up: bfloat16 [768, 3072], P(None, 'mp'), may hold values from -0.21875 to 0.21875
- w_down: bfloat16 [3072, 768], P('mp'), may hold values from -0.15625 to 0.15625
- cotangent: bfloat16 [8192, 768], P('dp'), may hold values from -6 to 6
Outputs:
- output: bfloat16 [8192, 768], P('dp')
- grad_inputs: float32 [8192, 768], P('dp')
- grad_page_feat: float32 [8, 8, 768], P('dp')
- grad_norm1_gain: float32 [768], P('dp')
- grad_w_query: float32 [768, 768], P('dp', 'mp')
- grad_w_key: float32 [768, 768], P('dp', 'mp')
- grad_w_value: float32 [768, 768], P('dp', 'mp')
- grad_rel_table: float32 [12, 32], P('mp')
- grad_hor_table: float32 [12, 32], P('mp')
- grad_ver_table: float32 [12, 32], P('mp')
- grad_w_output: float32 [768, 768], P('mp', 'dp')
- grad_norm2_gain: float32 [768], P('dp')
- grad_w_up: float32 [768, 3072], P('dp', 'mp')
- grad_w_down: float32 [3072, 768], P('mp', 'dp')
The draws below stay inside these ranges and needn't reach their ends.
Inputs may be any that keep to these rules, and one draw needn't show every extreme that they name: `lengths`: keys at or past a sequence's length are padding; in every draw some sequence uses all 1024 slots. `page_onehot`: each row has exactly one 1; within a sequence the page number never falls from one token to the next.
All inputs are finite; a program needn't handle non-finite values.
Results may differ from the reference program's by a relative error of at most 0.012.
Values may be sent and summed in bfloat16 or wider, within the bound.
No kernel may reach another device: no remote copies, remote signals or barrier semaphores. Data moves between devices by JAX's collectives and lax.ppermute only.
A program may use at most 192 MiB of HBM per device.

```python
import jax
import jax.numpy as jnp
from jax import lax

D = 768
H = 12
HD = 64
FF = 3072
NB = 32
PAGES = 8
SEQ_LEN = 1024
SEQS = 8
TOKENS = 8192


def draw_lengths(key, part):
    key = jax.random.fold_in(key, 11)
    first_key, second_key = jax.random.split(key)
    drawn = jax.random.randint(first_key, (SEQS,), SEQ_LEN // 4, SEQ_LEN + 1)
    chosen = jax.random.randint(second_key, (), 0, SEQS)
    return jnp.where(jnp.arange(SEQS) == chosen, SEQ_LEN, drawn).astype(jnp.int32)


def draw_page_onehot(key, part):
    key = jax.random.fold_in(key, 23)
    first_key, second_key = jax.random.split(key)
    page_count = jax.random.randint(first_key, (SEQS, 1), 1, PAGES + 1)
    cuts = jnp.sort(jax.random.randint(second_key, (SEQS, PAGES - 1), 1, SEQ_LEN), axis=1)
    active = jnp.arange(PAGES - 1)[None, :] < page_count - 1
    positions = jnp.arange(SEQ_LEN)
    passed = (cuts[:, :, None] <= positions[None, None, :]) & active[:, :, None]
    page_index = jnp.sum(passed.astype(jnp.int32), axis=1).reshape(SEQS * SEQ_LEN)
    return (page_index[:, None] == jnp.arange(PAGES)[None, :]).astype(jnp.int32)


def draw_cotangent(key, part):
    key = jax.random.fold_in(key, 37)
    row_seq = (jnp.arange(TOKENS) // SEQ_LEN).astype(jnp.float32)
    ramp = row_seq / max(SEQS - 1, 1)
    entries = jnp.clip(jax.random.normal(key, (TOKENS, D), jnp.float32), -4.0, 4.0)
    factor = 0.5 + ramp
    return (entries * factor[:, None]).astype(jnp.bfloat16)


def place_ends(values, stream_key, smallest, top_value):
    longest = values.shape.index(max(values.shape))
    spots = []
    for shift in (0, 1):
        where = [jax.random.randint(jax.random.fold_in(stream_key, axis), (), 0, length) for axis, length in enumerate(values.shape)]
        where[longest] = (where[longest] + shift) % values.shape[longest]
        spots.append(tuple(where))
    return values.at[spots[0]].set(smallest).at[spots[1]].set(top_value)


def spiked(values, stream_key, source, target, shards_of, factor):
    def block_of(position):
        return (jnp.arange(values.shape[position]) // (values.shape[position] // shards_of)).reshape((-1,) + (1,) * (values.ndim - 1 - position))

    one_side = jax.random.permutation(stream_key, shards_of)[block_of(target)]
    other_side = (block_of(target) + shards_of // 2) % shards_of
    return jnp.where((block_of(source) == one_side) | (block_of(source) == other_side), factor * values, values)


def level_of(stream_key, extent, cuts, low, largest):
    level, own = 1.0, jax.random.fold_in(stream_key, 6)
    for dim, parts in cuts:
        draws = jnp.exp(jax.random.uniform(jax.random.fold_in(own, dim), (parts,), jnp.float32, low / len(cuts), largest / len(cuts)))
        level = level * jnp.repeat(draws, extent[dim] // parts).reshape([-1 if axis == dim else 1 for axis in range(len(extent))])
    return level


def noise(key, shape, width, reach, shards=(), kind=jnp.bfloat16):
    values = width * jax.random.normal(key, shape, jnp.float32)
    if shards:
        values = values * level_of(key, shape, shards, -0.22, 0.18)
    return jnp.clip(values, -reach, reach).astype(kind)


def noise_with(key, dims, deviation, reach, cuts, heavy, held_as=jnp.bfloat16):
    values = deviation * jax.random.normal(key, dims, jnp.float32)
    if cuts:
        values = values * level_of(key, dims, cuts, -0.22, 0.18)
    return jnp.clip(spiked(values, jax.random.fold_in(key, 3), *heavy), -reach, reach).astype(held_as)


def setup_inputs(seed: int = 0) -> dict:
    streams_of = jax.random.split(jax.random.key(seed), 19)
    return {
        "inputs": noise_with(streams_of[0], (TOKENS, D), 1.0, 6.0, ((0, 8),), (0, 1, 8, 2.0)),
        "page_feat": noise(streams_of[1], (SEQS, PAGES, D), 1.0, 6.0, ((0, 8),)),
        "page_onehot": draw_page_onehot(jax.random.fold_in(streams_of[18], 71), 0),
        "lengths": draw_lengths(jax.random.fold_in(streams_of[18], 71), 0),
        "hor_pos": place_ends(jax.random.randint(streams_of[4], (TOKENS,), 0, 1000), jax.random.fold_in(streams_of[4], 1), 0, 999).astype(jnp.int32),
        "ver_pos": place_ends(jax.random.randint(streams_of[5], (TOKENS,), 0, 1000), jax.random.fold_in(streams_of[5], 1), 0, 999).astype(jnp.int32),
        "norm1_gain": jnp.clip(1.0 + 0.18 * jax.random.normal(streams_of[6], (D,), jnp.float32), 0.099609375, 1.8984375).astype(jnp.bfloat16),
        "w_query": noise(streams_of[7], (D, H * HD), D ** -0.5, 0.21875, ((1, 4),)),
        "w_key": noise(streams_of[8], (D, H * HD), D ** -0.5, 0.21875, ((1, 4),)),
        "w_value": noise(streams_of[9], (D, H * HD), D ** -0.5, 0.21875, ((1, 4),)),
        "rel_table": noise(streams_of[10], (H, NB), 0.7, 4.0, ((0, 4),)),
        "hor_table": noise(streams_of[11], (H, NB), 0.7, 4.0, ((0, 4),)),
        "ver_table": noise(streams_of[12], (H, NB), 0.7, 4.0, ((0, 4),)),
        "w_output": noise(streams_of[13], (H * HD, D), (H * HD // 16) ** -0.5, 0.875, ((0, 4),)),
        "norm2_gain": jnp.clip(1.0 + 0.18 * jax.random.normal(streams_of[14], (D,), jnp.float32), 0.099609375, 1.8984375).astype(jnp.bfloat16),
        "w_up": noise(streams_of[15], (D, FF), D ** -0.5, 0.21875, ((1, 4),)),
        "w_down": noise(streams_of[16], (FF, D), (FF // 2) ** -0.5, 0.15625, ((0, 4),)),
        "cotangent": draw_cotangent(jax.random.fold_in(streams_of[18], 71), 0),
    }


EPS = 1e-06
THRESHOLDS = (12, 16, 23, 32, 46, 64, 91)
HIGH = lax.Precision.HIGHEST

@jax.custom_vjp
def low(v):
    return lax.optimization_barrier(v.astype(jnp.bfloat16)).astype(jnp.float32)

@jax.custom_vjp
def low_back(v):
    return v

def low_keep(v):
    return (low(v), None)

def low_pass(kept, grad):
    return (grad,)

def back_keep(v):
    return (v, None)

def back_low(kept, grad):
    return (low(grad),)
low.defvjp(low_keep, low_pass)
low_back.defvjp(back_keep, back_low)

def bucket(delta):
    magnitude = jnp.abs(delta)
    coarse = 8 + sum(((magnitude >= limit).astype(jnp.int32) for limit in THRESHOLDS))
    return jnp.where(magnitude < 8, magnitude, coarse).astype(jnp.int32) + 16 * (delta > 0).astype(jnp.int32)

def matmul(left, right):
    return jnp.dot(left, right, precision=HIGH)

def normalize(field, gain_row):
    factor = lax.rsqrt(lax.optimization_barrier(jnp.mean(field * field, axis=-1, keepdims=True)) + EPS)
    return field * factor * gain_row

def forward(token_rows, feats, norm1_gain, w_query, w_key, w_value, rel_table, hor_table, ver_table, w_output, norm2_gain, w_up, w_down, onehot, length, hor_seq, ver_seq):
    seq_len = token_rows.shape[0]
    hidden_x = token_rows + matmul(onehot, feats)
    normed1 = low(normalize(hidden_x, norm1_gain))
    queries = low_back(low(matmul(normed1, w_query)))
    key_rows = low_back(low(matmul(normed1, w_key)))
    value_rows = low_back(low(matmul(normed1, w_value)))
    positions = jnp.arange(seq_len, dtype=jnp.int32)
    rel_ids = bucket(positions[None, :] - positions[:, None])
    hor_ids = bucket(hor_seq[None, :] - hor_seq[:, None])
    ver_ids = bucket(ver_seq[None, :] - ver_seq[:, None])
    valid = positions < length

    def per_head(pieces):
        head_query, head_key, head_value, rel_row, hor_row, ver_row = pieces
        bias_sum = rel_row[rel_ids] + hor_row[hor_ids] + ver_row[ver_ids]
        scores = low_back(0.125 * matmul(head_query, head_key.T) + bias_sum)
        scores = jnp.where(valid[None, :], scores, -1e+30)
        probs = jax.nn.softmax(scores, axis=-1)
        return matmul(low(probs), head_value)

    def split_heads(matrix):
        return matrix.reshape(seq_len, H, HD).transpose(1, 0, 2)
    heads_out = lax.map(jax.checkpoint(per_head), (split_heads(queries), split_heads(key_rows), split_heads(value_rows), low(rel_table), low(hor_table), low(ver_table)))
    attended = low_back(low(heads_out.transpose(1, 0, 2).reshape(seq_len, H * HD)))
    mixed = hidden_x + low_back(matmul(attended, w_output))
    normed2 = low(normalize(mixed, norm2_gain))
    upward = low_back(matmul(normed2, w_up))
    activated = low(jax.nn.gelu(upward))
    return mixed + low_back(matmul(activated, w_down))

def reference(inputs, page_feat, page_onehot, lengths, hor_pos, ver_pos, norm1_gain, w_query, w_key, w_value, rel_table, hor_table, ver_table, w_output, norm2_gain, w_up, w_down, cotangent):
    weights = tuple((weight_arg.astype(jnp.float32) for weight_arg in (norm1_gain, w_query, w_key, w_value, rel_table, hor_table, ver_table, w_output, norm2_gain, w_up, w_down)))
    seq_inputs = inputs.astype(jnp.float32).reshape(SEQS, SEQ_LEN, D)
    seq_feats = page_feat.astype(jnp.float32)
    seq_onehot = page_onehot.astype(jnp.float32).reshape(SEQS, SEQ_LEN, PAGES)
    seq_hor = hor_pos.reshape(SEQS, SEQ_LEN)
    seq_ver = ver_pos.reshape(SEQS, SEQ_LEN)
    seq_cotangent = cotangent.astype(jnp.float32).reshape(SEQS, SEQ_LEN, D)

    def step(carry, pieces):
        token_rows, feats, onehot, length, hor_seq, ver_seq, seq_grad = pieces

        def local(rows_arg, feats_arg, *params):
            return forward(rows_arg, feats_arg, *params, onehot, length, hor_seq, ver_seq)
        result, pullback = jax.vjp(local, token_rows, feats, *weights)
        grads = pullback(seq_grad)
        carry = tuple((running + gradient for running, gradient in zip(carry, grads[2:])))
        return (carry, (result.astype(jnp.bfloat16), grads[0], grads[1]))
    start = tuple((jnp.zeros_like(weight_arg) for weight_arg in weights))
    totals, (outputs, grad_rows, grad_feats) = lax.scan(step, start, (seq_inputs, seq_feats, seq_onehot, lengths, seq_hor, seq_ver, seq_cotangent))
    return (outputs.reshape(TOKENS, D), grad_rows.reshape(TOKENS, D), grad_feats, totals[0], totals[1], totals[2], totals[3], totals[4], totals[5], totals[6], totals[7], totals[8], totals[9], totals[10])
```

```python
import functools

import jax
import jax.numpy as jnp
import numpy as np
from jax import lax
from jax.experimental import pallas as pl
from jax.experimental.pallas import tpu as pltpu
from jax.sharding import PartitionSpec as P

EPS = 1e-06
THRESHOLDS = (12, 16, 23, 32, 46, 64, 91)
FAR = 91
HEADS = 3
HD = 64
PAD = 128
MARKS = 72
NEAR = 40
TILES = NEAR + 2
SPAN = 384
LOW = 92
TOP = 311
BF = jnp.bfloat16
F32 = jnp.float32
I32 = jnp.int32
FEED_PARTS = 3
GELU_C = float(np.sqrt(2.0 / np.pi))


def dot(left, right, dims=((1,), (0,))):
    return lax.dot_general(left, right, (dims, ((), ())), preferred_element_type=F32)


def bucket(delta):
    magnitude = jnp.abs(delta)
    coarse = 8 + sum((magnitude >= limit).astype(I32) for limit in THRESHOLDS)
    return jnp.where(magnitude < 8, magnitude, coarse) + 16 * (delta > 0).astype(I32)


def params(mib):
    return pltpu.CompilerParams(vmem_limit_bytes=mib * 2**20)


def cost(flops, nbytes):
    return pl.CostEstimate(flops=int(flops), bytes_accessed=int(nbytes), transcendentals=0)


def shape(dims, dtype):
    return jax.ShapeDtypeStruct(dims, dtype)


def whole(dims):
    return pl.BlockSpec(dims, lambda *a: (0,) * len(dims))


def hidden_rows(inputs, pages, feats):
    return inputs.astype(F32) + dot(pages.astype(F32).astype(BF), feats, ((0,), (0,)))


def unit_rows(field):
    factor = lax.rsqrt(jnp.mean(field * field, axis=-1, keepdims=True) + EPS)
    return field * factor, factor


def project_kernel(ids, x_ref, page_ref, feat_ref, gain_ref, wq_ref, wk_ref, wv_ref, n_ref, q_ref, k_ref, v_ref):
    step = pl.program_id(0)
    rows = x_ref.shape[0]
    unit, _ = unit_rows(hidden_rows(x_ref[...], page_ref[...], feat_ref[...]))
    normed = (unit * gain_ref[...].astype(F32)).astype(BF)
    n_ref[...] = normed
    lane = lax.broadcasted_iota(I32, (rows, PAD), 1)
    row = lax.broadcasted_iota(I32, (rows, PAD), 0) + step * rows
    masked = jnp.where((lane == HD) & (row >= ids[8]), -1e30, 0.0)
    block = lane - MARKS
    far_left = (block >= 0) & (block < 8) & (row < 128 * block - 96)
    far_right = (block >= 8) & (block < 16) & (row >= 128 * (block - 8) + 224)
    masked = jnp.where(far_left | far_right, 1.0, masked)
    query_extra = jnp.where(lane == HD, 1.0, 0.0)
    value_extra = jnp.where((lane == HD) | (lane == HD + 1), 1.0, 0.0)
    for out_ref, w_ref, extra, scale in (
        (q_ref, wq_ref, query_extra, 0.125),
        (k_ref, wk_ref, masked, None),
        (v_ref, wv_ref, value_extra, None),
    ):
        full = dot(normed, w_ref[...], ((1,), (1,)))
        if scale is not None:
            full = full * scale
        pair = full[:, :PAD]
        last = jnp.concatenate([full[:, PAD:], jnp.zeros((rows, PAD - HD), F32)], axis=1)
        heads = (pair, pltpu.roll(pair, HD, 1), last)
        for head in range(HEADS):
            out_ref[:, head * PAD : (head + 1) * PAD] = jnp.where(lane < HD, heads[head], extra).astype(BF)


def project(ids, inputs, onehot, feats, gain, w_query, w_key, w_value):
    seq, width = inputs.shape
    rows = 256
    columns = w_query.shape[0]
    wide = HEADS * PAD
    block = lambda cols: pl.BlockSpec((rows, cols), lambda i, s: (i, 0))
    lanes = lambda n: pl.BlockSpec((n, rows), lambda i, s: (0, i))
    return pl.pallas_call(
        project_kernel,
        grid_spec=pltpu.PrefetchScalarGridSpec(
            num_scalar_prefetch=1,
            grid=(seq // rows,),
            in_specs=[block(width), lanes(onehot.shape[0]), whole(feats.shape), whole(gain.shape)]
            + [whole((columns, width))] * 3,
            out_specs=[block(width), block(wide), block(wide), block(wide)],
        ),
        out_shape=[shape((seq, width), BF)] + [shape((seq, wide), BF)] * 3,
        compiler_params=params(24),
        cost_estimate=cost(2 * seq * width * 3 * columns, 4 * seq * width),
        name="project",
    )(ids, inputs, onehot, feats, gain, w_query, w_key, w_value)


def place(delta):
    magnitude = jnp.abs(delta)
    coarse = jnp.minimum(25 - lax.clz(delta * delta), 7)
    exact = magnitude < 8
    return jnp.where(exact, magnitude, coarse), exact, delta > 0


def look(table_ref, row, where):
    index, exact, after = where
    found = [jnp.take_along_axis(table_ref[row, part], index, axis=0) for part in range(4)]
    return jnp.where(after, jnp.where(exact, found[2], found[3]), jnp.where(exact, found[0], found[1]))


def tile_delta(tile):
    lane = lax.broadcasted_iota(I32, (8, 128), 1)
    sub = lax.broadcasted_iota(I32, (8, 128), 0)
    delta = 8 * (tile - 13) + sub - lane
    if tile == 0:
        delta = jnp.full_like(delta, -1000)
    if tile == TILES - 1:
        delta = jnp.full_like(delta, 1000)
    return delta


def attend_kernel(
    ids, q_ref, k_ref, v_ref, hor_ref, ver_ref, hor_all, ver_all, table_ref,
    e_ref, own_ref, other_ref, inv_ref, out_ref, s_ref, rel_ref, t8_ref, hor_col, ver_col, *, width, chunk,
):
    seq = k_ref.shape[0]
    lanes = width // 128
    step = pl.program_id(0)
    steps = seq // width

    @pl.when(step == 0)
    def _():
        for all_ref, col_ref in ((hor_all, hor_col), (ver_all, ver_col)):
            for b in range(seq // 128):
                cols = slice(128 * b, 128 * b + 128)
                spread = jnp.broadcast_to(all_ref[:, cols].astype(F32), (128, 128))
                col_ref[cols, :] = spread.T.astype(I32)
        for axis in range(3):
            for head in range(HEADS):
                at = axis * HEADS + head
                for part in range(4):
                    t8_ref[at, part] = jnp.broadcast_to(table_ref[8 * part : 8 * part + 8, at : at + 1], (8, 128))
        for tile in range(TILES):
            where = place(tile_delta(tile))
            for head in range(HEADS):
                rel_ref[head, tile] = look(t8_ref, head, where)

    queries = q_ref[...]
    for head in range(HEADS):
        cols = slice(head * PAD, (head + 1) * PAD)
        s_ref[head] = dot(k_ref[:, cols], queries[:, cols], ((1,), (1,)))
    hor = [jnp.broadcast_to(hor_ref[:, 128 * l : 128 * l + 128], (8, 128)) for l in range(lanes)]
    ver = [jnp.broadcast_to(ver_ref[:, 128 * l : 128 * l + 128], (8, 128)) for l in range(lanes)]
    first = ids[9 + step] * lanes

    def add_bias(c, tops):
        tops = list(tops)
        base = pl.multiple_of(c * chunk, chunk)
        for g in range(chunk // 8):
            rows = pl.ds(pl.multiple_of(base + 8 * g, 8), 8)
            hor_keys, ver_keys = hor_col[rows, :], ver_col[rows, :]
            for l in range(lanes):
                cols = pl.ds(128 * l, 128)
                hor_at, ver_at = place(hor_keys - hor[l]), place(ver_keys - ver[l])
                tile = jnp.clip(c * (chunk // 8) + g - 16 * (first + l) + 13, 0, TILES - 1)
                for head in range(HEADS):
                    s = s_ref[head, rows, cols] + rel_ref[head, tile]
                    s = s + (look(t8_ref, HEADS + head, hor_at) + look(t8_ref, 2 * HEADS + head, ver_at))
                    s_ref[head, rows, cols] = s
                    tops[head * lanes + l] = jnp.maximum(tops[head * lanes + l], s)
        return tuple(tops)

    tops = lax.fori_loop(
        0, seq // chunk, add_bias, tuple(jnp.full((8, 128), -1e30, F32) for _ in range(HEADS * lanes))
    )
    peaks = [jnp.broadcast_to(jnp.max(top, axis=0, keepdims=True), (16, 128)) for top in tops]

    def exps(c, carry):
        for g in range(4):
            rows = pl.ds(pl.multiple_of(c * 64 + 16 * g, 16), 16)
            for l in range(lanes):
                cols = pl.ds(128 * l, 128)
                for head in range(HEADS):
                    e_ref[head, rows, cols] = jnp.exp(s_ref[head, rows, cols] - peaks[head * lanes + l]).astype(BF)
        return carry

    lax.fori_loop(0, seq // 64, exps, 0)
    for head in range(HEADS):
        total = dot(v_ref[:, head * PAD : (head + 1) * PAD], e_ref[head], ((0,), (0,)))
        inverse = 1.0 / total[HD : HD + 1, :]
        inv_ref[head : head + 1, :] = inverse
        out_ref[head * HD : (head + 1) * HD, :] = total[:HD] * inverse

    @pl.when(step < steps // 2)
    def _():
        other_ref[...] = out_ref[...].astype(BF)

    @pl.when(step >= steps // 2)
    def _():
        own_ref[...] = out_ref[...].astype(BF)


def attend(ids, queries, keys, values, hor, ver, tables):
    seq, wide = queries.shape
    width = 256
    steps = seq // width
    half = steps // 2
    columns = HEADS * HD
    at = lambda i, s: (0, s[9 + i])
    return pl.pallas_call(
        functools.partial(attend_kernel, width=width, chunk=32),
        grid_spec=pltpu.PrefetchScalarGridSpec(
            num_scalar_prefetch=1,
            grid=(steps,),
            in_specs=[
                pl.BlockSpec((width, wide), lambda i, s: (s[9 + i], 0)),
                whole(keys.shape),
                whole(values.shape),
                pl.BlockSpec((1, width), at),
                pl.BlockSpec((1, width), at),
                whole(hor.shape),
                whole(ver.shape),
                whole(tables.shape),
            ],
            out_specs=[
                pl.BlockSpec((HEADS, seq, width), lambda i, s: (0, 0, s[9 + i])),
                pl.BlockSpec((columns, width), lambda i, s: (0, jnp.maximum(i - half, 0))),
                pl.BlockSpec((columns, width), lambda i, s: (0, jnp.minimum(i, half - 1))),
                pl.BlockSpec((HEADS, width), at),
                pl.BlockSpec((columns, width), at),
            ],
            scratch_shapes=[
                pltpu.VMEM((HEADS, seq, width), F32),
                pltpu.VMEM((HEADS, TILES, 8, 128), F32),
                pltpu.VMEM((3 * HEADS, 4, 8, 128), F32),
                pltpu.VMEM((seq, 128), I32),
                pltpu.VMEM((seq, 128), I32),
            ],
        ),
        out_shape=[
            shape((HEADS, seq, seq), BF),
            shape((columns, seq // 2), BF),
            shape((columns, seq // 2), BF),
            shape((HEADS, seq), F32),
            shape((columns, seq), F32),
        ],
        compiler_params=params(32),
        cost_estimate=cost(25e9, 10e6),
        name="attend",
    )(ids, queries, keys, values, hor, ver, hor, ver, tables)


def feed_kernel(
    ids, x_ref, page_ref, feat_ref, gain_ref, cot_ref, a0, a1, a2, a3, o0, o1, o2, o3, u0, u1, d0, d1,
    act0, act1, up0, up1, n_ref, mixed_ref, grad_ref, ffn_ref, grad_sum, ffn_sum,
):
    step = pl.program_id(0)
    half = pl.num_programs(0) // 2

    @pl.when(step == 0)
    def _():
        mixed = hidden_rows(x_ref[...], page_ref[...], feat_ref[...])
        for a_ref, o_ref in ((a0, o0), (a1, o1), (a2, o2), (a3, o3)):
            mixed = mixed + dot(a_ref[...], o_ref[...], ((0,), (0,)))
        mixed_ref[...] = mixed
        unit, _ = unit_rows(mixed)
        n_ref[...] = (unit * gain_ref[...].astype(F32)).astype(BF)
        grad_sum[...] = jnp.zeros_like(grad_sum)
        ffn_sum[...] = jnp.zeros_like(ffn_sum)

    def part(u_ref, d_ref, act_ref, up_ref):
        upward = dot(n_ref[...], u_ref[...])
        square = upward * upward
        tanh = jnp.tanh(GELU_C * upward * (1.0 + 0.044715 * square))
        lifted = 0.5 * (1.0 + tanh)
        activated = (upward * lifted).astype(BF)
        slope = lifted + 0.5 * upward * (1.0 - tanh * tanh) * (GELU_C * (1.0 + 3 * 0.044715 * square))
        grad_up = (dot(cot_ref[...], d_ref[...], ((1,), (1,))) * slope).astype(BF)
        act_ref[...] = activated
        up_ref[...] = grad_up
        ffn_sum[...] += dot(activated, d_ref[...])
        grad_sum[...] += dot(grad_up, u_ref[...], ((1,), (1,)))

    @pl.when(step < half)
    def _():
        part(u0, d0, act0, up0)

    @pl.when(step >= half)
    def _():
        part(u1, d1, act1, up1)

    @pl.when(step == 2 * half - 1)
    def _():
        grad_ref[...] = grad_sum[...].astype(grad_ref.dtype)
        ffn_ref[...] = ffn_sum[...].astype(ffn_ref.dtype)


def feed(ids, own, inputs, onehot, feats, gain, cotangent, attended, w_outputs, ups, downs):
    seq, width = inputs.shape
    rows = seq // 4
    units = ups[0].shape[1]
    half = FEED_PARTS
    chunk = units // half
    slot = 16 if own else 17
    quarter = lambda cols: pl.BlockSpec((rows, cols), lambda i, s: (s[slot], 0))
    pages = pl.BlockSpec((onehot.shape[0], rows), lambda i, s: (0, s[slot]))
    columns = HEADS * HD
    att = pl.BlockSpec((columns, rows), lambda i, s: (0, s[slot + 2]))
    low = lambda i: jnp.minimum(i, half - 1)
    high = lambda i: jnp.maximum(i - half, 0)
    kept = F32 if own else BF
    flops = 2 * rows * width * (width + 2 * units * 4)
    return pl.pallas_call(
        feed_kernel,
        grid_spec=pltpu.PrefetchScalarGridSpec(
            num_scalar_prefetch=1,
            grid=(2 * half,),
            in_specs=[quarter(width), pages, whole(feats.shape), whole(gain.shape), quarter(width)]
            + [att] * 4
            + [whole((columns, width))] * 4
            + [
                pl.BlockSpec((width, chunk), lambda i, s: (0, low(i))),
                pl.BlockSpec((width, chunk), lambda i, s: (0, high(i))),
                pl.BlockSpec((chunk, width), lambda i, s: (low(i), 0)),
                pl.BlockSpec((chunk, width), lambda i, s: (high(i), 0)),
            ],
            out_specs=[
                pl.BlockSpec((rows, chunk), lambda i, s: (0, low(i))),
                pl.BlockSpec((rows, chunk), lambda i, s: (0, high(i))),
                pl.BlockSpec((rows, chunk), lambda i, s: (0, low(i))),
                pl.BlockSpec((rows, chunk), lambda i, s: (0, high(i))),
                whole((rows, width)),
                whole((rows, width)),
                whole((rows, width)),
                whole((rows, width)),
            ],
            scratch_shapes=[pltpu.VMEM((rows, width), F32), pltpu.VMEM((rows, width), F32)],
        ),
        out_shape=[shape((rows, units), BF)] * 4
        + [shape((rows, width), BF), shape((rows, width), F32), shape((rows, width), kept), shape((rows, width), kept)],
        compiler_params=params(40),
        cost_estimate=cost(flops, 8e6),
        name="feed_own" if own else "feed_other",
    )(ids, inputs, onehot, feats, gain, cotangent, *attended, *w_outputs, *ups, *downs)


def mid_kernel(ids, mine_ref, sent_ref, mixed_ref, gain_ref, cot_ref, o0, o1, o2, o3, grad_ref, low_ref, g0, g1, g2, g3, part_ref):
    grad_normed = mine_ref[...] + sent_ref[...].astype(F32)
    unit, factor = unit_rows(mixed_ref[...])
    scaled = grad_normed * gain_ref[...].astype(F32)
    grad = factor * (scaled - unit * jnp.mean(scaled * unit, axis=-1, keepdims=True))
    grad = cot_ref[...].astype(F32) + grad
    grad_ref[...] = grad
    low = grad.astype(BF)
    low_ref[...] = low
    part_ref[...] = jnp.sum(grad_normed * unit, axis=0, keepdims=True)
    for o_ref, g_ref in ((o0, g0), (o1, g1), (o2, g2), (o3, g3)):
        g_ref[...] = dot(o_ref[...], low, ((1,), (1,))).astype(BF)


def mid(ids, mine, sent, mixed, gain, cotangent, w_outputs):
    rows, width = mine.shape
    columns = HEADS * HD
    full = whole((rows, width))
    return pl.pallas_call(
        mid_kernel,
        grid_spec=pltpu.PrefetchScalarGridSpec(
            num_scalar_prefetch=1,
            grid=(1,),
            in_specs=[full, full, full, whole(gain.shape), pl.BlockSpec((rows, width), lambda i, s: (s[16], 0))]
            + [whole((columns, width))] * 4,
            out_specs=[full, full] + [whole((columns, rows))] * 4 + [whole((1, width))],
        ),
        out_shape=[shape((rows, width), F32), shape((rows, width), BF)]
        + [shape((columns, rows), BF)] * 4
        + [shape((1, width), F32)],
        compiler_params=params(24),
        cost_estimate=cost(2 * rows * width * width, 4e6),
        name="mid",
    )(ids, mine, sent, mixed, gain, cotangent, *w_outputs)


def back_kernel(*refs, first):
    ids, ea_ref, eb_ref, qa_ref, qb_ref, inv_a, inv_b, out_a, out_b, k_ref, v_ref, ga_ref, gb_ref = refs[:13]
    refs = refs[13:]
    if first:
        ds_ref, dqa_ref, dqb_ref, key_ref, value_ref, near_ref, far_ref, x_ref = refs
    else:
        key_in, value_in, near_in, far_in = refs[:4]
        ds_ref, dqa_ref, dqb_ref, keep_ref, send_ref, near_ref, far_ref, x_ref = refs[4:]
    head = pl.program_id(0)
    seq = k_ref.shape[0]
    width = qa_ref.shape[0]
    both = 2 * width
    lanes = width // 128
    base = 0 if first else 2

    sub = lax.broadcasted_iota(I32, (HD, both), 0)
    head_sub = lax.broadcasted_iota(I32, (8, both), 0)
    inverse = jnp.concatenate([inv_a[...], inv_b[...]], axis=1)
    inverse = jnp.sum(jnp.where(head_sub[: inverse.shape[0]] == head, inverse, 0.0), axis=0, keepdims=True)
    grad = jnp.concatenate([ga_ref[...], gb_ref[...]], axis=1).astype(F32)
    grad = (grad * inverse).astype(BF).astype(F32)
    inner = jnp.sum(grad * jnp.concatenate([out_a[...], out_b[...]], axis=1), axis=0, keepdims=True)
    high = inner.astype(BF).astype(F32)
    extra = jnp.where(sub == 0, -high, jnp.where(sub == 1, high - inner, 0.0))
    right = jnp.concatenate([grad, extra], axis=0).astype(BF)
    x_ref[...] = dot(v_ref[...], right)
    value = dot(ea_ref[0], right[:, :width], ((1,), (1,))) + dot(eb_ref[0], right[:, width:], ((1,), (1,)))

    def grad_scores(c, carry):
        rows = pl.ds(pl.multiple_of(c * 64, 64), 64)
        for part, e_ref in enumerate((ea_ref, eb_ref)):
            cols = slice(part * width, part * width + width)
            ds_ref[0, rows, cols] = (e_ref[0, rows, :].astype(F32) * x_ref[rows, cols]).astype(BF)
        return carry

    lax.fori_loop(0, seq // 64, grad_scores, 0)
    grad = ds_ref[0]
    key = dot(grad, jnp.concatenate([qa_ref[...], qb_ref[...]], axis=0))
    query = dot(k_ref[...], grad, ((0,), (0,)))
    dqa_ref[...] = (query[:HD, :width] * 0.125).astype(BF)
    dqb_ref[...] = (query[:HD, width:] * 0.125).astype(BF)

    blocks = [ids[base + l // lanes] * lanes + l % lanes for l in range(2 * lanes)]
    for g in range(NEAR // 2):
        total = None if first else near_in[0, 16 * g : 16 * g + 16]
        for l, block in enumerate(blocks):
            start = 128 * block - 96 + 16 * g
            inside = (start >= 0) & (start < seq)
            rows = pl.ds(pl.multiple_of(jnp.clip(start, 0, seq - 16), 16), 16)
            found = ds_ref[0, rows, 128 * l : 128 * l + 128].astype(F32)
            found = jnp.where(inside, found, 0.0)
            total = found if total is None else total + found
        near_ref[0, 16 * g : 16 * g + 16] = total
    spot = lax.broadcasted_iota(I32, (8, 128), 0)
    for side in range(2):
        total = None if first else far_in[0, 8 * side : 8 * side + 8]
        for l, block in enumerate(blocks):
            marks = query[MARKS + 8 * side : MARKS + 8 * side + 8, 128 * l : 128 * l + 128]
            marks = jnp.where(spot == block, marks, 0.0)
            total = marks if total is None else total + marks
        far_ref[0, 8 * side : 8 * side + 8] = total

    if first:
        key_ref[...] = key
        value_ref[...] = value
    else:
        for part, acc in ((0, key_in[...] + key), (1, value_in[...] + value)):
            turned = acc.T[:HD].astype(BF)
            for k in range(4):
                goal = keep_ref if k % 2 == 0 else send_ref
                for q in range(4):

                    @pl.when(ids[k] == q)
                    def _(goal=goal, k=k, q=q, part=part, turned=turned):
                        goal[k // 2, part] = turned[:, q * width : (q + 1) * width]


def back(ids, e, queries, inverse, out, keys, values, grad_a, grad_b, carried):
    seq, wide = queries.shape
    width = seq // 4
    first = carried is None
    base = 0 if first else 2
    columns = HEADS * HD
    head_cols = pl.BlockSpec((seq, PAD), lambda h, s: (0, h))
    grad_rows = pl.BlockSpec((HD, width), lambda h, s: (h, 0))
    near = pl.BlockSpec((1, 8 * NEAR, 128), lambda h, s: (h, 0, 0))
    far = pl.BlockSpec((1, 16, 128), lambda h, s: (h, 0, 0))
    pieces = pl.BlockSpec((2, 2, HD, width), lambda h, s: (0, 0, h, 0))
    sums = [(shape((seq, wide), F32), head_cols)] * 2
    rel = [(shape((HEADS, 8 * NEAR, 128), F32), near), (shape((HEADS, 16, 128), F32), far)]
    outs = [(shape((HEADS, seq, 2 * width), BF), pl.BlockSpec((1, seq, 2 * width), lambda h, s: (h, 0, 0)))]
    outs += [(shape((columns, width), BF), grad_rows)] * 2
    outs += sums if first else [(shape((2, 2, columns, width), BF), pieces)] * 2
    outs += rel
    specs = []
    for make in (
        lambda q: pl.BlockSpec((1, seq, width), lambda h, s: (h, 0, s[q])),
        lambda q: pl.BlockSpec((width, PAD), lambda h, s: (s[q], h)),
        lambda q: pl.BlockSpec((HEADS, width), lambda h, s: (0, s[q])),
        lambda q: pl.BlockSpec((HD, width), lambda h, s: (h, s[q])),
    ):
        specs += [make(base), make(base + 1)]
    specs += [head_cols, head_cols, grad_rows, grad_rows]
    if not first:
        specs += [spec for _, spec in sums + rel]
    return pl.pallas_call(
        functools.partial(back_kernel, first=first),
        grid_spec=pltpu.PrefetchScalarGridSpec(
            num_scalar_prefetch=1,
            grid=(HEADS,),
            in_specs=specs,
            out_specs=[spec for _, spec in outs],
            scratch_shapes=[pltpu.VMEM((seq, 2 * width), F32)],
        ),
        out_shape=[o for o, _ in outs],
        compiler_params=params(40),
        cost_estimate=cost(6e9, 10e6),
        name="back_first" if first else "back_last",
    )(ids, e, e, queries, queries, inverse, inverse, out, out, keys, values, grad_a, grad_b, *(() if first else carried))


def tables_kernel(ids, s_ref, t_ref, keys_ref, q0, q1, q2, q3, near_ref, far_ref, out_ref, e_ref, y_ref):
    axis, block = pl.program_id(0), pl.program_id(1)
    places, seq = e_ref.shape
    width = s_ref.shape[2]
    groups = places // 128

    @pl.when(block == 0)
    def _():
        spot = lax.broadcasted_iota(I32, (places, seq), 0)
        e_ref[...] = jnp.where(spot == keys_ref[0], 1.0, 0.0).astype(BF)

    def windows(scores_ref, query):
        column = lax.broadcasted_iota(I32, (SPAN, width), 0)
        right = [
            jnp.where(column == jnp.clip(128 * b + TOP - LOW - query, 0, TOP), 1.0, 0.0).astype(BF) for b in range(groups)
        ]
        left = []
        for head in range(HEADS):
            moved = dot(e_ref[...], scores_ref[head]).astype(BF)
            left.append(jnp.concatenate([moved[128 * b : 128 * b + 128] for b in range(groups)], axis=1))
        return dot(jnp.concatenate(left, axis=0), jnp.concatenate(right, axis=1), ((1,), (1,)))

    @pl.when(block == 0)
    def _():
        y_ref[...] = windows(s_ref, jnp.concatenate([q0[0], q1[0]], axis=1))

    @pl.when(block == 1)
    def _():
        y_ref[...] += windows(t_ref, jnp.concatenate([q2[0], q3[0]], axis=1))

    def to_buckets(row, sums, delta):
        found = bucket(delta)
        spot = lax.broadcasted_iota(I32, (32, sums.shape[1]), 0)
        out_ref[row] = jnp.sum(jnp.where(found == spot, sums, 0.0), axis=1, keepdims=True)

    @pl.when(block == 1)
    def _():
        lane = lax.broadcasted_iota(I32, (1, 512), 1)
        for head in range(HEADS):
            grid = jnp.concatenate([y_ref[head * 128 : head * 128 + 128, :], jnp.zeros((128, 512 - SPAN), F32)], axis=1)
            grid = pltpu.roll(grid, 0, 1, stride=1, stride_axis=0)
            sums = jnp.sum(grid, axis=0, keepdims=True)
            to_buckets(head + HEADS * (1 + axis), sums, lane + LOW - TOP)

        @pl.when(axis == 0)
        def _():
            flip = 7 - lax.broadcasted_iota(I32, (8, 128), 0)
            for head in range(HEADS):
                near = [
                    jnp.take_along_axis(near_ref[head, 8 * t : 8 * t + 8], flip, axis=0) for t in reversed(range(NEAR))
                ]
                grid = jnp.concatenate(near, axis=0)
                grid = jnp.concatenate([grid, jnp.zeros((8 * NEAR, 384), F32)], axis=1)
                grid = pltpu.roll(grid, 0, 1, stride=1, stride_axis=0)
                sums = jnp.sum(grid, axis=0, keepdims=True)
                to_buckets(head, sums, 8 * NEAR - 1 - 8 * 12 - lane)
                spot = lax.broadcasted_iota(I32, (32, 1), 0)
                left = jnp.sum(jnp.sum(far_ref[head, :8], axis=0, keepdims=True), axis=1, keepdims=True)
                right = jnp.sum(jnp.sum(far_ref[head, 8:], axis=0, keepdims=True), axis=1, keepdims=True)
                out_ref[head] += jnp.where(spot == 15, left, 0.0) + jnp.where(spot == 31, right, 0.0)


def table_grads(ids, scores_a, scores_b, positions, near, far):
    seq = positions.shape[2]
    width = seq // 4
    places = 1024
    quarter = lambda k: pl.BlockSpec((1, 1, width), lambda a, b, s: (a, 0, s[k]))
    return pl.pallas_call(
        tables_kernel,
        grid_spec=pltpu.PrefetchScalarGridSpec(
            num_scalar_prefetch=1,
            grid=(2, 2),
            in_specs=[
                whole(scores_a.shape),
                whole(scores_b.shape),
                pl.BlockSpec((1, 1, seq), lambda a, b, s: (a, 0, 0)),
                quarter(0),
                quarter(1),
                quarter(2),
                quarter(3),
                whole(near.shape),
                whole(far.shape),
            ],
            out_specs=whole((3 * HEADS, 32, 1)),
            scratch_shapes=[pltpu.VMEM((places, seq), BF), pltpu.VMEM((HEADS * 128, SPAN), F32)],
        ),
        out_shape=shape((3 * HEADS, 32, 1), F32),
        compiler_params=params(48),
        cost_estimate=cost(16e9, 8e6),
        name="table_grads",
    )(ids, scores_a, scores_b, positions, positions, positions, positions, positions, near, far)


def terms_kernel(w0, w1, w2, p0, p1, p2, mine_q, mine_kv, sent_q, sent_kv, out_ref):
    total = None
    for refs, q_ref, kv_ref in (((w0, w1, w2), mine_q, mine_kv), ((p0, p1, p2), sent_q, sent_kv)):
        for w_ref, grad in zip(refs, (q_ref[...], kv_ref[0, 0], kv_ref[0, 1])):
            found = dot(grad, w_ref[...], ((0,), (0,)))
            total = found if total is None else total + found
    out_ref[...] = total.astype(out_ref.dtype)


def terms(own, weights, partner, mine_q, mine_kv, sent_q, sent_kv):
    columns, width = weights[0].shape
    rows = mine_q.shape[1]
    slot = 0 if own else 1
    pieces = pl.BlockSpec((1, 2, columns, rows), lambda i: (slot, 0, 0, 0))
    return pl.pallas_call(
        terms_kernel,
        grid=(1,),
        in_specs=[whole(weights[0].shape)] * 6 + [whole((columns, rows)), pieces] * 2,
        out_specs=whole((rows, width)),
        out_shape=shape((rows, width), F32 if own else BF),
        compiler_params=params(16),
        cost_estimate=cost(2 * rows * width * columns * 6, 3e6),
        name="terms_own" if own else "terms_other",
    )(*weights, *partner, mine_q, mine_kv, sent_q, sent_kv)


def last_kernel(ids, mine_ref, sent_ref, x_ref, page_ref, feat_ref, gain_ref, grad_ref, out_ref, part_ref):
    grad_normed = mine_ref[...] + sent_ref[...].astype(F32)
    unit, factor = unit_rows(hidden_rows(x_ref[...], page_ref[...], feat_ref[...]))
    scaled = grad_normed * gain_ref[...].astype(F32)
    grad = factor * (scaled - unit * jnp.mean(scaled * unit, axis=-1, keepdims=True))
    out_ref[...] = (grad_ref[...] + grad).astype(BF)
    part_ref[...] = jnp.sum(grad_normed * unit, axis=0, keepdims=True)


def last(ids, mine, sent, inputs, onehot, feats, gain, grad_mixed):
    rows, width = mine.shape
    full = whole((rows, width))
    quarter = lambda cols: pl.BlockSpec((rows, cols), lambda i, s: (s[16], 0))
    pages = pl.BlockSpec((onehot.shape[0], rows), lambda i, s: (0, s[16]))
    return pl.pallas_call(
        last_kernel,
        grid_spec=pltpu.PrefetchScalarGridSpec(
            num_scalar_prefetch=1,
            grid=(1,),
            in_specs=[full, full, quarter(width), pages, whole(feats.shape), whole(gain.shape), full],
            out_specs=[full, whole((1, width))],
        ),
        out_shape=[shape((rows, width), BF), shape((1, width), F32)],
        compiler_params=params(16),
        cost_estimate=cost(1e8, 4e6),
        name="last",
    )(ids, mine, sent, inputs, onehot, feats, gain, grad_mixed)


def join_kernel(ids, b0, b1, b2, b3, out_ref):
    for k, b_ref in enumerate((b0, b1, b2, b3)):

        @pl.when(pl.program_id(0) == k)
        def _(b_ref=b_ref):
            out_ref[...] = b_ref[...].astype(out_ref.dtype)


def join_feat_kernel(ids, b0, b1, b2, b3, page_ref, out_ref, feat_ref, all_ref):
    step = pl.program_id(0)
    rows = b0.shape[0]
    for k, b_ref in enumerate((b0, b1, b2, b3)):

        @pl.when(step == k)
        def _(b_ref=b_ref, k=k):
            out_ref[...] = b_ref[...].astype(out_ref.dtype)
            all_ref[pl.ds(pl.multiple_of(ids[k] * rows, rows), rows), :] = b_ref[...]

    @pl.when(step == 3)
    def _():
        feat_ref[...] = dot(page_ref[...].astype(F32).astype(BF), all_ref[...])


def join(ids, blocks, dtype, onehot=None):
    rows, width = blocks[0].shape
    specs = [whole((rows, width))] * 4
    outs, out_specs = [shape((4 * rows, width), dtype)], [pl.BlockSpec((rows, width), lambda i, s: (s[i], 0))]
    extra, scratch = (), []
    if onehot is not None:
        pages = onehot.shape[0]
        specs = specs + [whole(onehot.shape)]
        outs.append(shape((pages, width), F32))
        out_specs.append(whole((pages, width)))
        extra, scratch = (onehot,), [pltpu.VMEM((4 * rows, width), BF)]
    found = pl.pallas_call(
        join_kernel if onehot is None else join_feat_kernel,
        grid_spec=pltpu.PrefetchScalarGridSpec(
            num_scalar_prefetch=1, grid=(4,), in_specs=specs, out_specs=out_specs, scratch_shapes=scratch
        ),
        out_shape=outs,
        compiler_params=params(16),
        cost_estimate=cost(1e6, 6e6),
        name="join_output" if onehot is None else "join_grads",
    )(ids, *blocks, *extra)
    return found[0] if onehot is None else found


def split_rows(ids, total, keep_ref, send_ref, parity):
    groups, size = keep_ref.shape[0], keep_ref.shape[1]
    for g in range(groups):
        mine = pl.multiple_of((2 * g + parity) * size, 8)
        theirs = pl.multiple_of((2 * g + 1 - parity) * size, 8)
        keep_ref[g] = total[pl.ds(mine, size), :].astype(keep_ref.dtype)
        send_ref[g] = total[pl.ds(theirs, size), :].astype(BF)


def feed_grad_kernel(ids, *refs, fast, blocks):
    lefts, rights = refs[:blocks], refs[blocks : 2 * blocks]
    outs = refs[2 * blocks :]
    left = jnp.concatenate([r[...] for r in lefts], axis=0)
    right = jnp.concatenate([r[...] for r in rights], axis=0)
    total = outs[-1]
    total[...] = dot(left, right, ((0,), (0,)))
    if fast:
        split_rows(ids, total, outs[0], outs[1], ids[13])
    else:
        outs[0][...] = total[...]


def feed_grad(ids, lefts, left_places, rights, fast, name):
    blocks = len(rights)
    rows, units = rights[0].shape
    width = lefts[0].shape[1]
    specs = []
    for left, spot in zip(lefts, left_places):
        if spot is None:
            specs.append(whole((rows, width)))
        else:
            specs.append(pl.BlockSpec((rows, width), functools.partial(lambda i, s, spot: (s[spot], 0), spot=spot)))
    specs += [whole((rows, units))] * blocks
    if fast:
        outs = [shape((4, width // 8, units), F32), shape((4, width // 8, units), BF)]
    else:
        outs = [shape((width, units), F32)]
    return pl.pallas_call(
        functools.partial(feed_grad_kernel, fast=fast, blocks=blocks),
        grid_spec=pltpu.PrefetchScalarGridSpec(
            num_scalar_prefetch=1,
            grid=(1,),
            in_specs=specs,
            out_specs=[whole(o.shape) for o in outs],
            scratch_shapes=[pltpu.VMEM((width, units), F32)],
        ),
        out_shape=outs,
        compiler_params=params(32),
        cost_estimate=cost(2 * blocks * rows * width * units, 8e6),
        name=name,
    )(ids, *lefts, *rights)


def head_grad_kernel(ids, n0, n1, n2, n3, q0, q1, q2, q3, keep_kv, send_kv, l0, l1, l2, l3, a0, a1, a2, a3, *outs, fast):
    total, turned = outs[-2:]
    n = q0.shape[0]
    normed = jnp.concatenate([r[...] for r in (n0, n1, n2, n3)], axis=0)
    low = jnp.concatenate([r[...] for r in (l0, l1, l2, l3)], axis=0)
    pieces = [[r[...] for r in (q0, q1, q2, q3)]]
    for part in range(2):
        pieces.append([keep_kv[0, part], send_kv[0, part], keep_kv[1, part], send_kv[1, part]])
    pieces.append([r[...] for r in (a0, a1, a2, a3)])
    for at, piece in enumerate(pieces):
        right = low if at == 3 else normed
        total[at * n : (at + 1) * n, :] = dot(jnp.concatenate(piece, axis=1), right)
    turned[...] = total[...].T
    if fast:
        split_rows(ids, turned, outs[0], outs[1], ids[13])
    else:
        outs[0][...] = turned[...]


def head_grad(ids, normed, grad_q, keep_kv, send_kv, lows, own, other, fast):
    seq, width = normed.shape
    rows = seq // 4
    n = grad_q[0].shape[0]
    quarter = lambda k: pl.BlockSpec((rows, width), lambda i, s: (s[k], 0))
    halves = lambda k: pl.BlockSpec((n, rows), lambda i, s: (0, s[20 + k]))
    specs = [quarter(k) for k in range(4)]
    specs += [whole((n, rows))] * 4 + [whole(keep_kv.shape)] * 2 + [whole((rows, width))] * 4
    specs += [halves(k) for k in range(4)]
    if fast:
        outs = [shape((4, width // 8, 4 * n), F32), shape((4, width // 8, 4 * n), BF)]
    else:
        outs = [shape((width, 4 * n), F32)]
    return pl.pallas_call(
        functools.partial(head_grad_kernel, fast=fast),
        grid_spec=pltpu.PrefetchScalarGridSpec(
            num_scalar_prefetch=1,
            grid=(1,),
            in_specs=specs,
            out_specs=[whole(o.shape) for o in outs],
            scratch_shapes=[pltpu.VMEM((4 * n, width), F32), pltpu.VMEM((width, 4 * n), F32)],
        ),
        out_shape=outs,
        compiler_params=params(32),
        cost_estimate=cost(2 * seq * width * 4 * n, 8e6),
        name="head_grad",
    )(ids, *[normed] * 4, *grad_q, keep_kv, send_kv, *lows, own, other, own, other)


def pair_kernel(ids, keep_ref, got_ref, o0, o1, o2, o3):
    for k, o_ref in enumerate((o0, o1, o2, o3)):
        at = ids[24 + k]
        o_ref[...] = (keep_ref[at] + got_ref[at].astype(F32)).astype(o_ref.dtype)


def pair_sum(ids, keep, got):
    _, size, n = keep.shape
    return pl.pallas_call(
        pair_kernel,
        grid_spec=pltpu.PrefetchScalarGridSpec(
            num_scalar_prefetch=1,
            grid=(1,),
            in_specs=[whole(keep.shape), whole(got.shape)],
            out_specs=[whole((size, n))] * 4,
        ),
        out_shape=[shape((size, n), F32)] + [shape((size, n), BF)] * 3,
        compiler_params=params(16),
        cost_estimate=cost(1e6, 4e6),
        name="pair_sum",
    )(ids, keep, got)


def feed_final_kernel(a0, a1, a2, a3, b0, b1, b2, b3, up_ref, down_ref):
    up_ref[...] = a0[...] + a1[...].astype(F32) + a2[...].astype(F32) + a3[...].astype(F32)
    down_ref[...] = b0[...] + b1[...].astype(F32) + b2[...].astype(F32) + b3[...].astype(F32)


def head_final_kernel(a0, a1, a2, a3, q_ref, k_ref, v_ref, o_ref):
    total = a0[...] + a1[...].astype(F32) + a2[...].astype(F32) + a3[...].astype(F32)
    n = q_ref.shape[1]
    q_ref[...] = total[:, :n]
    k_ref[...] = total[:, n : 2 * n]
    v_ref[...] = total[:, 2 * n : 3 * n]
    o_ref[...] = total[:, 3 * n :].T


def finish(kernel, arrays, outs, name):
    return pl.pallas_call(
        kernel,
        grid=(1,),
        in_specs=[whole(a.shape) for a in arrays],
        out_specs=[whole(o.shape) for o in outs],
        out_shape=outs,
        compiler_params=params(16),
        cost_estimate=cost(1e6, 3e6),
        name=name,
    )(*arrays)


def swap(array, axis, size, bits):
    return lax.ppermute(array, axis, [(i, i ^ bits) for i in range(size)])


def after(arrays, *others):
    return lax.optimization_barrier((tuple(arrays), others))[0]


def local(
    inputs, page_feat, page_onehot, lengths, hor_pos, ver_pos, norm1_gain, w_query, w_key, w_value,
    rel_table, hor_table, ver_table, w_output, norm2_gain, w_up, w_down, cotangent, *, dp,
):
    seq, width = inputs.shape
    fast = dp == 8
    over = functools.partial(swap, axis="mp", size=4)
    m = lax.axis_index("mp").astype(I32)
    d = lax.axis_index("dp").astype(I32)
    k4 = jnp.arange(4, dtype=I32)
    spot = lambda who: (who & 1) * 2 + (who >> 1)
    core, chip = m & 1, m >> 1
    ids = jnp.concatenate([
        spot(m ^ k4),
        k4 * 0,
        lengths[:1],
        (k4 + 2 * (1 - core)) % 4,
        (d & 1)[None],
        (k4 * 0)[:2],
        jnp.stack([spot(m), spot(m ^ 2), chip, 1 - chip]),
        jnp.stack([chip, chip, 1 - chip, 1 - chip]),
        (d >> 1) ^ k4,
    ])
    gain_one, gain_two = norm1_gain[None], norm2_gain[None]
    feats = page_feat[0]
    hor, ver = hor_pos[None], ver_pos[None]
    tables = jnp.concatenate([rel_table, hor_table, ver_table], axis=0).astype(F32).T
    pages = page_onehot.T
    weights = [w_query.T, w_key.T, w_value.T]

    normed1, queries, keys, values = project(ids, inputs, pages, feats, gain_one, *weights)

    own_weights = after([w_output, w_up, w_down, *weights], normed1)
    w_output, w_up, w_down = own_weights[:3]
    wo_y = over(w_output, bits=2)
    w_outputs = [w_output, over(w_output, bits=1), wo_y, over(wo_y, bits=1)]
    ups = [w_up, over(w_up, bits=1)]
    downs = [w_down, over(w_down, bits=1)]
    partner = [over(w, bits=1) for w in own_weights[3:]]

    e, att_own, att_other, inverse, out = attend(ids, queries, keys, values, hor, ver, tables)
    attended = [att_own, over(att_other, bits=1), over(att_own, bits=2), over(att_other, bits=3)]

    feed_args = (inputs, pages, feats, gain_two, cotangent, attended, w_outputs, ups, downs)
    x_act0, x_act1, x_up0, x_up1, x_normed, _, x_grad, x_ffn = feed(ids, False, *feed_args)
    sent_grad = over(x_grad, bits=2)
    m_act0, m_act1, m_up0, m_up1, m_normed, mixed, m_grad, m_ffn = feed(ids, True, *feed_args)
    grad_mixed, low, ga0, ga1, ga2, ga3, gain_two_part = mid(ids, m_grad, sent_grad, mixed, gain_two, cotangent, w_outputs)
    ga1, ga2, ga3 = over(ga1, bits=1), over(ga2, bits=2), over(ga3, bits=3)

    c_act1, c_up1, c_normed = over(m_act1, bits=1), over(m_up1, bits=1), over(m_normed, bits=1)
    cx_act1, cx_up1, cx_normed = over(x_act1, bits=1), over(x_up1, bits=1), over(x_normed, bits=1)
    down_grad = feed_grad(
        ids, [cotangent] * 4, [0, 1, 2, 3], [m_act0, c_act1, x_act0, cx_act1], fast, "down_grad"
    )
    up_grad = feed_grad(
        ids, [m_normed, c_normed, x_normed, cx_normed], [None] * 4, [m_up0, c_up1, x_up0, cx_up1], fast, "up_grad"
    )

    sent_ffn = over(x_ffn, bits=2)
    rows_out = (mixed + m_ffn + sent_ffn.astype(F32)).astype(BF)
    rows_y = over(rows_out, bits=2)
    outputs = join(ids, [rows_out, over(rows_out, bits=1), rows_y, over(rows_y, bits=1)], BF)

    scores_a, dq0, dq1, key_sum, value_sum, near, far = back(
        ids, e, queries, inverse, out, keys, values, ga0, ga1, None
    )
    scores_b, dq2, dq3, keep_kv, send_kv, near, far = back(
        ids, e, queries, inverse, out, keys, values, ga2, ga3, (key_sum, value_sum, near, far)
    )
    got1, got3, got_kv = over(dq1, bits=1), over(dq3, bits=1), over(send_kv, bits=1)
    other_terms = terms(False, weights, partner, dq2, keep_kv, got3, got_kv)
    sent_terms = over(other_terms, bits=2)
    own_terms = terms(True, weights, partner, dq0, keep_kv, got1, got_kv)

    low_y = over(low, bits=2)
    lows = [low, over(low, bits=1), low_y, over(low_y, bits=1)]
    head_grads = head_grad(ids, normed1, [dq0, dq1, dq2, dq3], keep_kv, send_kv, lows, att_own, att_other, fast)

    grad_rows, gain_one_part = last(ids, own_terms, sent_terms, inputs, pages, feats, gain_one, grad_mixed)
    grad_y = over(grad_rows, bits=2)
    grad_inputs, grad_feats = join(
        ids, [grad_rows, over(grad_rows, bits=1), grad_y, over(grad_y, bits=1)], F32, pages
    )

    positions = jnp.stack([hor, ver])
    scores_b, _ = after([scores_b, scores_a], head_grads[0], own_terms)
    table_sums = table_grads(ids, scores_a, scores_b, positions, near, far)

    gains = jnp.concatenate([gain_one_part, gain_two_part], axis=0)
    gains = gains + over(gains, bits=1)
    gains = gains + over(gains, bits=2)
    small = jnp.concatenate([gains.reshape(-1), table_sums.reshape(-1)])[None]
    size = width // dp
    n = w_query.shape[1]
    if fast:
        around = functools.partial(swap, axis="dp", size=dp)
        for bits in (1, 2, 4):
            small = small + around(small, bits=bits)
        reduced = []
        for keep, send in (down_grad, up_grad, head_grads):
            parts = pair_sum(ids, keep, around(send, bits=1))
            reduced.append([parts[0]] + [around(part, bits=2 * k) for k, part in zip((1, 2, 3), parts[1:])])
        units = w_up.shape[1]
        grad_up, grad_down = finish(
            feed_final_kernel, reduced[1] + reduced[0], [shape((size, units), F32)] * 2, "feed_final"
        )
        grad_query, grad_key, grad_value, grad_output = finish(
            head_final_kernel, reduced[2], [shape((size, n), F32)] * 3 + [shape((n, size), F32)], "head_final"
        )
    else:
        small = lax.psum(small, "dp")
        scatter = lambda a: lax.psum_scatter(a[0], "dp", scatter_dimension=0, tiled=True)
        grad_up, grad_down, heads = scatter(up_grad), scatter(down_grad), scatter(head_grads)
        grad_query, grad_key, grad_value = heads[:, :n], heads[:, n : 2 * n], heads[:, 2 * n : 3 * n]
        grad_output = heads[:, 3 * n :].T
    gain_sums = small[0, : 2 * width].reshape(2, width)
    mine = lax.dynamic_slice(gain_sums, (0, d * size), (2, size))
    bins = rel_table.shape[1]
    table_sums = small[0, 2 * width :].reshape(3, HEADS, bins)
    return (
        outputs, grad_inputs, grad_feats[None], mine[0], grad_query, grad_key, grad_value,
        table_sums[0], table_sums[1], table_sums[2], grad_output, mine[1], grad_up, grad_down.T,
    )


def solution(mesh):
    return jax.shard_map(
        functools.partial(local, dp=mesh.shape["dp"]),
        mesh=mesh,
        in_specs=(
            P("dp", None),
            P("dp", None, None),
            P("dp", None),
            P("dp"),
            P("dp"),
            P("dp"),
            P(),
            P(None, "mp"),
            P(None, "mp"),
            P(None, "mp"),
            P("mp", None),
            P("mp", None),
            P("mp", None),
            P("mp", None),
            P(),
            P(None, "mp"),
            P("mp", None),
            P("dp", None),
        ),
        out_specs=(
            P("dp", None),
            P("dp", None),
            P("dp", None, None),
            P("dp"),
            P("dp", "mp"),
            P("dp", "mp"),
            P("dp", "mp"),
            P("mp", None),
            P("mp", None),
            P("mp", None),
            P("mp", "dp"),
            P("dp"),
            P("dp", "mp"),
            P("mp", "dp"),
        ),
        check_vma=False,
    )
```

```python
import functools

import jax
import jax.numpy as jnp
import numpy as np
from jax import lax
from jax.experimental import pallas as pl
from jax.experimental.pallas import tpu as pltpu
from jax.sharding import PartitionSpec as P

EPS = 1e-06
THRESHOLDS = (12, 16, 23, 32, 46, 64, 91)
FAR = 91
HEADS = 3
HD = 64
PAD = 128
MARKS = 72
NEAR = 40
TILES = NEAR + 2
SPAN = 384
LOW = 92
TOP = 311
BF = jnp.bfloat16
F32 = jnp.float32
I32 = jnp.int32
FEED_PARTS = 3
GELU_C = float(np.sqrt(2.0 / np.pi))


def dot(left, right, dims=((1,), (0,))):
    return lax.dot_general(left, right, (dims, ((), ())), preferred_element_type=F32)


def bucket(delta):
    magnitude = jnp.abs(delta)
    coarse = 8 + sum((magnitude >= limit).astype(I32) for limit in THRESHOLDS)
    return jnp.where(magnitude < 8, magnitude, coarse) + 16 * (delta > 0).astype(I32)


def params(mib):
    return pltpu.CompilerParams(vmem_limit_bytes=mib * 2**20)


def cost(microseconds):
    return pl.CostEstimate(flops=int(1.15e9 * microseconds), bytes_accessed=1, transcendentals=0)


def shape(dims, dtype):
    return jax.ShapeDtypeStruct(dims, dtype)


def whole(dims):
    return pl.BlockSpec(dims, lambda *a: (0,) * len(dims))


def hidden_rows(inputs, pages, feats):
    return inputs.astype(F32) + dot(pages.astype(F32).astype(BF), feats, ((0,), (0,)))


def unit_rows(field):
    factor = lax.rsqrt(jnp.mean(field * field, axis=-1, keepdims=True) + EPS)
    return field * factor, factor


def project_kernel(ids, x_ref, page_ref, feat_ref, gain_ref, wq_ref, wk_ref, wv_ref, n_ref, q_ref, k_ref, v_ref):
    step = pl.program_id(0)
    rows = x_ref.shape[0]
    unit, _ = unit_rows(hidden_rows(x_ref[...], page_ref[...], feat_ref[...]))
    normed = (unit * gain_ref[...].astype(F32)).astype(BF)
    n_ref[...] = normed
    lane = lax.broadcasted_iota(I32, (rows, PAD), 1)
    row = lax.broadcasted_iota(I32, (rows, PAD), 0) + step * rows
    masked = jnp.where((lane == HD) & (row >= ids[8]), -1e30, 0.0)
    block = lane - MARKS
    far_left = (block >= 0) & (block < 8) & (row < 128 * block - 96)
    far_right = (block >= 8) & (block < 16) & (row >= 128 * (block - 8) + 224)
    masked = jnp.where(far_left | far_right, 1.0, masked)
    query_extra = jnp.where(lane == HD, 1.0, 0.0)
    value_extra = jnp.where((lane == HD) | (lane == HD + 1), 1.0, 0.0)
    for out_ref, w_ref, extra, scale in (
        (q_ref, wq_ref, query_extra, 0.125),
        (k_ref, wk_ref, masked, None),
        (v_ref, wv_ref, value_extra, None),
    ):
        full = dot(normed, w_ref[...], ((1,), (1,)))
        if scale is not None:
            full = full * scale
        pair = full[:, :PAD]
        last = jnp.concatenate([full[:, PAD:], jnp.zeros((rows, PAD - HD), F32)], axis=1)
        heads = (pair, pltpu.roll(pair, HD, 1), last)
        for head in range(HEADS):
            out_ref[:, head * PAD : (head + 1) * PAD] = jnp.where(lane < HD, heads[head], extra).astype(BF)


def project(ids, inputs, onehot, feats, gain, w_query, w_key, w_value):
    seq, width = inputs.shape
    rows = 256
    columns = w_query.shape[0]
    wide = HEADS * PAD
    block = lambda cols: pl.BlockSpec((rows, cols), lambda i, s: (i, 0))
    lanes = lambda n: pl.BlockSpec((n, rows), lambda i, s: (0, i))
    return pl.pallas_call(
        project_kernel,
        grid_spec=pltpu.PrefetchScalarGridSpec(
            num_scalar_prefetch=1,
            grid=(seq // rows,),
            in_specs=[block(width), lanes(onehot.shape[0]), whole(feats.shape), whole(gain.shape)]
            + [whole((columns, width))] * 3,
            out_specs=[block(width), block(wide), block(wide), block(wide)],
        ),
        out_shape=[shape((seq, width), BF)] + [shape((seq, wide), BF)] * 3,
        compiler_params=params(16),
        cost_estimate=cost(7),
        name="project",
    )(ids, inputs, onehot, feats, gain, w_query, w_key, w_value)


def place(delta):
    magnitude = jnp.abs(delta)
    coarse = jnp.minimum(25 - lax.clz(delta * delta), 7)
    exact = magnitude < 8
    return jnp.where(exact, magnitude, coarse), exact, delta > 0


def look(table_ref, row, where):
    index, exact, after = where
    found = [jnp.take_along_axis(table_ref[row, part], index, axis=0) for part in range(4)]
    return jnp.where(after, jnp.where(exact, found[2], found[3]), jnp.where(exact, found[0], found[1]))


def tile_delta(tile):
    lane = lax.broadcasted_iota(I32, (8, 128), 1)
    sub = lax.broadcasted_iota(I32, (8, 128), 0)
    delta = 8 * (tile - 13) + sub - lane
    if tile == 0:
        delta = jnp.full_like(delta, -1000)
    if tile == TILES - 1:
        delta = jnp.full_like(delta, 1000)
    return delta


def attend_kernel(*refs, first, width, chunk):
    ids, q_ref, k_ref, v_ref, hor_ref, ver_ref = refs[:6]
    if first:
        hor_all, ver_all, rel_table, hor_table, ver_table, e_ref, att0, att1, inv_ref, out_ref = refs[6:16]
        rel_ref, t8_ref, hor_col, ver_col, s_ref = refs[16:]
    else:
        rel_ref, t8_ref, hor_col, ver_col, e_ref, att0, att1, inv_ref, out_ref, s_ref = refs[6:]
    seq = k_ref.shape[0]
    lanes = width // 128
    step = pl.program_id(0)

    if first:

        @pl.when(step == 0)
        def _():
            for all_ref, col_ref in ((hor_all, hor_col), (ver_all, ver_col)):
                for b in range(seq // 128):
                    cols = slice(128 * b, 128 * b + 128)
                    spread = jnp.broadcast_to(all_ref[:, cols].astype(F32), (128, 128))
                    col_ref[cols, :] = spread.T.astype(I32)
            lane = lax.broadcasted_iota(I32, (8, 32), 1)
            sub = lax.broadcasted_iota(I32, (8, 32), 0)
            for axis, table_ref in enumerate((rel_table, hor_table, ver_table)):
                table = table_ref[...].astype(F32)
                for head in range(HEADS):
                    row = jnp.broadcast_to(table[head : head + 1], (8, 32))
                    for part in range(4):
                        entries = jnp.sum(jnp.where(lane == sub + 8 * part, row, 0.0), axis=1, keepdims=True)
                        t8_ref[axis * HEADS + head, part] = jnp.broadcast_to(entries, (8, 128))
            for tile in range(TILES):
                where = place(tile_delta(tile))
                for head in range(HEADS):
                    rel_ref[head, tile] = look(t8_ref, head, where)

    queries = q_ref[...]
    for head in range(HEADS):
        cols = slice(head * PAD, (head + 1) * PAD)
        s_ref[head] = dot(k_ref[:, cols], queries[:, cols], ((1,), (1,)))
    hor = [jnp.broadcast_to(hor_ref[:, 128 * l : 128 * l + 128], (8, 128)) for l in range(lanes)]
    ver = [jnp.broadcast_to(ver_ref[:, 128 * l : 128 * l + 128], (8, 128)) for l in range(lanes)]
    block = ids[(0 if first else 2) + step] * lanes

    def add_bias(c, tops):
        tops = list(tops)
        base = pl.multiple_of(c * chunk, chunk)
        for g in range(chunk // 8):
            rows = pl.ds(pl.multiple_of(base + 8 * g, 8), 8)
            hor_keys, ver_keys = hor_col[rows, :], ver_col[rows, :]
            for l in range(lanes):
                cols = pl.ds(128 * l, 128)
                hor_at, ver_at = place(hor_keys - hor[l]), place(ver_keys - ver[l])
                tile = jnp.clip(c * (chunk // 8) + g - 16 * (block + l) + 13, 0, TILES - 1)
                for head in range(HEADS):
                    s = s_ref[head, rows, cols] + rel_ref[head, tile]
                    s = s + (look(t8_ref, HEADS + head, hor_at) + look(t8_ref, 2 * HEADS + head, ver_at))
                    s_ref[head, rows, cols] = s
                    tops[head * lanes + l] = jnp.maximum(tops[head * lanes + l], s)
        return tuple(tops)

    tops = lax.fori_loop(
        0, seq // chunk, add_bias, tuple(jnp.full((8, 128), -1e30, F32) for _ in range(HEADS * lanes))
    )
    peaks = [jnp.broadcast_to(jnp.max(top, axis=0, keepdims=True), (16, 128)) for top in tops]

    def exps(c, carry):
        for g in range(4):
            rows = pl.ds(pl.multiple_of(c * 64 + 16 * g, 16), 16)
            for l in range(lanes):
                cols = pl.ds(128 * l, 128)
                for head in range(HEADS):
                    e_ref[head, rows, cols] = jnp.exp(s_ref[head, rows, cols] - peaks[head * lanes + l]).astype(BF)
        return carry

    lax.fori_loop(0, seq // 64, exps, 0)
    for head in range(HEADS):
        total = dot(v_ref[:, head * PAD : (head + 1) * PAD], e_ref[head], ((0,), (0,)))
        inverse = 1.0 / total[HD : HD + 1, :]
        inv_ref[head : head + 1, :] = inverse
        out_ref[head * HD : (head + 1) * HD, :] = total[:HD] * inverse

    for k, att_ref in enumerate((att0, att1)):

        @pl.when(step == k)
        def _(att_ref=att_ref):
            att_ref[...] = out_ref[...].astype(BF)


def attend(ids, queries, keys, values, hor, ver, tables, lookups):
    seq, wide = queries.shape
    width = seq // 4
    first = lookups is None
    base = 0 if first else 2
    columns = HEADS * HD
    at = pl.BlockSpec((1, width), lambda i, s: (0, s[base + i]))
    made = [
        shape((HEADS, TILES, 8, 128), F32), shape((3 * HEADS, 4, 8, 128), F32), shape((seq, 128), I32), shape((seq, 128), I32)
    ]
    extra = (hor, ver, *tables) if first else tuple(lookups)
    outs = [
        (shape((HEADS, seq, 2 * width), BF), pl.BlockSpec((HEADS, seq, width), lambda i, s: (0, 0, i))),
        (shape((columns, width), BF), whole((columns, width))),
        (shape((columns, width), BF), whole((columns, width))),
        (shape((HEADS, 2 * width), F32), pl.BlockSpec((HEADS, width), lambda i, s: (0, i))),
        (shape((columns, 2 * width), F32), pl.BlockSpec((columns, width), lambda i, s: (0, i))),
    ]
    if first:
        outs += [(m, whole(m.shape)) for m in made]
    found = pl.pallas_call(
        functools.partial(attend_kernel, first=first, width=width, chunk=32),
        grid_spec=pltpu.PrefetchScalarGridSpec(
            num_scalar_prefetch=1,
            grid=(2,),
            in_specs=[
                pl.BlockSpec((width, wide), lambda i, s: (s[base + i], 0)),
                whole(keys.shape),
                whole(values.shape),
                at,
                at,
            ]
            + [whole(a.shape) for a in extra],
            out_specs=[spec for _, spec in outs],
            scratch_shapes=[pltpu.VMEM((HEADS, seq, width), F32)],
        ),
        out_shape=[o for o, _ in outs],
        compiler_params=params(18),
        cost_estimate=cost(14),
        name="attend_first" if first else "attend_last",
    )(ids, queries, keys, values, hor, ver, *extra)
    return found[:5], found[5:]


def feed_kernel(
    ids, x_ref, page_ref, feat_ref, gain_ref, cot_ref, a0, a1, a2, a3, o0, o1, o2, o3, u0, u1, d0, d1,
    keep_ref, send_ref, mixed_ref, grad_ref, ffn_ref, grad_sum, ffn_sum,
):
    step = pl.program_id(0)
    half = pl.num_programs(0) // 2
    chunk = u0.shape[1]

    @pl.when(step == 0)
    def _():
        mixed = hidden_rows(x_ref[...], page_ref[...], feat_ref[...])
        for a_ref, o_ref in ((a0, o0), (a1, o1), (a2, o2), (a3, o3)):
            mixed = mixed + dot(a_ref[...], o_ref[...], ((0,), (0,)))
        mixed_ref[...] = mixed
        unit, _ = unit_rows(mixed)
        send_ref[2] = (unit * gain_ref[...].astype(F32)).astype(BF)
        grad_sum[...] = jnp.zeros_like(grad_sum)
        ffn_sum[...] = jnp.zeros_like(ffn_sum)

    def part(u_ref, d_ref, goal, at):
        upward = dot(send_ref[2], u_ref[...])
        square = upward * upward
        tanh = jnp.tanh(GELU_C * upward * (1.0 + 0.044715 * square))
        lifted = 0.5 * (1.0 + tanh)
        activated = (upward * lifted).astype(BF)
        slope = lifted + 0.5 * upward * (1.0 - tanh * tanh) * (GELU_C * (1.0 + 3 * 0.044715 * square))
        grad_up = (dot(cot_ref[...], d_ref[...], ((1,), (1,))) * slope).astype(BF)
        cols = pl.ds(pl.multiple_of(at * chunk, 128), chunk)
        goal[0, :, cols] = activated
        goal[1, :, cols] = grad_up
        ffn_sum[...] += dot(activated, d_ref[...])
        grad_sum[...] += dot(grad_up, u_ref[...], ((1,), (1,)))

    @pl.when(step < half)
    def _():
        part(u0, d0, keep_ref, step)

    @pl.when(step >= half)
    def _():
        part(u1, d1, send_ref, step - half)

    @pl.when(step == 2 * half - 1)
    def _():
        grad_ref[...] = grad_sum[...].astype(grad_ref.dtype)
        ffn_ref[...] = ffn_sum[...].astype(ffn_ref.dtype)


def feed(ids, own, inputs, onehot, feats, gain, cotangent, attended, w_outputs, ups, downs):
    seq, width = inputs.shape
    rows = seq // 4
    units = ups[0].shape[1]
    half = FEED_PARTS
    chunk = units // half
    slot = 0 if own else 2
    quarter = lambda cols: pl.BlockSpec((rows, cols), lambda i, s: (s[slot], 0))
    pages = pl.BlockSpec((onehot.shape[0], rows), lambda i, s: (0, s[slot]))
    columns = HEADS * HD
    low = lambda i: jnp.minimum(i, half - 1)
    high = lambda i: jnp.maximum(i - half, 0)
    kept = F32 if own else BF
    outs = [
        shape((2, rows, units), BF), shape((3, rows, width), BF), shape((rows, width), F32),
        shape((rows, width), kept), shape((rows, width), kept),
    ]
    return pl.pallas_call(
        feed_kernel,
        grid_spec=pltpu.PrefetchScalarGridSpec(
            num_scalar_prefetch=1,
            grid=(2 * half,),
            in_specs=[quarter(width), pages, whole(feats.shape), whole(gain.shape), quarter(width)]
            + [whole((columns, rows))] * 4
            + [whole((columns, width))] * 4
            + [
                pl.BlockSpec((width, chunk), lambda i, s: (0, low(i))),
                pl.BlockSpec((width, chunk), lambda i, s: (0, high(i))),
                pl.BlockSpec((chunk, width), lambda i, s: (low(i), 0)),
                pl.BlockSpec((chunk, width), lambda i, s: (high(i), 0)),
            ],
            out_specs=[whole(o.shape) for o in outs],
            scratch_shapes=[pltpu.VMEM((rows, width), F32), pltpu.VMEM((rows, width), F32)],
        ),
        out_shape=outs,
        compiler_params=params(20),
        cost_estimate=cost(20 if own else 10),
        name="feed_own" if own else "feed_other",
    )(ids, inputs, onehot, feats, gain, cotangent, *attended, *w_outputs, *ups, *downs)


def mid_kernel(
    ids, mine_ref, sent_ref, mixed_ref, gain_ref, cot_ref, o0, o1, o2, o3,
    grad_ref, own_ref, core_ref, chip_ref, far_ref, part_ref,
):
    grad_normed = mine_ref[...] + sent_ref[...].astype(F32)
    unit, factor = unit_rows(mixed_ref[...])
    scaled = grad_normed * gain_ref[...].astype(F32)
    grad = factor * (scaled - unit * jnp.mean(scaled * unit, axis=-1, keepdims=True))
    grad = cot_ref[...].astype(F32) + grad
    grad_ref[...] = grad
    low = grad.astype(BF)
    rows = low.shape[0]
    core_ref[:rows] = low
    chip_ref[:rows] = low
    part_ref[...] = jnp.sum(grad_normed * unit, axis=0, keepdims=True)
    for o_ref, goal, at in ((o0, own_ref, 0), (o1, core_ref, rows), (o2, chip_ref, rows), (o3, far_ref, 0)):
        found = dot(o_ref[...], low, ((1,), (1,))).astype(BF)
        for head in range(HEADS):
            goal[at : at + HD, head * rows : (head + 1) * rows] = found[head * HD : (head + 1) * HD]


def mid(ids, mine, sent, mixed, gain, cotangent, w_outputs):
    rows, width = mine.shape
    columns = HEADS * HD
    full = whole((rows, width))
    outs = [
        shape((rows, width), F32), shape((HD, width), BF), shape((rows + HD, width), BF), shape((rows + HD, width), BF),
        shape((HD, width), BF), shape((1, width), F32),
    ]
    return pl.pallas_call(
        mid_kernel,
        grid_spec=pltpu.PrefetchScalarGridSpec(
            num_scalar_prefetch=1,
            grid=(1,),
            in_specs=[full, full, full, whole(gain.shape), pl.BlockSpec((rows, width), lambda i, s: (s[0], 0))]
            + [whole((columns, width))] * 4,
            out_specs=[whole(o.shape) for o in outs],
        ),
        out_shape=outs,
        compiler_params=params(24),
        cost_estimate=cost(2),
        name="mid",
    )(ids, mine, sent, mixed, gain, cotangent, *w_outputs)


def back_kernel(*refs, first):
    ids, e_ref, qa_ref, qb_ref, inv_ref, o_ref, k_ref, v_ref, ga_ref, gb_ref = refs[:10]
    refs = refs[10:]
    if first:
        ds_ref, dqa_ref, dqb_ref, key_ref, value_ref, near_ref, far_ref, x_ref = refs
    else:
        key_in, value_in, near_in, far_in, dqa_in, dqb_in = refs[:6]
        ds_ref, all_ref, near_ref, far_ref, x_ref = refs[6:]
    head = pl.program_id(0)
    seq = k_ref.shape[0]
    width = qa_ref.shape[0]
    both = 2 * width
    lanes = width // 128
    base = 0 if first else 2

    sub = lax.broadcasted_iota(I32, (HD, both), 0)
    head_sub = lax.broadcasted_iota(I32, (8, both), 0)
    inverse = jnp.sum(jnp.where(head_sub[:HEADS] == head, inv_ref[...], 0.0), axis=0, keepdims=True)
    grad = jnp.concatenate([ga_ref[...], gb_ref[...]], axis=1).astype(F32)
    grad = (grad * inverse).astype(BF).astype(F32)
    inner = jnp.sum(grad * o_ref[...], axis=0, keepdims=True)
    high = inner.astype(BF).astype(F32)
    extra = jnp.where(sub == 0, -high, jnp.where(sub == 1, high - inner, 0.0))
    right = jnp.concatenate([grad, extra], axis=0).astype(BF)
    x_ref[...] = dot(v_ref[...], right)
    value = dot(e_ref[0], right, ((1,), (1,)))

    def grad_scores(c, carry):
        rows = pl.ds(pl.multiple_of(c * 64, 64), 64)
        ds_ref[0, rows, :] = (e_ref[0, rows, :].astype(F32) * x_ref[rows, :]).astype(BF)
        return carry

    lax.fori_loop(0, seq // 64, grad_scores, 0)
    grad = ds_ref[0]
    key = dot(grad, jnp.concatenate([qa_ref[...], qb_ref[...]], axis=0))
    query = dot(k_ref[...], grad, ((0,), (0,)))
    query_a = (query[:HD, :width] * 0.125).astype(BF)
    query_b = (query[:HD, width:] * 0.125).astype(BF)

    blocks = [ids[base + l // lanes] * lanes + l % lanes for l in range(2 * lanes)]
    for g in range(NEAR // 2):
        total = None if first else near_in[0, 16 * g : 16 * g + 16]
        for l, block in enumerate(blocks):
            start = 128 * block - 96 + 16 * g
            inside = (start >= 0) & (start < seq)
            rows = pl.ds(pl.multiple_of(jnp.clip(start, 0, seq - 16), 16), 16)
            found = ds_ref[0, rows, 128 * l : 128 * l + 128].astype(F32)
            found = jnp.where(inside, found, 0.0)
            total = found if total is None else total + found
        near_ref[0, 16 * g : 16 * g + 16] = total
    spot = lax.broadcasted_iota(I32, (8, 128), 0)
    for side in range(2):
        total = None if first else far_in[0, 8 * side : 8 * side + 8]
        for l, block in enumerate(blocks):
            marks = query[MARKS + 8 * side : MARKS + 8 * side + 8, 128 * l : 128 * l + 128]
            marks = jnp.where(spot == block, marks, 0.0)
            total = marks if total is None else total + marks
        far_ref[0, 8 * side : 8 * side + 8] = total

    if first:
        key_ref[...] = key
        value_ref[...] = value
        dqa_ref[...] = query_a
        dqb_ref[...] = query_b
    else:
        for k, found in enumerate((dqa_in[...], dqb_in[...], query_a, query_b)):
            all_ref[k, 0] = found
        for part, acc in ((1, key_in[...] + key), (2, value_in[...] + value)):
            turned = acc.T[:HD].astype(BF)
            for k in range(4):
                for q in range(4):

                    @pl.when(ids[k] == q)
                    def _(k=k, q=q, part=part, turned=turned):
                        all_ref[k, part] = turned[:, q * width : (q + 1) * width]


def back(ids, e, queries, inverse, out, keys, values, grad_a, grad_b, carried):
    seq, wide = queries.shape
    width = seq // 4
    first = carried is None
    base = 0 if first else 2
    columns = HEADS * HD
    head_cols = pl.BlockSpec((seq, PAD), lambda h, s: (0, h))
    grad_rows = pl.BlockSpec((HD, width), lambda h, s: (h, 0))
    sent = lambda at: pl.BlockSpec((HD, width), lambda h, s: (at, h))
    starts = (0, width // HD) if first else (width // HD, 0)
    near = pl.BlockSpec((1, 8 * NEAR, 128), lambda h, s: (h, 0, 0))
    far = pl.BlockSpec((1, 16, 128), lambda h, s: (h, 0, 0))
    queried = [(shape((columns, width), BF), grad_rows)] * 2
    sums = [(shape((seq, wide), F32), head_cols)] * 2
    rel = [(shape((HEADS, 8 * NEAR, 128), F32), near), (shape((HEADS, 16, 128), F32), far)]
    outs = [(shape((HEADS, seq, 2 * width), BF), pl.BlockSpec((1, seq, 2 * width), lambda h, s: (h, 0, 0)))]
    if first:
        outs += queried + sums
    else:
        outs += [(shape((4, 3, columns, width), BF), pl.BlockSpec((4, 3, HD, width), lambda h, s: (0, 0, h, 0)))]
    outs += rel
    part = lambda q: pl.BlockSpec((width, PAD), lambda h, s: (s[base + q], h))
    specs = [
        pl.BlockSpec((1, seq, 2 * width), lambda h, s: (h, 0, 0)),
        part(0),
        part(1),
        whole(inverse.shape),
        pl.BlockSpec((HD, 2 * width), lambda h, s: (h, 0)),
    ]
    specs += [head_cols, head_cols, sent(starts[0]), sent(starts[1])]
    if not first:
        specs += [spec for _, spec in sums + rel + queried]
    return pl.pallas_call(
        functools.partial(back_kernel, first=first),
        grid_spec=pltpu.PrefetchScalarGridSpec(
            num_scalar_prefetch=1,
            grid=(HEADS,),
            in_specs=specs,
            out_specs=[spec for _, spec in outs],
            scratch_shapes=[pltpu.VMEM((seq, 2 * width), F32)],
        ),
        out_shape=[o for o, _ in outs],
        compiler_params=params(20),
        cost_estimate=cost(10 if first else 0.1),
        name="back_first" if first else "back_last",
    )(ids, e, queries, queries, inverse, out, keys, values, grad_a, grad_b, *(() if first else carried))


def tables_kernel(ids, s_ref, keys_ref, qa_ref, qb_ref, *refs):
    diagonals = refs[:-3]
    out_ref, e_ref, left_ref = refs[-3:]
    head = pl.program_id(0)
    places, seq = e_ref.shape
    width = s_ref.shape[2]
    groups = places // 128

    @pl.when(head == 0)
    def _():
        spot = lax.broadcasted_iota(I32, (places, seq), 0)
        e_ref[...] = jnp.where(spot == keys_ref[...], 1.0, 0.0).astype(BF)

    moved = dot(e_ref[...], s_ref[0]).astype(BF)
    rows = pl.ds(pl.multiple_of(head * 128, 128), 128)
    for b in range(groups):
        left_ref[rows, b * width : (b + 1) * width] = moved[128 * b : 128 * b + 128]

    def to_buckets(sums, delta):
        spot = lax.broadcasted_iota(I32, (32, sums.shape[1]), 0)
        return jnp.sum(jnp.where(bucket(delta) == spot, sums, 0.0), axis=1, keepdims=True)

    @pl.when(head == HEADS - 1)
    def _():
        query = jnp.concatenate([qa_ref[...], qb_ref[...]], axis=1)
        column = lax.broadcasted_iota(I32, (SPAN, width), 0)
        right = [
            jnp.where(column == jnp.clip(128 * b + TOP - LOW - query, 0, TOP), 1.0, 0.0).astype(BF) for b in range(groups)
        ]
        found = dot(left_ref[...], jnp.concatenate(right, axis=1), ((1,), (1,)))
        lane = lax.broadcasted_iota(I32, (1, 512), 1)
        columns = []
        for h in range(HEADS):
            grid = jnp.concatenate([found[h * 128 : h * 128 + 128, :], jnp.zeros((128, 512 - SPAN), F32)], axis=1)
            grid = pltpu.roll(grid, 0, 1, stride=1, stride_axis=0)
            columns.append(to_buckets(jnp.sum(grid, axis=0, keepdims=True), lane + LOW - TOP))
        if diagonals:
            near_ref, far_ref = diagonals
            flip = 7 - lax.broadcasted_iota(I32, (8, 128), 0)
            spot = lax.broadcasted_iota(I32, (32, 1), 0)
            for h in range(HEADS):
                near = [jnp.take_along_axis(near_ref[h, 8 * t : 8 * t + 8], flip, axis=0) for t in reversed(range(NEAR))]
                grid = jnp.concatenate(near, axis=0)
                grid = jnp.concatenate([grid, jnp.zeros((8 * NEAR, 384), F32)], axis=1)
                grid = pltpu.roll(grid, 0, 1, stride=1, stride_axis=0)
                found = to_buckets(jnp.sum(grid, axis=0, keepdims=True), 8 * NEAR - 1 - 8 * 12 - lane)
                left = jnp.sum(jnp.sum(far_ref[h, :8], axis=0, keepdims=True), axis=1, keepdims=True)
                right = jnp.sum(jnp.sum(far_ref[h, 8:], axis=0, keepdims=True), axis=1, keepdims=True)
                columns.append(found + jnp.where(spot == 15, left, 0.0) + jnp.where(spot == 31, right, 0.0))
        spread = lax.broadcasted_iota(I32, (32, 128), 1)
        total = sum(jnp.where(spread == at, column, 0.0) for at, column in enumerate(columns))
        out_ref[...] = total.T[:8]


def table_grads(ids, first, scores, positions, sums):
    seq = positions.shape[1]
    width = seq // 4
    places = 1024
    base = 0 if first else 2
    quarter = lambda k: pl.BlockSpec((1, width), lambda h, s: (0, s[base + k]))
    return pl.pallas_call(
        tables_kernel,
        grid_spec=pltpu.PrefetchScalarGridSpec(
            num_scalar_prefetch=1,
            grid=(HEADS,),
            in_specs=[
                pl.BlockSpec((1,) + scores.shape[1:], lambda h, s: (h, 0, 0)), whole((1, seq)), quarter(0), quarter(1),
            ]
            + [whole(a.shape) for a in sums],
            out_specs=whole((8, 32)),
            scratch_shapes=[
                pltpu.VMEM((places, seq), BF),
                pltpu.VMEM((HEADS * 128, places // 128 * 2 * width), BF),
            ],
        ),
        out_shape=shape((8, 32), F32),
        compiler_params=params(24),
        cost_estimate=cost(10 if sums else 0.01),
        name="table_grads",
    )(ids, scores, *[positions] * 3, *sums)


def terms_of(grads, weights):
    total = None
    for part, w_ref in enumerate(weights):
        found = dot(grads[part], w_ref[...], ((0,), (0,)))
        total = found if total is None else total + found
    return total


def terms_send_kernel(w0, w1, w2, grads_ref, out_ref):
    out_ref[0] = terms_of(grads_ref[0], (w0, w1, w2)).astype(BF)


def terms_keep_kernel(w0, w1, w2, grads_ref, got_ref, own_ref, other_ref):
    total = terms_of(grads_ref[0], (w0, w1, w2)) + got_ref[0].astype(F32)

    @pl.when(pl.program_id(0) == 0)
    def _():
        other_ref[...] = total.astype(BF)

    @pl.when(pl.program_id(0) == 1)
    def _():
        own_ref[...] = total


def terms_send(weights, grads):
    columns, width = weights[0].shape
    rows = grads.shape[3]
    return pl.pallas_call(
        terms_send_kernel,
        grid=(2,),
        in_specs=[whole(weights[0].shape)] * 3 + [pl.BlockSpec((1, 3, columns, rows), lambda i: (2 * i + 1, 0, 0, 0))],
        out_specs=pl.BlockSpec((1, rows, width), lambda i: (i, 0, 0)),
        out_shape=shape((2, rows, width), BF),
        compiler_params=params(16),
        cost_estimate=cost(0.1),
        name="terms_send",
    )(*weights, grads)


def terms_keep(weights, grads, got):
    columns, width = weights[0].shape
    rows = grads.shape[3]
    return pl.pallas_call(
        terms_keep_kernel,
        grid=(2,),
        in_specs=[whole(weights[0].shape)] * 3
        + [
            pl.BlockSpec((1, 3, columns, rows), lambda i: (2 - 2 * i, 0, 0, 0)),
            pl.BlockSpec((1, rows, width), lambda i: (1 - i, 0, 0)),
        ],
        out_specs=[whole((rows, width))] * 2,
        out_shape=[shape((rows, width), F32), shape((rows, width), BF)],
        compiler_params=params(16),
        cost_estimate=cost(0.1),
        name="terms_keep",
    )(*weights, grads, got)


def last_kernel(
    ids, mine_ref, sent_ref, x_ref, page_ref, feat_ref, gain_ref, grad_ref, second_ref, mixed_ref, ffn_ref, got_ref,
    out_ref, part_ref,
):
    grad_normed = mine_ref[...] + sent_ref[...].astype(F32)
    unit, factor = unit_rows(hidden_rows(x_ref[...], page_ref[...], feat_ref[...]))
    scaled = grad_normed * gain_ref[...].astype(F32)
    grad = factor * (scaled - unit * jnp.mean(scaled * unit, axis=-1, keepdims=True))
    out_ref[0] = (mixed_ref[...] + ffn_ref[...] + got_ref[...].astype(F32)).astype(BF)
    out_ref[1] = (grad_ref[...] + grad).astype(BF)
    part_ref[0:1] = jnp.sum(grad_normed * unit, axis=0, keepdims=True)
    part_ref[1:2] = second_ref[...]


def last(ids, mine, sent, inputs, onehot, feats, gain, grad_mixed, second, *ffn):
    rows, width = mine.shape
    full = whole((rows, width))
    quarter = lambda cols: pl.BlockSpec((rows, cols), lambda i, s: (s[0], 0))
    pages = pl.BlockSpec((onehot.shape[0], rows), lambda i, s: (0, s[0]))
    return pl.pallas_call(
        last_kernel,
        grid_spec=pltpu.PrefetchScalarGridSpec(
            num_scalar_prefetch=1,
            grid=(1,),
            in_specs=[full, full, quarter(width), pages, whole(feats.shape), whole(gain.shape), full, whole((1, width))]
            + [full] * 3,
            out_specs=[whole((2, rows, width)), whole((2, width))],
        ),
        out_shape=[shape((2, rows, width), BF), shape((2, width), F32)],
        compiler_params=params(16),
        cost_estimate=cost(0.01),
        name="last",
    )(ids, mine, sent, inputs, onehot, feats, gain, grad_mixed, second, *ffn)


def pack_kernel(gains_ref, got_ref, hor_a, hor_b, ver_a, ver_b, out_ref):
    gains = gains_ref[...] + got_ref[...]
    parts = gains.shape[1] // 128
    for row in range(2):
        for part in range(parts):
            at = row * parts + part
            out_ref[at : at + 1, :] = gains[row : row + 1, part * 128 : part * 128 + 128]
    bins = hor_a.shape[1]
    out_ref[2 * parts :, :] = jnp.zeros((out_ref.shape[0] - 2 * parts, 128), F32)
    at = 2 * parts
    out_ref[at : at + HEADS, :bins] = hor_b[HEADS : 2 * HEADS]
    out_ref[at + HEADS : at + 2 * HEADS, :bins] = hor_a[:HEADS] + hor_b[:HEADS]
    out_ref[at + 2 * HEADS : at + 3 * HEADS, :bins] = ver_a[:HEADS] + ver_b[:HEADS]


def pack(gains, got, *sums):
    rows = gains.shape[1] // 128 * 2 + 3 * HEADS
    rows = -(-rows // 8) * 8
    return pl.pallas_call(
        pack_kernel,
        in_specs=[pl.BlockSpec(memory_space=pltpu.VMEM)] * 6,
        out_specs=pl.BlockSpec(memory_space=pltpu.VMEM),
        out_shape=shape((rows, 128), F32),
        compiler_params=params(16),
        cost_estimate=cost(0.1),
        name="pack",
    )(gains, got, *sums)


def unpack_kernel(a_ref, b_ref, rel_ref, hor_ref, ver_ref, gains_ref):
    total = a_ref[...] + b_ref[...]
    parts = gains_ref.shape[1] // 128
    for row in range(2):
        for part in range(parts):
            at = row * parts + part
            gains_ref[row : row + 1, part * 128 : part * 128 + 128] = total[at : at + 1]
    at, bins = 2 * parts, rel_ref.shape[1]
    for goal in (rel_ref, hor_ref, ver_ref):
        goal[...] = total[at : at + HEADS, :bins]
        at += HEADS


def unpack(one, two, bins, width):
    spec = pl.BlockSpec(memory_space=pltpu.VMEM)
    return pl.pallas_call(
        unpack_kernel,
        in_specs=[spec] * 2,
        out_specs=[spec] * 4,
        out_shape=[shape((HEADS, bins), F32)] * 3 + [shape((2, width), F32)],
        compiler_params=params(16),
        cost_estimate=cost(0.1),
        name="unpack",
    )(one, two)


def join_kernel(ids, b0, b1, b2, b3, out_ref):
    for k, b_ref in enumerate((b0, b1, b2, b3)):

        @pl.when(pl.program_id(0) == k)
        def _(b_ref=b_ref):
            out_ref[...] = b_ref[0].astype(out_ref.dtype)


def join_feat_kernel(ids, b0, b1, b2, b3, page_ref, out_ref, feat_ref, all_ref):
    step = pl.program_id(0)
    rows = b0.shape[1]
    for k, b_ref in enumerate((b0, b1, b2, b3)):

        @pl.when(step == k)
        def _(b_ref=b_ref, k=k):
            out_ref[...] = b_ref[0].astype(out_ref.dtype)
            all_ref[pl.ds(pl.multiple_of(ids[k] * rows, rows), rows), :] = b_ref[0]

    @pl.when(step == 3)
    def _():
        feat_ref[...] = dot(page_ref[...].astype(F32).astype(BF), all_ref[...])


def join(ids, blocks, slot, dtype, onehot=None):
    _, rows, width = blocks[0].shape
    specs = [pl.BlockSpec((1, rows, width), lambda i, s: (slot, 0, 0))] * 4
    outs, out_specs = [shape((4 * rows, width), dtype)], [pl.BlockSpec((rows, width), lambda i, s: (s[i], 0))]
    extra, scratch = (), []
    if onehot is not None:
        pages = onehot.shape[0]
        specs = specs + [whole(onehot.shape)]
        outs.append(shape((pages, width), F32))
        out_specs.append(whole((pages, width)))
        extra, scratch = (onehot,), [pltpu.VMEM((4 * rows, width), BF)]
    found = pl.pallas_call(
        join_kernel if onehot is None else join_feat_kernel,
        grid_spec=pltpu.PrefetchScalarGridSpec(
            num_scalar_prefetch=1, grid=(4,), in_specs=specs, out_specs=out_specs, scratch_shapes=scratch
        ),
        out_shape=outs,
        compiler_params=params(16),
        cost_estimate=cost(10),
        name="join_output" if onehot is None else "join_grads",
    )(ids, *blocks, *extra)
    return found[0] if onehot is None else found


def split_rows(ids, total, keep_ref, send_ref, parity):
    groups, size = keep_ref.shape[0], keep_ref.shape[1]
    for g in range(groups):
        mine = pl.multiple_of((2 * g + parity) * size, 8)
        theirs = pl.multiple_of((2 * g + 1 - parity) * size, 8)
        keep_ref[g] = total[pl.ds(mine, size), :].astype(keep_ref.dtype)
        send_ref[g] = total[pl.ds(theirs, size), :].astype(BF)


def feed_grad_kernel(ids, k0, n0, k1, n1, c0, c1, t0, t1, t2, t3, *outs, fast):
    units = k0.shape[2]
    rows = lambda refs: jnp.concatenate(refs, axis=0)
    total = outs[-1]
    normed = rows([n0[0], c0[2], n1[0], c1[2]])
    total[:, :units] = dot(normed, rows([k0[1], c0[1], k1[1], c1[1]]), ((0,), (0,)))
    cotangent = rows([r[...] for r in (t0, t1, t2, t3)])
    total[:, units:] = dot(cotangent, rows([k0[0], c0[0], k1[0], c1[0]]), ((0,), (0,)))
    if fast:
        split_rows(ids, total, outs[0], outs[1], ids[9])
    else:
        outs[0][...] = total[...]


def feed_grad(ids, own, other, got_own, got_other, cotangent, fast):
    _, rows, units = own[0].shape
    width = cotangent.shape[1]
    quarter = lambda k: pl.BlockSpec((rows, width), lambda i, s: (s[k], 0))
    normed = pl.BlockSpec((1, rows, width), lambda i, s: (2, 0, 0))
    if fast:
        outs = [shape((4, width // 8, 2 * units), F32), shape((4, width // 8, 2 * units), BF)]
    else:
        outs = [shape((width, 2 * units), F32)]
    return pl.pallas_call(
        functools.partial(feed_grad_kernel, fast=fast),
        grid_spec=pltpu.PrefetchScalarGridSpec(
            num_scalar_prefetch=1,
            grid=(1,),
            in_specs=[
                whole(own[0].shape), normed, whole(other[0].shape), normed, whole(got_own.shape), whole(got_other.shape),
            ]
            + [quarter(k) for k in range(4)],
            out_specs=[whole(o.shape) for o in outs],
            scratch_shapes=[pltpu.VMEM((width, 2 * units), F32)],
        ),
        out_shape=outs,
        compiler_params=params(32),
        cost_estimate=cost(7),
        name="feed_grad",
    )(ids, *own, *other, got_own, got_other, *[cotangent] * 4)


def head_grad_kernel(ids, n0, n1, n2, n3, grads_ref, l0, l1, l2, l3, a0, a1, a2, a3, *outs, fast):
    total, turned = outs[-2:]
    n = a0.shape[0]
    normed = jnp.concatenate([r[...] for r in (n0, n1, n2, n3)], axis=0)
    for part in range(3):
        left = jnp.concatenate([grads_ref[k, part] for k in range(4)], axis=1)
        total[part * n : (part + 1) * n, :] = dot(left, normed)
    low = jnp.concatenate([r[...] for r in (l0, l1, l2, l3)], axis=0)
    total[3 * n :, :] = dot(jnp.concatenate([r[...] for r in (a0, a1, a2, a3)], axis=1), low)
    turned[...] = total[...].T
    if fast:
        split_rows(ids, turned, outs[0], outs[1], ids[9])
    else:
        outs[0][...] = turned[...]


def head_grad(ids, normed, grads, lows, attended, fast):
    seq, width = normed.shape
    rows = seq // 4
    n = grads.shape[2]
    quarter = lambda k: pl.BlockSpec((rows, width), lambda i, s: (s[k], 0))
    specs = [quarter(k) for k in range(4)] + [whole(grads.shape)]
    specs += [whole((rows, width))] * 4 + [whole((n, rows))] * 4
    if fast:
        outs = [shape((4, width // 8, 4 * n), F32), shape((4, width // 8, 4 * n), BF)]
    else:
        outs = [shape((width, 4 * n), F32)]
    return pl.pallas_call(
        functools.partial(head_grad_kernel, fast=fast),
        grid_spec=pltpu.PrefetchScalarGridSpec(
            num_scalar_prefetch=1,
            grid=(1,),
            in_specs=specs,
            out_specs=[whole(o.shape) for o in outs],
            scratch_shapes=[pltpu.VMEM((4 * n, width), F32), pltpu.VMEM((width, 4 * n), F32)],
        ),
        out_shape=outs,
        compiler_params=params(32),
        cost_estimate=cost(0.1),
        name="head_grad",
    )(ids, *[normed] * 4, grads, *lows, *attended)


def pair_kernel(ids, keep_ref, got_ref, *outs):
    for k, o_ref in enumerate(outs):
        at = ids[4 + k]
        o_ref[...] = (keep_ref[at] + got_ref[at].astype(F32)).astype(o_ref.dtype)


def pair_sum(ids, keep, got):
    _, size, n = keep.shape
    return pl.pallas_call(
        pair_kernel,
        grid_spec=pltpu.PrefetchScalarGridSpec(
            num_scalar_prefetch=1,
            grid=(1,),
            in_specs=[whole(keep.shape), whole(got.shape)],
            out_specs=[whole((size, n))] * 4,
        ),
        out_shape=[shape((size, n), F32)] + [shape((size, n), BF)] * 3,
        compiler_params=params(20),
        cost_estimate=cost(0.01),
        name="pair_sum",
    )(ids, keep, got)


def feed_final_kernel(a0, a1, a2, a3, up_ref, down_ref):
    total = a0[...] + a1[...].astype(F32) + a2[...].astype(F32) + a3[...].astype(F32)
    units = up_ref.shape[1]
    up_ref[...] = total[:, :units]
    down_ref[...] = total[:, units:]


def head_final_kernel(a0, a1, a2, a3, q_ref, k_ref, v_ref, o_ref):
    total = a0[...] + a1[...].astype(F32) + a2[...].astype(F32) + a3[...].astype(F32)
    n = q_ref.shape[1]
    q_ref[...] = total[:, :n]
    k_ref[...] = total[:, n : 2 * n]
    v_ref[...] = total[:, 2 * n : 3 * n]
    o_ref[...] = total[:, 3 * n :].T


def final(kernel, arrays, done, outs):
    arrays = [after(arrays[0], done)] + arrays[1:]
    return pl.pallas_call(
        kernel,
        grid=(1,),
        in_specs=[whole(a.shape) for a in arrays],
        out_specs=[whole(o.shape) for o in outs],
        out_shape=outs,
        compiler_params=params(16),
        cost_estimate=cost(1),
        name=kernel.__name__[:-7],
    )(*arrays)


def swap(array, axis, size, bits):
    return lax.ppermute(array, axis, [(i, i ^ bits) for i in range(size)])


def after(array, *others):
    return lax.optimization_barrier((array, others))[0]


def local(
    inputs, page_feat, page_onehot, lengths, hor_pos, ver_pos, norm1_gain, w_query, w_key, w_value,
    rel_table, hor_table, ver_table, w_output, norm2_gain, w_up, w_down, cotangent, *, dp,
):
    seq, width = inputs.shape
    fast = dp == 8
    over = functools.partial(swap, axis="mp", size=4)
    m = lax.axis_index("mp").astype(I32)
    d = lax.axis_index("dp").astype(I32)
    k4 = jnp.arange(4, dtype=I32)
    spot = lambda who: (who & 1) * 2 + (who >> 1)
    ids = jnp.concatenate([
        spot(m ^ k4),
        (d >> 1) ^ k4,
        lengths[:1],
        (d & 1)[None],
    ])
    gain_one, gain_two = norm1_gain[None], norm2_gain[None]
    feats = page_feat[0]
    hor, ver = hor_pos[None], ver_pos[None]
    tables = (rel_table, hor_table, ver_table)
    pages = page_onehot.T
    weights = [w_query.T, w_key.T, w_value.T]

    wo_y, wo_core = over(w_output, bits=2), over(w_output, bits=1)
    normed1, queries, keys, values = project(ids, inputs, pages, feats, gain_one, *weights)
    w_outputs = [w_output, wo_core, wo_y, over(after(wo_y, normed1), bits=1)]
    ups = [w_up, over(after(w_up, normed1), bits=1)]
    downs = [w_down, over(after(w_down, normed1), bits=1)]

    (e_a, att0, att1, inverse_a, out_a), lookups = attend(ids, queries, keys, values, hor, ver, tables, None)
    from_y, from_yc, own1 = over(att0, bits=2), over(att1, bits=3), over(att1, bits=1)
    ver_late = after(ver, att0, w_outputs[3], ups[1], downs[1])
    (e_b, att2, att3, inverse_b, out_b), _ = attend(ids, queries, keys, values, hor, ver_late, tables, lookups)
    attended = [att0, att1, att2, att3]
    for_other = [att2, over(att3, bits=1), from_y, from_yc]
    for_own = [att0, own1, over(att2, bits=2), over(att3, bits=3)]

    fixed = (inputs, pages, feats, gain_two, cotangent)
    x_keep, x_send, _, x_grad, x_ffn = feed(ids, False, *fixed, for_other, w_outputs, ups, downs)
    sent_grad, x_got = over(x_grad, bits=2), over(x_send, bits=1)
    for_own[0] = after(att0, x_ffn)
    m_keep, m_send, mixed, m_grad, m_ffn = feed(ids, True, *fixed, for_own, w_outputs, ups, downs)
    m_grad = after(m_grad, x_got)
    grad_mixed, ga0, core_send, chip_send, far_send, gain_two_part = mid(
        ids, m_grad, sent_grad, mixed, gain_two, cotangent, w_outputs
    )
    m_got = over(after(m_send, ga0), bits=1)
    core_got, chip_got, far_got = over(core_send, bits=1), over(chip_send, bits=2), over(far_send, bits=3)

    around = functools.partial(swap, axis="dp", size=dp)
    feed_grads = feed_grad(ids, (m_keep, m_send), (x_keep, x_send), m_got, x_got, cotangent, fast)
    feed_got = around(feed_grads[1], bits=1) if fast else ids

    scores_a, dq0, dq1, key_sum, value_sum, near, far = back(
        ids, e_a, queries, inverse_a, out_a, keys, values, after(ga0, feed_grads[0], far_got), core_got, None
    )
    chip_got = after(chip_got, dq0)
    core_far, sent_ffn = over(chip_got, bits=1), over(after(x_ffn, dq0), bits=2)
    scores_b, grads, near, far = back(
        ids, e_b, queries, inverse_b, out_b, keys, values, chip_got, far_got,
        (key_sum, value_sum, near, far, dq0, dq1),
    )
    to_core = terms_send(weights, after(grads, core_far, sent_ffn))
    got_terms = over(to_core, bits=1)
    lows = [core_send, core_got, chip_got, core_far]
    head_grads = head_grad(ids, normed1, after(grads, to_core, feed_got), lows, attended, fast)
    head_got = around(head_grads[1], bits=1) if fast else ids
    own_terms, other_terms = terms_keep(weights, after(grads, head_grads[0]), got_terms)
    sent_terms = over(other_terms, bits=2)

    to_z = lambda parts: [parts[0]] + [around(part, bits=2 * k) for k, part in zip((1, 2, 3), parts[1:])]
    size = width // dp
    n = w_query.shape[1]
    units = w_up.shape[1]
    done = own_terms
    if fast:
        feed_parts = to_z(pair_sum(ids, after(feed_grads[0], done), feed_got))
        done = feed_parts[0]
    hor_sums = [table_grads(ids, True, scores_a, after(hor, done), ())]
    rows, gains = last(
        ids, after(own_terms, hor_sums[0]), sent_terms, inputs, pages, feats, gain_one, grad_mixed, gain_two_part,
        mixed, m_ffn, sent_ffn,
    )
    rows_y, rows_core = over(rows, bits=2), over(rows, bits=1)
    done = gains
    if fast:
        head_parts = list(pair_sum(ids, after(head_grads[0], done), head_got))
        done = head_parts[0]
    ver_sums = [table_grads(ids, True, scores_a, after(ver, done), ())]
    done = ver_sums[0]
    if fast:
        grad_up, grad_down = final(feed_final_kernel, feed_parts, done, [shape((size, units), F32)] * 2)
        done = grad_up
        head_parts = to_z([head_parts[0]] + [after(part, done) for part in head_parts[1:]])
    gains = after(gains, done) + over(gains, bits=1)
    got_gains = over(gains, bits=2)
    hor_sums.append(table_grads(ids, False, scores_b, after(hor, done, gains), (near, far)))
    rows_far = over(after(rows_y, hor_sums[1]), bits=1)
    ver_sums.append(table_grads(ids, False, scores_b, after(ver, hor_sums[1]), ()))
    small = pack(gains, got_gains, *hor_sums, *ver_sums)
    if fast:
        got = around(small, bits=1)
        grad_query, grad_key, grad_value, grad_output = final(
            head_final_kernel, head_parts, small, [shape((size, n), F32)] * 3 + [shape((n, size), F32)]
        )
        small = after(small, grad_query) + got
        got = around(small, bits=2)
    else:
        small, got = lax.psum(small, "dp"), jnp.zeros_like(small)
        scatter = lambda a: lax.psum_scatter(a[0], "dp", scatter_dimension=0, tiled=True)
        grad_feed, heads = scatter(feed_grads), scatter(head_grads)
        grad_up, grad_down = grad_feed[:, :units], grad_feed[:, units:]
        grad_query, grad_key, grad_value = heads[:, :n], heads[:, n : 2 * n], heads[:, 2 * n : 3 * n]
        grad_output = heads[:, 3 * n :].T
    quarters = [rows, rows_core, rows_y, rows_far]
    outputs = join(ids, [after(rows, small)] + quarters[1:], 0, BF)
    small = [after(small, outputs), got]
    if fast:
        small = small[0] + small[1]
        small = [small, around(small, bits=4)]
    grad_inputs, grad_feats = join(ids, [after(rows, small[0])] + quarters[1:], 1, F32, pages)
    small[0] = after(small[0], grad_feats)
    grad_rel, grad_hor, grad_ver, gain_sums = unpack(*small, rel_table.shape[1], width)
    gain_sums = lax.dynamic_slice(gain_sums, (0, d * size), (2, size))
    return (
        outputs, grad_inputs, grad_feats[None], gain_sums[0], grad_query, grad_key, grad_value,
        grad_rel, grad_hor, grad_ver, grad_output, gain_sums[1], grad_up, grad_down.T,
    )


def solution(mesh):
    return jax.shard_map(
        functools.partial(local, dp=mesh.shape["dp"]),
        mesh=mesh,
        in_specs=(
            P("dp", None),
            P("dp", None, None),
            P("dp", None),
            P("dp"),
            P("dp"),
            P("dp"),
            P(),
            P(None, "mp"),
            P(None, "mp"),
            P(None, "mp"),
            P("mp", None),
            P("mp", None),
            P("mp", None),
            P("mp", None),
            P(),
            P(None, "mp"),
            P("mp", None),
            P("dp", None),
        ),
        out_specs=(
            P("dp", None),
            P("dp", None),
            P("dp", None, None),
            P("dp"),
            P("dp", "mp"),
            P("dp", "mp"),
            P("dp", "mp"),
            P("mp", None),
            P("mp", None),
            P("mp", None),
            P("mp", "dp"),
            P("dp"),
            P("dp", "mp"),
            P("mp", "dp"),
        ),
        check_vma=False,
    )
```

```python
import functools

import jax
import jax.numpy as jnp
import numpy as np
from jax import lax
from jax.experimental import pallas as pl
from jax.experimental.pallas import tpu as pltpu
from jax.sharding import PartitionSpec as P

EPS = 1e-06
THRESHOLDS = (12, 16, 23, 32, 46, 64, 91)
FAR = 91
HEADS = 3
HD = 64
PAD = 128
MARKS = 72
NEAR = 40
TILES = NEAR + 2
SPAN = 384
LOW = 92
TOP = 311
BF = jnp.bfloat16
F32 = jnp.float32
I32 = jnp.int32
FEED_CHUNK = 256
PLACES = 1024
TABLES_MIB = 18
GELU_C = float(np.sqrt(2.0 / np.pi))


def dot(left, right, dims=((1,), (0,))):
    return lax.dot_general(left, right, (dims, ((), ())), preferred_element_type=F32)


def bucket(delta):
    magnitude = jnp.abs(delta)
    coarse = 8 + sum((magnitude >= limit).astype(I32) for limit in THRESHOLDS)
    return jnp.where(magnitude < 8, magnitude, coarse) + 16 * (delta > 0).astype(I32)


def params(mib):
    return pltpu.CompilerParams(vmem_limit_bytes=mib * 2**20)


def cost(microseconds):
    return pl.CostEstimate(flops=int(1.15e9 * microseconds), bytes_accessed=1, transcendentals=0)


def shape(dims, dtype):
    return jax.ShapeDtypeStruct(dims, dtype)


def whole(dims):
    return pl.BlockSpec(dims, lambda *a: (0,) * len(dims))


VMEM = pl.BlockSpec(memory_space=pltpu.VMEM)


def call(kernel, name, ids, arrays, outs, *, mib, us, scratch=()):
    return pl.pallas_call(
        kernel,
        grid_spec=pltpu.PrefetchScalarGridSpec(
            num_scalar_prefetch=1,
            grid=(1,),
            in_specs=[VMEM] * len(arrays),
            out_specs=jax.tree.map(lambda _: VMEM, outs),
            scratch_shapes=list(scratch),
        ),
        out_shape=outs,
        compiler_params=params(mib),
        cost_estimate=cost(us),
        name=name,
    )(ids, *arrays)


def quarter_of(place, size):
    return pl.ds(pl.multiple_of(place * size, 128), size)


def hidden_rows(inputs, pages, feats):
    return inputs.astype(F32) + dot(pages.astype(F32).astype(BF), feats, ((0,), (0,)))


def unit_rows(field):
    factor = lax.rsqrt(jnp.mean(field * field, axis=-1, keepdims=True) + EPS)
    return field * factor, factor


def project_kernel(ids, x_ref, page_ref, feat_ref, gain_ref, wq_ref, wk_ref, wv_ref, n_ref, q_ref, k_ref, v_ref):
    rows = x_ref.shape[0]
    unit, _ = unit_rows(hidden_rows(x_ref[...], page_ref[...], feat_ref[...]))
    normed = (unit * gain_ref[...].astype(F32)).astype(BF)
    n_ref[...] = normed
    lane = lax.broadcasted_iota(I32, (rows, PAD), 1)
    row = lax.broadcasted_iota(I32, (rows, PAD), 0)
    masked = jnp.where((lane == HD) & (row >= ids[8]), -1e30, 0.0)
    block = lane - MARKS
    far_left = (block >= 0) & (block < 8) & (row < 128 * block - 96)
    far_right = (block >= 8) & (block < 16) & (row >= 128 * (block - 8) + 224)
    masked = jnp.where(far_left | far_right, 1.0, masked)
    query_extra = jnp.where(lane == HD, 1.0, 0.0)
    value_extra = jnp.where((lane == HD) | (lane == HD + 1), 1.0, 0.0)
    for out_ref, w_ref, extra, scale in (
        (q_ref, wq_ref, query_extra, 0.125),
        (k_ref, wk_ref, masked, None),
        (v_ref, wv_ref, value_extra, None),
    ):
        full = dot(normed, w_ref[...], ((1,), (1,)))
        if scale is not None:
            full = full * scale
        pair = full[:, :PAD]
        last = jnp.concatenate([full[:, PAD:], jnp.zeros((rows, PAD - HD), F32)], axis=1)
        heads = (pair, pltpu.roll(pair, HD, 1), last)
        for head in range(HEADS):
            out_ref[:, head * PAD : (head + 1) * PAD] = jnp.where(lane < HD, heads[head], extra).astype(BF)


def project(ids, *arrays):
    seq, width = arrays[0].shape
    outs = [shape((seq, width), BF)] + [shape((seq, HEADS * PAD), BF)] * 3
    return call(project_kernel, "project", ids, arrays, outs, mib=16, us=7)


def place(delta):
    magnitude = jnp.abs(delta)
    coarse = jnp.minimum(25 - lax.clz(delta * delta), 7)
    exact = magnitude < 8
    return jnp.where(exact, magnitude, coarse), exact, delta > 0


def look(table_ref, row, where):
    index, exact, after = where
    found = [jnp.take_along_axis(table_ref[row, part], index, axis=0) for part in range(4)]
    return jnp.where(after, jnp.where(exact, found[2], found[3]), jnp.where(exact, found[0], found[1]))


def tile_delta(tile):
    lane = lax.broadcasted_iota(I32, (8, 128), 1)
    sub = lax.broadcasted_iota(I32, (8, 128), 0)
    delta = 8 * (tile - 13) + sub - lane
    if tile == 0:
        delta = jnp.full_like(delta, -1000)
    if tile == TILES - 1:
        delta = jnp.full_like(delta, 1000)
    return delta


def attend_kernel(*refs, first, chunk):
    ids, q_ref, k_ref, v_ref, hor_ref, ver_ref = refs[:6]
    if first:
        hor_all, ver_all, rel_table, hor_table, ver_table, e_ref, att0, att1, inv_ref, out_ref = refs[6:16]
        rel_ref, t8_ref, hor_col, ver_col, s_ref = refs[16:]
    else:
        rel_ref, t8_ref, hor_col, ver_col, e_ref, att0, att1, inv_ref, out_ref, s_ref = refs[6:]
    seq = k_ref.shape[0]
    width = seq // 4
    lanes = width // 128

    if first:
        for all_ref, col_ref in ((hor_all, hor_col), (ver_all, ver_col)):
            for b in range(seq // 128):
                cols = slice(128 * b, 128 * b + 128)
                spread = jnp.broadcast_to(all_ref[:, cols].astype(F32), (128, 128))
                col_ref[cols, :] = spread.T.astype(I32)
        lane = lax.broadcasted_iota(I32, (8, 32), 1)
        sub = lax.broadcasted_iota(I32, (8, 32), 0)
        for axis, table_ref in enumerate((rel_table, hor_table, ver_table)):
            table = table_ref[...].astype(F32)
            for head in range(HEADS):
                row = jnp.broadcast_to(table[head : head + 1], (8, 32))
                for part in range(4):
                    entries = jnp.sum(jnp.where(lane == sub + 8 * part, row, 0.0), axis=1, keepdims=True)
                    t8_ref[axis * HEADS + head, part] = jnp.broadcast_to(entries, (8, 128))
        for tile in range(TILES):
            where = place(tile_delta(tile))
            for head in range(HEADS):
                rel_ref[head, tile] = look(t8_ref, head, where)

    for part, att_ref in enumerate((att0, att1)):
        place_of = ids[(0 if first else 2) + part]
        here = quarter_of(place_of, width)
        mine = slice(part * width, (part + 1) * width)
        queries = q_ref[here, :]
        hor_row, ver_row = hor_ref[:, here], ver_ref[:, here]
        for head in range(HEADS):
            cols = slice(head * PAD, (head + 1) * PAD)
            s_ref[part, head] = dot(k_ref[:, cols], queries[:, cols], ((1,), (1,)))
        hor = [jnp.broadcast_to(hor_row[:, 128 * l : 128 * l + 128], (8, 128)) for l in range(lanes)]
        ver = [jnp.broadcast_to(ver_row[:, 128 * l : 128 * l + 128], (8, 128)) for l in range(lanes)]
        block = place_of * lanes

        def add_bias(c, tops):
            tops = list(tops)
            base = pl.multiple_of(c * chunk, chunk)
            for g in range(chunk // 8):
                rows = pl.ds(pl.multiple_of(base + 8 * g, 8), 8)
                hor_keys, ver_keys = hor_col[rows, :], ver_col[rows, :]
                for l in range(lanes):
                    cols = pl.ds(128 * l, 128)
                    hor_at, ver_at = place(hor_keys - hor[l]), place(ver_keys - ver[l])
                    tile = jnp.clip(c * (chunk // 8) + g - 16 * (block + l) + 13, 0, TILES - 1)
                    for head in range(HEADS):
                        s = s_ref[part, head, rows, cols] + rel_ref[head, tile]
                        s = s + (look(t8_ref, HEADS + head, hor_at) + look(t8_ref, 2 * HEADS + head, ver_at))
                        s_ref[part, head, rows, cols] = s
                        tops[head * lanes + l] = jnp.maximum(tops[head * lanes + l], s)
            return tuple(tops)

        tops = lax.fori_loop(
            0, seq // chunk, add_bias, tuple(jnp.full((8, 128), -1e30, F32) for _ in range(HEADS * lanes))
        )
        peaks = [jnp.broadcast_to(jnp.max(top, axis=0, keepdims=True), (16, 128)) for top in tops]

        for head in range(HEADS):
            for g in range(seq // 16):
                rows = slice(16 * g, 16 * g + 16)
                for l in range(lanes):
                    cols = slice(128 * l, 128 * l + 128)
                    e_ref[head, rows, slice(part * width + 128 * l, part * width + 128 * l + 128)] = jnp.exp(s_ref[part, head, rows, cols] - peaks[head * lanes + l]).astype(BF)
            total = dot(v_ref[:, head * PAD : (head + 1) * PAD], e_ref[head, :, mine], ((0,), (0,)))
            inverse = 1.0 / total[HD : HD + 1, :]
            inv_ref[head : head + 1, mine] = inverse
            out_ref[head * HD : (head + 1) * HD, mine] = total[:HD] * inverse
        att_ref[...] = out_ref[:, mine].astype(BF)


def attend(ids, queries, keys, values, hor, ver, tables, lookups):
    seq = queries.shape[0]
    width = seq // 4
    first = lookups is None
    columns = HEADS * HD
    made = [
        shape((HEADS, TILES, 8, 128), F32), shape((3 * HEADS, 4, 8, 128), F32), shape((seq, 128), I32), shape((seq, 128), I32)
    ]
    extra = (hor, ver, *tables) if first else tuple(lookups)
    outs = [
        shape((HEADS, seq, 2 * width), BF), shape((columns, width), BF), shape((columns, width), BF),
        shape((HEADS, 2 * width), F32), shape((columns, 2 * width), F32),
    ]
    found = call(
        functools.partial(attend_kernel, first=first, chunk=64),
        "attend_first" if first else "attend_last",
        ids,
        (queries, keys, values, hor, ver, *extra),
        outs + made if first else outs,
        mib=14,
        us=14,
        scratch=[pltpu.VMEM((2, HEADS, seq, width), F32)],
    )
    return found[:5], found[5:]


def feed_kernel(
    ids, x_ref, page_ref, feat_ref, gain_ref, cot_ref, a0, a1, a2, a3, o0, o1, o2, o3, u0, u1, d0, d1,
    keep_ref, send_ref, mixed_ref, grad_ref, ffn_ref, *, slot,
):
    here = quarter_of(ids[slot], mixed_ref.shape[0])
    cotangent = cot_ref[here, :]
    mixed = hidden_rows(x_ref[here, :], page_ref[:, here], feat_ref[...])
    for a_ref, o_ref in ((a0, o0), (a1, o1), (a2, o2), (a3, o3)):
        mixed = mixed + dot(a_ref[...], o_ref[...], ((0,), (0,)))
    mixed_ref[...] = mixed
    unit, _ = unit_rows(mixed)
    normed = (unit * gain_ref[...].astype(F32)).astype(BF)
    send_ref[2] = normed
    units = u0.shape[1]
    for u_ref, d_ref, goal in ((u0, d0, keep_ref), (u1, d1, send_ref)):
        for at in range(0, units, FEED_CHUNK):
            cols = slice(at, at + FEED_CHUNK)
            upward = dot(normed, u_ref[:, cols])
            square = upward * upward
            tanh = jnp.tanh(GELU_C * upward * (1.0 + 0.044715 * square))
            lifted = 0.5 * (1.0 + tanh)
            activated = (upward * lifted).astype(BF)
            slope = lifted + 0.5 * upward * (1.0 - tanh * tanh) * (GELU_C * (1.0 + 3 * 0.044715 * square))
            grad_up = (dot(cotangent, d_ref[cols, :], ((1,), (1,))) * slope).astype(BF)
            goal[0, :, cols] = activated
            goal[1, :, cols] = grad_up
    ffn = dot(keep_ref[0], d0[...]) + dot(send_ref[0], d1[...])
    ffn_ref[...] = ffn.astype(ffn_ref.dtype)
    grad = dot(keep_ref[1], u0[...], ((1,), (1,))) + dot(send_ref[1], u1[...], ((1,), (1,)))
    grad_ref[...] = grad.astype(grad_ref.dtype)


def feed(ids, own, inputs, onehot, feats, gain, cotangent, attended, w_outputs, ups, downs):
    seq, width = inputs.shape
    rows = seq // 4
    units = ups[0].shape[1]
    kept = F32 if own else BF
    outs = [
        shape((2, rows, units), BF), shape((3, rows, width), BF), shape((rows, width), F32),
        shape((rows, width), BF), shape((rows, width), kept),
    ]
    return call(
        functools.partial(feed_kernel, slot=0 if own else 2),
        "feed_own" if own else "feed_other",
        ids,
        (inputs, onehot, feats, gain, cotangent, *attended, *w_outputs, *ups, *downs),
        outs,
        mib=16,
        us=20 if own else 10,
    )


def add_kernel(ids, one_ref, two_ref, out_ref):
    out_ref[...] = one_ref[...].astype(F32) + two_ref[...].astype(F32)


def add(ids, one, two):
    return call(add_kernel, "add", ids, (one, two), shape(one.shape, F32), mib=8, us=20)


def mid_kernel(
    ids, own_grad, own_mixed, other_grad, other_got, other_mixed, cot_ref, gain_ref, o0, o1,
    grad_ref, own_ref, core_ref, low_ref, part_ref,
):
    rows = own_grad.shape[0]
    other = other_grad[...].astype(F32) + other_got[...].astype(F32)
    for at, (grad_normed, mixed_ref) in enumerate(((own_grad[...], own_mixed), (other, other_mixed))):
        unit, factor = unit_rows(mixed_ref[...])
        scaled = grad_normed * gain_ref[...].astype(F32)
        grad = factor * (scaled - unit * jnp.mean(scaled * unit, axis=-1, keepdims=True))
        grad = cot_ref[quarter_of(ids[2 * at], rows), :].astype(F32) + grad
        low = grad.astype(BF)
        low_ref[at] = low
        if at == 0:
            grad_ref[...] = grad
            part_ref[...] = jnp.sum(grad_normed * unit, axis=0, keepdims=True)
        for o_ref, goal in ((o0, own_ref), (o1, core_ref)):
            goal[:, at * rows : (at + 1) * rows] = dot(o_ref[...], low, ((1,), (1,))).astype(BF)


def mid(ids, own, other, gain, cotangent, w_outputs):
    rows, width = own[0].shape
    columns = HEADS * HD
    outs = [
        shape((rows, width), F32), shape((columns, 2 * rows), BF), shape((columns, 2 * rows), BF), shape((2, rows, width), BF),
        shape((1, width), F32),
    ]
    arrays = (*own, *other, cotangent, gain, *w_outputs)
    return call(mid_kernel, "mid", ids, arrays, outs, mib=16, us=10)


def back_kernel(*refs, first):
    ids, ea_ref, eb_ref, inv_a, inv_b, out_a, out_b, q_ref, k_ref, v_ref, grad_ref = refs[:11]
    refs = refs[11:]
    if first:
        ds_ref, dqa_ref, dqb_ref, key_ref, value_ref, near_ref, far_ref, x_ref = refs
    else:
        key_in, value_in, near_in, far_in, dqa_in, dqb_in = refs[:6]
        ds_ref, all_ref, near_ref, far_ref, x_ref = refs[6:]
    seq = k_ref.shape[0]
    width = seq // 4
    both = 2 * width
    lanes = width // 128
    base = 0 if first else 1
    sub = lax.broadcasted_iota(I32, (HD, both), 0)
    blocks = [ids[base + 2 * (l // lanes)] * lanes + l % lanes for l in range(2 * lanes)]
    mine = slice(base * width, (base + 1) * width)
    here = [quarter_of(ids[base + 2 * n], width) for n in range(2)]
    beside = lambda one, two: jnp.concatenate([one, two], axis=1)
    spot = lax.broadcasted_iota(I32, (8, 128), 0)

    for head in range(HEADS):
        cols = slice(head * PAD, (head + 1) * PAD)
        rows = slice(head * HD, (head + 1) * HD)
        grad = grad_ref[rows, :].astype(F32)
        grad = (grad * beside(inv_a[head : head + 1, mine], inv_b[head : head + 1, mine])).astype(BF).astype(F32)
        inner = jnp.sum(grad * beside(out_a[rows, mine], out_b[rows, mine]), axis=0, keepdims=True)
        high = inner.astype(BF).astype(F32)
        extra = jnp.where(sub == 0, -high, jnp.where(sub == 1, high - inner, 0.0))
        right = jnp.concatenate([grad, extra], axis=0).astype(BF)
        x_ref[head % 2] = dot(v_ref[:, cols], right)
        value = dot(beside(ea_ref[head, :, mine], eb_ref[head, :, mine]), right, ((1,), (1,)))
        for c in range(seq // 16):
            at = slice(16 * c, 16 * c + 16)
            found = beside(ea_ref[head, at, mine], eb_ref[head, at, mine]).astype(F32)
            ds_ref[head, at, :] = (found * x_ref[head % 2, at, :]).astype(BF)
        grad = ds_ref[head]
        key = dot(grad, jnp.concatenate([q_ref[at, cols] for at in here], axis=0))
        query = dot(k_ref[:, cols], grad, ((0,), (0,)))
        query_a = (query[:HD, :width] * 0.125).astype(BF)
        query_b = (query[:HD, width:] * 0.125).astype(BF)

        for g in range(NEAR // 2):
            total = None if first else near_in[head, 16 * g : 16 * g + 16]
            for l, block in enumerate(blocks):
                start = 128 * block - 96 + 16 * g
                inside = (start >= 0) & (start < seq)
                at = pl.ds(pl.multiple_of(jnp.clip(start, 0, seq - 16), 16), 16)
                found = ds_ref[head, at, 128 * l : 128 * l + 128].astype(F32)
                found = jnp.where(inside, found, 0.0)
                total = found if total is None else total + found
            near_ref[head, 16 * g : 16 * g + 16] = total
        for side in range(2):
            total = None if first else far_in[head, 8 * side : 8 * side + 8]
            for l, block in enumerate(blocks):
                marks = query[MARKS + 8 * side : MARKS + 8 * side + 8, 128 * l : 128 * l + 128]
                marks = jnp.where(spot == block, marks, 0.0)
                total = marks if total is None else total + marks
            far_ref[head, 8 * side : 8 * side + 8] = total

        if first:
            key_ref[:, cols] = key
            value_ref[:, cols] = value
            dqa_ref[rows, :] = query_a
            dqb_ref[rows, :] = query_b
        else:
            for k, found in enumerate((dqa_in[rows, :], query_a, dqb_in[rows, :], query_b)):
                all_ref[k, 0, rows, :] = found
            for part, acc in ((1, key_in[:, cols] + key), (2, value_in[:, cols] + value)):
                turned = acc.T[:HD].astype(BF)
                for q in range(4):
                    k = sum((jnp.where(ids[n] == q, n, 0) for n in range(1, 4)))
                    all_ref[k, part, rows, :] = turned[:, q * width : (q + 1) * width]


def back(ids, attended, queries, keys, values, grads, carried):
    seq, wide = queries.shape
    width = seq // 4
    first = carried is None
    columns = HEADS * HD
    queried = [shape((columns, width), BF)] * 2
    sums = [shape((seq, wide), F32)] * 2
    rel = [shape((HEADS, 8 * NEAR, 128), F32), shape((HEADS, 16, 128), F32)]
    outs = [shape((HEADS, seq, 2 * width), BF)]
    outs += queried + sums if first else [shape((4, 3, columns, width), BF)]
    outs += rel
    arrays = (*attended[0], *attended[1], *attended[2], queries, keys, values, grads, *(() if first else carried))
    return call(
        functools.partial(back_kernel, first=first),
        "back_first" if first else "back_last",
        ids,
        arrays,
        outs,
        mib=16,
        us=2 if first else 0.01,
        scratch=[pltpu.VMEM((2, seq, 2 * width), F32)],
    )


def places_kernel(ids, hor_ref, ver_ref, hor_at, ver_at):
    places, seq = hor_at.shape
    for keys_ref, goal in ((hor_ref, hor_at), (ver_ref, ver_at)):
        for b in range(places // 128):
            spot = lax.broadcasted_iota(I32, (128, seq), 0) + 128 * b
            goal[128 * b : 128 * b + 128, :] = jnp.where(spot == keys_ref[...], 1.0, 0.0).astype(BF)


def places_of(ids, hor, ver):
    return call(places_kernel, "places", ids, (hor, ver), [shape((PLACES, hor.shape[1]), BF)] * 2, mib=8, us=0.01)


def tables_kernel(ids, s_ref, e_ref, q_ref, *refs, base):
    diagonals = refs[:-3]
    out_ref, left_ref, right_ref = refs[-3:]
    width = s_ref.shape[2]
    groups = e_ref.shape[0] // 128
    query = jnp.concatenate([q_ref[:, quarter_of(ids[base + n], width // 2)] for n in (0, 2)], axis=1)
    column = lax.broadcasted_iota(I32, (SPAN, width), 0)
    for b in range(groups):
        window = jnp.clip(128 * b + TOP - LOW - query, 0, TOP)
        right_ref[:, b * width : (b + 1) * width] = jnp.where(column == window, 1.0, 0.0).astype(BF)
    for head in range(HEADS):
        moved = dot(e_ref[...], s_ref[head]).astype(BF)
        for b in range(groups):
            left_ref[head * 128 : head * 128 + 128, b * width : (b + 1) * width] = moved[128 * b : 128 * b + 128]
    found = dot(left_ref[...], right_ref[...], ((1,), (1,)))

    def to_buckets(sums, delta):
        spot = lax.broadcasted_iota(I32, (32, sums.shape[1]), 0)
        return jnp.sum(jnp.where(bucket(delta) == spot, sums, 0.0), axis=1, keepdims=True)

    lane = lax.broadcasted_iota(I32, (1, 512), 1)
    columns = []
    for h in range(HEADS):
        grid = jnp.concatenate([found[h * 128 : h * 128 + 128, :], jnp.zeros((128, 512 - SPAN), F32)], axis=1)
        grid = pltpu.roll(grid, 0, 1, stride=1, stride_axis=0)
        columns.append(to_buckets(jnp.sum(grid, axis=0, keepdims=True), lane + LOW - TOP))
    spread = lax.broadcasted_iota(I32, (32, 128), 1)
    rows_of = lambda columns: sum(jnp.where(spread == at, column, 0.0) for at, column in enumerate(columns)).T[:8]
    out_ref[0] = rows_of(columns)
    if diagonals:
        near_ref, far_ref = diagonals
        flip = 7 - lax.broadcasted_iota(I32, (8, 128), 0)
        spot = lax.broadcasted_iota(I32, (32, 1), 0)
        columns = []
        for h in range(HEADS):
            near = [jnp.take_along_axis(near_ref[h, 8 * t : 8 * t + 8], flip, axis=0) for t in reversed(range(NEAR))]
            grid = jnp.concatenate(near, axis=0)
            grid = jnp.concatenate([grid, jnp.zeros((8 * NEAR, 384), F32)], axis=1)
            grid = pltpu.roll(grid, 0, 1, stride=1, stride_axis=0)
            near_sums = to_buckets(jnp.sum(grid, axis=0, keepdims=True), 8 * NEAR - 1 - 8 * 12 - lane)
            left = jnp.sum(jnp.sum(far_ref[h, :8], axis=0, keepdims=True), axis=1, keepdims=True)
            right = jnp.sum(jnp.sum(far_ref[h, 8:], axis=0, keepdims=True), axis=1, keepdims=True)
            columns.append(near_sums + jnp.where(spot == 15, left, 0.0) + jnp.where(spot == 31, right, 0.0))
        out_ref[1] = rows_of(columns)


def table_grads(ids, first, scores, places, positions, sums=()):
    wide = PLACES // 128 * positions.shape[1] // 2
    return call(
        functools.partial(tables_kernel, base=0 if first else 1),
        "table_grads",
        ids,
        (scores, places, positions, *sums),
        shape((2 if sums else 1, 8, 32), F32),
        mib=TABLES_MIB,
        us=0.01,
        scratch=[pltpu.VMEM((HEADS * 128, wide), BF), pltpu.VMEM((SPAN, wide), BF)],
    )


def terms_of(grads, weights):
    total = None
    for part, w_ref in enumerate(weights):
        found = dot(grads[part], w_ref[...], ((0,), (0,)))
        total = found if total is None else total + found
    return total


def terms_send_kernel(ids, w0, w1, w2, grads_ref, *outs):
    for at, out_ref in enumerate(outs):
        out_ref[...] = terms_of(grads_ref[2 * at + 1], (w0, w1, w2)).astype(BF)


def terms_keep_kernel(ids, w0, w1, w2, grads_ref, got_own, got_other, own_ref, other_ref):
    other_ref[...] = (terms_of(grads_ref[2], (w0, w1, w2)) + got_other[...].astype(F32)).astype(BF)
    own_ref[...] = terms_of(grads_ref[0], (w0, w1, w2)) + got_own[...].astype(F32)


def terms_send(ids, weights, grads):
    outs = [shape((grads.shape[3], weights[0].shape[1]), BF)] * 2
    return call(terms_send_kernel, "terms_send", ids, (*weights, grads), outs, mib=16, us=0.01)


def terms_keep(ids, weights, grads, got):
    outs = [shape(got[0].shape, F32), shape(got[0].shape, BF)]
    return call(terms_keep_kernel, "terms_keep", ids, (*weights, grads, *got), outs, mib=16, us=0.01)


def last_kernel(
    ids, mine_ref, sent_ref, x_ref, page_ref, feat_ref, gain_ref, grad_ref, second_ref, mixed_ref, ffn_ref, got_ref,
    out_ref, part_ref,
):
    grad_normed = mine_ref[...] + sent_ref[...].astype(F32)
    here = quarter_of(ids[0], mine_ref.shape[0])
    unit, factor = unit_rows(hidden_rows(x_ref[here, :], page_ref[:, here], feat_ref[...]))
    scaled = grad_normed * gain_ref[...].astype(F32)
    grad = factor * (scaled - unit * jnp.mean(scaled * unit, axis=-1, keepdims=True))
    rows, width = grad.shape
    out_ref[0, :rows] = (mixed_ref[...] + ffn_ref[...] + got_ref[...].astype(F32)).astype(BF)
    out_ref[1, :rows] = (grad_ref[...] + grad).astype(BF)
    part_ref[0:1] = jnp.sum(grad_normed * unit, axis=0, keepdims=True)
    part_ref[1:2] = second_ref[...]


def last(ids, mine, sent, inputs, onehot, feats, gain, grad_mixed, second, *ffn):
    rows, width = mine.shape
    arrays = (mine, sent, inputs, onehot, feats, gain, grad_mixed, second, *ffn)
    outs = [shape((2, rows, width), BF), shape((2, width), F32)]
    return call(last_kernel, "last", ids, arrays, outs, mib=16, us=0.01)


def pack_kernel(ids, gains_ref, got_ref, hor_a, ver_a, hor_b, ver_b, out_ref):
    gains = gains_ref[...] + got_ref[...]
    gains = [gains[slot : slot + 1] for slot in range(2)]
    parts = gains[0].shape[1] // 128
    for slot in range(2):
        gain = gains[slot]
        for part in range(parts):
            at = slot * parts + part
            out_ref[at : at + 1, :] = gain[:, part * 128 : part * 128 + 128]
    bins = hor_a.shape[2]
    at = 2 * parts
    out_ref[at:, :] = jnp.zeros((out_ref.shape[0] - at, 128), F32)
    for found in (hor_b[1], hor_a[0] + hor_b[0], ver_a[0] + ver_b[0]):
        out_ref[at : at + HEADS, :bins] = found[:HEADS]
        at += HEADS


def pack(ids, gains, got, *sums):
    size = gains.shape[1] // 128 * 2 + 3 * HEADS
    size = -(-size // 8) * 8
    return call(pack_kernel, "pack", ids, (gains, got, *sums), shape((size, 128), F32), mib=8, us=0.1)


def unpack_kernel(a_ref, b_ref, rel_ref, hor_ref, ver_ref, gains_ref):
    total = a_ref[...] + b_ref[...]
    parts = gains_ref.shape[1] // 128
    for row in range(2):
        for part in range(parts):
            at = row * parts + part
            gains_ref[row : row + 1, part * 128 : part * 128 + 128] = total[at : at + 1]
    at, bins = 2 * parts, rel_ref.shape[1]
    for goal in (rel_ref, hor_ref, ver_ref):
        goal[...] = total[at : at + HEADS, :bins]
        at += HEADS


def unpack(one, two, bins, width):
    spec = pl.BlockSpec(memory_space=pltpu.VMEM)
    return pl.pallas_call(
        unpack_kernel,
        in_specs=[spec] * 2,
        out_specs=[spec] * 4,
        out_shape=[shape((HEADS, bins), F32)] * 3 + [shape((2, width), F32)],
        compiler_params=params(16),
        cost_estimate=cost(0.1),
        name="unpack",
    )(one, two)


def join_kernel(ids, b0, b1, b2, b3, out_ref, *, slot):
    for k, b_ref in enumerate((b0, b1, b2, b3)):

        @pl.when(pl.program_id(0) == k)
        def _(b_ref=b_ref):
            out_ref[...] = b_ref[slot, : out_ref.shape[0]].astype(out_ref.dtype)


def join_feat_kernel(ids, b0, b1, b2, b3, page_ref, out_ref, feat_ref, all_ref, *, slot):
    step = pl.program_id(0)
    rows = out_ref.shape[0]
    for k, b_ref in enumerate((b0, b1, b2, b3)):

        @pl.when(step == k)
        def _(b_ref=b_ref, k=k):
            out_ref[...] = b_ref[slot, :rows].astype(out_ref.dtype)
            all_ref[pl.ds(pl.multiple_of(ids[k] * rows, rows), rows), :] = b_ref[slot, :rows]

    @pl.when(step == 3)
    def _():
        feat_ref[...] = dot(page_ref[...].astype(F32).astype(BF), all_ref[...])


def join(ids, blocks, slot, dtype, onehot=None):
    _, rows, width = blocks[0].shape
    specs = [VMEM] * 4
    outs, out_specs = [shape((4 * rows, width), dtype)], [pl.BlockSpec((rows, width), lambda i, s: (s[i], 0))]
    extra, scratch = (), []
    if onehot is not None:
        pages = onehot.shape[0]
        specs = specs + [VMEM]
        outs.append(shape((pages, width), F32))
        out_specs.append(whole((pages, width)))
        extra, scratch = (onehot,), [pltpu.VMEM((4 * rows, width), BF)]
    found = pl.pallas_call(
        functools.partial(join_kernel if onehot is None else join_feat_kernel, slot=slot),
        grid_spec=pltpu.PrefetchScalarGridSpec(
            num_scalar_prefetch=1, grid=(4,), in_specs=specs, out_specs=out_specs, scratch_shapes=scratch
        ),
        out_shape=outs,
        compiler_params=params(16),
        cost_estimate=cost(0.01),
        name="join_output" if onehot is None else "join_grads",
    )(ids, *blocks, *extra)
    return found[0] if onehot is None else found


def split_rows(ids, total, cols, keep_ref, send_ref, parity):
    groups, size = keep_ref.shape[0], keep_ref.shape[1]
    for g in range(groups):
        mine = pl.multiple_of((2 * g + parity) * size, 8)
        theirs = pl.multiple_of((2 * g + 1 - parity) * size, 8)
        keep_ref[g] = total[pl.ds(mine, size), cols].astype(keep_ref.dtype)
        send_ref[g] = total[pl.ds(theirs, size), cols].astype(BF)


def feed_grad_kernel(ids, k0, n0, k1, n1, c0, c1, cot_ref, *outs, fast):
    units = k0.shape[2]
    rows = lambda refs: jnp.concatenate(refs, axis=0)
    total = outs[-1]
    normed = rows([n0[2], c0[2], n1[2], c1[2]])
    total[:, :units] = dot(normed, rows([k0[1], c0[1], k1[1], c1[1]]), ((0,), (0,)))
    cotangent = rows([cot_ref[quarter_of(ids[n], k0.shape[1]), :] for n in range(4)])
    total[:, units:] = dot(cotangent, rows([k0[0], c0[0], k1[0], c1[0]]), ((0,), (0,)))
    if fast:
        split_rows(ids, total, slice(None), outs[0], outs[1], ids[9])
    else:
        outs[0][...] = total[...]


def feed_grad(ids, own, other, got_own, got_other, cotangent, fast):
    _, rows, units = own[0].shape
    width = cotangent.shape[1]
    if fast:
        outs = [shape((4, width // 8, 2 * units), F32), shape((4, width // 8, 2 * units), BF)]
    else:
        outs = [shape((width, 2 * units), F32)]
    return call(
        functools.partial(feed_grad_kernel, fast=fast),
        "feed_grad",
        ids,
        (*own, *other, got_own, got_other, cotangent),
        outs,
        mib=24,
        us=7,
        scratch=[pltpu.VMEM((width, 2 * units), F32)],
    )


def head_grad_kernel(ids, normed_ref, grads_ref, low_ref, got_ref, a0, a1, a2, a3, *outs, fast):
    total, turned = outs[-2:]
    n = a0.shape[0]
    normed = jnp.concatenate([normed_ref[quarter_of(ids[k], a0.shape[1]), :] for k in range(4)], axis=0)
    for part in range(3):
        left = jnp.concatenate([grads_ref[k, part] for k in range(4)], axis=1)
        total[part * n : (part + 1) * n, :] = dot(left, normed)
    low = jnp.concatenate([low_ref[0], got_ref[0], low_ref[1], got_ref[1]], axis=0)
    total[3 * n :, :] = dot(jnp.concatenate([r[...] for r in (a0, a1, a2, a3)], axis=1), low)
    turned[...] = total[...].T
    if fast:
        split_rows(ids, turned, slice(None), outs[0], outs[1], ids[9])
    else:
        outs[0][...] = turned[...]


def head_grad(ids, normed, grads, low, low_got, attended, fast):
    seq, width = normed.shape
    n = grads.shape[2]
    if fast:
        outs = [shape((4, width // 8, 4 * n), F32), shape((4, width // 8, 4 * n), BF)]
    else:
        outs = [shape((width, 4 * n), F32)]
    return call(
        functools.partial(head_grad_kernel, fast=fast),
        "head_grad",
        ids,
        (normed, grads, low, low_got, *attended),
        outs,
        mib=18,
        us=0.01,
        scratch=[pltpu.VMEM((4 * n, width), F32), pltpu.VMEM((width, 4 * n), F32)],
    )


def pair_kernel(ids, *refs):
    pairs, outs = refs[:-4], refs[-4:]
    for k, o_ref in enumerate(outs):
        at = ids[4 + k]
        start = 0
        for keep_ref, got_ref in zip(pairs[::2], pairs[1::2]):
            n = keep_ref.shape[2]
            o_ref[:, start : start + n] = (keep_ref[at] + got_ref[at].astype(F32)).astype(o_ref.dtype)
            start += n


def pair_sum(ids, *arrays):
    size = arrays[0].shape[1]
    n = sum(a.shape[2] for a in arrays[::2])
    outs = [shape((size, n), F32)] + [shape((size, n), BF)] * 3
    return call(pair_kernel, "pair_sum", ids, arrays, outs, mib=16, us=0.01)


def feed_final_kernel(a0, a1, a2, a3, up_ref, down_ref):
    total = a0[...] + a1[...].astype(F32) + a2[...].astype(F32) + a3[...].astype(F32)
    units = up_ref.shape[1]
    up_ref[...] = total[:, :units]
    down_ref[...] = total[:, units:]


def head_final_kernel(a0, a1, a2, a3, q_ref, k_ref, v_ref, o_ref):
    total = a0[...] + a1[...].astype(F32) + a2[...].astype(F32) + a3[...].astype(F32)
    n = q_ref.shape[1]
    for at, goal in enumerate((q_ref, k_ref, v_ref)):
        goal[...] = total[:, at * n : (at + 1) * n]
    o_ref[...] = total[:, 3 * n :].T


def final(kernel, arrays, done, outs):
    arrays = [after(arrays[0], done)] + arrays[1:]
    return pl.pallas_call(
        kernel,
        grid=(1,),
        in_specs=[VMEM] * len(arrays),
        out_specs=jax.tree.map(lambda o: whole(o.shape), outs),
        out_shape=outs,
        compiler_params=params(16),
        cost_estimate=cost(6 if kernel is feed_final_kernel else 0.01),
        name=kernel.__name__[:-7],
    )(*arrays)


def swap(array, axis, size, bits):
    return lax.ppermute(array, axis, [(i, i ^ bits) for i in range(size)])


def after(array, *others):
    return lax.optimization_barrier((array, others))[0]


def local(
    inputs, page_feat, page_onehot, lengths, hor_pos, ver_pos, norm1_gain, w_query, w_key, w_value,
    rel_table, hor_table, ver_table, w_output, norm2_gain, w_up, w_down, cotangent, *, dp,
):
    seq, width = inputs.shape
    fast = dp == 8
    over = functools.partial(swap, axis="mp", size=4)
    m = lax.axis_index("mp").astype(I32)
    d = lax.axis_index("dp").astype(I32)
    k4 = jnp.arange(4, dtype=I32)
    spot = lambda who: (who & 1) * 2 + (who >> 1)
    ids = jnp.concatenate([
        spot(m ^ k4),
        (d >> 1) ^ k4,
        lengths[:1],
        (d & 1)[None],
    ])
    gain_one, gain_two = norm1_gain[None], norm2_gain[None]
    feats = page_feat[0]
    hor, ver = hor_pos[None], ver_pos[None]
    tables = (rel_table, hor_table, ver_table)
    pages = page_onehot.T
    weights = [w_query.T, w_key.T, w_value.T]

    wo_y, wo_core = over(w_output, bits=2), over(w_output, bits=1)
    normed1, queries, keys, values = project(ids, inputs, pages, feats, gain_one, *weights)
    w_outputs = [w_output, wo_core, wo_y, over(after(wo_y, normed1), bits=1)]
    ups = [w_up, over(after(w_up, normed1), bits=1)]
    downs = [w_down, over(after(w_down, normed1), bits=1)]

    (e_a, att0, att1, inverse_a, out_a), lookups = attend(ids, queries, keys, values, hor, ver, tables, None)
    from_y, from_yc, own1 = over(att0, bits=2), over(att1, bits=3), over(att1, bits=1)
    ver_late = after(ver, att0, w_outputs[3], ups[1], downs[1])
    (e_b, att2, att3, inverse_b, out_b), _ = attend(ids, queries, keys, values, hor, ver_late, tables, lookups)
    attended = [att0, att1, att2, att3]
    for_other = [att2, over(att3, bits=1), from_y, from_yc]
    for_own = [att0, own1, over(att2, bits=2), over(att3, bits=3)]

    around = functools.partial(swap, axis="dp", size=dp)
    to_z = lambda parts: [parts[0]] + [around(part, bits=2 * k) for k, part in zip((1, 2, 3), parts[1:])]
    size = width // dp
    n = w_query.shape[1]
    units = w_up.shape[1]
    fixed = (inputs, pages, feats, gain_two, cotangent)
    x_keep, x_send, x_mixed, x_grad, x_ffn = feed(ids, False, *fixed, for_other, w_outputs, ups, downs)
    got_own, x_got = over(x_grad, bits=2), over(x_send, bits=1)
    for_own[0] = after(att0, x_ffn)
    m_keep, m_send, mixed, m_grad, m_ffn = feed(ids, True, *fixed, for_own, w_outputs, ups, downs)
    got_other, m_got = over(m_grad, bits=2), over(after(m_send, x_got), bits=1)
    own_grad = add(ids, m_grad, got_own)

    feed_grads = feed_grad(ids, (after(m_keep, own_grad), m_send), (x_keep, x_send), m_got, x_got, cotangent, fast)
    feed_got = around(feed_grads[1], bits=1) if fast else ids
    hor_at, ver_at = places_of(ids, after(hor, feed_grads[0]), ver)
    grad_mixed, ga, core_send, low, gain_two_part = mid(
        ids, (after(own_grad, hor_at), mixed), (x_grad, got_other, x_mixed), gain_two, cotangent, w_outputs[:2]
    )
    core_got = over(core_send, bits=1)
    sent_ffn = over(after(x_ffn, ga), bits=2)

    halves = ((e_a, e_b), (inverse_a, inverse_b), (out_a, out_b))
    scores_a, dq0, dq2, key_sum, value_sum, near, far = back(ids, halves, queries, keys, values, ga, None)
    scores_b, grads, near, far = back(
        ids, halves, queries, keys, values, after(core_got, dq0), (key_sum, value_sum, near, far, dq0, dq2)
    )
    low_got = over(low, bits=1)
    to_core = terms_send(ids, weights, after(grads, sent_ffn))
    got_terms = [over(part, bits=1) for part in to_core]
    own_terms, other_terms = terms_keep(ids, weights, after(grads, to_core[0]), got_terms)
    sent_terms = over(other_terms, bits=2)

    hor_a = table_grads(ids, True, scores_a, hor_at, after(hor, own_terms))
    head_grads = head_grad(ids, normed1, after(grads, hor_a), low, low_got, attended, fast)
    done = head_grads[0]
    if fast:
        feed_parts = to_z(pair_sum(ids, after(feed_grads[0], done, sent_terms), feed_got))
        done = feed_parts[0]
    head_got = around(after(head_grads[1], done), bits=1) if fast else ids
    rows, gains = last(
        ids, after(own_terms, done), sent_terms, inputs, pages, feats, gain_one, grad_mixed, gain_two_part,
        mixed, m_ffn, sent_ffn,
    )
    rows_y, rows_core = over(rows, bits=2), over(rows, bits=1)
    ver_a = table_grads(ids, True, scores_a, ver_at, after(ver, rows))
    gains = after(gains, ver_a) + over(gains, bits=1)
    got_gains = over(gains, bits=2)
    hor_b = table_grads(ids, False, scores_b, hor_at, after(hor, gains, head_got), (near, far))
    ver_b = table_grads(ids, False, scores_b, ver_at, after(ver, hor_b))

    small = pack(ids, gains, got_gains, hor_a, ver_a, hor_b, ver_b)
    if fast:
        small = small + around(small, bits=1)
        grad_up, grad_down = final(feed_final_kernel, feed_parts, small, [shape((size, units), F32)] * 2)
        head_parts = to_z(pair_sum(ids, after(head_grads[0], grad_up), head_got))
        got = around(small, bits=2)
        quarters = [rows, rows_core, rows_y, over(after(rows_y, grad_up), bits=1)]
        outputs = join(ids, [after(rows, small)] + quarters[1:], 0, BF)
        small = after(small, outputs) + got
        got = around(small, bits=4)
        grad_inputs, grad_feats = join(ids, [after(rows, small)] + quarters[1:], 1, F32, pages)
        grad_query, grad_key, grad_value, grad_output = final(
            head_final_kernel, head_parts, grad_feats, [shape((size, n), F32)] * 3 + [shape((n, size), F32)]
        )
        small = [after(small, grad_query), got]
    else:
        quarters = [rows, rows_core, rows_y, over(rows_y, bits=1)]
        outputs = join(ids, quarters, 0, BF)
        grad_inputs, grad_feats = join(ids, quarters, 1, F32, pages)
        small = [lax.psum(small, "dp"), jnp.zeros_like(small)]
        scatter = lambda a: lax.psum_scatter(a[0], "dp", scatter_dimension=0, tiled=True)
        grad_feed, heads = scatter(feed_grads), scatter(head_grads)
        grad_up, grad_down = grad_feed[:, :units], grad_feed[:, units:]
        grad_query, grad_key, grad_value = heads[:, :n], heads[:, n : 2 * n], heads[:, 2 * n : 3 * n]
        grad_output = heads[:, 3 * n :].T
    grad_rel, grad_hor, grad_ver, gain_sums = unpack(*small, rel_table.shape[1], width)
    gain_sums = lax.dynamic_slice(gain_sums, (0, d * size), (2, size))
    return (
        outputs, grad_inputs, grad_feats[None], gain_sums[0], grad_query, grad_key, grad_value,
        grad_rel, grad_hor, grad_ver, grad_output, gain_sums[1], grad_up, grad_down.T,
    )


def solution(mesh):
    return jax.shard_map(
        functools.partial(local, dp=mesh.shape["dp"]),
        mesh=mesh,
        in_specs=(
            P("dp", None),
            P("dp", None, None),
            P("dp", None),
            P("dp"),
            P("dp"),
            P("dp"),
            P(),
            P(None, "mp"),
            P(None, "mp"),
            P(None, "mp"),
            P("mp", None),
            P("mp", None),
            P("mp", None),
            P("mp", None),
            P(),
            P(None, "mp"),
            P("mp", None),
            P("dp", None),
        ),
        out_specs=(
            P("dp", None),
            P("dp", None),
            P("dp", None, None),
            P("dp"),
            P("dp", "mp"),
            P("dp", "mp"),
            P("dp", "mp"),
            P("mp", None),
            P("mp", None),
            P("mp", None),
            P("mp", "dp"),
            P("dp"),
            P("dp", "mp"),
            P("mp", "dp"),
        ),
        check_vma=False,
    )
```

```python
import functools

import jax
import jax.numpy as jnp
import numpy as np
from jax import lax
from jax.experimental import pallas as pl
from jax.experimental.pallas import tpu as pltpu
from jax.sharding import PartitionSpec as P

EPS = 1e-06
THRESHOLDS = (12, 16, 23, 32, 46, 64, 91)
FAR = 91
HEADS = 3
HD = 64
PAD = 128
MARKS = 72
NEAR = 40
TILES = NEAR + 2
SPAN = 384
LOW = 92
TOP = 311
BF = jnp.bfloat16
F32 = jnp.float32
I32 = jnp.int32
FEED_CHUNK = 256
PLACES = 1024
TABLES_MIB = 18
GELU_C = float(np.sqrt(2.0 / np.pi))


def dot(left, right, dims=((1,), (0,))):
    return lax.dot_general(left, right, (dims, ((), ())), preferred_element_type=F32)


def bucket(delta):
    magnitude = jnp.abs(delta)
    coarse = 8 + sum((magnitude >= limit).astype(I32) for limit in THRESHOLDS)
    return jnp.where(magnitude < 8, magnitude, coarse) + 16 * (delta > 0).astype(I32)


def params(mib):
    return pltpu.CompilerParams(vmem_limit_bytes=mib * 2**20)


def cost(microseconds):
    return pl.CostEstimate(flops=int(1.15e9 * microseconds), bytes_accessed=1, transcendentals=0)


def shape(dims, dtype):
    return jax.ShapeDtypeStruct(dims, dtype)


def whole(dims):
    return pl.BlockSpec(dims, lambda *a: (0,) * len(dims))


VMEM = pl.BlockSpec(memory_space=pltpu.VMEM)


def call(kernel, name, ids, arrays, outs, *, mib, us, scratch=()):
    return pl.pallas_call(
        kernel,
        grid_spec=pltpu.PrefetchScalarGridSpec(
            num_scalar_prefetch=1,
            grid=(1,),
            in_specs=[VMEM] * len(arrays),
            out_specs=jax.tree.map(lambda _: VMEM, outs),
            scratch_shapes=list(scratch),
        ),
        out_shape=outs,
        compiler_params=params(mib),
        cost_estimate=cost(us),
        name=name,
    )(ids, *arrays)


def quarter_of(place, size):
    return pl.ds(pl.multiple_of(place * size, 128), size)


def hidden_rows(inputs, pages, feats):
    return inputs.astype(F32) + dot(pages.astype(F32).astype(BF), feats, ((0,), (0,)))


def unit_rows(field):
    factor = lax.rsqrt(jnp.mean(field * field, axis=-1, keepdims=True) + EPS)
    return field * factor, factor


def project_kernel(ids, x_ref, page_ref, feat_ref, gain_ref, wq_ref, wk_ref, wv_ref, n_ref, q_ref, k_ref, v_ref):
    rows = x_ref.shape[0]
    unit, _ = unit_rows(hidden_rows(x_ref[...], page_ref[...], feat_ref[...]))
    normed = (unit * gain_ref[...].astype(F32)).astype(BF)
    n_ref[...] = normed
    lane = lax.broadcasted_iota(I32, (rows, PAD), 1)
    row = lax.broadcasted_iota(I32, (rows, PAD), 0)
    masked = jnp.where((lane == HD) & (row >= ids[8]), -1e30, 0.0)
    block = lane - MARKS
    far_left = (block >= 0) & (block < 8) & (row < 128 * block - 96)
    far_right = (block >= 8) & (block < 16) & (row >= 128 * (block - 8) + 224)
    masked = jnp.where(far_left | far_right, 1.0, masked)
    query_extra = jnp.where(lane == HD, 1.0, 0.0)
    value_extra = jnp.where((lane == HD) | (lane == HD + 1), 1.0, 0.0)
    for out_ref, w_ref, extra, scale in (
        (q_ref, wq_ref, query_extra, 0.125),
        (k_ref, wk_ref, masked, None),
        (v_ref, wv_ref, value_extra, None),
    ):
        full = dot(normed, w_ref[...], ((1,), (1,)))
        if scale is not None:
            full = full * scale
        pair = full[:, :PAD]
        last = jnp.concatenate([full[:, PAD:], jnp.zeros((rows, PAD - HD), F32)], axis=1)
        heads = (pair, pltpu.roll(pair, HD, 1), last)
        for head in range(HEADS):
            out_ref[:, head * PAD : (head + 1) * PAD] = jnp.where(lane < HD, heads[head], extra).astype(BF)


def project(ids, *arrays):
    seq, width = arrays[0].shape
    outs = [shape((seq, width), BF)] + [shape((seq, HEADS * PAD), BF)] * 3
    return call(project_kernel, "project", ids, arrays, outs, mib=16, us=7)


def place(delta):
    magnitude = jnp.abs(delta)
    coarse = jnp.minimum(25 - lax.clz(delta * delta), 7)
    exact = magnitude < 8
    return jnp.where(exact, magnitude, coarse), exact, delta > 0


def look(table_ref, row, where):
    index, exact, after = where
    found = [jnp.take_along_axis(table_ref[row, part], index, axis=0) for part in range(4)]
    return jnp.where(after, jnp.where(exact, found[2], found[3]), jnp.where(exact, found[0], found[1]))


def tile_delta(tile):
    lane = lax.broadcasted_iota(I32, (8, 128), 1)
    sub = lax.broadcasted_iota(I32, (8, 128), 0)
    delta = 8 * (tile - 13) + sub - lane
    if tile == 0:
        delta = jnp.full_like(delta, -1000)
    if tile == TILES - 1:
        delta = jnp.full_like(delta, 1000)
    return delta


def attend_kernel(*refs, first, chunk):
    ids, q_ref, k_ref, v_ref, hor_ref, ver_ref = refs[:6]
    if first:
        hor_all, ver_all, rel_table, hor_table, ver_table, e_ref, att0, att1, inv_ref, out_ref = refs[6:16]
        rel_ref, t8_ref, hor_col, ver_col, s_ref = refs[16:]
    else:
        rel_ref, t8_ref, hor_col, ver_col, e_ref, att0, att1, inv_ref, out_ref, s_ref = refs[6:]
    seq = k_ref.shape[0]
    width = seq // 4
    lanes = width // 128

    if first:
        for all_ref, col_ref in ((hor_all, hor_col), (ver_all, ver_col)):
            for b in range(seq // 128):
                cols = slice(128 * b, 128 * b + 128)
                spread = jnp.broadcast_to(all_ref[:, cols].astype(F32), (128, 128))
                col_ref[cols, :] = spread.T.astype(I32)
        lane = lax.broadcasted_iota(I32, (8, 32), 1)
        sub = lax.broadcasted_iota(I32, (8, 32), 0)
        for axis, table_ref in enumerate((rel_table, hor_table, ver_table)):
            table = table_ref[...].astype(F32)
            for head in range(HEADS):
                row = jnp.broadcast_to(table[head : head + 1], (8, 32))
                for part in range(4):
                    entries = jnp.sum(jnp.where(lane == sub + 8 * part, row, 0.0), axis=1, keepdims=True)
                    t8_ref[axis * HEADS + head, part] = jnp.broadcast_to(entries, (8, 128))
        for tile in range(TILES):
            where = place(tile_delta(tile))
            for head in range(HEADS):
                rel_ref[head, tile] = look(t8_ref, head, where)

    for part, att_ref in enumerate((att0, att1)):
        place_of = ids[(0 if first else 2) + part]
        here = quarter_of(place_of, width)
        mine = slice(part * width, (part + 1) * width)
        queries = q_ref[here, :]
        hor_row, ver_row = hor_ref[:, here], ver_ref[:, here]
        for head in range(HEADS):
            cols = slice(head * PAD, (head + 1) * PAD)
            s_ref[part, head] = dot(k_ref[:, cols], queries[:, cols], ((1,), (1,)))
        hor = [jnp.broadcast_to(hor_row[:, 128 * l : 128 * l + 128], (8, 128)) for l in range(lanes)]
        ver = [jnp.broadcast_to(ver_row[:, 128 * l : 128 * l + 128], (8, 128)) for l in range(lanes)]
        block = place_of * lanes

        def add_bias(c, tops):
            tops = list(tops)
            base = pl.multiple_of(c * chunk, chunk)
            for g in range(chunk // 8):
                rows = pl.ds(pl.multiple_of(base + 8 * g, 8), 8)
                hor_keys, ver_keys = hor_col[rows, :], ver_col[rows, :]
                for l in range(lanes):
                    cols = pl.ds(128 * l, 128)
                    hor_at, ver_at = place(hor_keys - hor[l]), place(ver_keys - ver[l])
                    tile = jnp.clip(c * (chunk // 8) + g - 16 * (block + l) + 13, 0, TILES - 1)
                    for head in range(HEADS):
                        s = s_ref[part, head, rows, cols] + rel_ref[head, tile]
                        s = s + (look(t8_ref, HEADS + head, hor_at) + look(t8_ref, 2 * HEADS + head, ver_at))
                        s_ref[part, head, rows, cols] = s
                        tops[head * lanes + l] = jnp.maximum(tops[head * lanes + l], s)
            return tuple(tops)

        tops = lax.fori_loop(
            0, seq // chunk, add_bias, tuple(jnp.full((8, 128), -1e30, F32) for _ in range(HEADS * lanes))
        )
        peaks = [jnp.broadcast_to(jnp.max(top, axis=0, keepdims=True), (16, 128)) for top in tops]

        for head in range(HEADS):
            for g in range(seq // 16):
                rows = slice(16 * g, 16 * g + 16)
                for l in range(lanes):
                    cols = slice(128 * l, 128 * l + 128)
                    e_ref[head, rows, slice(part * width + 128 * l, part * width + 128 * l + 128)] = jnp.exp(s_ref[part, head, rows, cols] - peaks[head * lanes + l]).astype(BF)
            total = dot(v_ref[:, head * PAD : (head + 1) * PAD], e_ref[head, :, mine], ((0,), (0,)))
            inverse = 1.0 / total[HD : HD + 1, :]
            inv_ref[head : head + 1, mine] = inverse
            out_ref[head * HD : (head + 1) * HD, mine] = total[:HD] * inverse
        att_ref[...] = out_ref[:, mine].astype(BF)


def attend(ids, queries, keys, values, hor, ver, tables, lookups):
    seq = queries.shape[0]
    width = seq // 4
    first = lookups is None
    columns = HEADS * HD
    made = [
        shape((HEADS, TILES, 8, 128), F32), shape((3 * HEADS, 4, 8, 128), F32), shape((seq, 128), I32), shape((seq, 128), I32)
    ]
    extra = (hor, ver, *tables) if first else tuple(lookups)
    outs = [
        shape((HEADS, seq, 2 * width), BF), shape((columns, width), BF), shape((columns, width), BF),
        shape((HEADS, 2 * width), F32), shape((columns, 2 * width), F32),
    ]
    found = call(
        functools.partial(attend_kernel, first=first, chunk=64),
        "attend_first" if first else "attend_last",
        ids,
        (queries, keys, values, hor, ver, *extra),
        outs + made if first else outs,
        mib=14,
        us=14,
        scratch=[pltpu.VMEM((2, HEADS, seq, width), F32)],
    )
    return found[:5], found[5:]


def feed_kernel(
    ids, x_ref, page_ref, feat_ref, gain_ref, cot_ref, a0, a1, a2, a3, o0, o1, o2, o3, u0, u1, d0, d1,
    keep_ref, send_ref, mixed_ref, grad_ref, ffn_ref, *, slot,
):
    here = quarter_of(ids[slot], mixed_ref.shape[0])
    cotangent = cot_ref[here, :]
    mixed = hidden_rows(x_ref[here, :], page_ref[:, here], feat_ref[...])
    for a_ref, o_ref in ((a0, o0), (a1, o1), (a2, o2), (a3, o3)):
        mixed = mixed + dot(a_ref[...], o_ref[...], ((0,), (0,)))
    mixed_ref[...] = mixed
    unit, _ = unit_rows(mixed)
    normed = (unit * gain_ref[...].astype(F32)).astype(BF)
    send_ref[2] = normed
    units = u0.shape[1]
    for u_ref, d_ref, goal in ((u0, d0, keep_ref), (u1, d1, send_ref)):
        for at in range(0, units, FEED_CHUNK):
            cols = slice(at, at + FEED_CHUNK)
            upward = dot(normed, u_ref[:, cols])
            square = upward * upward
            tanh = jnp.tanh(GELU_C * upward * (1.0 + 0.044715 * square))
            lifted = 0.5 * (1.0 + tanh)
            activated = (upward * lifted).astype(BF)
            slope = lifted + 0.5 * upward * (1.0 - tanh * tanh) * (GELU_C * (1.0 + 3 * 0.044715 * square))
            grad_up = (dot(cotangent, d_ref[cols, :], ((1,), (1,))) * slope).astype(BF)
            goal[0, :, cols] = activated
            goal[1, :, cols] = grad_up
    ffn = dot(keep_ref[0], d0[...]) + dot(send_ref[0], d1[...])
    ffn_ref[...] = ffn.astype(ffn_ref.dtype)
    grad = dot(keep_ref[1], u0[...], ((1,), (1,))) + dot(send_ref[1], u1[...], ((1,), (1,)))
    grad_ref[...] = grad.astype(grad_ref.dtype)


def feed(ids, own, inputs, onehot, feats, gain, cotangent, attended, w_outputs, ups, downs):
    seq, width = inputs.shape
    rows = seq // 4
    units = ups[0].shape[1]
    kept = F32 if own else BF
    outs = [
        shape((2, rows, units), BF), shape((3, rows, width), BF), shape((rows, width), F32),
        shape((rows, width), BF), shape((rows, width), kept),
    ]
    return call(
        functools.partial(feed_kernel, slot=0 if own else 2),
        "feed_own" if own else "feed_other",
        ids,
        (inputs, onehot, feats, gain, cotangent, *attended, *w_outputs, *ups, *downs),
        outs,
        mib=16,
        us=20 if own else 10,
    )


def add_kernel(ids, one_ref, two_ref, out_ref):
    out_ref[...] = one_ref[...].astype(F32) + two_ref[...].astype(F32)


def add(ids, one, two):
    return call(add_kernel, "add", ids, (one, two), shape(one.shape, F32), mib=8, us=20)


def mid_kernel(
    ids, own_grad, own_mixed, other_grad, other_got, other_mixed, cot_ref, gain_ref, o0, o1,
    grad_ref, own_ref, core_ref, low_own, low_other, part_ref,
):
    rows = own_grad.shape[0]
    other = other_grad[...].astype(F32) + other_got[...].astype(F32)
    for at, (grad_normed, mixed_ref) in enumerate(((own_grad[...], own_mixed), (other, other_mixed))):
        unit, factor = unit_rows(mixed_ref[...])
        scaled = grad_normed * gain_ref[...].astype(F32)
        grad = factor * (scaled - unit * jnp.mean(scaled * unit, axis=-1, keepdims=True))
        grad = cot_ref[quarter_of(ids[2 * at], rows), :].astype(F32) + grad
        low = grad.astype(BF)
        (low_own, low_other)[at][...] = low
        if at == 0:
            grad_ref[...] = grad
            part_ref[...] = jnp.sum(grad_normed * unit, axis=0, keepdims=True)
        for o_ref, goal in ((o0, own_ref), (o1, core_ref)):
            goal[:, at * rows : (at + 1) * rows] = dot(o_ref[...], low, ((1,), (1,))).astype(BF)


def mid(ids, own, other, gain, cotangent, w_outputs):
    rows, width = own[0].shape
    columns = HEADS * HD
    outs = [
        shape((rows, width), F32), shape((columns, 2 * rows), BF), shape((columns, 2 * rows), BF), shape((rows, width), BF),
        shape((rows, width), BF), shape((1, width), F32),
    ]
    arrays = (*own, *other, cotangent, gain, *w_outputs)
    return call(mid_kernel, "mid", ids, arrays, outs, mib=16, us=0.01)


def back_kernel(*refs, first):
    ids, ea_ref, eb_ref, inv_a, inv_b, out_a, out_b, q_ref, k_ref, v_ref, grad_ref = refs[:11]
    refs = refs[11:]
    if first:
        ds_ref, dqa_ref, dqb_ref, key_ref, value_ref, near_ref, far_ref, x_ref = refs
    else:
        key_in, value_in, near_in, far_in, dqa_in, dqb_in = refs[:6]
        ds_ref, all_ref, near_ref, far_ref, x_ref = refs[6:]
    seq = k_ref.shape[0]
    width = seq // 4
    both = 2 * width
    lanes = width // 128
    base = 0 if first else 1
    sub = lax.broadcasted_iota(I32, (HD, both), 0)
    blocks = [ids[base + 2 * (l // lanes)] * lanes + l % lanes for l in range(2 * lanes)]
    mine = slice(base * width, (base + 1) * width)
    here = [quarter_of(ids[base + 2 * n], width) for n in range(2)]
    beside = lambda one, two: jnp.concatenate([one, two], axis=1)
    spot = lax.broadcasted_iota(I32, (8, 128), 0)

    for head in range(HEADS):
        cols = slice(head * PAD, (head + 1) * PAD)
        rows = slice(head * HD, (head + 1) * HD)
        grad = grad_ref[rows, :].astype(F32)
        grad = (grad * beside(inv_a[head : head + 1, mine], inv_b[head : head + 1, mine])).astype(BF).astype(F32)
        inner = jnp.sum(grad * beside(out_a[rows, mine], out_b[rows, mine]), axis=0, keepdims=True)
        high = inner.astype(BF).astype(F32)
        extra = jnp.where(sub == 0, -high, jnp.where(sub == 1, high - inner, 0.0))
        right = jnp.concatenate([grad, extra], axis=0).astype(BF)
        x_ref[head % 2] = dot(v_ref[:, cols], right)
        value = dot(beside(ea_ref[head, :, mine], eb_ref[head, :, mine]), right, ((1,), (1,)))
        for c in range(seq // 16):
            at = slice(16 * c, 16 * c + 16)
            found = beside(ea_ref[head, at, mine], eb_ref[head, at, mine]).astype(F32)
            ds_ref[head, at, :] = (found * x_ref[head % 2, at, :]).astype(BF)
        grad = ds_ref[head]
        key = dot(grad, jnp.concatenate([q_ref[at, cols] for at in here], axis=0))
        query = dot(k_ref[:, cols], grad, ((0,), (0,)))
        query_a = (query[:HD, :width] * 0.125).astype(BF)
        query_b = (query[:HD, width:] * 0.125).astype(BF)

        for g in range(NEAR // 2):
            total = None if first else near_in[head, 16 * g : 16 * g + 16]
            for l, block in enumerate(blocks):
                start = 128 * block - 96 + 16 * g
                inside = (start >= 0) & (start < seq)
                at = pl.ds(pl.multiple_of(jnp.clip(start, 0, seq - 16), 16), 16)
                found = ds_ref[head, at, 128 * l : 128 * l + 128].astype(F32)
                found = jnp.where(inside, found, 0.0)
                total = found if total is None else total + found
            near_ref[head, 16 * g : 16 * g + 16] = total
        for side in range(2):
            total = None if first else far_in[head, 8 * side : 8 * side + 8]
            for l, block in enumerate(blocks):
                marks = query[MARKS + 8 * side : MARKS + 8 * side + 8, 128 * l : 128 * l + 128]
                marks = jnp.where(spot == block, marks, 0.0)
                total = marks if total is None else total + marks
            far_ref[head, 8 * side : 8 * side + 8] = total

        if first:
            key_ref[:, cols] = key
            value_ref[:, cols] = value
            dqa_ref[rows, :] = query_a
            dqb_ref[rows, :] = query_b
        else:
            for k, found in enumerate((dqa_in[rows, :], query_a, dqb_in[rows, :], query_b)):
                all_ref[k, 0, rows, :] = found
            for part, acc in ((1, key_in[:, cols] + key), (2, value_in[:, cols] + value)):
                turned = acc.T[:HD].astype(BF)
                for q in range(4):
                    k = sum((jnp.where(ids[n] == q, n, 0) for n in range(1, 4)))
                    all_ref[k, part, rows, :] = turned[:, q * width : (q + 1) * width]


def back(ids, attended, queries, keys, values, grads, carried):
    seq, wide = queries.shape
    width = seq // 4
    first = carried is None
    columns = HEADS * HD
    queried = [shape((columns, width), BF)] * 2
    sums = [shape((seq, wide), F32)] * 2
    rel = [shape((HEADS, 8 * NEAR, 128), F32), shape((HEADS, 16, 128), F32)]
    outs = [shape((HEADS, seq, 2 * width), BF)]
    outs += queried + sums if first else [shape((4, 3, columns, width), BF)]
    outs += rel
    arrays = (*attended[0], *attended[1], *attended[2], queries, keys, values, grads, *(() if first else carried))
    return call(
        functools.partial(back_kernel, first=first),
        "back_first" if first else "back_last",
        ids,
        arrays,
        outs,
        mib=16,
        us=2 if first else 0.01,
        scratch=[pltpu.VMEM((2, seq, 2 * width), F32)],
    )


def places_kernel(ids, hor_ref, ver_ref, hor_at, ver_at):
    places, seq = hor_at.shape
    for keys_ref, goal in ((hor_ref, hor_at), (ver_ref, ver_at)):
        for b in range(places // 128):
            spot = lax.broadcasted_iota(I32, (128, seq), 0) + 128 * b
            goal[128 * b : 128 * b + 128, :] = jnp.where(spot == keys_ref[...], 1.0, 0.0).astype(BF)


def places_of(ids, hor, ver):
    return call(places_kernel, "places", ids, (hor, ver), [shape((PLACES, hor.shape[1]), BF)] * 2, mib=8, us=0.01)


def tables_kernel(ids, s_ref, e_ref, q_ref, *refs, base):
    diagonals = refs[:-3]
    out_ref, left_ref, right_ref = refs[-3:]
    width = s_ref.shape[2]
    groups = e_ref.shape[0] // 128
    query = jnp.concatenate([q_ref[:, quarter_of(ids[base + n], width // 2)] for n in (0, 2)], axis=1)
    column = lax.broadcasted_iota(I32, (SPAN, width), 0)
    for b in range(groups):
        window = jnp.clip(128 * b + TOP - LOW - query, 0, TOP)
        right_ref[:, b * width : (b + 1) * width] = jnp.where(column == window, 1.0, 0.0).astype(BF)
    for head in range(HEADS):
        moved = dot(e_ref[...], s_ref[head]).astype(BF)
        for b in range(groups):
            left_ref[head * 128 : head * 128 + 128, b * width : (b + 1) * width] = moved[128 * b : 128 * b + 128]
    found = dot(left_ref[...], right_ref[...], ((1,), (1,)))

    def to_buckets(sums, delta):
        spot = lax.broadcasted_iota(I32, (32, sums.shape[1]), 0)
        return jnp.sum(jnp.where(bucket(delta) == spot, sums, 0.0), axis=1, keepdims=True)

    lane = lax.broadcasted_iota(I32, (1, 512), 1)
    columns = []
    for h in range(HEADS):
        grid = jnp.concatenate([found[h * 128 : h * 128 + 128, :], jnp.zeros((128, 512 - SPAN), F32)], axis=1)
        grid = pltpu.roll(grid, 0, 1, stride=1, stride_axis=0)
        columns.append(to_buckets(jnp.sum(grid, axis=0, keepdims=True), lane + LOW - TOP))
    spread = lax.broadcasted_iota(I32, (32, 128), 1)
    rows_of = lambda columns: sum(jnp.where(spread == at, column, 0.0) for at, column in enumerate(columns)).T[:8]
    out_ref[0] = rows_of(columns)
    if diagonals:
        near_ref, far_ref = diagonals
        flip = 7 - lax.broadcasted_iota(I32, (8, 128), 0)
        spot = lax.broadcasted_iota(I32, (32, 1), 0)
        columns = []
        for h in range(HEADS):
            near = [jnp.take_along_axis(near_ref[h, 8 * t : 8 * t + 8], flip, axis=0) for t in reversed(range(NEAR))]
            grid = jnp.concatenate(near, axis=0)
            grid = jnp.concatenate([grid, jnp.zeros((8 * NEAR, 384), F32)], axis=1)
            grid = pltpu.roll(grid, 0, 1, stride=1, stride_axis=0)
            near_sums = to_buckets(jnp.sum(grid, axis=0, keepdims=True), 8 * NEAR - 1 - 8 * 12 - lane)
            left = jnp.sum(jnp.sum(far_ref[h, :8], axis=0, keepdims=True), axis=1, keepdims=True)
            right = jnp.sum(jnp.sum(far_ref[h, 8:], axis=0, keepdims=True), axis=1, keepdims=True)
            columns.append(near_sums + jnp.where(spot == 15, left, 0.0) + jnp.where(spot == 31, right, 0.0))
        out_ref[1] = rows_of(columns)


def table_grads(ids, first, scores, places, positions, sums=()):
    wide = PLACES // 128 * positions.shape[1] // 2
    return call(
        functools.partial(tables_kernel, base=0 if first else 1),
        "table_grads",
        ids,
        (scores, places, positions, *sums),
        shape((2 if sums else 1, 8, 32), F32),
        mib=TABLES_MIB,
        us=0.01,
        scratch=[pltpu.VMEM((HEADS * 128, wide), BF), pltpu.VMEM((SPAN, wide), BF)],
    )


def terms_of(grads, weights):
    total = None
    for part, w_ref in enumerate(weights):
        found = dot(grads[part], w_ref[...], ((0,), (0,)))
        total = found if total is None else total + found
    return total


def terms_send_kernel(ids, w0, w1, w2, grads_ref, *outs):
    for at, out_ref in enumerate(outs):
        out_ref[...] = terms_of(grads_ref[2 * at + 1], (w0, w1, w2)).astype(BF)


def terms_keep_kernel(ids, w0, w1, w2, grads_ref, got_own, got_other, own_ref, other_ref):
    other_ref[...] = (terms_of(grads_ref[2], (w0, w1, w2)) + got_other[...].astype(F32)).astype(BF)
    own_ref[...] = terms_of(grads_ref[0], (w0, w1, w2)) + got_own[...].astype(F32)


def terms_send(ids, weights, grads):
    outs = [shape((grads.shape[3], weights[0].shape[1]), BF)] * 2
    return call(terms_send_kernel, "terms_send", ids, (*weights, grads), outs, mib=16, us=0.01)


def terms_keep(ids, weights, grads, got):
    outs = [shape(got[0].shape, F32), shape(got[0].shape, BF)]
    return call(terms_keep_kernel, "terms_keep", ids, (*weights, grads, *got), outs, mib=16, us=0.01)


def last_kernel(
    ids, mine_ref, sent_ref, x_ref, page_ref, feat_ref, gain_ref, grad_ref, second_ref, mixed_ref, ffn_ref, got_ref,
    out_ref, part_ref,
):
    grad_normed = mine_ref[...] + sent_ref[...].astype(F32)
    here = quarter_of(ids[0], mine_ref.shape[0])
    unit, factor = unit_rows(hidden_rows(x_ref[here, :], page_ref[:, here], feat_ref[...]))
    scaled = grad_normed * gain_ref[...].astype(F32)
    grad = factor * (scaled - unit * jnp.mean(scaled * unit, axis=-1, keepdims=True))
    rows, width = grad.shape
    out_ref[0, :rows] = (mixed_ref[...] + ffn_ref[...] + got_ref[...].astype(F32)).astype(BF)
    out_ref[1, :rows] = (grad_ref[...] + grad).astype(BF)
    part_ref[0:1] = jnp.sum(grad_normed * unit, axis=0, keepdims=True)
    part_ref[1:2] = second_ref[...]


def last(ids, mine, sent, inputs, onehot, feats, gain, grad_mixed, second, *ffn):
    rows, width = mine.shape
    arrays = (mine, sent, inputs, onehot, feats, gain, grad_mixed, second, *ffn)
    outs = [shape((2, rows, width), BF), shape((2, width), F32)]
    return call(last_kernel, "last", ids, arrays, outs, mib=16, us=0.01)


def pack_kernel(ids, gains_ref, got_ref, hor_a, ver_a, hor_b, ver_b, out_ref):
    gains = gains_ref[...] + got_ref[...]
    gains = [gains[slot : slot + 1] for slot in range(2)]
    parts = gains[0].shape[1] // 128
    for slot in range(2):
        gain = gains[slot]
        for part in range(parts):
            at = slot * parts + part
            out_ref[at : at + 1, :] = gain[:, part * 128 : part * 128 + 128]
    bins = hor_a.shape[2]
    at = 2 * parts
    out_ref[at:, :] = jnp.zeros((out_ref.shape[0] - at, 128), F32)
    for found in (hor_b[1], hor_a[0] + hor_b[0], ver_a[0] + ver_b[0]):
        out_ref[at : at + HEADS, :bins] = found[:HEADS]
        at += HEADS


def pack(ids, gains, got, *sums):
    size = gains.shape[1] // 128 * 2 + 3 * HEADS
    size = -(-size // 8) * 8
    return call(pack_kernel, "pack", ids, (gains, got, *sums), shape((size, 128), F32), mib=8, us=0.1)


def join_kernel(ids, b0, b1, b2, b3, out_ref, *, slot):
    for k, b_ref in enumerate((b0, b1, b2, b3)):

        @pl.when(pl.program_id(0) == k)
        def _(b_ref=b_ref):
            out_ref[...] = b_ref[slot, : out_ref.shape[0]].astype(out_ref.dtype)


def join_feat_kernel(ids, b0, b1, b2, b3, page_ref, out_ref, feat_ref, all_ref, *, slot):
    step = pl.program_id(0)
    rows = out_ref.shape[0]
    for k, b_ref in enumerate((b0, b1, b2, b3)):

        @pl.when(step == k)
        def _(b_ref=b_ref, k=k):
            out_ref[...] = b_ref[slot, :rows].astype(out_ref.dtype)
            all_ref[pl.ds(pl.multiple_of(ids[k] * rows, rows), rows), :] = b_ref[slot, :rows]

    @pl.when(step == 3)
    def _():
        feat_ref[...] = dot(page_ref[...].astype(F32).astype(BF), all_ref[...])


def join(ids, blocks, slot, dtype, onehot=None):
    _, rows, width = blocks[0].shape
    specs = [VMEM] * 4
    outs, out_specs = [shape((4 * rows, width), dtype)], [pl.BlockSpec((rows, width), lambda i, s: (s[i], 0))]
    extra, scratch = (), []
    if onehot is not None:
        pages = onehot.shape[0]
        specs = specs + [VMEM]
        outs.append(shape((pages, width), F32))
        out_specs.append(whole((pages, width)))
        extra, scratch = (onehot,), [pltpu.VMEM((4 * rows, width), BF)]
    found = pl.pallas_call(
        functools.partial(join_kernel if onehot is None else join_feat_kernel, slot=slot),
        grid_spec=pltpu.PrefetchScalarGridSpec(
            num_scalar_prefetch=1, grid=(4,), in_specs=specs, out_specs=out_specs, scratch_shapes=scratch
        ),
        out_shape=outs,
        compiler_params=params(16),
        cost_estimate=cost(0.01),
        name="join_output" if onehot is None else "join_grads",
    )(ids, *blocks, *extra)
    return found[0] if onehot is None else found


def split_rows(ids, total, cols, keep_ref, send_ref, parity):
    groups, size = keep_ref.shape[0], keep_ref.shape[1]
    for g in range(groups):
        mine = pl.multiple_of((2 * g + parity) * size, 8)
        theirs = pl.multiple_of((2 * g + 1 - parity) * size, 8)
        keep_ref[g] = total[pl.ds(mine, size), cols].astype(keep_ref.dtype)
        send_ref[g] = total[pl.ds(theirs, size), cols].astype(BF)


def feed_grad_kernel(ids, k0, n0, k1, n1, c0, c1, cot_ref, *outs, fast):
    units = k0.shape[2]
    rows = lambda refs: jnp.concatenate(refs, axis=0)
    total = outs[-1]
    normed = rows([n0[2], c0[2], n1[2], c1[2]])
    total[:, :units] = dot(normed, rows([k0[1], c0[1], k1[1], c1[1]]), ((0,), (0,)))
    cotangent = rows([cot_ref[quarter_of(ids[n], k0.shape[1]), :] for n in range(4)])
    total[:, units:] = dot(cotangent, rows([k0[0], c0[0], k1[0], c1[0]]), ((0,), (0,)))
    if fast:
        split_rows(ids, total, slice(None), outs[0], outs[1], ids[9])
    else:
        outs[0][...] = total[...]


def feed_grad(ids, own, other, got_own, got_other, cotangent, fast):
    _, rows, units = own[0].shape
    width = cotangent.shape[1]
    if fast:
        outs = [shape((4, width // 8, 2 * units), F32), shape((4, width // 8, 2 * units), BF)]
    else:
        outs = [shape((width, 2 * units), F32)]
    return call(
        functools.partial(feed_grad_kernel, fast=fast),
        "feed_grad",
        ids,
        (*own, *other, got_own, got_other, cotangent),
        outs,
        mib=24,
        us=7,
        scratch=[pltpu.VMEM((width, 2 * units), F32)],
    )


def head_grad_kernel(ids, normed_ref, grads_ref, l0, l2, l1, l3, a0, a1, a2, a3, *outs, fast):
    total, turned = outs[-2:]
    n = a0.shape[0]
    normed = jnp.concatenate([normed_ref[quarter_of(ids[k], a0.shape[1]), :] for k in range(4)], axis=0)
    for part in range(3):
        left = jnp.concatenate([grads_ref[k, part] for k in range(4)], axis=1)
        total[part * n : (part + 1) * n, :] = dot(left, normed)
    low = jnp.concatenate([r[...] for r in (l0, l1, l2, l3)], axis=0)
    total[3 * n :, :] = dot(jnp.concatenate([r[...] for r in (a0, a1, a2, a3)], axis=1), low)
    turned[...] = total[...].T
    if fast:
        split_rows(ids, turned, slice(None), outs[0], outs[1], ids[9])
    else:
        outs[0][...] = turned[...]


def head_grad(ids, normed, grads, low, low_got, attended, fast):
    seq, width = normed.shape
    n = grads.shape[2]
    if fast:
        outs = [shape((4, width // 8, 4 * n), F32), shape((4, width // 8, 4 * n), BF)]
    else:
        outs = [shape((width, 4 * n), F32)]
    return call(
        functools.partial(head_grad_kernel, fast=fast),
        "head_grad",
        ids,
        (normed, grads, *low, *low_got, *attended),
        outs,
        mib=18,
        us=0.01,
        scratch=[pltpu.VMEM((4 * n, width), F32), pltpu.VMEM((width, 4 * n), F32)],
    )


def pair_kernel(ids, *refs):
    pairs, outs = refs[:-4], refs[-4:]
    for k, o_ref in enumerate(outs):
        at = ids[4 + k]
        start = 0
        for keep_ref, got_ref in zip(pairs[::2], pairs[1::2]):
            n = keep_ref.shape[2]
            o_ref[:, start : start + n] = (keep_ref[at] + got_ref[at].astype(F32)).astype(o_ref.dtype)
            start += n


def pair_sum(ids, *arrays):
    size = arrays[0].shape[1]
    n = sum(a.shape[2] for a in arrays[::2])
    outs = [shape((size, n), F32)] + [shape((size, n), BF)] * 3
    return call(pair_kernel, "pair_sum", ids, arrays, outs, mib=16, us=0.01)


def feed_final_kernel(a0, a1, a2, a3, up_ref, down_ref):
    total = a0[...] + a1[...].astype(F32) + a2[...].astype(F32) + a3[...].astype(F32)
    units = up_ref.shape[1]
    up_ref[...] = total[:, :units]
    down_ref[...] = total[:, units:]


def head_final_kernel(a0, a1, a2, a3, one_ref, two_ref, q_ref, k_ref, v_ref, o_ref, *smalls):
    total = a0[...] + a1[...].astype(F32) + a2[...].astype(F32) + a3[...].astype(F32)
    n = q_ref.shape[1]
    for at, goal in enumerate((q_ref, k_ref, v_ref)):
        goal[...] = total[:, at * n : (at + 1) * n]
    o_ref[...] = total[:, 3 * n :].T
    *tables, gains_ref = smalls
    total = one_ref[...] + two_ref[...]
    parts = gains_ref.shape[1] // 128
    for slot in range(2):
        for part in range(parts):
            at = slot * parts + part
            gains_ref[slot : slot + 1, part * 128 : part * 128 + 128] = total[at : at + 1]
    at, bins = 2 * parts, tables[0].shape[1]
    for goal in tables:
        goal[...] = total[at : at + HEADS, :bins]
        at += HEADS


def final(kernel, arrays, done, outs):
    arrays = [after(arrays[0], done)] + arrays[1:]
    return pl.pallas_call(
        kernel,
        grid=(1,),
        in_specs=[VMEM] * len(arrays),
        out_specs=jax.tree.map(lambda o: whole(o.shape), outs),
        out_shape=outs,
        compiler_params=params(16),
        cost_estimate=cost(5 if kernel is feed_final_kernel else 0.01),
        name=kernel.__name__[:-7],
    )(*arrays)


def swap(array, axis, size, bits):
    return lax.ppermute(array, axis, [(i, i ^ bits) for i in range(size)])


def after(array, *others):
    return lax.optimization_barrier((array, others))[0]


def local(
    inputs, page_feat, page_onehot, lengths, hor_pos, ver_pos, norm1_gain, w_query, w_key, w_value,
    rel_table, hor_table, ver_table, w_output, norm2_gain, w_up, w_down, cotangent, *, dp,
):
    seq, width = inputs.shape
    fast = dp == 8
    over = functools.partial(swap, axis="mp", size=4)
    m = lax.axis_index("mp").astype(I32)
    d = lax.axis_index("dp").astype(I32)
    k4 = jnp.arange(4, dtype=I32)
    spot = lambda who: (who & 1) * 2 + (who >> 1)
    ids = jnp.concatenate([
        spot(m ^ k4),
        (d >> 1) ^ k4,
        lengths[:1],
        (d & 1)[None],
    ])
    gain_one, gain_two = norm1_gain[None], norm2_gain[None]
    feats = page_feat[0]
    hor, ver = hor_pos[None], ver_pos[None]
    tables = (rel_table, hor_table, ver_table)
    pages = page_onehot.T
    weights = [w_query.T, w_key.T, w_value.T]

    wo_y, wo_core = over(w_output, bits=2), over(w_output, bits=1)
    normed1, queries, keys, values = project(ids, inputs, pages, feats, gain_one, *weights)
    w_outputs = [w_output, wo_core, wo_y, over(after(wo_y, normed1), bits=1)]
    ups = [w_up, over(after(w_up, normed1), bits=1)]
    downs = [w_down, over(after(w_down, normed1), bits=1)]

    (e_a, att0, att1, inverse_a, out_a), lookups = attend(ids, queries, keys, values, hor, ver, tables, None)
    from_y, from_yc, own1 = over(att0, bits=2), over(att1, bits=3), over(att1, bits=1)
    ver_late = after(ver, att0, w_outputs[3], ups[1], downs[1])
    (e_b, att2, att3, inverse_b, out_b), _ = attend(ids, queries, keys, values, hor, ver_late, tables, lookups)
    attended = [att0, att1, att2, att3]
    for_other = [att2, over(att3, bits=1), from_y, from_yc]
    for_own = [att0, own1, over(att2, bits=2), over(att3, bits=3)]

    around = functools.partial(swap, axis="dp", size=dp)
    to_z = lambda parts: [parts[0]] + [around(part, bits=2 * k) for k, part in zip((1, 2, 3), parts[1:])]
    size = width // dp
    n = w_query.shape[1]
    units = w_up.shape[1]
    fixed = (inputs, pages, feats, gain_two, cotangent)
    x_keep, x_send, x_mixed, x_grad, x_ffn = feed(ids, False, *fixed, for_other, w_outputs, ups, downs)
    got_own, x_got = over(x_grad, bits=2), over(x_send, bits=1)
    for_own[0] = after(att0, x_ffn)
    m_keep, m_send, mixed, m_grad, m_ffn = feed(ids, True, *fixed, for_own, w_outputs, ups, downs)
    got_other, m_got = over(m_grad, bits=2), over(after(m_send, x_got), bits=1)
    own_grad = add(ids, m_grad, got_own)

    feed_grads = feed_grad(ids, (after(m_keep, own_grad), m_send), (x_keep, x_send), m_got, x_got, cotangent, fast)
    feed_got = around(feed_grads[1], bits=1) if fast else ids
    hor_at, ver_at = places_of(ids, after(hor, feed_grads[0]), ver)
    grad_mixed, ga, core_send, *low, gain_two_part = mid(
        ids, (after(own_grad, hor_at), mixed), (x_grad, got_other, x_mixed), gain_two, cotangent, w_outputs[:2]
    )
    core_got = over(core_send, bits=1)
    sent_ffn = over(after(x_ffn, got_other, hor_at), bits=2)

    halves = ((e_a, e_b), (inverse_a, inverse_b), (out_a, out_b))
    scores_a, dq0, dq2, key_sum, value_sum, near, far = back(ids, halves, queries, keys, values, ga, None)
    scores_b, grads, near, far = back(
        ids, halves, queries, keys, values, after(core_got, dq0), (key_sum, value_sum, near, far, dq0, dq2)
    )
    low_got = [over(part, bits=1) for part in low]
    to_core = terms_send(ids, weights, after(grads, sent_ffn))
    got_terms = [over(part, bits=1) for part in to_core]
    head_grads = head_grad(ids, normed1, after(grads, to_core[0]), low, low_got, attended, fast)
    own_terms, other_terms = terms_keep(ids, weights, after(grads, head_grads[0]), got_terms)
    sent_terms = over(other_terms, bits=2)

    hor_a = table_grads(ids, True, scores_a, hor_at, after(hor, own_terms))
    done = hor_a
    if fast:
        feed_parts = to_z(pair_sum(ids, after(feed_grads[0], done), feed_got))
        done = feed_parts[0]
    head_got = around(after(head_grads[1], done), bits=1) if fast else ids
    rows, gains = last(
        ids, after(own_terms, done), sent_terms, inputs, pages, feats, gain_one, grad_mixed, gain_two_part,
        mixed, m_ffn, sent_ffn,
    )
    rows_y, rows_core = over(rows, bits=2), over(rows, bits=1)
    ver_a = table_grads(ids, True, scores_a, ver_at, after(ver, rows))
    gains = after(gains, ver_a) + over(gains, bits=1)
    got_gains = over(gains, bits=2)
    hor_b = table_grads(ids, False, scores_b, hor_at, after(hor, gains), (near, far))
    ver_b = table_grads(ids, False, scores_b, ver_at, after(ver, hor_b, head_got))

    small = pack(ids, gains, got_gains, hor_a, ver_a, hor_b, ver_b)
    if fast:
        got = around(small, bits=1)
        grad_up, grad_down = final(feed_final_kernel, feed_parts, small, [shape((size, units), F32)] * 2)
        head_parts = to_z(pair_sum(ids, after(head_grads[0], grad_up), head_got))
        small = after(small, head_parts[0]) + got
        got = around(small, bits=2)
        quarters = [rows, rows_core, rows_y, over(after(rows_y, grad_up), bits=1)]
        outputs = join(ids, [after(rows, small)] + quarters[1:], 0, BF)
        grad_inputs, grad_feats = join(ids, [after(rows, outputs)] + quarters[1:], 1, F32, pages)
        small = after(small, grad_feats) + got
        bins = rel_table.shape[1]
        outs = [shape((size, n), F32)] * 3 + [shape((n, size), F32)] + [shape((HEADS, bins), F32)] * 3
        *found, gain_sums = final(
            head_final_kernel, head_parts + [small, around(small, bits=4)], grad_feats, outs + [shape((2, width), F32)]
        )
        grad_query, grad_key, grad_value, grad_output, grad_rel, grad_hor, grad_ver = found
    else:
        quarters = [rows, rows_core, rows_y, over(rows_y, bits=1)]
        outputs = join(ids, quarters, 0, BF)
        grad_inputs, grad_feats = join(ids, quarters, 1, F32, pages)
        small = lax.psum(small, "dp")
        scatter = lambda a: lax.psum_scatter(a[0], "dp", scatter_dimension=0, tiled=True)
        grad_feed, heads = scatter(feed_grads), scatter(head_grads)
        grad_up, grad_down = grad_feed[:, :units], grad_feed[:, units:]
        grad_query, grad_key, grad_value = heads[:, :n], heads[:, n : 2 * n], heads[:, 2 * n : 3 * n]
        grad_output = heads[:, 3 * n :].T
        gain_sums = small[: width // 128 * 2].reshape(2, width)
        table_sums = small[width // 128 * 2 :, : rel_table.shape[1]]
        grad_rel, grad_hor, grad_ver = (table_sums[at : at + HEADS] for at in range(0, 3 * HEADS, HEADS))
    gain_sums = lax.dynamic_slice(gain_sums, (0, d * size), (2, size))
    return (
        outputs, grad_inputs, grad_feats[None], gain_sums[0], grad_query, grad_key, grad_value,
        grad_rel, grad_hor, grad_ver, grad_output, gain_sums[1], grad_up, grad_down.T,
    )


def solution(mesh):
    return jax.shard_map(
        functools.partial(local, dp=mesh.shape["dp"]),
        mesh=mesh,
        in_specs=(
            P("dp", None),
            P("dp", None, None),
            P("dp", None),
            P("dp"),
            P("dp"),
            P("dp"),
            P(),
            P(None, "mp"),
            P(None, "mp"),
            P(None, "mp"),
            P("mp", None),
            P("mp", None),
            P("mp", None),
            P("mp", None),
            P(),
            P(None, "mp"),
            P("mp", None),
            P("dp", None),
        ),
        out_specs=(
            P("dp", None),
            P("dp", None),
            P("dp", None, None),
            P("dp"),
            P("dp", "mp"),
            P("dp", "mp"),
            P("dp", "mp"),
            P("mp", None),
            P("mp", None),
            P("mp", None),
            P("mp", "dp"),
            P("dp"),
            P("dp", "mp"),
            P("mp", "dp"),
        ),
        check_vma=False,
    )
```

```python
import functools

import jax
import jax.numpy as jnp
import numpy as np
from jax import lax
from jax.experimental import pallas as pl
from jax.experimental.pallas import tpu as pltpu
from jax.sharding import PartitionSpec as P

EPS = 1e-06
THRESHOLDS = (12, 16, 23, 32, 46, 64, 91)
FAR = 91
HEADS = 3
HD = 64
PAD = 128
MARKS = 72
NEAR = 40
TILES = NEAR + 2
SPAN = 384
LOW = 92
TOP = 311
BF = jnp.bfloat16
F32 = jnp.float32
I32 = jnp.int32
FEED_CHUNK = 256
PLACES = 1024
TABLES_MIB = 18
GELU_C = float(np.sqrt(2.0 / np.pi))


def dot(left, right, dims=((1,), (0,))):
    return lax.dot_general(left, right, (dims, ((), ())), preferred_element_type=F32)


def bucket(delta):
    magnitude = jnp.abs(delta)
    coarse = 8 + sum((magnitude >= limit).astype(I32) for limit in THRESHOLDS)
    return jnp.where(magnitude < 8, magnitude, coarse) + 16 * (delta > 0).astype(I32)


def params(mib):
    return pltpu.CompilerParams(vmem_limit_bytes=mib * 2**20)


def cost(microseconds):
    return pl.CostEstimate(flops=int(1.15e9 * microseconds), bytes_accessed=1, transcendentals=0)


def shape(dims, dtype):
    return jax.ShapeDtypeStruct(dims, dtype)


def whole(dims):
    return pl.BlockSpec(dims, lambda *a: (0,) * len(dims))


VMEM = pl.BlockSpec(memory_space=pltpu.VMEM)


def call(kernel, name, ids, arrays, outs, *, mib, us, scratch=()):
    return pl.pallas_call(
        kernel,
        grid_spec=pltpu.PrefetchScalarGridSpec(
            num_scalar_prefetch=1,
            grid=(1,),
            in_specs=[VMEM] * len(arrays),
            out_specs=jax.tree.map(lambda _: VMEM, outs),
            scratch_shapes=list(scratch),
        ),
        out_shape=outs,
        compiler_params=params(mib),
        cost_estimate=cost(us),
        name=name,
    )(ids, *arrays)


def quarter_of(place, size):
    return pl.ds(pl.multiple_of(place * size, 128), size)


def hidden_rows(inputs, pages, feats):
    return inputs.astype(F32) + dot(pages.astype(F32).astype(BF), feats, ((0,), (0,)))


def unit_rows(field):
    factor = lax.rsqrt(jnp.mean(field * field, axis=-1, keepdims=True) + EPS)
    return field * factor, factor


def project_kernel(ids, x_ref, page_ref, feat_ref, gain_ref, wq_ref, wk_ref, wv_ref, n_ref, q_ref, k_ref, v_ref):
    rows = x_ref.shape[0]
    unit, _ = unit_rows(hidden_rows(x_ref[...], page_ref[...], feat_ref[...]))
    normed = (unit * gain_ref[...].astype(F32)).astype(BF)
    n_ref[...] = normed
    lane = lax.broadcasted_iota(I32, (rows, PAD), 1)
    row = lax.broadcasted_iota(I32, (rows, PAD), 0)
    masked = jnp.where((lane == HD) & (row >= ids[8]), -1e30, 0.0)
    block = lane - MARKS
    far_left = (block >= 0) & (block < 8) & (row < 128 * block - 96)
    far_right = (block >= 8) & (block < 16) & (row >= 128 * (block - 8) + 224)
    masked = jnp.where(far_left | far_right, 1.0, masked)
    query_extra = jnp.where(lane == HD, 1.0, 0.0)
    value_extra = jnp.where((lane == HD) | (lane == HD + 1), 1.0, 0.0)
    for out_ref, w_ref, extra, scale in (
        (q_ref, wq_ref, query_extra, 0.125),
        (k_ref, wk_ref, masked, None),
        (v_ref, wv_ref, value_extra, None),
    ):
        full = dot(normed, w_ref[...], ((1,), (1,)))
        if scale is not None:
            full = full * scale
        pair = full[:, :PAD]
        last = jnp.concatenate([full[:, PAD:], jnp.zeros((rows, PAD - HD), F32)], axis=1)
        heads = (pair, pltpu.roll(pair, HD, 1), last)
        for head in range(HEADS):
            out_ref[:, head * PAD : (head + 1) * PAD] = jnp.where(lane < HD, heads[head], extra).astype(BF)


def project(ids, *arrays):
    seq, width = arrays[0].shape
    outs = [shape((seq, width), BF)] + [shape((seq, HEADS * PAD), BF)] * 3
    return call(project_kernel, "project", ids, arrays, outs, mib=16, us=7)


def place(delta):
    magnitude = jnp.abs(delta)
    coarse = jnp.minimum(25 - lax.clz(delta * delta), 7)
    exact = magnitude < 8
    return jnp.where(exact, magnitude, coarse), exact, delta > 0


def look(table_ref, row, where):
    index, exact, after = where
    found = [jnp.take_along_axis(table_ref[row, part], index, axis=0) for part in range(4)]
    return jnp.where(after, jnp.where(exact, found[2], found[3]), jnp.where(exact, found[0], found[1]))


def tile_delta(tile):
    lane = lax.broadcasted_iota(I32, (8, 128), 1)
    sub = lax.broadcasted_iota(I32, (8, 128), 0)
    delta = 8 * (tile - 13) + sub - lane
    if tile == 0:
        delta = jnp.full_like(delta, -1000)
    if tile == TILES - 1:
        delta = jnp.full_like(delta, 1000)
    return delta


def attend_kernel(*refs, first, chunk):
    ids, q_ref, k_ref, v_ref, hor_ref, ver_ref = refs[:6]
    if first:
        hor_all, ver_all, rel_table, hor_table, ver_table, e_ref, att0, att1, inv_ref, out_ref = refs[6:16]
        rel_ref, t8_ref, hor_col, ver_col, s_ref = refs[16:]
    else:
        rel_ref, t8_ref, hor_col, ver_col, e_ref, att0, att1, inv_ref, out_ref, s_ref = refs[6:]
    seq = k_ref.shape[0]
    width = seq // 4
    lanes = width // 128

    if first:
        for all_ref, col_ref in ((hor_all, hor_col), (ver_all, ver_col)):
            for b in range(seq // 128):
                cols = slice(128 * b, 128 * b + 128)
                spread = jnp.broadcast_to(all_ref[:, cols].astype(F32), (128, 128))
                col_ref[cols, :] = spread.T.astype(I32)
        lane = lax.broadcasted_iota(I32, (8, 32), 1)
        sub = lax.broadcasted_iota(I32, (8, 32), 0)
        for axis, table_ref in enumerate((rel_table, hor_table, ver_table)):
            table = table_ref[...].astype(F32)
            for head in range(HEADS):
                row = jnp.broadcast_to(table[head : head + 1], (8, 32))
                for part in range(4):
                    entries = jnp.sum(jnp.where(lane == sub + 8 * part, row, 0.0), axis=1, keepdims=True)
                    t8_ref[axis * HEADS + head, part] = jnp.broadcast_to(entries, (8, 128))
        for tile in range(TILES):
            where = place(tile_delta(tile))
            for head in range(HEADS):
                rel_ref[head, tile] = look(t8_ref, head, where)

    def quarter(part, carry):
        place_of = ids[(0 if first else 2) + part]
        here = quarter_of(place_of, width)
        mine = quarter_of(part, width)
        queries = q_ref[here, :]
        hor_row, ver_row = hor_ref[:, here], ver_ref[:, here]
        for head in range(HEADS):
            cols = slice(head * PAD, (head + 1) * PAD)
            s_ref[head] = dot(k_ref[:, cols], queries[:, cols], ((1,), (1,)))
        hor = [jnp.broadcast_to(hor_row[:, 128 * l : 128 * l + 128], (8, 128)) for l in range(lanes)]
        ver = [jnp.broadcast_to(ver_row[:, 128 * l : 128 * l + 128], (8, 128)) for l in range(lanes)]
        block = place_of * lanes

        def add_bias(c, tops):
            tops = list(tops)
            base = pl.multiple_of(c * chunk, chunk)
            for g in range(chunk // 8):
                rows = pl.ds(pl.multiple_of(base + 8 * g, 8), 8)
                hor_keys, ver_keys = hor_col[rows, :], ver_col[rows, :]
                for l in range(lanes):
                    cols = pl.ds(128 * l, 128)
                    hor_at, ver_at = place(hor_keys - hor[l]), place(ver_keys - ver[l])
                    tile = jnp.clip(c * (chunk // 8) + g - 16 * (block + l) + 13, 0, TILES - 1)
                    for head in range(HEADS):
                        s = s_ref[head, rows, cols] + rel_ref[head, tile]
                        s = s + (look(t8_ref, HEADS + head, hor_at) + look(t8_ref, 2 * HEADS + head, ver_at))
                        s_ref[head, rows, cols] = s
                        tops[head * lanes + l] = jnp.maximum(tops[head * lanes + l], s)
            return tuple(tops)

        tops = lax.fori_loop(
            0, seq // chunk, add_bias, tuple(jnp.full((8, 128), -1e30, F32) for _ in range(HEADS * lanes))
        )
        peaks = [jnp.broadcast_to(jnp.max(top, axis=0, keepdims=True), (16, 128)) for top in tops]

        for head in range(HEADS):
            for g in range(seq // 16):
                rows = slice(16 * g, 16 * g + 16)
                for l in range(lanes):
                    cols = slice(128 * l, 128 * l + 128)
                    e_ref[head, rows, pl.ds(pl.multiple_of(part * width + 128 * l, 128), 128)] = jnp.exp(s_ref[head, rows, cols] - peaks[head * lanes + l]).astype(BF)
            total = dot(v_ref[:, head * PAD : (head + 1) * PAD], e_ref[head, :, mine], ((0,), (0,)))
            inverse = 1.0 / total[HD : HD + 1, :]
            inv_ref[head : head + 1, mine] = inverse
            out_ref[head * HD : (head + 1) * HD, mine] = total[:HD] * inverse
        for at, att_ref in enumerate((att0, att1)):

            @pl.when(part == at)
            def _(att_ref=att_ref):
                att_ref[...] = out_ref[:, mine].astype(BF)

        return carry

    lax.fori_loop(0, 2, quarter, 0)


def attend(ids, queries, keys, values, hor, ver, tables, lookups):
    seq = queries.shape[0]
    width = seq // 4
    first = lookups is None
    columns = HEADS * HD
    made = [
        shape((HEADS, TILES, 8, 128), F32), shape((3 * HEADS, 4, 8, 128), F32), shape((seq, 128), I32), shape((seq, 128), I32)
    ]
    extra = (hor, ver, *tables) if first else tuple(lookups)
    outs = [
        shape((HEADS, seq, 2 * width), BF), shape((columns, width), BF), shape((columns, width), BF),
        shape((HEADS, 2 * width), F32), shape((columns, 2 * width), F32),
    ]
    found = call(
        functools.partial(attend_kernel, first=first, chunk=64),
        "attend_first" if first else "attend_last",
        ids,
        (queries, keys, values, hor, ver, *extra),
        outs + made if first else outs,
        mib=14,
        us=14,
        scratch=[pltpu.VMEM((HEADS, seq, width), F32)],
    )
    return found[:5], found[5:]


def feed_kernel(
    ids, x_ref, page_ref, feat_ref, gain_ref, cot_ref, a0, a1, a2, a3, o0, o1, o2, o3, u0, u1, d0, d1,
    keep_ref, send_ref, mixed_ref, grad_ref, ffn_ref, *, slot,
):
    here = quarter_of(ids[slot], mixed_ref.shape[0])
    cotangent = cot_ref[here, :]
    mixed = hidden_rows(x_ref[here, :], page_ref[:, here], feat_ref[...])
    for a_ref, o_ref in ((a0, o0), (a1, o1), (a2, o2), (a3, o3)):
        mixed = mixed + dot(a_ref[...], o_ref[...], ((0,), (0,)))
    mixed_ref[...] = mixed
    unit, _ = unit_rows(mixed)
    normed = (unit * gain_ref[...].astype(F32)).astype(BF)
    send_ref[2] = normed
    units = u0.shape[1]
    for u_ref, d_ref, goal in ((u0, d0, keep_ref), (u1, d1, send_ref)):
        for at in range(0, units, FEED_CHUNK):
            cols = slice(at, at + FEED_CHUNK)
            upward = dot(normed, u_ref[:, cols])
            square = upward * upward
            tanh = jnp.tanh(GELU_C * upward * (1.0 + 0.044715 * square))
            lifted = 0.5 * (1.0 + tanh)
            activated = (upward * lifted).astype(BF)
            slope = lifted + 0.5 * upward * (1.0 - tanh * tanh) * (GELU_C * (1.0 + 3 * 0.044715 * square))
            grad_up = (dot(cotangent, d_ref[cols, :], ((1,), (1,))) * slope).astype(BF)
            goal[0, :, cols] = activated
            goal[1, :, cols] = grad_up
    ffn = dot(keep_ref[0], d0[...]) + dot(send_ref[0], d1[...])
    ffn_ref[...] = ffn.astype(ffn_ref.dtype)
    grad = dot(keep_ref[1], u0[...], ((1,), (1,))) + dot(send_ref[1], u1[...], ((1,), (1,)))
    grad_ref[...] = grad.astype(grad_ref.dtype)


def feed(ids, own, inputs, onehot, feats, gain, cotangent, attended, w_outputs, ups, downs):
    seq, width = inputs.shape
    rows = seq // 4
    units = ups[0].shape[1]
    kept = F32 if own else BF
    outs = [
        shape((2, rows, units), BF), shape((3, rows, width), BF), shape((rows, width), F32),
        shape((rows, width), BF), shape((rows, width), kept),
    ]
    return call(
        functools.partial(feed_kernel, slot=0 if own else 2),
        "feed_own" if own else "feed_other",
        ids,
        (inputs, onehot, feats, gain, cotangent, *attended, *w_outputs, *ups, *downs),
        outs,
        mib=16,
        us=20 if own else 10,
    )


def add_kernel(ids, one_ref, two_ref, out_ref):
    out_ref[...] = one_ref[...].astype(F32) + two_ref[...].astype(F32)


def add(ids, one, two):
    return call(add_kernel, "add", ids, (one, two), shape(one.shape, F32), mib=8, us=20)


def mid_kernel(
    ids, own_grad, own_mixed, other_grad, other_got, other_mixed, cot_ref, gain_ref, o0, o1,
    grad_ref, own_ref, core_ref, low_own, low_other, part_ref,
):
    rows = own_grad.shape[0]
    other = other_grad[...].astype(F32) + other_got[...].astype(F32)
    for at, (grad_normed, mixed_ref) in enumerate(((own_grad[...], own_mixed), (other, other_mixed))):
        unit, factor = unit_rows(mixed_ref[...])
        scaled = grad_normed * gain_ref[...].astype(F32)
        grad = factor * (scaled - unit * jnp.mean(scaled * unit, axis=-1, keepdims=True))
        grad = cot_ref[quarter_of(ids[2 * at], rows), :].astype(F32) + grad
        low = grad.astype(BF)
        (low_own, low_other)[at][...] = low
        if at == 0:
            grad_ref[...] = grad
            part_ref[...] = jnp.sum(grad_normed * unit, axis=0, keepdims=True)
        for o_ref, goal in ((o0, own_ref), (o1, core_ref)):
            goal[:, at * rows : (at + 1) * rows] = dot(o_ref[...], low, ((1,), (1,))).astype(BF)


def mid(ids, own, other, gain, cotangent, w_outputs):
    rows, width = own[0].shape
    columns = HEADS * HD
    outs = [
        shape((rows, width), F32), shape((columns, 2 * rows), BF), shape((columns, 2 * rows), BF), shape((rows, width), BF),
        shape((rows, width), BF), shape((1, width), F32),
    ]
    arrays = (*own, *other, cotangent, gain, *w_outputs)
    return call(mid_kernel, "mid", ids, arrays, outs, mib=16, us=0.01)


def back_kernel(*refs, first):
    ids, ea_ref, eb_ref, inv_a, inv_b, out_a, out_b, q_ref, k_ref, v_ref, grad_ref = refs[:11]
    refs = refs[11:]
    if first:
        ds_ref, dqa_ref, dqb_ref, key_ref, value_ref, near_ref, far_ref, x_ref = refs
    else:
        key_in, value_in, near_in, far_in, dqa_in, dqb_in = refs[:6]
        ds_ref, all_ref, near_ref, far_ref, x_ref = refs[6:]
    seq = k_ref.shape[0]
    width = seq // 4
    both = 2 * width
    lanes = width // 128
    base = 0 if first else 1
    sub = lax.broadcasted_iota(I32, (HD, both), 0)
    blocks = [ids[base + 2 * (l // lanes)] * lanes + l % lanes for l in range(2 * lanes)]
    mine = slice(base * width, (base + 1) * width)
    here = [quarter_of(ids[base + 2 * n], width) for n in range(2)]
    beside = lambda one, two: jnp.concatenate([one, two], axis=1)
    spot = lax.broadcasted_iota(I32, (8, 128), 0)

    def one_head(head, carry):
        cols = quarter_of(head, PAD)
        rows = pl.ds(pl.multiple_of(head * HD, HD), HD)
        grad = grad_ref[rows, :].astype(F32)
        grad = (grad * beside(inv_a[pl.ds(head, 1), mine], inv_b[pl.ds(head, 1), mine])).astype(BF).astype(F32)
        inner = jnp.sum(grad * beside(out_a[rows, mine], out_b[rows, mine]), axis=0, keepdims=True)
        high = inner.astype(BF).astype(F32)
        extra = jnp.where(sub == 0, -high, jnp.where(sub == 1, high - inner, 0.0))
        right = jnp.concatenate([grad, extra], axis=0).astype(BF)
        x_ref[0] = dot(v_ref[:, cols], right)
        value = dot(beside(ea_ref[head, :, mine], eb_ref[head, :, mine]), right, ((1,), (1,)))
        for c in range(seq // 16):
            at = slice(16 * c, 16 * c + 16)
            found = beside(ea_ref[head, at, mine], eb_ref[head, at, mine]).astype(F32)
            ds_ref[head, at, :] = (found * x_ref[0, at, :]).astype(BF)
        grad = ds_ref[head]
        key = dot(grad, jnp.concatenate([q_ref[at, cols] for at in here], axis=0))
        query = dot(k_ref[:, cols], grad, ((0,), (0,)))
        query_a = (query[:HD, :width] * 0.125).astype(BF)
        query_b = (query[:HD, width:] * 0.125).astype(BF)

        for g in range(NEAR // 2):
            total = None if first else near_in[head, 16 * g : 16 * g + 16]
            for l, block in enumerate(blocks):
                start = 128 * block - 96 + 16 * g
                inside = (start >= 0) & (start < seq)
                at = pl.ds(pl.multiple_of(jnp.clip(start, 0, seq - 16), 16), 16)
                found = ds_ref[head, at, 128 * l : 128 * l + 128].astype(F32)
                found = jnp.where(inside, found, 0.0)
                total = found if total is None else total + found
            near_ref[head, 16 * g : 16 * g + 16] = total
        for side in range(2):
            total = None if first else far_in[head, 8 * side : 8 * side + 8]
            for l, block in enumerate(blocks):
                marks = query[MARKS + 8 * side : MARKS + 8 * side + 8, 128 * l : 128 * l + 128]
                marks = jnp.where(spot == block, marks, 0.0)
                total = marks if total is None else total + marks
            far_ref[head, 8 * side : 8 * side + 8] = total

        if first:
            key_ref[:, cols] = key
            value_ref[:, cols] = value
            dqa_ref[rows, :] = query_a
            dqb_ref[rows, :] = query_b
        else:
            for k, found in enumerate((dqa_in[rows, :], query_a, dqb_in[rows, :], query_b)):
                all_ref[k, 0, rows, :] = found
            for part, acc in ((1, key_in[:, cols] + key), (2, value_in[:, cols] + value)):
                turned = acc.T[:HD].astype(BF)
                for q in range(4):
                    k = sum((jnp.where(ids[n] == q, n, 0) for n in range(1, 4)))
                    all_ref[k, part, rows, :] = turned[:, q * width : (q + 1) * width]
        return carry

    lax.fori_loop(0, HEADS, one_head, 0)


def back(ids, attended, queries, keys, values, grads, carried):
    seq, wide = queries.shape
    width = seq // 4
    first = carried is None
    columns = HEADS * HD
    queried = [shape((columns, width), BF)] * 2
    sums = [shape((seq, wide), F32)] * 2
    rel = [shape((HEADS, 8 * NEAR, 128), F32), shape((HEADS, 16, 128), F32)]
    outs = [shape((HEADS, seq, 2 * width), BF)]
    outs += queried + sums if first else [shape((4, 3, columns, width), BF)]
    outs += rel
    arrays = (*attended[0], *attended[1], *attended[2], queries, keys, values, grads, *(() if first else carried))
    return call(
        functools.partial(back_kernel, first=first),
        "back_first" if first else "back_last",
        ids,
        arrays,
        outs,
        mib=16,
        us=2 if first else 0.01,
        scratch=[pltpu.VMEM((1, seq, 2 * width), F32)],
    )


def places_kernel(ids, hor_ref, ver_ref, hor_at, ver_at):
    places, seq = hor_at.shape
    for keys_ref, goal in ((hor_ref, hor_at), (ver_ref, ver_at)):
        for b in range(places // 128):
            spot = lax.broadcasted_iota(I32, (128, seq), 0) + 128 * b
            goal[128 * b : 128 * b + 128, :] = jnp.where(spot == keys_ref[...], 1.0, 0.0).astype(BF)


def places_of(ids, hor, ver):
    return call(places_kernel, "places", ids, (hor, ver), [shape((PLACES, hor.shape[1]), BF)] * 2, mib=8, us=0.01)


def tables_kernel(ids, s_ref, e_ref, q_ref, *refs, base):
    diagonals = refs[:-3]
    out_ref, left_ref, right_ref = refs[-3:]
    width = s_ref.shape[2]
    groups = e_ref.shape[0] // 128
    query = jnp.concatenate([q_ref[:, quarter_of(ids[base + n], width // 2)] for n in (0, 2)], axis=1)
    column = lax.broadcasted_iota(I32, (SPAN, width), 0)
    for b in range(groups):
        window = jnp.clip(128 * b + TOP - LOW - query, 0, TOP)
        right_ref[:, b * width : (b + 1) * width] = jnp.where(column == window, 1.0, 0.0).astype(BF)

    def move(head, carry):
        moved = dot(e_ref[...], s_ref[head]).astype(BF)
        rows = quarter_of(head, 128)
        for b in range(groups):
            left_ref[rows, b * width : (b + 1) * width] = moved[128 * b : 128 * b + 128]
        return carry

    lax.fori_loop(0, HEADS, move, 0)
    found = dot(left_ref[...], right_ref[...], ((1,), (1,)))

    def to_buckets(sums, delta):
        spot = lax.broadcasted_iota(I32, (32, sums.shape[1]), 0)
        return jnp.sum(jnp.where(bucket(delta) == spot, sums, 0.0), axis=1, keepdims=True)

    lane = lax.broadcasted_iota(I32, (1, 512), 1)
    columns = []
    for h in range(HEADS):
        grid = jnp.concatenate([found[h * 128 : h * 128 + 128, :], jnp.zeros((128, 512 - SPAN), F32)], axis=1)
        grid = pltpu.roll(grid, 0, 1, stride=1, stride_axis=0)
        columns.append(to_buckets(jnp.sum(grid, axis=0, keepdims=True), lane + LOW - TOP))
    spread = lax.broadcasted_iota(I32, (32, 128), 1)
    rows_of = lambda columns: sum(jnp.where(spread == at, column, 0.0) for at, column in enumerate(columns)).T[:8]
    out_ref[0] = rows_of(columns)
    if diagonals:
        near_ref, far_ref = diagonals
        flip = 7 - lax.broadcasted_iota(I32, (8, 128), 0)
        spot = lax.broadcasted_iota(I32, (32, 1), 0)
        columns = []
        for h in range(HEADS):
            near = [jnp.take_along_axis(near_ref[h, 8 * t : 8 * t + 8], flip, axis=0) for t in reversed(range(NEAR))]
            grid = jnp.concatenate(near, axis=0)
            grid = jnp.concatenate([grid, jnp.zeros((8 * NEAR, 384), F32)], axis=1)
            grid = pltpu.roll(grid, 0, 1, stride=1, stride_axis=0)
            near_sums = to_buckets(jnp.sum(grid, axis=0, keepdims=True), 8 * NEAR - 1 - 8 * 12 - lane)
            left = jnp.sum(jnp.sum(far_ref[h, :8], axis=0, keepdims=True), axis=1, keepdims=True)
            right = jnp.sum(jnp.sum(far_ref[h, 8:], axis=0, keepdims=True), axis=1, keepdims=True)
            columns.append(near_sums + jnp.where(spot == 15, left, 0.0) + jnp.where(spot == 31, right, 0.0))
        out_ref[1] = rows_of(columns)


def table_grads(ids, first, scores, places, positions, sums=()):
    wide = PLACES // 128 * positions.shape[1] // 2
    return call(
        functools.partial(tables_kernel, base=0 if first else 1),
        "table_grads",
        ids,
        (scores, places, positions, *sums),
        shape((2 if sums else 1, 8, 32), F32),
        mib=TABLES_MIB,
        us=0.01,
        scratch=[pltpu.VMEM((HEADS * 128, wide), BF), pltpu.VMEM((SPAN, wide), BF)],
    )


def terms_of(grads, weights):
    total = None
    for part, w_ref in enumerate(weights):
        found = dot(grads[part], w_ref[...], ((0,), (0,)))
        total = found if total is None else total + found
    return total


def terms_send_kernel(ids, w0, w1, w2, grads_ref, *outs):
    for at, out_ref in enumerate(outs):
        out_ref[...] = terms_of(grads_ref[2 * at + 1], (w0, w1, w2)).astype(BF)


def terms_keep_kernel(ids, w0, w1, w2, grads_ref, got_own, got_other, own_ref, other_ref):
    other_ref[...] = (terms_of(grads_ref[2], (w0, w1, w2)) + got_other[...].astype(F32)).astype(BF)
    own_ref[...] = terms_of(grads_ref[0], (w0, w1, w2)) + got_own[...].astype(F32)


def terms_send(ids, weights, grads):
    outs = [shape((grads.shape[3], weights[0].shape[1]), BF)] * 2
    return call(terms_send_kernel, "terms_send", ids, (*weights, grads), outs, mib=16, us=0.01)


def terms_keep(ids, weights, grads, got):
    outs = [shape(got[0].shape, F32), shape(got[0].shape, BF)]
    return call(terms_keep_kernel, "terms_keep", ids, (*weights, grads, *got), outs, mib=16, us=0.01)


def last_kernel(
    ids, mine_ref, sent_ref, x_ref, page_ref, feat_ref, gain_ref, grad_ref, second_ref, mixed_ref, ffn_ref, got_ref,
    out_ref, part_ref,
):
    grad_normed = mine_ref[...] + sent_ref[...].astype(F32)
    here = quarter_of(ids[0], mine_ref.shape[0])
    unit, factor = unit_rows(hidden_rows(x_ref[here, :], page_ref[:, here], feat_ref[...]))
    scaled = grad_normed * gain_ref[...].astype(F32)
    grad = factor * (scaled - unit * jnp.mean(scaled * unit, axis=-1, keepdims=True))
    rows, width = grad.shape
    out_ref[0, :rows] = (mixed_ref[...] + ffn_ref[...] + got_ref[...].astype(F32)).astype(BF)
    out_ref[1, :rows] = (grad_ref[...] + grad).astype(BF)
    part_ref[0:1] = jnp.sum(grad_normed * unit, axis=0, keepdims=True)
    part_ref[1:2] = second_ref[...]


def last(ids, mine, sent, inputs, onehot, feats, gain, grad_mixed, second, *ffn):
    rows, width = mine.shape
    arrays = (mine, sent, inputs, onehot, feats, gain, grad_mixed, second, *ffn)
    outs = [shape((2, rows, width), BF), shape((2, width), F32)]
    return call(last_kernel, "last", ids, arrays, outs, mib=16, us=0.01)


def pack_kernel(ids, gains_ref, got_ref, hor_a, ver_a, hor_b, ver_b, out_ref):
    gains = gains_ref[...] + got_ref[...]
    gains = [gains[slot : slot + 1] for slot in range(2)]
    parts = gains[0].shape[1] // 128
    for slot in range(2):
        gain = gains[slot]
        for part in range(parts):
            at = slot * parts + part
            out_ref[at : at + 1, :] = gain[:, part * 128 : part * 128 + 128]
    bins = hor_a.shape[2]
    at = 2 * parts
    out_ref[at:, :] = jnp.zeros((out_ref.shape[0] - at, 128), F32)
    for found in (hor_b[1], hor_a[0] + hor_b[0], ver_a[0] + ver_b[0]):
        out_ref[at : at + HEADS, :bins] = found[:HEADS]
        at += HEADS


def pack(ids, gains, got, *sums):
    size = gains.shape[1] // 128 * 2 + 3 * HEADS
    size = -(-size // 8) * 8
    return call(pack_kernel, "pack", ids, (gains, got, *sums), shape((size, 128), F32), mib=8, us=0.1)


def join_kernel(ids, b0, b1, b2, b3, out_ref, *, slot):
    for k, b_ref in enumerate((b0, b1, b2, b3)):

        @pl.when(pl.program_id(0) == k)
        def _(b_ref=b_ref):
            out_ref[...] = b_ref[slot, : out_ref.shape[0]].astype(out_ref.dtype)


def join_feat_kernel(ids, b0, b1, b2, b3, page_ref, out_ref, feat_ref, all_ref, *, slot):
    step = pl.program_id(0)
    rows = out_ref.shape[0]
    for k, b_ref in enumerate((b0, b1, b2, b3)):

        @pl.when(step == k)
        def _(b_ref=b_ref, k=k):
            out_ref[...] = b_ref[slot, :rows].astype(out_ref.dtype)
            all_ref[pl.ds(pl.multiple_of(ids[k] * rows, rows), rows), :] = b_ref[slot, :rows]

    @pl.when(step == 3)
    def _():
        feat_ref[...] = dot(page_ref[...].astype(F32).astype(BF), all_ref[...])


def join(ids, blocks, slot, dtype, onehot=None):
    _, rows, width = blocks[0].shape
    specs = [VMEM] * 4
    outs, out_specs = [shape((4 * rows, width), dtype)], [pl.BlockSpec((rows, width), lambda i, s: (s[i], 0))]
    extra, scratch = (), []
    if onehot is not None:
        pages = onehot.shape[0]
        specs = specs + [VMEM]
        outs.append(shape((pages, width), F32))
        out_specs.append(whole((pages, width)))
        extra, scratch = (onehot,), [pltpu.VMEM((4 * rows, width), BF)]
    found = pl.pallas_call(
        functools.partial(join_kernel if onehot is None else join_feat_kernel, slot=slot),
        grid_spec=pltpu.PrefetchScalarGridSpec(
            num_scalar_prefetch=1, grid=(4,), in_specs=specs, out_specs=out_specs, scratch_shapes=scratch
        ),
        out_shape=outs,
        compiler_params=params(16),
        cost_estimate=cost(0.01),
        name="join_output" if onehot is None else "join_grads",
    )(ids, *blocks, *extra)
    return found[0] if onehot is None else found


def split_rows(ids, total, cols, keep_ref, send_ref, parity):
    groups, size = keep_ref.shape[0], keep_ref.shape[1]
    for g in range(groups):
        mine = pl.multiple_of((2 * g + parity) * size, 8)
        theirs = pl.multiple_of((2 * g + 1 - parity) * size, 8)
        keep_ref[g] = total[pl.ds(mine, size), cols].astype(keep_ref.dtype)
        send_ref[g] = total[pl.ds(theirs, size), cols].astype(BF)


def feed_grad_kernel(ids, k0, n0, k1, n1, c0, c1, cot_ref, *outs, fast):
    units = k0.shape[2]
    rows = lambda refs: jnp.concatenate(refs, axis=0)
    total = outs[-1]
    normed = rows([n0[2], c0[2], n1[2], c1[2]])
    total[:, :units] = dot(normed, rows([k0[1], c0[1], k1[1], c1[1]]), ((0,), (0,)))
    cotangent = rows([cot_ref[quarter_of(ids[n], k0.shape[1]), :] for n in range(4)])
    total[:, units:] = dot(cotangent, rows([k0[0], c0[0], k1[0], c1[0]]), ((0,), (0,)))
    if fast:
        split_rows(ids, total, slice(None), outs[0], outs[1], ids[9])
    else:
        outs[0][...] = total[...]


def feed_grad(ids, own, other, got_own, got_other, cotangent, fast):
    _, rows, units = own[0].shape
    width = cotangent.shape[1]
    if fast:
        outs = [shape((4, width // 8, 2 * units), F32), shape((4, width // 8, 2 * units), BF)]
    else:
        outs = [shape((width, 2 * units), F32)]
    return call(
        functools.partial(feed_grad_kernel, fast=fast),
        "feed_grad",
        ids,
        (*own, *other, got_own, got_other, cotangent),
        outs,
        mib=24,
        us=7,
        scratch=[pltpu.VMEM((width, 2 * units), F32)],
    )


def head_grad_kernel(ids, normed_ref, grads_ref, l0, l2, l1, l3, a0, a1, a2, a3, *outs, fast):
    total, turned = outs[-2:]
    n = a0.shape[0]
    normed = jnp.concatenate([normed_ref[quarter_of(ids[k], a0.shape[1]), :] for k in range(4)], axis=0)
    for part in range(3):
        left = jnp.concatenate([grads_ref[k, part] for k in range(4)], axis=1)
        total[part * n : (part + 1) * n, :] = dot(left, normed)
    low = jnp.concatenate([r[...] for r in (l0, l1, l2, l3)], axis=0)
    total[3 * n :, :] = dot(jnp.concatenate([r[...] for r in (a0, a1, a2, a3)], axis=1), low)
    turned[...] = total[...].T
    if fast:
        split_rows(ids, turned, slice(None), outs[0], outs[1], ids[9])
    else:
        outs[0][...] = turned[...]


def head_grad(ids, normed, grads, low, low_got, attended, fast):
    seq, width = normed.shape
    n = grads.shape[2]
    if fast:
        outs = [shape((4, width // 8, 4 * n), F32), shape((4, width // 8, 4 * n), BF)]
    else:
        outs = [shape((width, 4 * n), F32)]
    return call(
        functools.partial(head_grad_kernel, fast=fast),
        "head_grad",
        ids,
        (normed, grads, *low, *low_got, *attended),
        outs,
        mib=18,
        us=0.01,
        scratch=[pltpu.VMEM((4 * n, width), F32), pltpu.VMEM((width, 4 * n), F32)],
    )


def pair_kernel(ids, *refs):
    pairs, outs = refs[:-4], refs[-4:]
    for k, o_ref in enumerate(outs):
        at = ids[4 + k]
        start = 0
        for keep_ref, got_ref in zip(pairs[::2], pairs[1::2]):
            n = keep_ref.shape[2]
            o_ref[:, start : start + n] = (keep_ref[at] + got_ref[at].astype(F32)).astype(o_ref.dtype)
            start += n


def pair_sum(ids, *arrays):
    size = arrays[0].shape[1]
    n = sum(a.shape[2] for a in arrays[::2])
    outs = [shape((size, n), F32)] + [shape((size, n), BF)] * 3
    return call(pair_kernel, "pair_sum", ids, arrays, outs, mib=16, us=0.01)


def feed_final_kernel(a0, a1, a2, a3, up_ref, down_ref):
    total = a0[...] + a1[...].astype(F32) + a2[...].astype(F32) + a3[...].astype(F32)
    units = up_ref.shape[1]
    up_ref[...] = total[:, :units]
    down_ref[...] = total[:, units:]


def head_final_kernel(a0, a1, a2, a3, one_ref, two_ref, q_ref, k_ref, v_ref, o_ref, *smalls):
    total = a0[...] + a1[...].astype(F32) + a2[...].astype(F32) + a3[...].astype(F32)
    n = q_ref.shape[1]
    for at, goal in enumerate((q_ref, k_ref, v_ref)):
        goal[...] = total[:, at * n : (at + 1) * n]
    o_ref[...] = total[:, 3 * n :].T
    *tables, gains_ref = smalls
    total = one_ref[...] + two_ref[...]
    parts = gains_ref.shape[1] // 128
    for slot in range(2):
        for part in range(parts):
            at = slot * parts + part
            gains_ref[slot : slot + 1, part * 128 : part * 128 + 128] = total[at : at + 1]
    at, bins = 2 * parts, tables[0].shape[1]
    for goal in tables:
        goal[...] = total[at : at + HEADS, :bins]
        at += HEADS


def final(kernel, arrays, done, outs):
    arrays = [after(arrays[0], done)] + arrays[1:]
    return pl.pallas_call(
        kernel,
        grid=(1,),
        in_specs=[VMEM] * len(arrays),
        out_specs=jax.tree.map(lambda o: whole(o.shape), outs),
        out_shape=outs,
        compiler_params=params(16),
        cost_estimate=cost(5 if kernel is feed_final_kernel else 0.01),
        name=kernel.__name__[:-7],
    )(*arrays)


def swap(array, axis, size, bits):
    return lax.ppermute(array, axis, [(i, i ^ bits) for i in range(size)])


def after(array, *others):
    return lax.optimization_barrier((array, others))[0]


def local(
    inputs, page_feat, page_onehot, lengths, hor_pos, ver_pos, norm1_gain, w_query, w_key, w_value,
    rel_table, hor_table, ver_table, w_output, norm2_gain, w_up, w_down, cotangent, *, dp,
):
    seq, width = inputs.shape
    fast = dp == 8
    over = functools.partial(swap, axis="mp", size=4)
    m = lax.axis_index("mp").astype(I32)
    d = lax.axis_index("dp").astype(I32)
    k4 = jnp.arange(4, dtype=I32)
    spot = lambda who: (who & 1) * 2 + (who >> 1)
    ids = jnp.concatenate([
        spot(m ^ k4),
        (d >> 1) ^ k4,
        lengths[:1],
        (d & 1)[None],
    ])
    gain_one, gain_two = norm1_gain[None], norm2_gain[None]
    feats = page_feat[0]
    hor, ver = hor_pos[None], ver_pos[None]
    tables = (rel_table, hor_table, ver_table)
    pages = page_onehot.T
    weights = [w_query.T, w_key.T, w_value.T]

    wo_y, wo_core = over(w_output, bits=2), over(w_output, bits=1)
    normed1, queries, keys, values = project(ids, inputs, pages, feats, gain_one, *weights)
    w_outputs = [w_output, wo_core, wo_y, over(after(wo_y, normed1), bits=1)]
    ups = [w_up, over(after(w_up, normed1), bits=1)]
    downs = [w_down, over(after(w_down, normed1), bits=1)]

    (e_a, att0, att1, inverse_a, out_a), lookups = attend(ids, queries, keys, values, hor, ver, tables, None)
    from_y, from_yc, own1 = over(att0, bits=2), over(att1, bits=3), over(att1, bits=1)
    ver_late = after(ver, att0, w_outputs[3], ups[1], downs[1])
    (e_b, att2, att3, inverse_b, out_b), _ = attend(ids, queries, keys, values, hor, ver_late, tables, lookups)
    attended = [att0, att1, att2, att3]
    for_other = [att2, over(att3, bits=1), from_y, from_yc]
    for_own = [att0, own1, over(att2, bits=2), over(att3, bits=3)]

    around = functools.partial(swap, axis="dp", size=dp)
    to_z = lambda parts: [parts[0]] + [around(part, bits=2 * k) for k, part in zip((1, 2, 3), parts[1:])]
    size = width // dp
    n = w_query.shape[1]
    units = w_up.shape[1]
    fixed = (inputs, pages, feats, gain_two, cotangent)
    x_keep, x_send, x_mixed, x_grad, x_ffn = feed(ids, False, *fixed, for_other, w_outputs, ups, downs)
    got_own, x_got = over(x_grad, bits=2), over(x_send, bits=1)
    for_own[0] = after(att0, x_ffn)
    m_keep, m_send, mixed, m_grad, m_ffn = feed(ids, True, *fixed, for_own, w_outputs, ups, downs)
    got_other, m_got = over(m_grad, bits=2), over(after(m_send, x_got), bits=1)
    own_grad = add(ids, m_grad, got_own)

    feed_grads = feed_grad(ids, (after(m_keep, own_grad), m_send), (x_keep, x_send), m_got, x_got, cotangent, fast)
    feed_got = around(feed_grads[1], bits=1) if fast else ids
    hor_at, ver_at = places_of(ids, after(hor, feed_grads[0]), ver)
    grad_mixed, ga, core_send, *low, gain_two_part = mid(
        ids, (after(own_grad, hor_at), mixed), (x_grad, got_other, x_mixed), gain_two, cotangent, w_outputs[:2]
    )
    core_got = over(core_send, bits=1)
    sent_ffn = over(after(x_ffn, got_other, hor_at), bits=2)

    halves = ((e_a, e_b), (inverse_a, inverse_b), (out_a, out_b))
    scores_a, dq0, dq2, key_sum, value_sum, near, far = back(ids, halves, queries, keys, values, ga, None)
    scores_b, grads, near, far = back(
        ids, halves, queries, keys, values, after(core_got, dq0), (key_sum, value_sum, near, far, dq0, dq2)
    )
    low_got = [over(part, bits=1) for part in low]
    to_core = terms_send(ids, weights, after(grads, sent_ffn))
    got_terms = [over(part, bits=1) for part in to_core]
    head_grads = head_grad(ids, normed1, after(grads, to_core[0]), low, low_got, attended, fast)
    own_terms, other_terms = terms_keep(ids, weights, after(grads, head_grads[0]), got_terms)
    sent_terms = over(other_terms, bits=2)

    hor_a = table_grads(ids, True, scores_a, hor_at, after(hor, own_terms))
    done = hor_a
    if fast:
        feed_parts = to_z(pair_sum(ids, after(feed_grads[0], done), feed_got))
        done = feed_parts[0]
    head_got = around(after(head_grads[1], done), bits=1) if fast else ids
    rows, gains = last(
        ids, after(own_terms, done), sent_terms, inputs, pages, feats, gain_one, grad_mixed, gain_two_part,
        mixed, m_ffn, sent_ffn,
    )
    rows_y, rows_core = over(rows, bits=2), over(rows, bits=1)
    ver_a = table_grads(ids, True, scores_a, ver_at, after(ver, rows))
    gains = after(gains, ver_a) + over(gains, bits=1)
    got_gains = over(gains, bits=2)
    hor_b = table_grads(ids, False, scores_b, hor_at, after(hor, gains), (near, far))
    ver_b = table_grads(ids, False, scores_b, ver_at, after(ver, hor_b, head_got))

    small = pack(ids, gains, got_gains, hor_a, ver_a, hor_b, ver_b)
    if fast:
        got = around(small, bits=1)
        grad_up, grad_down = final(feed_final_kernel, feed_parts, small, [shape((size, units), F32)] * 2)
        head_parts = to_z(pair_sum(ids, after(head_grads[0], grad_up), head_got))
        small = after(small, head_parts[0]) + got
        got = around(small, bits=2)
        quarters = [rows, rows_core, rows_y, over(after(rows_y, grad_up), bits=1)]
        outputs = join(ids, [after(rows, small)] + quarters[1:], 0, BF)
        grad_inputs, grad_feats = join(ids, [after(rows, outputs)] + quarters[1:], 1, F32, pages)
        small = after(small, grad_feats) + got
        bins = rel_table.shape[1]
        outs = [shape((size, n), F32)] * 3 + [shape((n, size), F32)] + [shape((HEADS, bins), F32)] * 3
        *found, gain_sums = final(
            head_final_kernel, head_parts + [small, around(small, bits=4)], grad_feats, outs + [shape((2, width), F32)]
        )
        grad_query, grad_key, grad_value, grad_output, grad_rel, grad_hor, grad_ver = found
    else:
        quarters = [rows, rows_core, rows_y, over(rows_y, bits=1)]
        outputs = join(ids, quarters, 0, BF)
        grad_inputs, grad_feats = join(ids, quarters, 1, F32, pages)
        small = lax.psum(small, "dp")
        scatter = lambda a: lax.psum_scatter(a[0], "dp", scatter_dimension=0, tiled=True)
        grad_feed, heads = scatter(feed_grads), scatter(head_grads)
        grad_up, grad_down = grad_feed[:, :units], grad_feed[:, units:]
        grad_query, grad_key, grad_value = heads[:, :n], heads[:, n : 2 * n], heads[:, 2 * n : 3 * n]
        grad_output = heads[:, 3 * n :].T
        gain_sums = small[: width // 128 * 2].reshape(2, width)
        table_sums = small[width // 128 * 2 :, : rel_table.shape[1]]
        grad_rel, grad_hor, grad_ver = (table_sums[at : at + HEADS] for at in range(0, 3 * HEADS, HEADS))
    gain_sums = lax.dynamic_slice(gain_sums, (0, d * size), (2, size))
    return (
        outputs, grad_inputs, grad_feats[None], gain_sums[0], grad_query, grad_key, grad_value,
        grad_rel, grad_hor, grad_ver, grad_output, gain_sums[1], grad_up, grad_down.T,
    )


def solution(mesh):
    return jax.shard_map(
        functools.partial(local, dp=mesh.shape["dp"]),
        mesh=mesh,
        in_specs=(
            P("dp", None),
            P("dp", None, None),
            P("dp", None),
            P("dp"),
            P("dp"),
            P("dp"),
            P(),
            P(None, "mp"),
            P(None, "mp"),
            P(None, "mp"),
            P("mp", None),
            P("mp", None),
            P("mp", None),
            P("mp", None),
            P(),
            P(None, "mp"),
            P("mp", None),
            P("dp", None),
        ),
        out_specs=(
            P("dp", None),
            P("dp", None),
            P("dp", None, None),
            P("dp"),
            P("dp", "mp"),
            P("dp", "mp"),
            P("dp", "mp"),
            P("mp", None),
            P("mp", None),
            P("mp", None),
            P("mp", "dp"),
            P("dp"),
            P("dp", "mp"),
            P("mp", "dp"),
        ),
        check_vma=False,
    )
```

```python
import functools

import jax
import jax.numpy as jnp
import numpy as np
from jax import lax
from jax.experimental import pallas as pl
from jax.experimental.pallas import tpu as pltpu
from jax.sharding import PartitionSpec as P

EPS = 1e-06
THRESHOLDS = (12, 16, 23, 32, 46, 64, 91)
FAR = 91
HEADS = 3
HD = 64
PAD = 128
MARKS = 72
NEAR = 40
TILES = NEAR + 2
SPAN = 384
LOW = 92
TOP = 311
BF = jnp.bfloat16
F32 = jnp.float32
I32 = jnp.int32
FEED_CHUNK = 256
PLACES = 1024
TABLES_MIB = 18
GELU_C = float(np.sqrt(2.0 / np.pi))


def dot(left, right, dims=((1,), (0,))):
    return lax.dot_general(left, right, (dims, ((), ())), preferred_element_type=F32)


def bucket(delta):
    magnitude = jnp.abs(delta)
    coarse = 8 + sum((magnitude >= limit).astype(I32) for limit in THRESHOLDS)
    return jnp.where(magnitude < 8, magnitude, coarse) + 16 * (delta > 0).astype(I32)


def params(mib):
    return pltpu.CompilerParams(vmem_limit_bytes=mib * 2**20)


def cost(microseconds):
    return pl.CostEstimate(flops=int(1.15e9 * microseconds), bytes_accessed=1, transcendentals=0)


def shape(dims, dtype):
    return jax.ShapeDtypeStruct(dims, dtype)


def whole(dims):
    return pl.BlockSpec(dims, lambda *a: (0,) * len(dims))


VMEM = pl.BlockSpec(memory_space=pltpu.VMEM)


def call(kernel, name, ids, arrays, outs, *, mib, us, scratch=()):
    return pl.pallas_call(
        kernel,
        grid_spec=pltpu.PrefetchScalarGridSpec(
            num_scalar_prefetch=1,
            grid=(1,),
            in_specs=[VMEM] * len(arrays),
            out_specs=jax.tree.map(lambda _: VMEM, outs),
            scratch_shapes=list(scratch),
        ),
        out_shape=outs,
        compiler_params=params(mib),
        cost_estimate=cost(us),
        name=name,
    )(ids, *arrays)


def quarter_of(place, size):
    return pl.ds(pl.multiple_of(place * size, 128), size)


def hidden_rows(inputs, pages, feats):
    return inputs.astype(F32) + dot(pages.astype(F32).astype(BF), feats, ((0,), (0,)))


def unit_rows(field):
    factor = lax.rsqrt(jnp.mean(field * field, axis=-1, keepdims=True) + EPS)
    return field * factor, factor


def project_kernel(ids, x_ref, page_ref, feat_ref, gain_ref, wq_ref, wk_ref, wv_ref, n_ref, q_ref, k_ref, v_ref):
    rows = x_ref.shape[0]
    unit, _ = unit_rows(hidden_rows(x_ref[...], page_ref[...], feat_ref[...]))
    normed = (unit * gain_ref[...].astype(F32).reshape(1, -1)).astype(BF)
    n_ref[...] = normed
    lane = lax.broadcasted_iota(I32, (rows, PAD), 1)
    row = lax.broadcasted_iota(I32, (rows, PAD), 0)
    masked = jnp.where((lane == HD) & (row >= ids[8]), -1e30, 0.0)
    block = lane - MARKS
    far_left = (block >= 0) & (block < 8) & (row < 128 * block - 96)
    far_right = (block >= 8) & (block < 16) & (row >= 128 * (block - 8) + 224)
    masked = jnp.where(far_left | far_right, 1.0, masked)
    query_extra = jnp.where(lane == HD, 1.0, 0.0)
    value_extra = jnp.where((lane == HD) | (lane == HD + 1), 1.0, 0.0)
    for out_ref, w_ref, extra, scale in (
        (q_ref, wq_ref, query_extra, 0.125),
        (k_ref, wk_ref, masked, None),
        (v_ref, wv_ref, value_extra, None),
    ):
        full = dot(normed, w_ref[...], ((1,), (1,)))
        if scale is not None:
            full = full * scale
        pair = full[:, :PAD]
        last = jnp.concatenate([full[:, PAD:], jnp.zeros((rows, PAD - HD), F32)], axis=1)
        heads = (pair, pltpu.roll(pair, HD, 1), last)
        for head in range(HEADS):
            out_ref[:, head * PAD : (head + 1) * PAD] = jnp.where(lane < HD, heads[head], extra).astype(BF)


def project(ids, *arrays):
    seq, width = arrays[0].shape
    outs = [shape((seq, width), BF)] + [shape((seq, HEADS * PAD), BF)] * 3
    return call(project_kernel, "project", ids, arrays, outs, mib=16, us=7)


def place(delta):
    magnitude = jnp.abs(delta)
    coarse = jnp.minimum(25 - lax.clz(delta * delta), 7)
    exact = magnitude < 8
    return jnp.where(exact, magnitude, coarse), exact, delta > 0


def look(table_ref, row, where):
    index, exact, after = where
    found = [jnp.take_along_axis(table_ref[row, part], index, axis=0) for part in range(4)]
    return jnp.where(after, jnp.where(exact, found[2], found[3]), jnp.where(exact, found[0], found[1]))


def tile_delta(tile):
    lane = lax.broadcasted_iota(I32, (8, 128), 1)
    sub = lax.broadcasted_iota(I32, (8, 128), 0)
    delta = 8 * (tile - 13) + sub - lane
    if tile == 0:
        delta = jnp.full_like(delta, -1000)
    if tile == TILES - 1:
        delta = jnp.full_like(delta, 1000)
    return delta


def attend_kernel(*refs, first, chunk):
    ids, q_ref, k_ref, v_ref, hor_ref, ver_ref = refs[:6]
    if first:
        hor_all, ver_all, rel_table, hor_table, ver_table, e_ref, att0, att1, inv_ref, out_ref = refs[6:16]
        rel_ref, t8_ref, hor_col, ver_col, s_ref = refs[16:]
    else:
        rel_ref, t8_ref, hor_col, ver_col, e_ref, att0, att1, inv_ref, out_ref, s_ref = refs[6:]
    seq = k_ref.shape[0]
    width = seq // 4
    lanes = width // 128

    if first:
        for all_ref, col_ref in ((hor_all, hor_col), (ver_all, ver_col)):
            for b in range(seq // 128):
                cols = slice(128 * b, 128 * b + 128)
                spread = jnp.broadcast_to(all_ref[:, cols].astype(F32), (128, 128))
                col_ref[cols, :] = spread.T.astype(I32)
        lane = lax.broadcasted_iota(I32, (8, 32), 1)
        sub = lax.broadcasted_iota(I32, (8, 32), 0)
        for axis, table_ref in enumerate((rel_table, hor_table, ver_table)):
            table = table_ref[...].astype(F32)
            for head in range(HEADS):
                row = jnp.broadcast_to(table[head : head + 1], (8, 32))
                for part in range(4):
                    entries = jnp.sum(jnp.where(lane == sub + 8 * part, row, 0.0), axis=1, keepdims=True)
                    t8_ref[axis * HEADS + head, part] = jnp.broadcast_to(entries, (8, 128))
        for tile in range(TILES):
            where = place(tile_delta(tile))
            for head in range(HEADS):
                rel_ref[head, tile] = look(t8_ref, head, where)

    places = [ids[(0 if first else 2) + part] for part in range(2)]
    here = [quarter_of(at, width) for at in places]

    def products(part):
        queries = q_ref[here[part], :]
        for head in range(HEADS):
            cols = slice(head * PAD, (head + 1) * PAD)
            s_ref[part, head] = dot(k_ref[:, cols], queries[:, cols], ((1,), (1,)))

    def biases(part):
        hor_row, ver_row = hor_ref[:, here[part]], ver_ref[:, here[part]]
        hor = [jnp.broadcast_to(hor_row[:, 128 * l : 128 * l + 128], (8, 128)) for l in range(lanes)]
        ver = [jnp.broadcast_to(ver_row[:, 128 * l : 128 * l + 128], (8, 128)) for l in range(lanes)]
        block = places[part] * lanes

        def add_bias(c, tops):
            tops = list(tops)
            base = pl.multiple_of(c * chunk, chunk)
            for g in range(chunk // 8):
                rows = pl.ds(pl.multiple_of(base + 8 * g, 8), 8)
                hor_keys, ver_keys = hor_col[rows, :], ver_col[rows, :]
                for l in range(lanes):
                    cols = pl.ds(128 * l, 128)
                    hor_at, ver_at = place(hor_keys - hor[l]), place(ver_keys - ver[l])
                    tile = jnp.clip(c * (chunk // 8) + g - 16 * (block + l) + 13, 0, TILES - 1)
                    for head in range(HEADS):
                        s = s_ref[part, head, rows, cols] + rel_ref[head, tile]
                        s = s + (look(t8_ref, HEADS + head, hor_at) + look(t8_ref, 2 * HEADS + head, ver_at))
                        s_ref[part, head, rows, cols] = s
                        tops[head * lanes + l] = jnp.maximum(tops[head * lanes + l], s)
            return tuple(tops)

        tops = lax.fori_loop(
            0, seq // chunk, add_bias, tuple(jnp.full((8, 128), -1e30, F32) for _ in range(HEADS * lanes))
        )
        return [jnp.broadcast_to(jnp.max(top, axis=0, keepdims=True), (16, 128)) for top in tops]

    def attended(part, peaks, att_ref):
        mine = slice(part * width, (part + 1) * width)
        for head in range(HEADS):
            for g in range(seq // 16):
                rows = slice(16 * g, 16 * g + 16)
                for l in range(lanes):
                    cols = slice(128 * l, 128 * l + 128)
                    into = slice(part * width + 128 * l, part * width + 128 * l + 128)
                    e_ref[head, rows, into] = jnp.exp(s_ref[part, head, rows, cols] - peaks[head * lanes + l]).astype(BF)
            total = dot(v_ref[:, head * PAD : (head + 1) * PAD], e_ref[head, :, mine], ((0,), (0,)))
            inverse = 1.0 / total[HD : HD + 1, :]
            inv_ref[head : head + 1, mine] = inverse
            out_ref[head * HD : (head + 1) * HD, mine] = total[:HD] * inverse
        att_ref[...] = out_ref[:, mine].astype(BF)

    products(0)
    peaks = biases(0)
    products(1)
    attended(0, peaks, att0)
    attended(1, biases(1), att1)


def attend(ids, queries, keys, values, hor, ver, tables, lookups):
    seq = queries.shape[0]
    width = seq // 4
    first = lookups is None
    columns = HEADS * HD
    made = [
        shape((HEADS, TILES, 8, 128), F32), shape((3 * HEADS, 4, 8, 128), F32), shape((seq, 128), I32), shape((seq, 128), I32)
    ]
    extra = (hor, ver, *tables) if first else tuple(lookups)
    outs = [
        shape((HEADS, seq, 2 * width), BF), shape((columns, width), BF), shape((columns, width), BF),
        shape((HEADS, 2 * width), F32), shape((columns, 2 * width), F32),
    ]
    found = call(
        functools.partial(attend_kernel, first=first, chunk=128),
        "attend_first" if first else "attend_last",
        ids,
        (queries, keys, values, hor, ver, *extra),
        outs + made if first else outs,
        mib=14,
        us=14,
        scratch=[pltpu.VMEM((2, HEADS, seq, width), F32)],
    )
    return found[:5], found[5:]


def feed_kernel(
    ids, x_ref, page_ref, feat_ref, gain_ref, cot_ref, a0, a1, a2, a3, o0, o1, o2, o3, u0, u1, d0, d1,
    keep_ref, send_ref, mixed_ref, grad_ref, ffn_ref, *, slot,
):
    here = quarter_of(ids[slot], mixed_ref.shape[0])
    cotangent = cot_ref[here, :]
    mixed = hidden_rows(x_ref[here, :], page_ref[:, here], feat_ref[...])
    for a_ref, o_ref in ((a0, o0), (a1, o1), (a2, o2), (a3, o3)):
        mixed = mixed + dot(a_ref[...], o_ref[...], ((0,), (0,)))
    mixed_ref[...] = mixed
    unit, _ = unit_rows(mixed)
    normed = (unit * gain_ref[...].astype(F32).reshape(1, -1)).astype(BF)
    send_ref[2] = normed
    units = u0.shape[1]
    for u_ref, d_ref, goal in ((u0, d0, keep_ref), (u1, d1, send_ref)):
        for at in range(0, units, FEED_CHUNK):
            cols = slice(at, at + FEED_CHUNK)
            upward = dot(normed, u_ref[:, cols])
            square = upward * upward
            tanh = jnp.tanh(GELU_C * upward * (1.0 + 0.044715 * square))
            lifted = 0.5 * (1.0 + tanh)
            activated = (upward * lifted).astype(BF)
            slope = lifted + 0.5 * upward * (1.0 - tanh * tanh) * (GELU_C * (1.0 + 3 * 0.044715 * square))
            grad_up = (dot(cotangent, d_ref[cols, :], ((1,), (1,))) * slope).astype(BF)
            goal[0, :, cols] = activated
            goal[1, :, cols] = grad_up
    ffn = dot(keep_ref[0], d0[...]) + dot(send_ref[0], d1[...])
    ffn_ref[...] = ffn.astype(ffn_ref.dtype)
    grad = dot(keep_ref[1], u0[...], ((1,), (1,))) + dot(send_ref[1], u1[...], ((1,), (1,)))
    grad_ref[...] = grad.astype(grad_ref.dtype)


def feed(ids, own, inputs, onehot, feats, gain, cotangent, attended, w_outputs, ups, downs):
    seq, width = inputs.shape
    rows = seq // 4
    units = ups[0].shape[1]
    kept = F32 if own else BF
    outs = [
        shape((2, rows, units), BF), shape((3, rows, width), BF), shape((rows, width), F32),
        shape((rows, width), BF), shape((rows, width), kept),
    ]
    return call(
        functools.partial(feed_kernel, slot=0 if own else 2),
        "feed_own" if own else "feed_other",
        ids,
        (inputs, onehot, feats, gain, cotangent, *attended, *w_outputs, *ups, *downs),
        outs,
        mib=16,
        us=20 if own else 10,
    )


def add_kernel(ids, one_ref, two_ref, out_ref):
    out_ref[...] = one_ref[...].astype(F32) + two_ref[...].astype(F32)


def add(ids, one, two):
    return call(add_kernel, "add", ids, (one, two), shape(one.shape, F32), mib=8, us=20)


def mid_kernel(
    ids, own_grad, own_mixed, other_grad, other_got, other_mixed, cot_ref, gain_ref, o0, o1,
    grad_ref, own_ref, core_ref, low_own, low_other, part_ref,
):
    rows = own_grad.shape[0]
    other = other_grad[...].astype(F32) + other_got[...].astype(F32)
    for at, (grad_normed, mixed_ref) in enumerate(((own_grad[...], own_mixed), (other, other_mixed))):
        unit, factor = unit_rows(mixed_ref[...])
        scaled = grad_normed * gain_ref[...].astype(F32).reshape(1, -1)
        grad = factor * (scaled - unit * jnp.mean(scaled * unit, axis=-1, keepdims=True))
        grad = cot_ref[quarter_of(ids[2 * at], rows), :].astype(F32) + grad
        low = grad.astype(BF)
        (low_own, low_other)[at][...] = low
        if at == 0:
            grad_ref[...] = grad
            part_ref[...] = jnp.sum(grad_normed * unit, axis=0, keepdims=True)
        for o_ref, goal in ((o0, own_ref), (o1, core_ref)):
            goal[:, at * rows : (at + 1) * rows] = dot(o_ref[...], low, ((1,), (1,))).astype(BF)


def mid(ids, own, other, gain, cotangent, w_outputs):
    rows, width = own[0].shape
    columns = HEADS * HD
    outs = [
        shape((rows, width), F32), shape((columns, 2 * rows), BF), shape((columns, 2 * rows), BF), shape((rows, width), BF),
        shape((rows, width), BF), shape((1, width), F32),
    ]
    arrays = (*own, *other, cotangent, gain, *w_outputs)
    return call(mid_kernel, "mid", ids, arrays, outs, mib=16, us=0.01)


def back_kernel(*refs, first):
    ids, ea_ref, eb_ref, inv_a, inv_b, out_a, out_b, q_ref, k_ref, v_ref, grad_ref = refs[:11]
    refs = refs[11:]
    if first:
        ds_ref, dqa_ref, dqb_ref, key_ref, value_ref, near_ref, far_ref, x_ref = refs
    else:
        key_in, value_in, near_in, far_in, dqa_in, dqb_in = refs[:6]
        ds_ref, all_ref, near_ref, far_ref, x_ref = refs[6:]
    seq = k_ref.shape[0]
    width = seq // 4
    both = 2 * width
    lanes = width // 128
    base = 0 if first else 1
    sub = lax.broadcasted_iota(I32, (HD, both), 0)
    blocks = [ids[base + 2 * (l // lanes)] * lanes + l % lanes for l in range(2 * lanes)]
    mine = slice(base * width, (base + 1) * width)
    here = [quarter_of(ids[base + 2 * n], width) for n in range(2)]
    beside = lambda one, two: jnp.concatenate([one, two], axis=1)
    spot = lax.broadcasted_iota(I32, (8, 128), 0)

    for head in range(HEADS):
        cols = slice(head * PAD, (head + 1) * PAD)
        rows = slice(head * HD, (head + 1) * HD)
        grad = grad_ref[rows, :].astype(F32)
        grad = (grad * beside(inv_a[head : head + 1, mine], inv_b[head : head + 1, mine])).astype(BF).astype(F32)
        inner = jnp.sum(grad * beside(out_a[rows, mine], out_b[rows, mine]), axis=0, keepdims=True)
        high = inner.astype(BF).astype(F32)
        extra = jnp.where(sub == 0, -high, jnp.where(sub == 1, high - inner, 0.0))
        right = jnp.concatenate([grad, extra], axis=0).astype(BF)
        x_ref[head % 2] = dot(v_ref[:, cols], right)
        value = dot(beside(ea_ref[head, :, mine], eb_ref[head, :, mine]), right, ((1,), (1,)))
        for c in range(seq // 16):
            at = slice(16 * c, 16 * c + 16)
            found = beside(ea_ref[head, at, mine], eb_ref[head, at, mine]).astype(F32)
            ds_ref[head, at, :] = (found * x_ref[head % 2, at, :]).astype(BF)
        grad = ds_ref[head]
        key = dot(grad, jnp.concatenate([q_ref[at, cols] for at in here], axis=0))
        query = dot(k_ref[:, cols], grad, ((0,), (0,)))
        query_a = (query[:HD, :width] * 0.125).astype(BF)
        query_b = (query[:HD, width:] * 0.125).astype(BF)

        for g in range(NEAR // 2):
            total = None if first else near_in[head, 16 * g : 16 * g + 16]
            for l, block in enumerate(blocks):
                start = 128 * block - 96 + 16 * g
                inside = (start >= 0) & (start < seq)
                at = pl.ds(pl.multiple_of(jnp.clip(start, 0, seq - 16), 16), 16)
                found = ds_ref[head, at, 128 * l : 128 * l + 128].astype(F32)
                found = jnp.where(inside, found, 0.0)
                total = found if total is None else total + found
            near_ref[head, 16 * g : 16 * g + 16] = total
        for side in range(2):
            total = None if first else far_in[head, 8 * side : 8 * side + 8]
            for l, block in enumerate(blocks):
                marks = query[MARKS + 8 * side : MARKS + 8 * side + 8, 128 * l : 128 * l + 128]
                marks = jnp.where(spot == block, marks, 0.0)
                total = marks if total is None else total + marks
            far_ref[head, 8 * side : 8 * side + 8] = total

        if first:
            key_ref[:, cols] = key
            value_ref[:, cols] = value
            dqa_ref[rows, :] = query_a
            dqb_ref[rows, :] = query_b
        else:
            for k, found in enumerate((dqa_in[rows, :], query_a, dqb_in[rows, :], query_b)):
                all_ref[k, 0, rows, :] = found
            for part, acc in ((1, key_in[:, cols] + key), (2, value_in[:, cols] + value)):
                turned = acc.T[:HD].astype(BF)
                for q in range(4):
                    k = sum((jnp.where(ids[n] == q, n, 0) for n in range(1, 4)))
                    all_ref[k, part, rows, :] = turned[:, q * width : (q + 1) * width]


def back(ids, attended, queries, keys, values, grads, carried):
    seq, wide = queries.shape
    width = seq // 4
    first = carried is None
    columns = HEADS * HD
    queried = [shape((columns, width), BF)] * 2
    sums = [shape((seq, wide), F32)] * 2
    rel = [shape((HEADS, 8 * NEAR, 128), F32), shape((HEADS, 16, 128), F32)]
    outs = [shape((HEADS, seq, 2 * width), BF)]
    outs += queried + sums if first else [shape((4, 3, columns, width), BF)]
    outs += rel
    arrays = (*attended[0], *attended[1], *attended[2], queries, keys, values, grads, *(() if first else carried))
    return call(
        functools.partial(back_kernel, first=first),
        "back_first" if first else "back_last",
        ids,
        arrays,
        outs,
        mib=16,
        us=2 if first else 0.01,
        scratch=[pltpu.VMEM((2, seq, 2 * width), F32)],
    )


def places_kernel(ids, hor_ref, ver_ref, hor_at, ver_at):
    places, seq = hor_at.shape
    for keys_ref, goal in ((hor_ref, hor_at), (ver_ref, ver_at)):
        for b in range(places // 128):
            spot = lax.broadcasted_iota(I32, (128, seq), 0) + 128 * b
            goal[128 * b : 128 * b + 128, :] = jnp.where(spot == keys_ref[...], 1.0, 0.0).astype(BF)


def places_of(ids, hor, ver):
    return call(places_kernel, "places", ids, (hor, ver), [shape((PLACES, hor.shape[1]), BF)] * 2, mib=8, us=0.01)


def tables_kernel(ids, s_ref, e_ref, q_ref, *refs, base):
    diagonals = refs[:-3]
    out_ref, left_ref, right_ref = refs[-3:]
    width = s_ref.shape[2]
    groups = e_ref.shape[0] // 128
    query = jnp.concatenate([q_ref[:, quarter_of(ids[base + n], width // 2)] for n in (0, 2)], axis=1)
    column = lax.broadcasted_iota(I32, (SPAN, width), 0)
    for b in range(groups):
        window = jnp.clip(128 * b + TOP - LOW - query, 0, TOP)
        right_ref[:, b * width : (b + 1) * width] = jnp.where(column == window, 1.0, 0.0).astype(BF)
    for head in range(HEADS):
        moved = dot(e_ref[...], s_ref[head]).astype(BF)
        for b in range(groups):
            left_ref[head * 128 : head * 128 + 128, b * width : (b + 1) * width] = moved[128 * b : 128 * b + 128]
    found = dot(left_ref[...], right_ref[...], ((1,), (1,)))

    def to_buckets(sums, delta):
        spot = lax.broadcasted_iota(I32, (32, sums.shape[1]), 0)
        return jnp.sum(jnp.where(bucket(delta) == spot, sums, 0.0), axis=1, keepdims=True)

    lane = lax.broadcasted_iota(I32, (1, 512), 1)
    columns = []
    for h in range(HEADS):
        grid = jnp.concatenate([found[h * 128 : h * 128 + 128, :], jnp.zeros((128, 512 - SPAN), F32)], axis=1)
        grid = pltpu.roll(grid, 0, 1, stride=1, stride_axis=0)
        columns.append(to_buckets(jnp.sum(grid, axis=0, keepdims=True), lane + LOW - TOP))
    spread = lax.broadcasted_iota(I32, (32, 128), 1)
    rows_of = lambda columns: sum(jnp.where(spread == at, column, 0.0) for at, column in enumerate(columns)).T[:8]
    out_ref[0] = rows_of(columns)
    if diagonals:
        near_ref, far_ref = diagonals
        flip = 7 - lax.broadcasted_iota(I32, (8, 128), 0)
        spot = lax.broadcasted_iota(I32, (32, 1), 0)
        columns = []
        for h in range(HEADS):
            near = [jnp.take_along_axis(near_ref[h, 8 * t : 8 * t + 8], flip, axis=0) for t in reversed(range(NEAR))]
            grid = jnp.concatenate(near, axis=0)
            grid = jnp.concatenate([grid, jnp.zeros((8 * NEAR, 384), F32)], axis=1)
            grid = pltpu.roll(grid, 0, 1, stride=1, stride_axis=0)
            near_sums = to_buckets(jnp.sum(grid, axis=0, keepdims=True), 8 * NEAR - 1 - 8 * 12 - lane)
            left = jnp.sum(jnp.sum(far_ref[h, :8], axis=0, keepdims=True), axis=1, keepdims=True)
            right = jnp.sum(jnp.sum(far_ref[h, 8:], axis=0, keepdims=True), axis=1, keepdims=True)
            columns.append(near_sums + jnp.where(spot == 15, left, 0.0) + jnp.where(spot == 31, right, 0.0))
        out_ref[1] = rows_of(columns)


def table_grads(ids, first, scores, places, positions, sums=()):
    wide = PLACES // 128 * positions.shape[1] // 2
    return call(
        functools.partial(tables_kernel, base=0 if first else 1),
        "table_grads",
        ids,
        (scores, places, positions, *sums),
        shape((2 if sums else 1, 8, 32), F32),
        mib=TABLES_MIB,
        us=0.01,
        scratch=[pltpu.VMEM((HEADS * 128, wide), BF), pltpu.VMEM((SPAN, wide), BF)],
    )


def terms_of(grads, weights):
    total = None
    for part, w_ref in enumerate(weights):
        found = dot(grads[part], w_ref[...], ((0,), (0,)))
        total = found if total is None else total + found
    return total


def terms_send_kernel(ids, w0, w1, w2, grads_ref, *outs):
    for at, out_ref in enumerate(outs):
        out_ref[...] = terms_of(grads_ref[2 * at + 1], (w0, w1, w2)).astype(BF)


def terms_keep_kernel(ids, w0, w1, w2, grads_ref, got_own, got_other, own_ref, other_ref):
    other_ref[...] = (terms_of(grads_ref[2], (w0, w1, w2)) + got_other[...].astype(F32)).astype(BF)
    own_ref[...] = terms_of(grads_ref[0], (w0, w1, w2)) + got_own[...].astype(F32)


def terms_send(ids, weights, grads):
    outs = [shape((grads.shape[3], weights[0].shape[1]), BF)] * 2
    return call(terms_send_kernel, "terms_send", ids, (*weights, grads), outs, mib=16, us=0.01)


def terms_keep(ids, weights, grads, got):
    outs = [shape(got[0].shape, F32), shape(got[0].shape, BF)]
    return call(terms_keep_kernel, "terms_keep", ids, (*weights, grads, *got), outs, mib=16, us=0.01)


def last_kernel(
    ids, mine_ref, sent_ref, x_ref, page_ref, feat_ref, gain_ref, grad_ref, second_ref, mixed_ref, ffn_ref, got_ref,
    out_ref, part_ref,
):
    grad_normed = mine_ref[...] + sent_ref[...].astype(F32)
    here = quarter_of(ids[0], mine_ref.shape[0])
    unit, factor = unit_rows(hidden_rows(x_ref[here, :], page_ref[:, here], feat_ref[...]))
    scaled = grad_normed * gain_ref[...].astype(F32).reshape(1, -1)
    grad = factor * (scaled - unit * jnp.mean(scaled * unit, axis=-1, keepdims=True))
    rows, width = grad.shape
    out_ref[0, :rows] = (mixed_ref[...] + ffn_ref[...] + got_ref[...].astype(F32)).astype(BF)
    out_ref[1, :rows] = (grad_ref[...] + grad).astype(BF)
    part_ref[0:1] = jnp.sum(grad_normed * unit, axis=0, keepdims=True)
    part_ref[1:2] = second_ref[...]


def last(ids, mine, sent, inputs, onehot, feats, gain, grad_mixed, second, *ffn):
    rows, width = mine.shape
    arrays = (mine, sent, inputs, onehot, feats, gain, grad_mixed, second, *ffn)
    outs = [shape((2, rows, width), BF), shape((2, width), F32)]
    return call(last_kernel, "last", ids, arrays, outs, mib=16, us=0.01)


def pack_kernel(ids, gains_ref, got_ref, hor_a, ver_a, hor_b, ver_b, out_ref):
    gains = gains_ref[...] + got_ref[...]
    gains = [gains[slot : slot + 1] for slot in range(2)]
    parts = gains[0].shape[1] // 128
    for slot in range(2):
        gain = gains[slot]
        for part in range(parts):
            at = slot * parts + part
            out_ref[at : at + 1, :] = gain[:, part * 128 : part * 128 + 128]
    bins = hor_a.shape[2]
    at = 2 * parts
    out_ref[at:, :] = jnp.zeros((out_ref.shape[0] - at, 128), F32)
    for found in (hor_b[1], hor_a[0] + hor_b[0], ver_a[0] + ver_b[0]):
        out_ref[at : at + HEADS, :bins] = found[:HEADS]
        at += HEADS


def pack(ids, gains, got, *sums):
    size = gains.shape[1] // 128 * 2 + 3 * HEADS
    size = -(-size // 8) * 8
    return call(pack_kernel, "pack", ids, (gains, got, *sums), shape((size, 128), F32), mib=8, us=0.1)


def join_kernel(ids, b0, b1, b2, b3, out_ref, *, slot):
    for k, b_ref in enumerate((b0, b1, b2, b3)):

        @pl.when(pl.program_id(0) == k)
        def _(b_ref=b_ref):
            out_ref[...] = b_ref[slot, : out_ref.shape[0]].astype(out_ref.dtype)


def join_feat_kernel(ids, b0, b1, b2, b3, page_ref, out_ref, feat_ref, all_ref, *, slot):
    step = pl.program_id(0)
    rows = out_ref.shape[0]
    for k, b_ref in enumerate((b0, b1, b2, b3)):

        @pl.when(step == k)
        def _(b_ref=b_ref, k=k):
            out_ref[...] = b_ref[slot, :rows].astype(out_ref.dtype)
            all_ref[pl.ds(pl.multiple_of(ids[k] * rows, rows), rows), :] = b_ref[slot, :rows]

    @pl.when(step == 3)
    def _():
        feat_ref[...] = dot(page_ref[...].astype(F32).astype(BF), all_ref[...])


def join(ids, blocks, slot, dtype, onehot=None):
    _, rows, width = blocks[0].shape
    specs = [VMEM] * 4
    outs, out_specs = [shape((4 * rows, width), dtype)], [pl.BlockSpec((rows, width), lambda i, s: (s[i], 0))]
    extra, scratch = (), []
    if onehot is not None:
        pages = onehot.shape[0]
        specs = specs + [VMEM]
        outs.append(shape((pages, width), F32))
        out_specs.append(whole((pages, width)))
        extra, scratch = (onehot,), [pltpu.VMEM((4 * rows, width), BF)]
    found = pl.pallas_call(
        functools.partial(join_kernel if onehot is None else join_feat_kernel, slot=slot),
        grid_spec=pltpu.PrefetchScalarGridSpec(
            num_scalar_prefetch=1, grid=(4,), in_specs=specs, out_specs=out_specs, scratch_shapes=scratch
        ),
        out_shape=outs,
        compiler_params=params(16),
        cost_estimate=cost(0.01),
        name="join_output" if onehot is None else "join_grads",
    )(ids, *blocks, *extra)
    return found[0] if onehot is None else found


def split_rows(ids, total, cols, keep_ref, send_ref, parity):
    groups, size = keep_ref.shape[0], keep_ref.shape[1]
    for g in range(groups):
        mine = pl.multiple_of((2 * g + parity) * size, 8)
        theirs = pl.multiple_of((2 * g + 1 - parity) * size, 8)
        keep_ref[g] = total[pl.ds(mine, size), cols].astype(keep_ref.dtype)
        send_ref[g] = total[pl.ds(theirs, size), cols].astype(BF)


def feed_grad_kernel(ids, k0, n0, k1, n1, c0, c1, cot_ref, *outs, fast):
    units = k0.shape[2]
    rows = lambda refs: jnp.concatenate(refs, axis=0)
    total = outs[-1]
    normed = rows([n0[2], c0[2], n1[2], c1[2]])
    total[:, :units] = dot(normed, rows([k0[1], c0[1], k1[1], c1[1]]), ((0,), (0,)))
    cotangent = rows([cot_ref[quarter_of(ids[n], k0.shape[1]), :] for n in range(4)])
    total[:, units:] = dot(cotangent, rows([k0[0], c0[0], k1[0], c1[0]]), ((0,), (0,)))
    if fast:
        split_rows(ids, total, slice(None), outs[0], outs[1], ids[9])
    else:
        outs[0][...] = total[...]


def feed_grad(ids, own, other, got_own, got_other, cotangent, fast):
    _, rows, units = own[0].shape
    width = cotangent.shape[1]
    if fast:
        outs = [shape((4, width // 8, 2 * units), F32), shape((4, width // 8, 2 * units), BF)]
    else:
        outs = [shape((width, 2 * units), F32)]
    return call(
        functools.partial(feed_grad_kernel, fast=fast),
        "feed_grad",
        ids,
        (*own, *other, got_own, got_other, cotangent),
        outs,
        mib=24,
        us=7,
        scratch=[pltpu.VMEM((width, 2 * units), F32)],
    )


def head_grad_kernel(ids, normed_ref, grads_ref, l0, l2, l1, l3, a0, a1, a2, a3, *outs, fast):
    total, turned = outs[-2:]
    n = a0.shape[0]
    normed = jnp.concatenate([normed_ref[quarter_of(ids[k], a0.shape[1]), :] for k in range(4)], axis=0)
    for part in range(3):
        left = jnp.concatenate([grads_ref[k, part] for k in range(4)], axis=1)
        total[part * n : (part + 1) * n, :] = dot(left, normed)
    low = jnp.concatenate([r[...] for r in (l0, l1, l2, l3)], axis=0)
    total[3 * n :, :] = dot(jnp.concatenate([r[...] for r in (a0, a1, a2, a3)], axis=1), low)
    turned[...] = total[...].T
    if fast:
        split_rows(ids, turned, slice(None), outs[0], outs[1], ids[9])
    else:
        outs[0][...] = turned[...]


def head_grad(ids, normed, grads, low, low_got, attended, fast):
    seq, width = normed.shape
    n = grads.shape[2]
    if fast:
        outs = [shape((4, width // 8, 4 * n), F32), shape((4, width // 8, 4 * n), BF)]
    else:
        outs = [shape((width, 4 * n), F32)]
    return call(
        functools.partial(head_grad_kernel, fast=fast),
        "head_grad",
        ids,
        (normed, grads, *low, *low_got, *attended),
        outs,
        mib=18,
        us=0.01,
        scratch=[pltpu.VMEM((4 * n, width), F32), pltpu.VMEM((width, 4 * n), F32)],
    )


def pair_kernel(ids, *refs):
    pairs, outs = refs[:-4], refs[-4:]
    for k, o_ref in enumerate(outs):
        at = ids[4 + k]
        start = 0
        for keep_ref, got_ref in zip(pairs[::2], pairs[1::2]):
            n = keep_ref.shape[2]
            o_ref[:, start : start + n] = (keep_ref[at] + got_ref[at].astype(F32)).astype(o_ref.dtype)
            start += n


def pair_sum(ids, *arrays):
    size = arrays[0].shape[1]
    n = sum(a.shape[2] for a in arrays[::2])
    outs = [shape((size, n), F32)] + [shape((size, n), BF)] * 3
    return call(pair_kernel, "pair_sum", ids, arrays, outs, mib=16, us=0.01)


def feed_final_kernel(a0, a1, a2, a3, up_ref, down_ref):
    total = a0[...] + a1[...].astype(F32) + a2[...].astype(F32) + a3[...].astype(F32)
    units = up_ref.shape[1]
    up_ref[...] = total[:, :units]
    down_ref[...] = total[:, units:]


def head_final_kernel(a0, a1, a2, a3, one_ref, two_ref, q_ref, k_ref, v_ref, o_ref, *smalls):
    total = a0[...] + a1[...].astype(F32) + a2[...].astype(F32) + a3[...].astype(F32)
    n = q_ref.shape[1]
    for at, goal in enumerate((q_ref, k_ref, v_ref)):
        goal[...] = total[:, at * n : (at + 1) * n]
    o_ref[...] = total[:, 3 * n :].T
    *tables, gains_ref = smalls
    total = one_ref[...] + two_ref[...]
    parts = gains_ref.shape[1] // 128
    for slot in range(2):
        for part in range(parts):
            at = slot * parts + part
            gains_ref[slot : slot + 1, part * 128 : part * 128 + 128] = total[at : at + 1]
    at, bins = 2 * parts, tables[0].shape[1]
    for goal in tables:
        goal[...] = total[at : at + HEADS, :bins]
        at += HEADS


def final(kernel, arrays, done, outs):
    arrays = [after(arrays[0], done)] + arrays[1:]
    return pl.pallas_call(
        kernel,
        grid=(1,),
        in_specs=[VMEM] * len(arrays),
        out_specs=jax.tree.map(lambda o: whole(o.shape), outs),
        out_shape=outs,
        compiler_params=params(16),
        cost_estimate=cost(5 if kernel is feed_final_kernel else 0.01),
        name=kernel.__name__[:-7],
    )(*arrays)


def swap(array, axis, size, bits):
    return lax.ppermute(array, axis, [(i, i ^ bits) for i in range(size)])


def after(array, *others):
    return lax.optimization_barrier((array, others))[0]


def local(
    inputs, page_feat, page_onehot, lengths, hor_pos, ver_pos, norm1_gain, w_query, w_key, w_value,
    rel_table, hor_table, ver_table, w_output, norm2_gain, w_up, w_down, cotangent, *, dp,
):
    seq, width = inputs.shape
    fast = dp == 8
    over = functools.partial(swap, axis="mp", size=4)
    m = lax.axis_index("mp").astype(I32)
    d = lax.axis_index("dp").astype(I32)
    k4 = jnp.arange(4, dtype=I32)
    spot = lambda who: (who & 1) * 2 + (who >> 1)
    ids = jnp.concatenate([
        spot(m ^ k4),
        (d >> 1) ^ k4,
        lengths[:1],
        (d & 1)[None],
    ])
    gain_one, gain_two = norm1_gain, norm2_gain
    feats = page_feat[0]
    hor, ver = hor_pos[None], ver_pos[None]
    tables = (rel_table, hor_table, ver_table)
    pages = page_onehot.T
    weights = [w_query.T, w_key.T, w_value.T]

    wo_y, wo_core = over(w_output, bits=2), over(w_output, bits=1)
    normed1, queries, keys, values = project(ids, inputs, pages, feats, gain_one, *weights)
    w_outputs = [w_output, wo_core, wo_y, over(after(wo_y, normed1), bits=1)]
    ups = [w_up, over(after(w_up, normed1), bits=1)]
    downs = [w_down, over(after(w_down, normed1), bits=1)]

    (e_a, att0, att1, inverse_a, out_a), lookups = attend(ids, queries, keys, values, hor, ver, tables, None)
    from_y, from_yc, own1 = over(att0, bits=2), over(att1, bits=3), over(att1, bits=1)
    ver_late = after(ver, att0, w_outputs[3], ups[1], downs[1])
    (e_b, att2, att3, inverse_b, out_b), _ = attend(ids, queries, keys, values, hor, ver_late, tables, lookups)
    attended = [att0, att1, att2, att3]
    for_other = [att2, over(att3, bits=1), from_y, from_yc]
    for_own = [att0, own1, over(att2, bits=2), over(att3, bits=3)]

    around = functools.partial(swap, axis="dp", size=dp)
    to_z = lambda parts: [parts[0]] + [around(part, bits=2 * k) for k, part in zip((1, 2, 3), parts[1:])]
    size = width // dp
    n = w_query.shape[1]
    units = w_up.shape[1]
    fixed = (inputs, pages, feats, gain_two, cotangent)
    x_keep, x_send, x_mixed, x_grad, x_ffn = feed(ids, False, *fixed, for_other, w_outputs, ups, downs)
    got_own, x_got = over(x_grad, bits=2), over(x_send, bits=1)
    for_own[0] = after(att0, x_ffn)
    m_keep, m_send, mixed, m_grad, m_ffn = feed(ids, True, *fixed, for_own, w_outputs, ups, downs)
    got_other, m_got = over(m_grad, bits=2), over(after(m_send, x_got), bits=1)
    own_grad = add(ids, m_grad, got_own)

    feed_grads = feed_grad(ids, (after(m_keep, own_grad), m_send), (x_keep, x_send), m_got, x_got, cotangent, fast)
    feed_got = around(feed_grads[1], bits=1) if fast else ids
    hor_at, ver_at = places_of(ids, after(hor, feed_grads[0]), ver)
    grad_mixed, ga, core_send, *low, gain_two_part = mid(
        ids, (after(own_grad, hor_at), mixed), (x_grad, got_other, x_mixed), gain_two, cotangent, w_outputs[:2]
    )
    core_got = over(core_send, bits=1)
    sent_ffn = over(after(x_ffn, got_other, hor_at), bits=2)

    halves = ((e_a, e_b), (inverse_a, inverse_b), (out_a, out_b))
    scores_a, dq0, dq2, key_sum, value_sum, near, far = back(ids, halves, queries, keys, values, ga, None)
    scores_b, grads, near, far = back(
        ids, halves, queries, keys, values, after(core_got, dq0), (key_sum, value_sum, near, far, dq0, dq2)
    )
    low_got = [over(part, bits=1) for part in low]
    to_core = terms_send(ids, weights, after(grads, sent_ffn))
    got_terms = [over(part, bits=1) for part in to_core]
    head_grads = head_grad(ids, normed1, after(grads, to_core[0]), low, low_got, attended, fast)
    own_terms, other_terms = terms_keep(ids, weights, after(grads, head_grads[0]), got_terms)
    sent_terms = over(other_terms, bits=2)

    hor_a = table_grads(ids, True, scores_a, hor_at, after(hor, own_terms))
    done = hor_a
    if fast:
        feed_parts = to_z(pair_sum(ids, after(feed_grads[0], done), feed_got))
        done = feed_parts[0]
    head_got = around(after(head_grads[1], done), bits=1) if fast else ids
    rows, gains = last(
        ids, after(own_terms, done), sent_terms, inputs, pages, feats, gain_one, grad_mixed, gain_two_part,
        mixed, m_ffn, sent_ffn,
    )
    rows_y, rows_core = over(rows, bits=2), over(rows, bits=1)
    ver_a = table_grads(ids, True, scores_a, ver_at, after(ver, rows))
    gains = after(gains, ver_a) + over(gains, bits=1)
    got_gains = over(gains, bits=2)
    hor_b = table_grads(ids, False, scores_b, hor_at, after(hor, gains), (near, far))
    ver_b = table_grads(ids, False, scores_b, ver_at, after(ver, hor_b, head_got))

    small = pack(ids, gains, got_gains, hor_a, ver_a, hor_b, ver_b)
    if fast:
        got = around(small, bits=1)
        grad_up, grad_down = final(feed_final_kernel, feed_parts, small, [shape((size, units), F32)] * 2)
        head_parts = to_z(pair_sum(ids, after(head_grads[0], grad_up), head_got))
        small = after(small, head_parts[0]) + got
        got = around(small, bits=2)
        quarters = [rows, rows_core, rows_y, over(after(rows_y, grad_up), bits=1)]
        outputs = join(ids, [after(rows, small)] + quarters[1:], 0, BF)
        grad_inputs, grad_feats = join(ids, [after(rows, outputs)] + quarters[1:], 1, F32, pages)
        small = after(small, grad_feats) + got
        bins = rel_table.shape[1]
        outs = [shape((size, n), F32)] * 3 + [shape((n, size), F32)] + [shape((HEADS, bins), F32)] * 3
        *found, gain_sums = final(
            head_final_kernel, head_parts + [small, around(small, bits=4)], grad_feats, outs + [shape((2, width), F32)]
        )
        grad_query, grad_key, grad_value, grad_output, grad_rel, grad_hor, grad_ver = found
    else:
        quarters = [rows, rows_core, rows_y, over(rows_y, bits=1)]
        outputs = join(ids, quarters, 0, BF)
        grad_inputs, grad_feats = join(ids, quarters, 1, F32, pages)
        small = lax.psum(small, "dp")
        scatter = lambda a: lax.psum_scatter(a[0], "dp", scatter_dimension=0, tiled=True)
        grad_feed, heads = scatter(feed_grads), scatter(head_grads)
        grad_up, grad_down = grad_feed[:, :units], grad_feed[:, units:]
        grad_query, grad_key, grad_value = heads[:, :n], heads[:, n : 2 * n], heads[:, 2 * n : 3 * n]
        grad_output = heads[:, 3 * n :].T
        gain_sums = small[: width // 128 * 2].reshape(2, width)
        table_sums = small[width // 128 * 2 :, : rel_table.shape[1]]
        grad_rel, grad_hor, grad_ver = (table_sums[at : at + HEADS] for at in range(0, 3 * HEADS, HEADS))
    gain_sums = lax.dynamic_slice(gain_sums, (0, d * size), (2, size))
    return (
        outputs, grad_inputs, grad_feats[None], gain_sums[0], grad_query, grad_key, grad_value,
        grad_rel, grad_hor, grad_ver, grad_output, gain_sums[1], grad_up, grad_down.T,
    )


def solution(mesh):
    return jax.shard_map(
        functools.partial(local, dp=mesh.shape["dp"]),
        mesh=mesh,
        in_specs=(
            P("dp", None),
            P("dp", None, None),
            P("dp", None),
            P("dp"),
            P("dp"),
            P("dp"),
            P(),
            P(None, "mp"),
            P(None, "mp"),
            P(None, "mp"),
            P("mp", None),
            P("mp", None),
            P("mp", None),
            P("mp", None),
            P(),
            P(None, "mp"),
            P("mp", None),
            P("dp", None),
        ),
        out_specs=(
            P("dp", None),
            P("dp", None),
            P("dp", None, None),
            P("dp"),
            P("dp", "mp"),
            P("dp", "mp"),
            P("dp", "mp"),
            P("mp", None),
            P("mp", None),
            P("mp", None),
            P("mp", "dp"),
            P("dp"),
            P("dp", "mp"),
            P("mp", "dp"),
        ),
        check_vma=False,
    )
```

```python
import functools

import jax
import jax.numpy as jnp
import numpy as np
from jax import lax
from jax.experimental import pallas as pl
from jax.experimental.pallas import tpu as pltpu
from jax.sharding import PartitionSpec as P

EPS = 1e-06
THRESHOLDS = (12, 16, 23, 32, 46, 64, 91)
FAR = 91
HEADS = 3
HD = 64
PAD = 128
MARKS = 72
NEAR = 40
TILES = NEAR + 2
SPAN = 384
LOW = 92
TOP = 311
BF = jnp.bfloat16
F32 = jnp.float32
I32 = jnp.int32
FEED_CHUNK = 256
PLACES = 1024
TABLES_MIB = 18
GELU_C = float(np.sqrt(2.0 / np.pi))


def dot(left, right, dims=((1,), (0,))):
    return lax.dot_general(left, right, (dims, ((), ())), preferred_element_type=F32)


def bucket(delta):
    magnitude = jnp.abs(delta)
    coarse = 8 + sum((magnitude >= limit).astype(I32) for limit in THRESHOLDS)
    return jnp.where(magnitude < 8, magnitude, coarse) + 16 * (delta > 0).astype(I32)


def params(mib):
    return pltpu.CompilerParams(vmem_limit_bytes=mib * 2**20)


def cost(microseconds):
    return pl.CostEstimate(flops=int(1.15e9 * microseconds), bytes_accessed=1, transcendentals=0)


def shape(dims, dtype):
    return jax.ShapeDtypeStruct(dims, dtype)


def whole(dims):
    return pl.BlockSpec(dims, lambda *a: (0,) * len(dims))


VMEM = pl.BlockSpec(memory_space=pltpu.VMEM)


def call(kernel, name, ids, arrays, outs, *, mib, us, scratch=()):
    return pl.pallas_call(
        kernel,
        grid_spec=pltpu.PrefetchScalarGridSpec(
            num_scalar_prefetch=1,
            grid=(1,),
            in_specs=[VMEM] * len(arrays),
            out_specs=jax.tree.map(lambda _: VMEM, outs),
            scratch_shapes=list(scratch),
        ),
        out_shape=outs,
        compiler_params=params(mib),
        cost_estimate=cost(us),
        name=name,
    )(ids, *arrays)


def quarter_of(place, size):
    return pl.ds(pl.multiple_of(place * size, 128), size)


def hidden_rows(inputs, pages, feats):
    return inputs.astype(F32) + dot(pages.astype(F32).astype(BF), feats, ((0,), (0,)))


def unit_rows(field):
    factor = lax.rsqrt(jnp.mean(field * field, axis=-1, keepdims=True) + EPS)
    return field * factor, factor


def project_kernel(ids, x_ref, page_ref, feat_ref, gain_ref, wq_ref, wk_ref, wv_ref, n_ref, q_ref, k_ref, v_ref):
    rows = 256

    def block_of(step, carry):
        here = quarter_of(step, rows)
        unit, _ = unit_rows(hidden_rows(x_ref[here, :], page_ref[:, here], feat_ref[...]))
        normed = (unit * gain_ref[...].astype(F32).reshape(1, -1)).astype(BF)
        n_ref[here, :] = normed
        lane = lax.broadcasted_iota(I32, (rows, PAD), 1)
        row = lax.broadcasted_iota(I32, (rows, PAD), 0) + step * rows
        masked = jnp.where((lane == HD) & (row >= ids[8]), -1e30, 0.0)
        block = lane - MARKS
        far_left = (block >= 0) & (block < 8) & (row < 128 * block - 96)
        far_right = (block >= 8) & (block < 16) & (row >= 128 * (block - 8) + 224)
        masked = jnp.where(far_left | far_right, 1.0, masked)
        query_extra = jnp.where(lane == HD, 1.0, 0.0)
        value_extra = jnp.where((lane == HD) | (lane == HD + 1), 1.0, 0.0)
        for out_ref, w_ref, extra, scale in (
            (q_ref, wq_ref, query_extra, 0.125),
            (k_ref, wk_ref, masked, None),
            (v_ref, wv_ref, value_extra, None),
        ):
            full = dot(normed, w_ref[...], ((1,), (1,)))
            if scale is not None:
                full = full * scale
            pair = full[:, :PAD]
            last = jnp.concatenate([full[:, PAD:], jnp.zeros((rows, PAD - HD), F32)], axis=1)
            heads = (pair, pltpu.roll(pair, HD, 1), last)
            for head in range(HEADS):
                out_ref[here, head * PAD : (head + 1) * PAD] = jnp.where(lane < HD, heads[head], extra).astype(BF)
        return carry

    lax.fori_loop(0, x_ref.shape[0] // rows, block_of, 0)


def project(ids, *arrays):
    seq, width = arrays[0].shape
    outs = [shape((seq, width), BF)] + [shape((seq, HEADS * PAD), BF)] * 3
    return call(project_kernel, "project", ids, arrays, outs, mib=16, us=7)


def place(delta):
    magnitude = jnp.abs(delta)
    coarse = jnp.minimum(25 - lax.clz(delta * delta), 7)
    exact = magnitude < 8
    return jnp.where(exact, magnitude, coarse), exact, delta > 0


def look(table_ref, row, where):
    index, exact, after = where
    found = [jnp.take_along_axis(table_ref[row, part], index, axis=0) for part in range(4)]
    return jnp.where(after, jnp.where(exact, found[2], found[3]), jnp.where(exact, found[0], found[1]))


def tile_delta(tile):
    lane = lax.broadcasted_iota(I32, (8, 128), 1)
    sub = lax.broadcasted_iota(I32, (8, 128), 0)
    delta = 8 * (tile - 13) + sub - lane
    if tile == 0:
        delta = jnp.full_like(delta, -1000)
    if tile == TILES - 1:
        delta = jnp.full_like(delta, 1000)
    return delta


def attend_kernel(*refs, first, chunk):
    ids, q_ref, k_ref, v_ref, hor_ref, ver_ref = refs[:6]
    if first:
        hor_all, ver_all, rel_table, hor_table, ver_table, e_ref, att0, att1, inv_ref, out_ref = refs[6:16]
        rel_ref, t8_ref, hor_col, ver_col, s_ref = refs[16:]
    else:
        rel_ref, t8_ref, hor_col, ver_col, e_ref, att0, att1, inv_ref, out_ref, s_ref = refs[6:]
    seq = k_ref.shape[0]
    width = seq // 4
    lanes = width // 128

    if first:
        for all_ref, col_ref in ((hor_all, hor_col), (ver_all, ver_col)):
            for b in range(seq // 128):
                cols = slice(128 * b, 128 * b + 128)
                spread = jnp.broadcast_to(all_ref[:, cols].astype(F32), (128, 128))
                col_ref[cols, :] = spread.T.astype(I32)
        lane = lax.broadcasted_iota(I32, (8, 32), 1)
        sub = lax.broadcasted_iota(I32, (8, 32), 0)
        for axis, table_ref in enumerate((rel_table, hor_table, ver_table)):
            table = table_ref[...].astype(F32)
            for head in range(HEADS):
                row = jnp.broadcast_to(table[head : head + 1], (8, 32))
                for part in range(4):
                    entries = jnp.sum(jnp.where(lane == sub + 8 * part, row, 0.0), axis=1, keepdims=True)
                    t8_ref[axis * HEADS + head, part] = jnp.broadcast_to(entries, (8, 128))
        for tile in range(TILES):
            where = place(tile_delta(tile))
            for head in range(HEADS):
                rel_ref[head, tile] = look(t8_ref, head, where)

    def products(here):
        queries = q_ref[here, :]
        for head in range(HEADS):
            cols = slice(head * PAD, (head + 1) * PAD)
            s_ref[head] = dot(k_ref[:, cols], queries[:, cols], ((1,), (1,)))

    def biases(place_of, here):
        hor_row, ver_row = hor_ref[:, here], ver_ref[:, here]
        hor = [jnp.broadcast_to(hor_row[:, 128 * l : 128 * l + 128], (8, 128)) for l in range(lanes)]
        ver = [jnp.broadcast_to(ver_row[:, 128 * l : 128 * l + 128], (8, 128)) for l in range(lanes)]
        block = place_of * lanes

        def add_bias(c, tops):
            tops = list(tops)
            base = pl.multiple_of(c * chunk, chunk)
            for g in range(chunk // 8):
                rows = pl.ds(pl.multiple_of(base + 8 * g, 8), 8)
                hor_keys, ver_keys = hor_col[rows, :], ver_col[rows, :]
                for l in range(lanes):
                    cols = pl.ds(128 * l, 128)
                    hor_at, ver_at = place(hor_keys - hor[l]), place(ver_keys - ver[l])
                    tile = jnp.clip(c * (chunk // 8) + g - 16 * (block + l) + 13, 0, TILES - 1)
                    for head in range(HEADS):
                        s = s_ref[head, rows, cols] + rel_ref[head, tile]
                        s = s + (look(t8_ref, HEADS + head, hor_at) + look(t8_ref, 2 * HEADS + head, ver_at))
                        s_ref[head, rows, cols] = s
                        tops[head * lanes + l] = jnp.maximum(tops[head * lanes + l], s)
            return tuple(tops)

        tops = lax.fori_loop(
            0, seq // chunk, add_bias, tuple(jnp.full((8, 128), -1e30, F32) for _ in range(HEADS * lanes))
        )
        return [jnp.broadcast_to(jnp.max(top, axis=0, keepdims=True), (16, 128)) for top in tops]

    def attended(part, peaks):
        mine = quarter_of(part, width)
        for head in range(HEADS):
            for g in range(seq // 16):
                rows = slice(16 * g, 16 * g + 16)
                for l in range(lanes):
                    cols = slice(128 * l, 128 * l + 128)
                    into = pl.ds(pl.multiple_of(part * width + 128 * l, 128), 128)
                    e_ref[head, rows, into] = jnp.exp(s_ref[head, rows, cols] - peaks[head * lanes + l]).astype(BF)
            total = dot(v_ref[:, head * PAD : (head + 1) * PAD], e_ref[head, :, mine], ((0,), (0,)))
            inverse = 1.0 / total[HD : HD + 1, :]
            inv_ref[head : head + 1, mine] = inverse
            out_ref[head * HD : (head + 1) * HD, mine] = total[:HD] * inverse
        for at, att_ref in enumerate((att0, att1)):

            @pl.when(part == at)
            def _(att_ref=att_ref):
                att_ref[...] = out_ref[:, mine].astype(BF)

    def quarter(part, carry):
        place_of = ids[(0 if first else 2) + part]
        here = quarter_of(place_of, width)
        products(here)
        attended(part, biases(place_of, here))
        return carry

    lax.fori_loop(0, 2, quarter, 0)


def attend(ids, queries, keys, values, hor, ver, tables, lookups):
    seq = queries.shape[0]
    width = seq // 4
    first = lookups is None
    columns = HEADS * HD
    made = [
        shape((HEADS, TILES, 8, 128), F32), shape((3 * HEADS, 4, 8, 128), F32), shape((seq, 128), I32), shape((seq, 128), I32)
    ]
    extra = (hor, ver, *tables) if first else tuple(lookups)
    outs = [
        shape((HEADS, seq, 2 * width), BF), shape((columns, width), BF), shape((columns, width), BF),
        shape((HEADS, 2 * width), F32), shape((columns, 2 * width), F32),
    ]
    found = call(
        functools.partial(attend_kernel, first=first, chunk=128),
        "attend_first" if first else "attend_last",
        ids,
        (queries, keys, values, hor, ver, *extra),
        outs + made if first else outs,
        mib=14,
        us=14,
        scratch=[pltpu.VMEM((HEADS, seq, width), F32)],
    )
    return found[:5], found[5:]


def feed_kernel(
    ids, x_ref, page_ref, feat_ref, gain_ref, cot_ref, a0, a1, a2, a3, o0, o1, o2, o3, u0, u1, d0, d1,
    keep_ref, send_ref, mixed_ref, grad_ref, ffn_ref, *, slot,
):
    here = quarter_of(ids[slot], mixed_ref.shape[0])
    cotangent = cot_ref[here, :]
    mixed = hidden_rows(x_ref[here, :], page_ref[:, here], feat_ref[...])
    for a_ref, o_ref in ((a0, o0), (a1, o1), (a2, o2), (a3, o3)):
        mixed = mixed + dot(a_ref[...], o_ref[...], ((0,), (0,)))
    mixed_ref[...] = mixed
    unit, _ = unit_rows(mixed)
    normed = (unit * gain_ref[...].astype(F32).reshape(1, -1)).astype(BF)
    send_ref[2] = normed
    units = u0.shape[1]
    for u_ref, d_ref, goal in ((u0, d0, keep_ref), (u1, d1, send_ref)):
        for at in range(0, units, FEED_CHUNK):
            cols = slice(at, at + FEED_CHUNK)
            upward = dot(normed, u_ref[:, cols])
            square = upward * upward
            tanh = jnp.tanh(GELU_C * upward * (1.0 + 0.044715 * square))
            lifted = 0.5 * (1.0 + tanh)
            activated = (upward * lifted).astype(BF)
            slope = lifted + 0.5 * upward * (1.0 - tanh * tanh) * (GELU_C * (1.0 + 3 * 0.044715 * square))
            grad_up = (dot(cotangent, d_ref[cols, :], ((1,), (1,))) * slope).astype(BF)
            goal[0, :, cols] = activated
            goal[1, :, cols] = grad_up
    ffn = dot(keep_ref[0], d0[...]) + dot(send_ref[0], d1[...])
    ffn_ref[...] = ffn.astype(ffn_ref.dtype)
    grad = dot(keep_ref[1], u0[...], ((1,), (1,))) + dot(send_ref[1], u1[...], ((1,), (1,)))
    grad_ref[...] = grad.astype(grad_ref.dtype)


def feed(ids, own, inputs, onehot, feats, gain, cotangent, attended, w_outputs, ups, downs):
    seq, width = inputs.shape
    rows = seq // 4
    units = ups[0].shape[1]
    kept = F32 if own else BF
    outs = [
        shape((2, rows, units), BF), shape((3, rows, width), BF), shape((rows, width), F32),
        shape((rows, width), BF), shape((rows, width), kept),
    ]
    return call(
        functools.partial(feed_kernel, slot=0 if own else 2),
        "feed_own" if own else "feed_other",
        ids,
        (inputs, onehot, feats, gain, cotangent, *attended, *w_outputs, *ups, *downs),
        outs,
        mib=16,
        us=20 if own else 10,
    )


def add_kernel(ids, one_ref, two_ref, out_ref):
    out_ref[...] = one_ref[...].astype(F32) + two_ref[...].astype(F32)


def add(ids, one, two):
    return call(add_kernel, "add", ids, (one, two), shape(one.shape, F32), mib=8, us=20)


def mid_kernel(
    ids, own_grad, own_mixed, other_grad, other_got, other_mixed, cot_ref, gain_ref, o0, o1,
    grad_ref, own_ref, core_ref, low_own, low_other, part_ref,
):
    rows = own_grad.shape[0]
    other = other_grad[...].astype(F32) + other_got[...].astype(F32)
    for at, (grad_normed, mixed_ref) in enumerate(((own_grad[...], own_mixed), (other, other_mixed))):
        unit, factor = unit_rows(mixed_ref[...])
        scaled = grad_normed * gain_ref[...].astype(F32).reshape(1, -1)
        grad = factor * (scaled - unit * jnp.mean(scaled * unit, axis=-1, keepdims=True))
        grad = cot_ref[quarter_of(ids[2 * at], rows), :].astype(F32) + grad
        low = grad.astype(BF)
        (low_own, low_other)[at][...] = low
        if at == 0:
            grad_ref[...] = grad
            part_ref[...] = jnp.sum(grad_normed * unit, axis=0, keepdims=True)
        for o_ref, goal in ((o0, own_ref), (o1, core_ref)):
            goal[:, at * rows : (at + 1) * rows] = dot(o_ref[...], low, ((1,), (1,))).astype(BF)


def mid(ids, own, other, gain, cotangent, w_outputs):
    rows, width = own[0].shape
    columns = HEADS * HD
    outs = [
        shape((rows, width), F32), shape((columns, 2 * rows), BF), shape((columns, 2 * rows), BF), shape((rows, width), BF),
        shape((rows, width), BF), shape((1, width), F32),
    ]
    arrays = (*own, *other, cotangent, gain, *w_outputs)
    return call(mid_kernel, "mid", ids, arrays, outs, mib=16, us=0.01)


def back_kernel(*refs, first):
    ids, ea_ref, eb_ref, inv_a, inv_b, out_a, out_b, q_ref, k_ref, v_ref, grad_ref = refs[:11]
    refs = refs[11:]
    if first:
        ds_ref, dqa_ref, dqb_ref, key_ref, value_ref, near_ref, far_ref, x_ref = refs
    else:
        key_in, value_in, near_in, far_in, dqa_in, dqb_in = refs[:6]
        ds_ref, all_ref, near_ref, far_ref, x_ref = refs[6:]
    seq = k_ref.shape[0]
    width = seq // 4
    both = 2 * width
    lanes = width // 128
    base = 0 if first else 1
    sub = lax.broadcasted_iota(I32, (HD, both), 0)
    blocks = [ids[base + 2 * (l // lanes)] * lanes + l % lanes for l in range(2 * lanes)]
    mine = slice(base * width, (base + 1) * width)
    here = [quarter_of(ids[base + 2 * n], width) for n in range(2)]
    beside = lambda one, two: jnp.concatenate([one, two], axis=1)
    spot = lax.broadcasted_iota(I32, (8, 128), 0)

    def one_head(head, carry):
        cols = quarter_of(head, PAD)
        rows = pl.ds(pl.multiple_of(head * HD, HD), HD)
        grad = grad_ref[rows, :].astype(F32)
        grad = (grad * beside(inv_a[pl.ds(head, 1), mine], inv_b[pl.ds(head, 1), mine])).astype(BF).astype(F32)
        inner = jnp.sum(grad * beside(out_a[rows, mine], out_b[rows, mine]), axis=0, keepdims=True)
        high = inner.astype(BF).astype(F32)
        extra = jnp.where(sub == 0, -high, jnp.where(sub == 1, high - inner, 0.0))
        right = jnp.concatenate([grad, extra], axis=0).astype(BF)
        x_ref[...] = dot(v_ref[:, cols], right)
        value = dot(beside(ea_ref[head, :, mine], eb_ref[head, :, mine]), right, ((1,), (1,)))
        for c in range(seq // 16):
            at = slice(16 * c, 16 * c + 16)
            found = beside(ea_ref[head, at, mine], eb_ref[head, at, mine]).astype(F32)
            ds_ref[head, at, :] = (found * x_ref[at, :]).astype(BF)
        grad = ds_ref[head]
        key = dot(grad, jnp.concatenate([q_ref[at, cols] for at in here], axis=0))
        query = dot(k_ref[:, cols], grad, ((0,), (0,)))
        query_a = (query[:HD, :width] * 0.125).astype(BF)
        query_b = (query[:HD, width:] * 0.125).astype(BF)

        for g in range(NEAR // 2):
            total = None if first else near_in[head, 16 * g : 16 * g + 16]
            for l, block in enumerate(blocks):
                start = 128 * block - 96 + 16 * g
                inside = (start >= 0) & (start < seq)
                at = pl.ds(pl.multiple_of(jnp.clip(start, 0, seq - 16), 16), 16)
                found = ds_ref[head, at, 128 * l : 128 * l + 128].astype(F32)
                found = jnp.where(inside, found, 0.0)
                total = found if total is None else total + found
            near_ref[head, 16 * g : 16 * g + 16] = total
        for side in range(2):
            total = None if first else far_in[head, 8 * side : 8 * side + 8]
            for l, block in enumerate(blocks):
                marks = query[MARKS + 8 * side : MARKS + 8 * side + 8, 128 * l : 128 * l + 128]
                marks = jnp.where(spot == block, marks, 0.0)
                total = marks if total is None else total + marks
            far_ref[head, 8 * side : 8 * side + 8] = total

        if first:
            key_ref[:, cols] = key
            value_ref[:, cols] = value
            dqa_ref[rows, :] = query_a
            dqb_ref[rows, :] = query_b
        else:
            for k, found in enumerate((dqa_in[rows, :], query_a, dqb_in[rows, :], query_b)):
                all_ref[k, 0, rows, :] = found
            for part, acc in ((1, key_in[:, cols] + key), (2, value_in[:, cols] + value)):
                turned = acc.T[:HD].astype(BF)
                for q in range(4):
                    k = sum((jnp.where(ids[n] == q, n, 0) for n in range(1, 4)))
                    all_ref[k, part, rows, :] = turned[:, q * width : (q + 1) * width]
        return carry

    lax.fori_loop(0, HEADS, one_head, 0)


def back(ids, attended, queries, keys, values, grads, carried):
    seq, wide = queries.shape
    width = seq // 4
    first = carried is None
    columns = HEADS * HD
    queried = [shape((columns, width), BF)] * 2
    sums = [shape((seq, wide), F32)] * 2
    rel = [shape((HEADS, 8 * NEAR, 128), F32), shape((HEADS, 16, 128), F32)]
    outs = [shape((HEADS, seq, 2 * width), BF)]
    outs += queried + sums if first else [shape((4, 3, columns, width), BF)]
    outs += rel
    arrays = (*attended[0], *attended[1], *attended[2], queries, keys, values, grads, *(() if first else carried))
    return call(
        functools.partial(back_kernel, first=first),
        "back_first" if first else "back_last",
        ids,
        arrays,
        outs,
        mib=16,
        us=2 if first else 0.01,
        scratch=[pltpu.VMEM((seq, 2 * width), F32)],
    )


def places_kernel(ids, hor_ref, ver_ref, at_ref, both_ref):
    _, places, seq = at_ref.shape
    both_ref[0:1, :] = hor_ref[...]
    both_ref[1:2, :] = ver_ref[...]
    for axis, keys_ref in enumerate((hor_ref, ver_ref)):
        for b in range(places // 128):
            spot = lax.broadcasted_iota(I32, (128, seq), 0) + 128 * b
            at_ref[axis, 128 * b : 128 * b + 128, :] = jnp.where(spot == keys_ref[...], 1.0, 0.0).astype(BF)


def places_of(ids, hor, ver):
    seq = hor.shape[1]
    outs = [shape((2, PLACES, seq), BF), shape((2, seq), I32)]
    return call(places_kernel, "places", ids, (hor, ver), outs, mib=8, us=0.01)


def tables_kernel(ids, s_ref, e_ref, q_ref, *refs, base, axes):
    diagonals = refs[:-4]
    out_ref, left_ref, right_ref, found_ref = refs[-4:]
    width = s_ref.shape[2]
    groups = e_ref.shape[1] // 128

    def to_buckets(sums, delta):
        spot = lax.broadcasted_iota(I32, (32, sums.shape[1]), 0)
        return jnp.sum(jnp.where(bucket(delta) == spot, sums, 0.0), axis=1, keepdims=True)

    lane = lax.broadcasted_iota(I32, (1, 512), 1)
    spread = lax.broadcasted_iota(I32, (32, 128), 1)

    def heads_rows(column_of):
        add = lambda head, total: total + jnp.where(spread == head, column_of(head), 0.0)
        return lax.fori_loop(0, HEADS, add, jnp.zeros((32, 128), F32)).T[:8]

    def coordinate(axis, out_at):
        query = jnp.concatenate([q_ref[pl.ds(axis, 1), quarter_of(ids[base + n], width // 2)] for n in (0, 2)], axis=1)
        column = lax.broadcasted_iota(I32, (SPAN, width), 0)
        for b in range(groups):
            window = jnp.clip(128 * b + TOP - LOW - query, 0, TOP)
            right_ref[:, b * width : (b + 1) * width] = jnp.where(column == window, 1.0, 0.0).astype(BF)
        for head in range(HEADS):
            moved = dot(e_ref[axis], s_ref[head]).astype(BF)
            for b in range(groups):
                left_ref[head * 128 : head * 128 + 128, b * width : (b + 1) * width] = moved[128 * b : 128 * b + 128]
        found_ref[...] = dot(left_ref[...], right_ref[...], ((1,), (1,)))

        def column_of(head):
            grid = jnp.concatenate([found_ref[quarter_of(head, 128), :], jnp.zeros((128, 512 - SPAN), F32)], axis=1)
            grid = pltpu.roll(grid, 0, 1, stride=1, stride_axis=0)
            return to_buckets(jnp.sum(grid, axis=0, keepdims=True), lane + LOW - TOP)

        out_ref[out_at] = heads_rows(column_of)

    if len(axes) == 1:
        coordinate(axes[0], 0)
        return

    def one(axis, carry):
        coordinate(axis, axis)
        return carry

    lax.fori_loop(0, 2, one, 0)
    near_ref, far_ref = diagonals
    flip = 7 - lax.broadcasted_iota(I32, (8, 128), 0)
    spot = lax.broadcasted_iota(I32, (32, 1), 0)

    def near_column(head):
        near = [jnp.take_along_axis(near_ref[head, 8 * t : 8 * t + 8], flip, axis=0) for t in reversed(range(NEAR))]
        grid = jnp.concatenate(near, axis=0)
        grid = jnp.concatenate([grid, jnp.zeros((8 * NEAR, 384), F32)], axis=1)
        grid = pltpu.roll(grid, 0, 1, stride=1, stride_axis=0)
        near_sums = to_buckets(jnp.sum(grid, axis=0, keepdims=True), 8 * NEAR - 1 - 8 * 12 - lane)
        left = jnp.sum(jnp.sum(far_ref[head, :8], axis=0, keepdims=True), axis=1, keepdims=True)
        right = jnp.sum(jnp.sum(far_ref[head, 8:], axis=0, keepdims=True), axis=1, keepdims=True)
        return near_sums + jnp.where(spot == 15, left, 0.0) + jnp.where(spot == 31, right, 0.0)

    out_ref[2] = heads_rows(near_column)


def table_grads(ids, first, axes, scores, places, positions, sums=()):
    seq = positions.shape[1]
    wide = PLACES // 128 * seq // 2
    return call(
        functools.partial(tables_kernel, base=0 if first else 1, axes=axes),
        "table_grads",
        ids,
        (scores, places, positions, *sums),
        shape((3 if sums else 1, 8, 32), F32),
        mib=TABLES_MIB,
        us=0.01,
        scratch=[
            pltpu.VMEM((HEADS * 128, wide), BF), pltpu.VMEM((SPAN, wide), BF), pltpu.VMEM((HEADS * 128, SPAN), F32),
        ],
    )


def terms_of(grads, weights):
    total = None
    for part, w_ref in enumerate(weights):
        found = dot(grads[part], w_ref[...], ((0,), (0,)))
        total = found if total is None else total + found
    return total


def terms_send_kernel(ids, w0, w1, w2, grads_ref, *outs):
    for at, out_ref in enumerate(outs):
        out_ref[...] = terms_of(grads_ref[2 * at + 1], (w0, w1, w2)).astype(BF)


def terms_keep_kernel(ids, w0, w1, w2, grads_ref, got_own, got_other, own_ref, other_ref):
    other_ref[...] = (terms_of(grads_ref[2], (w0, w1, w2)) + got_other[...].astype(F32)).astype(BF)
    own_ref[...] = terms_of(grads_ref[0], (w0, w1, w2)) + got_own[...].astype(F32)


def terms_send(ids, weights, grads):
    outs = [shape((grads.shape[3], weights[0].shape[1]), BF)] * 2
    return call(terms_send_kernel, "terms_send", ids, (*weights, grads), outs, mib=16, us=0.01)


def terms_keep(ids, weights, grads, got):
    outs = [shape(got[0].shape, F32), shape(got[0].shape, BF)]
    return call(terms_keep_kernel, "terms_keep", ids, (*weights, grads, *got), outs, mib=16, us=0.01)


def last_kernel(
    ids, mine_ref, sent_ref, x_ref, page_ref, feat_ref, gain_ref, grad_ref, second_ref, mixed_ref, ffn_ref, got_ref,
    out_ref, part_ref,
):
    grad_normed = mine_ref[...] + sent_ref[...].astype(F32)
    here = quarter_of(ids[0], mine_ref.shape[0])
    unit, factor = unit_rows(hidden_rows(x_ref[here, :], page_ref[:, here], feat_ref[...]))
    scaled = grad_normed * gain_ref[...].astype(F32).reshape(1, -1)
    grad = factor * (scaled - unit * jnp.mean(scaled * unit, axis=-1, keepdims=True))
    rows, width = grad.shape
    out_ref[0, :rows] = (mixed_ref[...] + ffn_ref[...] + got_ref[...].astype(F32)).astype(BF)
    out_ref[1, :rows] = (grad_ref[...] + grad).astype(BF)
    part_ref[0:1] = jnp.sum(grad_normed * unit, axis=0, keepdims=True)
    part_ref[1:2] = second_ref[...]


def last(ids, mine, sent, inputs, onehot, feats, gain, grad_mixed, second, *ffn):
    rows, width = mine.shape
    arrays = (mine, sent, inputs, onehot, feats, gain, grad_mixed, second, *ffn)
    outs = [shape((2, rows, width), BF), shape((2, width), F32)]
    return call(last_kernel, "last", ids, arrays, outs, mib=16, us=0.01)


def pack_kernel(ids, gains_ref, got_ref, hor_a, ver_a, late, out_ref):
    gains = gains_ref[...] + got_ref[...]
    gains = [gains[slot : slot + 1] for slot in range(2)]
    parts = gains[0].shape[1] // 128
    for slot in range(2):
        gain = gains[slot]
        for part in range(parts):
            at = slot * parts + part
            out_ref[at : at + 1, :] = gain[:, part * 128 : part * 128 + 128]
    bins = hor_a.shape[2]
    at = 2 * parts
    out_ref[at:, :] = jnp.zeros((out_ref.shape[0] - at, 128), F32)
    for found in (late[2], hor_a[0] + late[0], ver_a[0] + late[1]):
        out_ref[at : at + HEADS, :bins] = found[:HEADS]
        at += HEADS


def pack(ids, gains, got, *sums):
    size = gains.shape[1] // 128 * 2 + 3 * HEADS
    size = -(-size // 8) * 8
    return call(pack_kernel, "pack", ids, (gains, got, *sums), shape((size, 128), F32), mib=8, us=0.1)


def join_kernel(ids, b0, b1, b2, b3, out_ref, *, slot):
    for k, b_ref in enumerate((b0, b1, b2, b3)):

        @pl.when(pl.program_id(0) == k)
        def _(b_ref=b_ref):
            out_ref[...] = b_ref[slot, : out_ref.shape[0]].astype(out_ref.dtype)


def join_feat_kernel(ids, b0, b1, b2, b3, page_ref, out_ref, feat_ref, all_ref, *, slot):
    step = pl.program_id(0)
    rows = out_ref.shape[0]
    for k, b_ref in enumerate((b0, b1, b2, b3)):

        @pl.when(step == k)
        def _(b_ref=b_ref, k=k):
            out_ref[...] = b_ref[slot, :rows].astype(out_ref.dtype)
            all_ref[pl.ds(pl.multiple_of(ids[k] * rows, rows), rows), :] = b_ref[slot, :rows]

    @pl.when(step == 3)
    def _():
        feat_ref[...] = dot(page_ref[...].astype(F32).astype(BF), all_ref[...])


def join(ids, blocks, slot, dtype, onehot=None):
    _, rows, width = blocks[0].shape
    specs = [VMEM] * 4
    outs, out_specs = [shape((4 * rows, width), dtype)], [pl.BlockSpec((rows, width), lambda i, s: (s[i], 0))]
    extra, scratch = (), []
    if onehot is not None:
        pages = onehot.shape[0]
        specs = specs + [VMEM]
        outs.append(shape((pages, width), F32))
        out_specs.append(whole((pages, width)))
        extra, scratch = (onehot,), [pltpu.VMEM((4 * rows, width), BF)]
    found = pl.pallas_call(
        functools.partial(join_kernel if onehot is None else join_feat_kernel, slot=slot),
        grid_spec=pltpu.PrefetchScalarGridSpec(
            num_scalar_prefetch=1, grid=(4,), in_specs=specs, out_specs=out_specs, scratch_shapes=scratch
        ),
        out_shape=outs,
        compiler_params=params(16),
        cost_estimate=cost(0.01),
        name="join_output" if onehot is None else "join_grads",
    )(ids, *blocks, *extra)
    return found[0] if onehot is None else found


def split_rows(ids, total, cols, keep_ref, send_ref, parity):
    groups, size = keep_ref.shape[0], keep_ref.shape[1]
    for g in range(groups):
        mine = pl.multiple_of((2 * g + parity) * size, 8)
        theirs = pl.multiple_of((2 * g + 1 - parity) * size, 8)
        keep_ref[g] = total[pl.ds(mine, size), cols].astype(keep_ref.dtype)
        send_ref[g] = total[pl.ds(theirs, size), cols].astype(BF)


def feed_grad_kernel(ids, k0, n0, k1, n1, c0, c1, cot_ref, *outs, fast):
    units = k0.shape[2]
    rows = lambda refs: jnp.concatenate(refs, axis=0)
    total = outs[-1]
    normed = rows([n0[2], c0[2], n1[2], c1[2]])
    total[:, :units] = dot(normed, rows([k0[1], c0[1], k1[1], c1[1]]), ((0,), (0,)))
    cotangent = rows([cot_ref[quarter_of(ids[n], k0.shape[1]), :] for n in range(4)])
    total[:, units:] = dot(cotangent, rows([k0[0], c0[0], k1[0], c1[0]]), ((0,), (0,)))
    if fast:
        split_rows(ids, total, slice(None), outs[0], outs[1], ids[9])
    else:
        outs[0][...] = total[...]


def feed_grad(ids, own, other, got_own, got_other, cotangent, fast):
    _, rows, units = own[0].shape
    width = cotangent.shape[1]
    if fast:
        outs = [shape((4, width // 8, 2 * units), F32), shape((4, width // 8, 2 * units), BF)]
    else:
        outs = [shape((width, 2 * units), F32)]
    return call(
        functools.partial(feed_grad_kernel, fast=fast),
        "feed_grad",
        ids,
        (*own, *other, got_own, got_other, cotangent),
        outs,
        mib=24,
        us=7,
        scratch=[pltpu.VMEM((width, 2 * units), F32)],
    )


def head_grad_kernel(ids, normed_ref, grads_ref, l0, l2, l1, l3, a0, a1, a2, a3, *outs, fast):
    total, turned = outs[-2:]
    n = a0.shape[0]
    normed = jnp.concatenate([normed_ref[quarter_of(ids[k], a0.shape[1]), :] for k in range(4)], axis=0)
    for part in range(3):
        left = jnp.concatenate([grads_ref[k, part] for k in range(4)], axis=1)
        total[part * n : (part + 1) * n, :] = dot(left, normed)
    low = jnp.concatenate([r[...] for r in (l0, l1, l2, l3)], axis=0)
    total[3 * n :, :] = dot(jnp.concatenate([r[...] for r in (a0, a1, a2, a3)], axis=1), low)
    turned[...] = total[...].T
    if fast:
        split_rows(ids, turned, slice(None), outs[0], outs[1], ids[9])
    else:
        outs[0][...] = turned[...]


def head_grad(ids, normed, grads, low, low_got, attended, fast):
    seq, width = normed.shape
    n = grads.shape[2]
    if fast:
        outs = [shape((4, width // 8, 4 * n), F32), shape((4, width // 8, 4 * n), BF)]
    else:
        outs = [shape((width, 4 * n), F32)]
    return call(
        functools.partial(head_grad_kernel, fast=fast),
        "head_grad",
        ids,
        (normed, grads, *low, *low_got, *attended),
        outs,
        mib=18,
        us=0.01,
        scratch=[pltpu.VMEM((4 * n, width), F32), pltpu.VMEM((width, 4 * n), F32)],
    )


def pair_kernel(ids, *refs):
    pairs, outs = refs[:-4], refs[-4:]
    for k, o_ref in enumerate(outs):
        at = ids[4 + k]
        start = 0
        for keep_ref, got_ref in zip(pairs[::2], pairs[1::2]):
            n = keep_ref.shape[2]
            o_ref[:, start : start + n] = (keep_ref[at] + got_ref[at].astype(F32)).astype(o_ref.dtype)
            start += n


def pair_sum(ids, *arrays):
    size = arrays[0].shape[1]
    n = sum(a.shape[2] for a in arrays[::2])
    outs = [shape((size, n), F32)] + [shape((size, n), BF)] * 3
    return call(pair_kernel, "pair_sum", ids, arrays, outs, mib=16, us=0.01)


def feed_final_kernel(a0, a1, a2, a3, up_ref, down_ref):
    total = a0[...] + a1[...].astype(F32) + a2[...].astype(F32) + a3[...].astype(F32)
    units = up_ref.shape[1]
    up_ref[...] = total[:, :units]
    down_ref[...] = total[:, units:]


def head_final_kernel(a0, a1, a2, a3, one_ref, two_ref, q_ref, k_ref, v_ref, o_ref, *smalls):
    total = a0[...] + a1[...].astype(F32) + a2[...].astype(F32) + a3[...].astype(F32)
    n = q_ref.shape[1]
    for at, goal in enumerate((q_ref, k_ref, v_ref)):
        goal[...] = total[:, at * n : (at + 1) * n]
    o_ref[...] = total[:, 3 * n :].T
    *tables, gains_ref = smalls
    total = one_ref[...] + two_ref[...]
    parts = gains_ref.shape[1] // 128
    for slot in range(2):
        for part in range(parts):
            at = slot * parts + part
            gains_ref[slot : slot + 1, part * 128 : part * 128 + 128] = total[at : at + 1]
    at, bins = 2 * parts, tables[0].shape[1]
    for goal in tables:
        goal[...] = total[at : at + HEADS, :bins]
        at += HEADS


def final(kernel, arrays, done, outs):
    arrays = [after(arrays[0], done)] + arrays[1:]
    return pl.pallas_call(
        kernel,
        grid=(1,),
        in_specs=[VMEM] * len(arrays),
        out_specs=jax.tree.map(lambda o: whole(o.shape), outs),
        out_shape=outs,
        compiler_params=params(16),
        cost_estimate=cost(5 if kernel is feed_final_kernel else 0.01),
        name=kernel.__name__[:-7],
    )(*arrays)


def swap(array, axis, size, bits):
    return lax.ppermute(array, axis, [(i, i ^ bits) for i in range(size)])


def after(array, *others):
    return lax.optimization_barrier((array, others))[0]


def local(
    inputs, page_feat, page_onehot, lengths, hor_pos, ver_pos, norm1_gain, w_query, w_key, w_value,
    rel_table, hor_table, ver_table, w_output, norm2_gain, w_up, w_down, cotangent, *, dp,
):
    seq, width = inputs.shape
    fast = dp == 8
    over = functools.partial(swap, axis="mp", size=4)
    m = lax.axis_index("mp").astype(I32)
    d = lax.axis_index("dp").astype(I32)
    k4 = jnp.arange(4, dtype=I32)
    spot = lambda who: (who & 1) * 2 + (who >> 1)
    ids = jnp.concatenate([
        spot(m ^ k4),
        (d >> 1) ^ k4,
        lengths[:1],
        (d & 1)[None],
    ])
    gain_one, gain_two = norm1_gain, norm2_gain
    feats = page_feat[0]
    hor, ver = hor_pos[None], ver_pos[None]
    tables = (rel_table, hor_table, ver_table)
    pages = page_onehot.T
    weights = [w_query.T, w_key.T, w_value.T]

    wo_y, wo_core = over(w_output, bits=2), over(w_output, bits=1)
    normed1, queries, keys, values = project(ids, inputs, pages, feats, gain_one, *weights)
    w_outputs = [w_output, wo_core, wo_y, over(after(wo_y, normed1), bits=1)]
    ups = [w_up, over(after(w_up, normed1), bits=1)]
    downs = [w_down, over(after(w_down, normed1), bits=1)]

    (e_a, att0, att1, inverse_a, out_a), lookups = attend(ids, queries, keys, values, hor, ver, tables, None)
    from_y, from_yc, own1 = over(att0, bits=2), over(att1, bits=3), over(att1, bits=1)
    ver_late = after(ver, att0, w_outputs[3], ups[1], downs[1])
    (e_b, att2, att3, inverse_b, out_b), _ = attend(ids, queries, keys, values, hor, ver_late, tables, lookups)
    attended = [att0, att1, att2, att3]
    for_other = [att2, over(att3, bits=1), from_y, from_yc]
    for_own = [att0, own1, over(att2, bits=2), over(att3, bits=3)]

    around = functools.partial(swap, axis="dp", size=dp)
    to_z = lambda parts: [parts[0]] + [around(part, bits=2 * k) for k, part in zip((1, 2, 3), parts[1:])]
    size = width // dp
    n = w_query.shape[1]
    units = w_up.shape[1]
    fixed = (inputs, pages, feats, gain_two, cotangent)
    x_keep, x_send, x_mixed, x_grad, x_ffn = feed(ids, False, *fixed, for_other, w_outputs, ups, downs)
    got_own, x_got = over(x_grad, bits=2), over(x_send, bits=1)
    for_own[0] = after(att0, x_ffn)
    m_keep, m_send, mixed, m_grad, m_ffn = feed(ids, True, *fixed, for_own, w_outputs, ups, downs)
    got_other, m_got = over(m_grad, bits=2), over(after(m_send, x_got), bits=1)
    own_grad = add(ids, m_grad, got_own)

    feed_grads = feed_grad(ids, (after(m_keep, own_grad), m_send), (x_keep, x_send), m_got, x_got, cotangent, fast)
    feed_got = around(feed_grads[1], bits=1) if fast else ids
    places_at, both = places_of(ids, after(hor, feed_grads[0]), ver)
    grad_mixed, ga, core_send, *low, gain_two_part = mid(
        ids, (after(own_grad, places_at), mixed), (x_grad, got_other, x_mixed), gain_two, cotangent, w_outputs[:2]
    )
    core_got = over(core_send, bits=1)
    sent_ffn = over(after(x_ffn, got_other, places_at), bits=2)

    halves = ((e_a, e_b), (inverse_a, inverse_b), (out_a, out_b))
    scores_a, dq0, dq2, key_sum, value_sum, near, far = back(ids, halves, queries, keys, values, ga, None)
    scores_b, grads, near, far = back(
        ids, halves, queries, keys, values, after(core_got, dq0), (key_sum, value_sum, near, far, dq0, dq2)
    )
    low_got = [over(part, bits=1) for part in low]
    to_core = terms_send(ids, weights, after(grads, sent_ffn))
    got_terms = [over(part, bits=1) for part in to_core]
    head_grads = head_grad(ids, normed1, after(grads, to_core[0]), low, low_got, attended, fast)
    own_terms, other_terms = terms_keep(ids, weights, after(grads, head_grads[0]), got_terms)
    sent_terms = over(other_terms, bits=2)

    hor_a = table_grads(ids, True, (0,), scores_a, places_at, after(both, own_terms))
    done = hor_a
    if fast:
        feed_parts = to_z(pair_sum(ids, after(feed_grads[0], done), feed_got))
        done = feed_parts[0]
    head_got = around(after(head_grads[1], done), bits=1) if fast else ids
    rows, gains = last(
        ids, after(own_terms, done), sent_terms, inputs, pages, feats, gain_one, grad_mixed, gain_two_part,
        mixed, m_ffn, sent_ffn,
    )
    rows_y, rows_core = over(rows, bits=2), over(rows, bits=1)
    ver_a = table_grads(ids, True, (1,), scores_a, places_at, after(both, rows))
    gains = after(gains, ver_a) + over(gains, bits=1)
    got_gains = over(gains, bits=2)
    late = table_grads(ids, False, (0, 1), scores_b, places_at, after(both, gains, head_got), (near, far))

    small = pack(ids, gains, got_gains, hor_a, ver_a, late)
    if fast:
        got = around(small, bits=1)
        grad_up, grad_down = final(feed_final_kernel, feed_parts, small, [shape((size, units), F32)] * 2)
        head_parts = to_z(pair_sum(ids, after(head_grads[0], grad_up), head_got))
        small = after(small, head_parts[0]) + got
        got = around(small, bits=2)
        quarters = [rows, rows_core, rows_y, over(after(rows_y, grad_up), bits=1)]
        outputs = join(ids, [after(rows, small)] + quarters[1:], 0, BF)
        grad_inputs, grad_feats = join(ids, [after(rows, outputs)] + quarters[1:], 1, F32, pages)
        small = after(small, grad_feats) + got
        bins = rel_table.shape[1]
        outs = [shape((size, n), F32)] * 3 + [shape((n, size), F32)] + [shape((HEADS, bins), F32)] * 3
        *found, gain_sums = final(
            head_final_kernel, head_parts + [small, around(small, bits=4)], grad_feats, outs + [shape((2, width), F32)]
        )
        grad_query, grad_key, grad_value, grad_output, grad_rel, grad_hor, grad_ver = found
    else:
        quarters = [rows, rows_core, rows_y, over(rows_y, bits=1)]
        outputs = join(ids, quarters, 0, BF)
        grad_inputs, grad_feats = join(ids, quarters, 1, F32, pages)
        small = lax.psum(small, "dp")
        scatter = lambda a: lax.psum_scatter(a[0], "dp", scatter_dimension=0, tiled=True)
        grad_feed, heads = scatter(feed_grads), scatter(head_grads)
        grad_up, grad_down = grad_feed[:, :units], grad_feed[:, units:]
        grad_query, grad_key, grad_value = heads[:, :n], heads[:, n : 2 * n], heads[:, 2 * n : 3 * n]
        grad_output = heads[:, 3 * n :].T
        gain_sums = small[: width // 128 * 2].reshape(2, width)
        table_sums = small[width // 128 * 2 :, : rel_table.shape[1]]
        grad_rel, grad_hor, grad_ver = (table_sums[at : at + HEADS] for at in range(0, 3 * HEADS, HEADS))
    gain_sums = lax.dynamic_slice(gain_sums, (0, d * size), (2, size))
    return (
        outputs, grad_inputs, grad_feats[None], gain_sums[0], grad_query, grad_key, grad_value,
        grad_rel, grad_hor, grad_ver, grad_output, gain_sums[1], grad_up, grad_down.T,
    )


def solution(mesh):
    return jax.shard_map(
        functools.partial(local, dp=mesh.shape["dp"]),
        mesh=mesh,
        in_specs=(
            P("dp", None),
            P("dp", None, None),
            P("dp", None),
            P("dp"),
            P("dp"),
            P("dp"),
            P(),
            P(None, "mp"),
            P(None, "mp"),
            P(None, "mp"),
            P("mp", None),
            P("mp", None),
            P("mp", None),
            P("mp", None),
            P(),
            P(None, "mp"),
            P("mp", None),
            P("dp", None),
        ),
        out_specs=(
            P("dp", None),
            P("dp", None),
            P("dp", None, None),
            P("dp"),
            P("dp", "mp"),
            P("dp", "mp"),
            P("dp", "mp"),
            P("mp", None),
            P("mp", None),
            P("mp", None),
            P("mp", "dp"),
            P("dp"),
            P("dp", "mp"),
            P("mp", "dp"),
        ),
        check_vma=False,
    )
```

```python
import functools

import jax
import jax.numpy as jnp
import numpy as np
from jax import lax
from jax.experimental import pallas as pl
from jax.experimental.pallas import tpu as pltpu
from jax.sharding import PartitionSpec as P

EPS = 1e-06
THRESHOLDS = (12, 16, 23, 32, 46, 64, 91)
FAR = 91
HEADS = 3
HD = 64
PAD = 128
MARKS = 72
NEAR = 40
TILES = NEAR + 2
SPAN = 384
LOW = 92
TOP = 311
BF = jnp.bfloat16
F32 = jnp.float32
I32 = jnp.int32
FEED_CHUNK = 256
PLACES = 1024
TABLES_MIB = 18
GELU_C = float(np.sqrt(2.0 / np.pi))


def dot(left, right, dims=((1,), (0,))):
    return lax.dot_general(left, right, (dims, ((), ())), preferred_element_type=F32)


def bucket(delta):
    magnitude = jnp.abs(delta)
    coarse = 8 + sum((magnitude >= limit).astype(I32) for limit in THRESHOLDS)
    return jnp.where(magnitude < 8, magnitude, coarse) + 16 * (delta > 0).astype(I32)


def params(mib):
    return pltpu.CompilerParams(vmem_limit_bytes=mib * 2**20)


def cost(microseconds):
    return pl.CostEstimate(flops=int(1.15e9 * microseconds), bytes_accessed=1, transcendentals=0)


def shape(dims, dtype):
    return jax.ShapeDtypeStruct(dims, dtype)


def whole(dims):
    return pl.BlockSpec(dims, lambda *a: (0,) * len(dims))


VMEM = pl.BlockSpec(memory_space=pltpu.VMEM)


def call(kernel, name, ids, arrays, outs, *, mib, us, scratch=()):
    return pl.pallas_call(
        kernel,
        grid_spec=pltpu.PrefetchScalarGridSpec(
            num_scalar_prefetch=1,
            grid=(1,),
            in_specs=[VMEM] * len(arrays),
            out_specs=jax.tree.map(lambda _: VMEM, outs),
            scratch_shapes=list(scratch),
        ),
        out_shape=outs,
        compiler_params=params(mib),
        cost_estimate=cost(us),
        name=name,
    )(ids, *arrays)


def quarter_of(place, size):
    return pl.ds(pl.multiple_of(place * size, 128), size)


def hidden_rows(inputs, pages, feats):
    return inputs.astype(F32) + dot(pages.astype(F32).astype(BF), feats, ((0,), (0,)))


def unit_rows(field):
    factor = lax.rsqrt(jnp.mean(field * field, axis=-1, keepdims=True) + EPS)
    return field * factor, factor


def project_kernel(ids, x_ref, page_ref, feat_ref, gain_ref, wq_ref, wk_ref, wv_ref, n_ref, q_ref, k_ref, v_ref):
    rows = 512

    def block_of(step, carry):
        here = quarter_of(step, rows)
        unit, _ = unit_rows(hidden_rows(x_ref[here, :], page_ref[:, here], feat_ref[...]))
        normed = (unit * gain_ref[...].astype(F32).reshape(1, -1)).astype(BF)
        n_ref[here, :] = normed
        lane = lax.broadcasted_iota(I32, (rows, PAD), 1)
        row = lax.broadcasted_iota(I32, (rows, PAD), 0) + step * rows
        masked = jnp.where((lane == HD) & (row >= ids[8]), -1e30, 0.0)
        block = lane - MARKS
        far_left = (block >= 0) & (block < 8) & (row < 128 * block - 96)
        far_right = (block >= 8) & (block < 16) & (row >= 128 * (block - 8) + 224)
        masked = jnp.where(far_left | far_right, 1.0, masked)
        query_extra = jnp.where(lane == HD, 1.0, 0.0)
        value_extra = jnp.where((lane == HD) | (lane == HD + 1), 1.0, 0.0)
        for out_ref, w_ref, extra, scale in (
            (q_ref, wq_ref, query_extra, 0.125),
            (k_ref, wk_ref, masked, None),
            (v_ref, wv_ref, value_extra, None),
        ):
            full = dot(normed, w_ref[...], ((1,), (1,)))
            if scale is not None:
                full = full * scale
            pair = full[:, :PAD]
            last = jnp.concatenate([full[:, PAD:], jnp.zeros((rows, PAD - HD), F32)], axis=1)
            heads = (pair, pltpu.roll(pair, HD, 1), last)
            for head in range(HEADS):
                out_ref[here, head * PAD : (head + 1) * PAD] = jnp.where(lane < HD, heads[head], extra).astype(BF)
        return carry

    lax.fori_loop(0, x_ref.shape[0] // rows, block_of, 0)


def project(ids, *arrays):
    seq, width = arrays[0].shape
    outs = [shape((seq, width), BF)] + [shape((seq, HEADS * PAD), BF)] * 3
    return call(project_kernel, "project", ids, arrays, outs, mib=16, us=7)


def place(delta):
    magnitude = jnp.abs(delta)
    coarse = jnp.minimum(25 - lax.clz(delta * delta), 7)
    exact = magnitude < 8
    return jnp.where(exact, magnitude, coarse), exact, delta > 0


def look(table_ref, row, where):
    index, exact, after = where
    found = [jnp.take_along_axis(table_ref[row, part], index, axis=0) for part in range(4)]
    return jnp.where(after, jnp.where(exact, found[2], found[3]), jnp.where(exact, found[0], found[1]))


def tile_delta(tile):
    lane = lax.broadcasted_iota(I32, (8, 128), 1)
    sub = lax.broadcasted_iota(I32, (8, 128), 0)
    delta = 8 * (tile - 13) + sub - lane
    if tile == 0:
        delta = jnp.full_like(delta, -1000)
    if tile == TILES - 1:
        delta = jnp.full_like(delta, 1000)
    return delta


def attend_kernel(*refs, first, chunk):
    ids, q_ref, k_ref, v_ref, hor_ref, ver_ref = refs[:6]
    if first:
        hor_all, ver_all, rel_table, hor_table, ver_table, e_ref, att0, att1, inv_ref, out_ref = refs[6:16]
        rel_ref, t8_ref, hor_col, ver_col, s_ref = refs[16:]
    else:
        rel_ref, t8_ref, hor_col, ver_col, e_ref, att0, att1, inv_ref, out_ref, s_ref = refs[6:]
    seq = k_ref.shape[0]
    width = seq // 4
    lanes = width // 128

    if first:
        for all_ref, col_ref in ((hor_all, hor_col), (ver_all, ver_col)):
            for b in range(seq // 128):
                cols = slice(128 * b, 128 * b + 128)
                spread = jnp.broadcast_to(all_ref[:, cols].astype(F32), (128, 128))
                col_ref[cols, :] = spread.T.astype(I32)
        lane = lax.broadcasted_iota(I32, (8, 32), 1)
        sub = lax.broadcasted_iota(I32, (8, 32), 0)
        for axis, table_ref in enumerate((rel_table, hor_table, ver_table)):
            table = table_ref[...].astype(F32)
            for head in range(HEADS):
                row = jnp.broadcast_to(table[head : head + 1], (8, 32))
                for part in range(4):
                    entries = jnp.sum(jnp.where(lane == sub + 8 * part, row, 0.0), axis=1, keepdims=True)
                    t8_ref[axis * HEADS + head, part] = jnp.broadcast_to(entries, (8, 128))
        for tile in range(TILES):
            where = place(tile_delta(tile))
            for head in range(HEADS):
                rel_ref[head, tile] = look(t8_ref, head, where)

    def products(here):
        queries = q_ref[here, :]
        for head in range(HEADS):
            cols = slice(head * PAD, (head + 1) * PAD)
            s_ref[head] = dot(k_ref[:, cols], queries[:, cols], ((1,), (1,)))

    def biases(place_of, here):
        hor_row, ver_row = hor_ref[:, here], ver_ref[:, here]
        hor = [jnp.broadcast_to(hor_row[:, 128 * l : 128 * l + 128], (8, 128)) for l in range(lanes)]
        ver = [jnp.broadcast_to(ver_row[:, 128 * l : 128 * l + 128], (8, 128)) for l in range(lanes)]
        block = place_of * lanes

        def add_bias(c, tops):
            tops = list(tops)
            base = pl.multiple_of(c * chunk, chunk)
            for g in range(chunk // 8):
                rows = pl.ds(pl.multiple_of(base + 8 * g, 8), 8)
                hor_keys, ver_keys = hor_col[rows, :], ver_col[rows, :]
                for l in range(lanes):
                    cols = pl.ds(128 * l, 128)
                    hor_at, ver_at = place(hor_keys - hor[l]), place(ver_keys - ver[l])
                    tile = jnp.clip(c * (chunk // 8) + g - 16 * (block + l) + 13, 0, TILES - 1)
                    for head in range(HEADS):
                        s = s_ref[head, rows, cols] + rel_ref[head, tile]
                        s = s + (look(t8_ref, HEADS + head, hor_at) + look(t8_ref, 2 * HEADS + head, ver_at))
                        s_ref[head, rows, cols] = s
                        tops[head * lanes + l] = jnp.maximum(tops[head * lanes + l], s)
            return tuple(tops)

        tops = lax.fori_loop(
            0, seq // chunk, add_bias, tuple(jnp.full((8, 128), -1e30, F32) for _ in range(HEADS * lanes))
        )
        return [jnp.broadcast_to(jnp.max(top, axis=0, keepdims=True), (16, 128)) for top in tops]

    def attended(part, peaks):
        mine = quarter_of(part, width)
        for head in range(HEADS):
            for g in range(seq // 16):
                rows = slice(16 * g, 16 * g + 16)
                for l in range(lanes):
                    cols = slice(128 * l, 128 * l + 128)
                    into = pl.ds(pl.multiple_of(part * width + 128 * l, 128), 128)
                    e_ref[head, rows, into] = jnp.exp(s_ref[head, rows, cols] - peaks[head * lanes + l]).astype(BF)
            total = dot(v_ref[:, head * PAD : (head + 1) * PAD], e_ref[head, :, mine], ((0,), (0,)))
            inverse = 1.0 / total[HD : HD + 1, :]
            inv_ref[head : head + 1, mine] = inverse
            out_ref[head * HD : (head + 1) * HD, mine] = total[:HD] * inverse
        for at, att_ref in enumerate((att0, att1)):

            @pl.when(part == at)
            def _(att_ref=att_ref):
                att_ref[...] = out_ref[:, mine].astype(BF)

    def quarter(part, carry):
        place_of = ids[(0 if first else 2) + part]
        here = quarter_of(place_of, width)
        products(here)
        attended(part, biases(place_of, here))
        return carry

    lax.fori_loop(0, 2, quarter, 0)


def attend(ids, queries, keys, values, hor, ver, tables, lookups):
    seq = queries.shape[0]
    width = seq // 4
    first = lookups is None
    columns = HEADS * HD
    made = [
        shape((HEADS, TILES, 8, 128), F32), shape((3 * HEADS, 4, 8, 128), F32), shape((seq, 128), I32), shape((seq, 128), I32)
    ]
    extra = (hor, ver, *tables) if first else tuple(lookups)
    outs = [
        shape((HEADS, seq, 2 * width), BF), shape((columns, width), BF), shape((columns, width), BF),
        shape((HEADS, 2 * width), F32), shape((columns, 2 * width), F32),
    ]
    found = call(
        functools.partial(attend_kernel, first=first, chunk=128),
        "attend_first" if first else "attend_last",
        ids,
        (queries, keys, values, hor, ver, *extra),
        outs + made if first else outs,
        mib=14,
        us=14,
        scratch=[pltpu.VMEM((HEADS, seq, width), F32)],
    )
    return found[:5], found[5:]


def feed_kernel(
    ids, x_ref, page_ref, feat_ref, gain_ref, cot_ref, a0, a1, a2, a3, o0, o1, o2, o3, u0, u1, d0, d1,
    keep_ref, send_ref, mixed_ref, grad_ref, ffn_ref, *, slot,
):
    here = quarter_of(ids[slot], mixed_ref.shape[0])
    cotangent = cot_ref[here, :]
    mixed = hidden_rows(x_ref[here, :], page_ref[:, here], feat_ref[...])
    for a_ref, o_ref in ((a0, o0), (a1, o1), (a2, o2), (a3, o3)):
        mixed = mixed + dot(a_ref[...], o_ref[...], ((0,), (0,)))
    mixed_ref[...] = mixed
    unit, _ = unit_rows(mixed)
    normed = (unit * gain_ref[...].astype(F32).reshape(1, -1)).astype(BF)
    send_ref[2] = normed
    units = u0.shape[1]
    for u_ref, d_ref, goal in ((u0, d0, keep_ref), (u1, d1, send_ref)):
        for at in range(0, units, FEED_CHUNK):
            cols = slice(at, at + FEED_CHUNK)
            upward = dot(normed, u_ref[:, cols])
            square = upward * upward
            tanh = jnp.tanh(GELU_C * upward * (1.0 + 0.044715 * square))
            lifted = 0.5 * (1.0 + tanh)
            activated = (upward * lifted).astype(BF)
            slope = lifted + 0.5 * upward * (1.0 - tanh * tanh) * (GELU_C * (1.0 + 3 * 0.044715 * square))
            grad_up = (dot(cotangent, d_ref[cols, :], ((1,), (1,))) * slope).astype(BF)
            goal[0, :, cols] = activated
            goal[1, :, cols] = grad_up
    ffn = dot(keep_ref[0], d0[...]) + dot(send_ref[0], d1[...])
    ffn_ref[...] = ffn.astype(ffn_ref.dtype)
    grad = dot(keep_ref[1], u0[...], ((1,), (1,))) + dot(send_ref[1], u1[...], ((1,), (1,)))
    grad_ref[...] = grad.astype(grad_ref.dtype)


def feed(ids, own, inputs, onehot, feats, gain, cotangent, attended, w_outputs, ups, downs):
    seq, width = inputs.shape
    rows = seq // 4
    units = ups[0].shape[1]
    kept = F32 if own else BF
    outs = [
        shape((2, rows, units), BF), shape((3, rows, width), BF), shape((rows, width), F32),
        shape((rows, width), BF), shape((rows, width), kept),
    ]
    return call(
        functools.partial(feed_kernel, slot=0 if own else 2),
        "feed_own" if own else "feed_other",
        ids,
        (inputs, onehot, feats, gain, cotangent, *attended, *w_outputs, *ups, *downs),
        outs,
        mib=16,
        us=20 if own else 10,
    )


def add_kernel(ids, one_ref, two_ref, out_ref):
    out_ref[...] = one_ref[...].astype(F32) + two_ref[...].astype(F32)


def add(ids, one, two):
    return call(add_kernel, "add", ids, (one, two), shape(one.shape, F32), mib=8, us=20)


def mid_kernel(
    ids, own_grad, own_mixed, other_grad, other_got, other_mixed, cot_ref, gain_ref, o0, o1,
    grad_ref, own_ref, core_ref, low_own, low_other, part_ref,
):
    rows = own_grad.shape[0]
    other = other_grad[...].astype(F32) + other_got[...].astype(F32)
    for at, (grad_normed, mixed_ref) in enumerate(((own_grad[...], own_mixed), (other, other_mixed))):
        unit, factor = unit_rows(mixed_ref[...])
        scaled = grad_normed * gain_ref[...].astype(F32).reshape(1, -1)
        grad = factor * (scaled - unit * jnp.mean(scaled * unit, axis=-1, keepdims=True))
        grad = cot_ref[quarter_of(ids[2 * at], rows), :].astype(F32) + grad
        low = grad.astype(BF)
        (low_own, low_other)[at][...] = low
        if at == 0:
            grad_ref[...] = grad
            part_ref[...] = jnp.sum(grad_normed * unit, axis=0, keepdims=True)
        for o_ref, goal in ((o0, own_ref), (o1, core_ref)):
            goal[:, at * rows : (at + 1) * rows] = dot(o_ref[...], low, ((1,), (1,))).astype(BF)


def mid(ids, own, other, gain, cotangent, w_outputs):
    rows, width = own[0].shape
    columns = HEADS * HD
    outs = [
        shape((rows, width), F32), shape((columns, 2 * rows), BF), shape((columns, 2 * rows), BF), shape((rows, width), BF),
        shape((rows, width), BF), shape((1, width), F32),
    ]
    arrays = (*own, *other, cotangent, gain, *w_outputs)
    return call(mid_kernel, "mid", ids, arrays, outs, mib=16, us=0.01)


def back_kernel(*refs, first):
    ids, ea_ref, eb_ref, inv_a, inv_b, out_a, out_b, q_ref, k_ref, v_ref, grad_ref = refs[:11]
    refs = refs[11:]
    if first:
        ds_ref, dqa_ref, dqb_ref, key_ref, value_ref, near_ref, far_ref, x_ref = refs
    else:
        key_in, value_in, near_in, far_in, dqa_in, dqb_in = refs[:6]
        ds_ref, all_ref, near_ref, far_ref, x_ref = refs[6:]
    seq = k_ref.shape[0]
    width = seq // 4
    both = 2 * width
    lanes = width // 128
    base = 0 if first else 1
    sub = lax.broadcasted_iota(I32, (HD, both), 0)
    blocks = [ids[base + 2 * (l // lanes)] * lanes + l % lanes for l in range(2 * lanes)]
    mine = slice(base * width, (base + 1) * width)
    here = [quarter_of(ids[base + 2 * n], width) for n in range(2)]
    beside = lambda one, two: jnp.concatenate([one, two], axis=1)
    spot = lax.broadcasted_iota(I32, (8, 128), 0)

    def one_head(head, carry):
        cols = quarter_of(head, PAD)
        rows = pl.ds(pl.multiple_of(head * HD, HD), HD)
        grad = grad_ref[rows, :].astype(F32)
        grad = (grad * beside(inv_a[pl.ds(head, 1), mine], inv_b[pl.ds(head, 1), mine])).astype(BF).astype(F32)
        inner = jnp.sum(grad * beside(out_a[rows, mine], out_b[rows, mine]), axis=0, keepdims=True)
        high = inner.astype(BF).astype(F32)
        extra = jnp.where(sub == 0, -high, jnp.where(sub == 1, high - inner, 0.0))
        right = jnp.concatenate([grad, extra], axis=0).astype(BF)
        x_ref[...] = dot(v_ref[:, cols], right)
        value = dot(beside(ea_ref[head, :, mine], eb_ref[head, :, mine]), right, ((1,), (1,)))
        for c in range(seq // 16):
            at = slice(16 * c, 16 * c + 16)
            found = beside(ea_ref[head, at, mine], eb_ref[head, at, mine]).astype(F32)
            ds_ref[head, at, :] = (found * x_ref[at, :]).astype(BF)
        grad = ds_ref[head]
        key = dot(grad, jnp.concatenate([q_ref[at, cols] for at in here], axis=0))
        query = dot(k_ref[:, cols], grad, ((0,), (0,)))
        query_a = (query[:HD, :width] * 0.125).astype(BF)
        query_b = (query[:HD, width:] * 0.125).astype(BF)

        for g in range(NEAR // 2):
            total = None if first else near_in[head, 16 * g : 16 * g + 16]
            for l, block in enumerate(blocks):
                start = 128 * block - 96 + 16 * g
                inside = (start >= 0) & (start < seq)
                at = pl.ds(pl.multiple_of(jnp.clip(start, 0, seq - 16), 16), 16)
                found = ds_ref[head, at, 128 * l : 128 * l + 128].astype(F32)
                found = jnp.where(inside, found, 0.0)
                total = found if total is None else total + found
            near_ref[head, 16 * g : 16 * g + 16] = total
        for side in range(2):
            total = None if first else far_in[head, 8 * side : 8 * side + 8]
            for l, block in enumerate(blocks):
                marks = query[MARKS + 8 * side : MARKS + 8 * side + 8, 128 * l : 128 * l + 128]
                marks = jnp.where(spot == block, marks, 0.0)
                total = marks if total is None else total + marks
            far_ref[head, 8 * side : 8 * side + 8] = total

        if first:
            key_ref[:, cols] = key
            value_ref[:, cols] = value
            dqa_ref[rows, :] = query_a
            dqb_ref[rows, :] = query_b
        else:
            for k, found in enumerate((dqa_in[rows, :], query_a, dqb_in[rows, :], query_b)):
                all_ref[k, 0, rows, :] = found
            for part, acc in ((1, key_in[:, cols] + key), (2, value_in[:, cols] + value)):
                turned = acc.T[:HD].astype(BF)
                for q in range(4):
                    k = sum((jnp.where(ids[n] == q, n, 0) for n in range(1, 4)))
                    all_ref[k, part, rows, :] = turned[:, q * width : (q + 1) * width]
        return carry

    lax.fori_loop(0, HEADS, one_head, 0)


def back(ids, attended, queries, keys, values, grads, carried):
    seq, wide = queries.shape
    width = seq // 4
    first = carried is None
    columns = HEADS * HD
    queried = [shape((columns, width), BF)] * 2
    sums = [shape((seq, wide), F32)] * 2
    rel = [shape((HEADS, 8 * NEAR, 128), F32), shape((HEADS, 16, 128), F32)]
    outs = [shape((HEADS, seq, 2 * width), BF)]
    outs += queried + sums if first else [shape((4, 3, columns, width), BF)]
    outs += rel
    arrays = (*attended[0], *attended[1], *attended[2], queries, keys, values, grads, *(() if first else carried))
    return call(
        functools.partial(back_kernel, first=first),
        "back_first" if first else "back_last",
        ids,
        arrays,
        outs,
        mib=16,
        us=2 if first else 0.01,
        scratch=[pltpu.VMEM((seq, 2 * width), F32)],
    )


def places_kernel(ids, hor_ref, ver_ref, at_ref, both_ref):
    _, places, seq = at_ref.shape
    both_ref[0:1, :] = hor_ref[...]
    both_ref[1:2, :] = ver_ref[...]
    for axis, keys_ref in enumerate((hor_ref, ver_ref)):

        def block(b, carry, axis=axis, keys_ref=keys_ref):
            spot = lax.broadcasted_iota(I32, (128, seq), 0) + 128 * b
            at_ref[axis, quarter_of(b, 128), :] = jnp.where(spot == keys_ref[...], 1.0, 0.0).astype(BF)
            return carry

        lax.fori_loop(0, places // 128, block, 0)


def places_of(ids, hor, ver):
    seq = hor.shape[1]
    outs = [shape((2, PLACES, seq), BF), shape((2, seq), I32)]
    return call(places_kernel, "places", ids, (hor, ver), outs, mib=8, us=0.01)


def tables_kernel(ids, s_ref, e_ref, q_ref, *refs, base, axes):
    diagonals = refs[:-4]
    out_ref, left_ref, right_ref, found_ref = refs[-4:]
    width = s_ref.shape[2]
    groups = e_ref.shape[1] // 128

    def to_buckets(sums, delta):
        spot = lax.broadcasted_iota(I32, (32, sums.shape[1]), 0)
        return jnp.sum(jnp.where(bucket(delta) == spot, sums, 0.0), axis=1, keepdims=True)

    lane = lax.broadcasted_iota(I32, (1, 512), 1)
    spread = lax.broadcasted_iota(I32, (32, 128), 1)

    def heads_rows(column_of):
        return sum(jnp.where(spread == head, column_of(head), 0.0) for head in range(HEADS)).T[:8]

    def coordinate(axis, out_at):
        query = jnp.concatenate([q_ref[pl.ds(axis, 1), quarter_of(ids[base + n], width // 2)] for n in (0, 2)], axis=1)
        column = lax.broadcasted_iota(I32, (SPAN, width), 0)
        for b in range(groups):
            window = jnp.clip(128 * b + TOP - LOW - query, 0, TOP)
            right_ref[:, b * width : (b + 1) * width] = jnp.where(column == window, 1.0, 0.0).astype(BF)
        for head in range(HEADS):
            moved = dot(e_ref[axis], s_ref[head]).astype(BF)
            for b in range(groups):
                left_ref[head * 128 : head * 128 + 128, b * width : (b + 1) * width] = moved[128 * b : 128 * b + 128]
        found_ref[...] = dot(left_ref[...], right_ref[...], ((1,), (1,)))

        def column_of(head):
            grid = jnp.concatenate([found_ref[quarter_of(head, 128), :], jnp.zeros((128, 512 - SPAN), F32)], axis=1)
            grid = pltpu.roll(grid, 0, 1, stride=1, stride_axis=0)
            return to_buckets(jnp.sum(grid, axis=0, keepdims=True), lane + LOW - TOP)

        out_ref[out_at] = heads_rows(column_of)

    if len(axes) == 1:
        coordinate(axes[0], 0)
        return

    def one(axis, carry):
        coordinate(axis, axis)
        return carry

    lax.fori_loop(0, 2, one, 0)
    near_ref, far_ref = diagonals
    flip = 7 - lax.broadcasted_iota(I32, (8, 128), 0)
    spot = lax.broadcasted_iota(I32, (32, 1), 0)

    def near_column(head):
        near = [jnp.take_along_axis(near_ref[head, 8 * t : 8 * t + 8], flip, axis=0) for t in reversed(range(NEAR))]
        grid = jnp.concatenate(near, axis=0)
        grid = jnp.concatenate([grid, jnp.zeros((8 * NEAR, 384), F32)], axis=1)
        grid = pltpu.roll(grid, 0, 1, stride=1, stride_axis=0)
        near_sums = to_buckets(jnp.sum(grid, axis=0, keepdims=True), 8 * NEAR - 1 - 8 * 12 - lane)
        left = jnp.sum(jnp.sum(far_ref[head, :8], axis=0, keepdims=True), axis=1, keepdims=True)
        right = jnp.sum(jnp.sum(far_ref[head, 8:], axis=0, keepdims=True), axis=1, keepdims=True)
        return near_sums + jnp.where(spot == 15, left, 0.0) + jnp.where(spot == 31, right, 0.0)

    out_ref[2] = heads_rows(near_column)


def table_grads(ids, first, axes, scores, places, positions, sums=()):
    seq = positions.shape[1]
    wide = PLACES // 128 * seq // 2
    return call(
        functools.partial(tables_kernel, base=0 if first else 1, axes=axes),
        "table_grads",
        ids,
        (scores, places, positions, *sums),
        shape((3 if sums else 1, 8, 32), F32),
        mib=TABLES_MIB,
        us=0.01,
        scratch=[
            pltpu.VMEM((HEADS * 128, wide), BF), pltpu.VMEM((SPAN, wide), BF), pltpu.VMEM((HEADS * 128, SPAN), F32),
        ],
    )


def terms_of(grads, weights):
    total = None
    for part, w_ref in enumerate(weights):
        found = dot(grads[part], w_ref[...], ((0,), (0,)))
        total = found if total is None else total + found
    return total


def terms_send_kernel(ids, w0, w1, w2, grads_ref, *outs):
    for at, out_ref in enumerate(outs):
        out_ref[...] = terms_of(grads_ref[2 * at + 1], (w0, w1, w2)).astype(BF)


def terms_keep_kernel(ids, w0, w1, w2, grads_ref, got_own, got_other, own_ref, other_ref):
    other_ref[...] = (terms_of(grads_ref[2], (w0, w1, w2)) + got_other[...].astype(F32)).astype(BF)
    own_ref[...] = terms_of(grads_ref[0], (w0, w1, w2)) + got_own[...].astype(F32)


def terms_send(ids, weights, grads):
    outs = [shape((grads.shape[3], weights[0].shape[1]), BF)] * 2
    return call(terms_send_kernel, "terms_send", ids, (*weights, grads), outs, mib=16, us=0.01)


def terms_keep(ids, weights, grads, got):
    outs = [shape(got[0].shape, F32), shape(got[0].shape, BF)]
    return call(terms_keep_kernel, "terms_keep", ids, (*weights, grads, *got), outs, mib=16, us=0.01)


def last_kernel(
    ids, mine_ref, sent_ref, x_ref, page_ref, feat_ref, gain_ref, grad_ref, second_ref, mixed_ref, ffn_ref, got_ref,
    out_ref, part_ref,
):
    grad_normed = mine_ref[...] + sent_ref[...].astype(F32)
    here = quarter_of(ids[0], mine_ref.shape[0])
    unit, factor = unit_rows(hidden_rows(x_ref[here, :], page_ref[:, here], feat_ref[...]))
    scaled = grad_normed * gain_ref[...].astype(F32).reshape(1, -1)
    grad = factor * (scaled - unit * jnp.mean(scaled * unit, axis=-1, keepdims=True))
    rows, width = grad.shape
    out_ref[0, :rows] = (mixed_ref[...] + ffn_ref[...] + got_ref[...].astype(F32)).astype(BF)
    out_ref[1, :rows] = (grad_ref[...] + grad).astype(BF)
    part_ref[0:1] = jnp.sum(grad_normed * unit, axis=0, keepdims=True)
    part_ref[1:2] = second_ref[...]


def last(ids, mine, sent, inputs, onehot, feats, gain, grad_mixed, second, *ffn):
    rows, width = mine.shape
    arrays = (mine, sent, inputs, onehot, feats, gain, grad_mixed, second, *ffn)
    outs = [shape((2, rows, width), BF), shape((2, width), F32)]
    return call(last_kernel, "last", ids, arrays, outs, mib=16, us=0.01)


def pack_kernel(ids, gains_ref, got_ref, hor_a, ver_a, late, out_ref):
    gains = gains_ref[...] + got_ref[...]
    gains = [gains[slot : slot + 1] for slot in range(2)]
    parts = gains[0].shape[1] // 128
    for slot in range(2):
        gain = gains[slot]
        for part in range(parts):
            at = slot * parts + part
            out_ref[at : at + 1, :] = gain[:, part * 128 : part * 128 + 128]
    bins = hor_a.shape[2]
    at = 2 * parts
    out_ref[at:, :] = jnp.zeros((out_ref.shape[0] - at, 128), F32)
    for found in (late[2], hor_a[0] + late[0], ver_a[0] + late[1]):
        out_ref[at : at + HEADS, :bins] = found[:HEADS]
        at += HEADS


def pack(ids, gains, got, *sums):
    size = gains.shape[1] // 128 * 2 + 3 * HEADS
    size = -(-size // 8) * 8
    return call(pack_kernel, "pack", ids, (gains, got, *sums), shape((size, 128), F32), mib=8, us=0.1)


def join_kernel(ids, b0, b1, b2, b3, out_ref, *, slot):
    for k, b_ref in enumerate((b0, b1, b2, b3)):

        @pl.when(pl.program_id(0) == k)
        def _(b_ref=b_ref):
            out_ref[...] = b_ref[slot, : out_ref.shape[0]].astype(out_ref.dtype)


def join_feat_kernel(ids, b0, b1, b2, b3, page_ref, out_ref, feat_ref, all_ref, *, slot):
    step = pl.program_id(0)
    rows = out_ref.shape[0]
    for k, b_ref in enumerate((b0, b1, b2, b3)):

        @pl.when(step == k)
        def _(b_ref=b_ref, k=k):
            out_ref[...] = b_ref[slot, :rows].astype(out_ref.dtype)
            all_ref[pl.ds(pl.multiple_of(ids[k] * rows, rows), rows), :] = b_ref[slot, :rows]

    @pl.when(step == 3)
    def _():
        feat_ref[...] = dot(page_ref[...].astype(F32).astype(BF), all_ref[...])


def join(ids, blocks, slot, dtype, onehot=None):
    _, rows, width = blocks[0].shape
    specs = [VMEM] * 4
    outs, out_specs = [shape((4 * rows, width), dtype)], [pl.BlockSpec((rows, width), lambda i, s: (s[i], 0))]
    extra, scratch = (), []
    if onehot is not None:
        pages = onehot.shape[0]
        specs = specs + [VMEM]
        outs.append(shape((pages, width), F32))
        out_specs.append(whole((pages, width)))
        extra, scratch = (onehot,), [pltpu.VMEM((4 * rows, width), BF)]
    found = pl.pallas_call(
        functools.partial(join_kernel if onehot is None else join_feat_kernel, slot=slot),
        grid_spec=pltpu.PrefetchScalarGridSpec(
            num_scalar_prefetch=1, grid=(4,), in_specs=specs, out_specs=out_specs, scratch_shapes=scratch
        ),
        out_shape=outs,
        compiler_params=params(16),
        cost_estimate=cost(0.01),
        name="join_output" if onehot is None else "join_grads",
    )(ids, *blocks, *extra)
    return found[0] if onehot is None else found


def split_rows(ids, total, cols, keep_ref, send_ref, parity):
    groups, size = keep_ref.shape[0], keep_ref.shape[1]
    for g in range(groups):
        mine = pl.multiple_of((2 * g + parity) * size, 8)
        theirs = pl.multiple_of((2 * g + 1 - parity) * size, 8)
        keep_ref[g] = total[pl.ds(mine, size), cols].astype(keep_ref.dtype)
        send_ref[g] = total[pl.ds(theirs, size), cols].astype(BF)


def feed_grad_kernel(ids, k0, n0, k1, n1, c0, c1, cot_ref, *outs, fast):
    units = k0.shape[2]
    rows = lambda refs: jnp.concatenate(refs, axis=0)
    total = outs[-1]
    normed = rows([n0[2], c0[2], n1[2], c1[2]])
    total[:, :units] = dot(normed, rows([k0[1], c0[1], k1[1], c1[1]]), ((0,), (0,)))
    cotangent = rows([cot_ref[quarter_of(ids[n], k0.shape[1]), :] for n in range(4)])
    total[:, units:] = dot(cotangent, rows([k0[0], c0[0], k1[0], c1[0]]), ((0,), (0,)))
    if fast:
        split_rows(ids, total, slice(None), outs[0], outs[1], ids[9])
    else:
        outs[0][...] = total[...]


def feed_grad(ids, own, other, got_own, got_other, cotangent, fast):
    _, rows, units = own[0].shape
    width = cotangent.shape[1]
    if fast:
        outs = [shape((4, width // 8, 2 * units), F32), shape((4, width // 8, 2 * units), BF)]
    else:
        outs = [shape((width, 2 * units), F32)]
    return call(
        functools.partial(feed_grad_kernel, fast=fast),
        "feed_grad",
        ids,
        (*own, *other, got_own, got_other, cotangent),
        outs,
        mib=24,
        us=7,
        scratch=[pltpu.VMEM((width, 2 * units), F32)],
    )


def head_grad_kernel(ids, normed_ref, grads_ref, l0, l2, l1, l3, a0, a1, a2, a3, *outs, fast):
    total, turned = outs[-2:]
    n = a0.shape[0]
    normed = jnp.concatenate([normed_ref[quarter_of(ids[k], a0.shape[1]), :] for k in range(4)], axis=0)
    for part in range(3):
        left = jnp.concatenate([grads_ref[k, part] for k in range(4)], axis=1)
        total[part * n : (part + 1) * n, :] = dot(left, normed)
    low = jnp.concatenate([r[...] for r in (l0, l1, l2, l3)], axis=0)
    total[3 * n :, :] = dot(jnp.concatenate([r[...] for r in (a0, a1, a2, a3)], axis=1), low)
    turned[...] = total[...].T
    if fast:
        split_rows(ids, turned, slice(None), outs[0], outs[1], ids[9])
    else:
        outs[0][...] = turned[...]


def head_grad(ids, normed, grads, low, low_got, attended, fast):
    seq, width = normed.shape
    n = grads.shape[2]
    if fast:
        outs = [shape((4, width // 8, 4 * n), F32), shape((4, width // 8, 4 * n), BF)]
    else:
        outs = [shape((width, 4 * n), F32)]
    return call(
        functools.partial(head_grad_kernel, fast=fast),
        "head_grad",
        ids,
        (normed, grads, *low, *low_got, *attended),
        outs,
        mib=18,
        us=0.01,
        scratch=[pltpu.VMEM((4 * n, width), F32), pltpu.VMEM((width, 4 * n), F32)],
    )


def pair_kernel(ids, *refs):
    pairs, outs = refs[:-4], refs[-4:]
    for k, o_ref in enumerate(outs):
        at = ids[4 + k]
        start = 0
        for keep_ref, got_ref in zip(pairs[::2], pairs[1::2]):
            n = keep_ref.shape[2]
            o_ref[:, start : start + n] = (keep_ref[at] + got_ref[at].astype(F32)).astype(o_ref.dtype)
            start += n


def pair_sum(ids, *arrays):
    size = arrays[0].shape[1]
    n = sum(a.shape[2] for a in arrays[::2])
    outs = [shape((size, n), F32)] + [shape((size, n), BF)] * 3
    return call(pair_kernel, "pair_sum", ids, arrays, outs, mib=16, us=0.01)


def feed_final_kernel(a0, a1, a2, a3, up_ref, down_ref):
    total = a0[...] + a1[...].astype(F32) + a2[...].astype(F32) + a3[...].astype(F32)
    units = up_ref.shape[1]
    up_ref[...] = total[:, :units]
    down_ref[...] = total[:, units:]


def head_final_kernel(a0, a1, a2, a3, one_ref, two_ref, q_ref, k_ref, v_ref, o_ref, *smalls):
    total = a0[...] + a1[...].astype(F32) + a2[...].astype(F32) + a3[...].astype(F32)
    n = q_ref.shape[1]
    for at, goal in enumerate((q_ref, k_ref, v_ref)):
        goal[...] = total[:, at * n : (at + 1) * n]
    o_ref[...] = total[:, 3 * n :].T
    *tables, gains_ref = smalls
    total = one_ref[...] + two_ref[...]
    parts = gains_ref.shape[1] // 128
    for slot in range(2):
        for part in range(parts):
            at = slot * parts + part
            gains_ref[slot : slot + 1, part * 128 : part * 128 + 128] = total[at : at + 1]
    at, bins = 2 * parts, tables[0].shape[1]
    for goal in tables:
        goal[...] = total[at : at + HEADS, :bins]
        at += HEADS


def final(kernel, arrays, done, outs):
    arrays = [after(arrays[0], done)] + arrays[1:]
    return pl.pallas_call(
        kernel,
        grid=(1,),
        in_specs=[VMEM] * len(arrays),
        out_specs=jax.tree.map(lambda o: whole(o.shape), outs),
        out_shape=outs,
        compiler_params=params(16),
        cost_estimate=cost(5 if kernel is feed_final_kernel else 0.01),
        name=kernel.__name__[:-7],
    )(*arrays)


def swap(array, axis, size, bits):
    return lax.ppermute(array, axis, [(i, i ^ bits) for i in range(size)])


def after(array, *others):
    return lax.optimization_barrier((array, others))[0]


def local(
    inputs, page_feat, page_onehot, lengths, hor_pos, ver_pos, norm1_gain, w_query, w_key, w_value,
    rel_table, hor_table, ver_table, w_output, norm2_gain, w_up, w_down, cotangent, *, dp,
):
    seq, width = inputs.shape
    fast = dp == 8
    over = functools.partial(swap, axis="mp", size=4)
    m = lax.axis_index("mp").astype(I32)
    d = lax.axis_index("dp").astype(I32)
    k4 = jnp.arange(4, dtype=I32)
    spot = lambda who: (who & 1) * 2 + (who >> 1)
    ids = jnp.concatenate([
        spot(m ^ k4),
        (d >> 1) ^ k4,
        lengths[:1],
        (d & 1)[None],
    ])
    gain_one, gain_two = norm1_gain, norm2_gain
    feats = page_feat[0]
    hor, ver = hor_pos[None], ver_pos[None]
    tables = (rel_table, hor_table, ver_table)
    pages = page_onehot.T
    weights = [w_query.T, w_key.T, w_value.T]

    wo_y, wo_core = over(w_output, bits=2), over(w_output, bits=1)
    normed1, queries, keys, values = project(ids, inputs, pages, feats, gain_one, *weights)
    w_outputs = [w_output, wo_core, wo_y, over(after(wo_y, normed1), bits=1)]
    ups = [w_up, over(after(w_up, normed1), bits=1)]
    downs = [w_down, over(after(w_down, normed1), bits=1)]

    (e_a, att0, att1, inverse_a, out_a), lookups = attend(ids, queries, keys, values, hor, ver, tables, None)
    from_y, from_yc, own1 = over(att0, bits=2), over(att1, bits=3), over(att1, bits=1)
    ver_late = after(ver, att0, w_outputs[3], ups[1], downs[1])
    (e_b, att2, att3, inverse_b, out_b), _ = attend(ids, queries, keys, values, hor, ver_late, tables, lookups)
    attended = [att0, att1, att2, att3]
    for_other = [att2, over(att3, bits=1), from_y, from_yc]
    for_own = [att0, own1, over(att2, bits=2), over(att3, bits=3)]

    around = functools.partial(swap, axis="dp", size=dp)
    to_z = lambda parts: [parts[0]] + [around(part, bits=2 * k) for k, part in zip((1, 2, 3), parts[1:])]
    size = width // dp
    n = w_query.shape[1]
    units = w_up.shape[1]
    fixed = (inputs, pages, feats, gain_two, cotangent)
    x_keep, x_send, x_mixed, x_grad, x_ffn = feed(ids, False, *fixed, for_other, w_outputs, ups, downs)
    got_own, x_got = over(x_grad, bits=2), over(x_send, bits=1)
    for_own[0] = after(att0, x_ffn)
    m_keep, m_send, mixed, m_grad, m_ffn = feed(ids, True, *fixed, for_own, w_outputs, ups, downs)
    got_other, m_got = over(m_grad, bits=2), over(after(m_send, x_got), bits=1)
    own_grad = add(ids, m_grad, got_own)

    feed_grads = feed_grad(ids, (after(m_keep, own_grad), m_send), (x_keep, x_send), m_got, x_got, cotangent, fast)
    feed_got = around(feed_grads[1], bits=1) if fast else ids
    places_at, both = places_of(ids, after(hor, feed_grads[0]), ver)
    grad_mixed, ga, core_send, *low, gain_two_part = mid(
        ids, (after(own_grad, places_at), mixed), (x_grad, got_other, x_mixed), gain_two, cotangent, w_outputs[:2]
    )
    core_got = over(core_send, bits=1)
    sent_ffn = over(after(x_ffn, got_other, places_at), bits=2)

    halves = ((e_a, e_b), (inverse_a, inverse_b), (out_a, out_b))
    scores_a, dq0, dq2, key_sum, value_sum, near, far = back(ids, halves, queries, keys, values, ga, None)
    scores_b, grads, near, far = back(
        ids, halves, queries, keys, values, after(core_got, dq0), (key_sum, value_sum, near, far, dq0, dq2)
    )
    low_got = [over(part, bits=1) for part in low]
    to_core = terms_send(ids, weights, after(grads, sent_ffn))
    got_terms = [over(part, bits=1) for part in to_core]
    head_grads = head_grad(ids, normed1, after(grads, to_core[0]), low, low_got, attended, fast)
    own_terms, other_terms = terms_keep(ids, weights, after(grads, head_grads[0]), got_terms)
    sent_terms = over(other_terms, bits=2)

    hor_a = table_grads(ids, True, (0,), scores_a, places_at, after(both, own_terms))
    done = hor_a
    if fast:
        feed_parts = to_z(pair_sum(ids, after(feed_grads[0], done), feed_got))
        done = feed_parts[0]
    head_got = around(after(head_grads[1], done), bits=1) if fast else ids
    rows, gains = last(
        ids, after(own_terms, done), sent_terms, inputs, pages, feats, gain_one, grad_mixed, gain_two_part,
        mixed, m_ffn, sent_ffn,
    )
    rows_y, rows_core = over(rows, bits=2), over(rows, bits=1)
    ver_a = table_grads(ids, True, (1,), scores_a, places_at, after(both, rows))
    gains = after(gains, ver_a) + over(gains, bits=1)
    got_gains = over(gains, bits=2)
    late = table_grads(ids, False, (0, 1), scores_b, places_at, after(both, gains, head_got), (near, far))

    small = pack(ids, gains, got_gains, hor_a, ver_a, late)
    if fast:
        got = around(small, bits=1)
        grad_up, grad_down = final(feed_final_kernel, feed_parts, small, [shape((size, units), F32)] * 2)
        head_parts = to_z(pair_sum(ids, after(head_grads[0], grad_up), head_got))
        small = after(small, head_parts[0]) + got
        got = around(small, bits=2)
        quarters = [rows, rows_core, rows_y, over(after(rows_y, grad_up), bits=1)]
        outputs = join(ids, [after(rows, small)] + quarters[1:], 0, BF)
        grad_inputs, grad_feats = join(ids, [after(rows, outputs)] + quarters[1:], 1, F32, pages)
        small = after(small, grad_feats) + got
        bins = rel_table.shape[1]
        outs = [shape((size, n), F32)] * 3 + [shape((n, size), F32)] + [shape((HEADS, bins), F32)] * 3
        *found, gain_sums = final(
            head_final_kernel, head_parts + [small, around(small, bits=4)], grad_feats, outs + [shape((2, width), F32)]
        )
        grad_query, grad_key, grad_value, grad_output, grad_rel, grad_hor, grad_ver = found
    else:
        quarters = [rows, rows_core, rows_y, over(rows_y, bits=1)]
        outputs = join(ids, quarters, 0, BF)
        grad_inputs, grad_feats = join(ids, quarters, 1, F32, pages)
        small = lax.psum(small, "dp")
        scatter = lambda a: lax.psum_scatter(a[0], "dp", scatter_dimension=0, tiled=True)
        grad_feed, heads = scatter(feed_grads), scatter(head_grads)
        grad_up, grad_down = grad_feed[:, :units], grad_feed[:, units:]
        grad_query, grad_key, grad_value = heads[:, :n], heads[:, n : 2 * n], heads[:, 2 * n : 3 * n]
        grad_output = heads[:, 3 * n :].T
        gain_sums = small[: width // 128 * 2].reshape(2, width)
        table_sums = small[width // 128 * 2 :, : rel_table.shape[1]]
        grad_rel, grad_hor, grad_ver = (table_sums[at : at + HEADS] for at in range(0, 3 * HEADS, HEADS))
    gain_sums = lax.dynamic_slice(gain_sums, (0, d * size), (2, size))
    return (
        outputs, grad_inputs, grad_feats[None], gain_sums[0], grad_query, grad_key, grad_value,
        grad_rel, grad_hor, grad_ver, grad_output, gain_sums[1], grad_up, grad_down.T,
    )


def solution(mesh):
    return jax.shard_map(
        functools.partial(local, dp=mesh.shape["dp"]),
        mesh=mesh,
        in_specs=(
            P("dp", None),
            P("dp", None, None),
            P("dp", None),
            P("dp"),
            P("dp"),
            P("dp"),
            P(),
            P(None, "mp"),
            P(None, "mp"),
            P(None, "mp"),
            P("mp", None),
            P("mp", None),
            P("mp", None),
            P("mp", None),
            P(),
            P(None, "mp"),
            P("mp", None),
            P("dp", None),
        ),
        out_specs=(
            P("dp", None),
            P("dp", None),
            P("dp", None, None),
            P("dp"),
            P("dp", "mp"),
            P("dp", "mp"),
            P("dp", "mp"),
            P("mp", None),
            P("mp", None),
            P("mp", None),
            P("mp", "dp"),
            P("dp"),
            P("dp", "mp"),
            P("mp", "dp"),
        ),
        check_vma=False,
    )
```

```python
import functools

import jax
import jax.numpy as jnp
import numpy as np
from jax import lax
from jax.experimental import pallas as pl
from jax.experimental.pallas import tpu as pltpu
from jax.sharding import PartitionSpec as P

EPS = 1e-06
THRESHOLDS = (12, 16, 23, 32, 46, 64, 91)
FAR = 91
HEADS = 3
HD = 64
PAD = 128
MARKS = 72
NEAR = 40
TILES = NEAR + 2
SPAN = 384
LOW = 92
TOP = 311
BF = jnp.bfloat16
F32 = jnp.float32
I32 = jnp.int32
FEED_CHUNK = 256
PLACES = 1024
TABLES_MIB = 18
GELU_C = float(np.sqrt(2.0 / np.pi))


def dot(left, right, dims=((1,), (0,))):
    return lax.dot_general(left, right, (dims, ((), ())), preferred_element_type=F32)


def bucket(delta):
    magnitude = jnp.abs(delta)
    coarse = 8 + sum((magnitude >= limit).astype(I32) for limit in THRESHOLDS)
    return jnp.where(magnitude < 8, magnitude, coarse) + 16 * (delta > 0).astype(I32)


def params(mib):
    return pltpu.CompilerParams(vmem_limit_bytes=mib * 2**20)


def cost(microseconds):
    return pl.CostEstimate(flops=int(1.15e9 * microseconds), bytes_accessed=1, transcendentals=0)


def shape(dims, dtype):
    return jax.ShapeDtypeStruct(dims, dtype)


def whole(dims):
    return pl.BlockSpec(dims, lambda *a: (0,) * len(dims))


VMEM = pl.BlockSpec(memory_space=pltpu.VMEM)


def call(kernel, name, ids, arrays, outs, *, mib, us, scratch=()):
    return pl.pallas_call(
        kernel,
        grid_spec=pltpu.PrefetchScalarGridSpec(
            num_scalar_prefetch=1,
            grid=(1,),
            in_specs=[VMEM] * len(arrays),
            out_specs=jax.tree.map(lambda _: VMEM, outs),
            scratch_shapes=list(scratch),
        ),
        out_shape=outs,
        compiler_params=params(mib),
        cost_estimate=cost(us),
        name=name,
    )(ids, *arrays)


def quarter_of(place, size):
    return pl.ds(pl.multiple_of(place * size, 128), size)


def hidden_rows(inputs, pages, feats):
    return inputs.astype(F32) + dot(pages.astype(F32).astype(BF), feats, ((0,), (0,)))


def unit_rows(field):
    factor = lax.rsqrt(jnp.mean(field * field, axis=-1, keepdims=True) + EPS)
    return field * factor, factor


def project_kernel(ids, x_ref, page_ref, feat_ref, gain_ref, wq_ref, wk_ref, wv_ref, n_ref, q_ref, k_ref, v_ref):
    rows = 512

    def block_of(step, carry):
        here = quarter_of(step, rows)
        unit, _ = unit_rows(hidden_rows(x_ref[here, :], page_ref[:, here], feat_ref[...]))
        normed = (unit * gain_ref[...].astype(F32).reshape(1, -1)).astype(BF)
        n_ref[here, :] = normed
        lane = lax.broadcasted_iota(I32, (rows, PAD), 1)
        row = lax.broadcasted_iota(I32, (rows, PAD), 0) + step * rows
        masked = jnp.where((lane == HD) & (row >= ids[8]), -1e30, 0.0)
        block = lane - MARKS
        far_left = (block >= 0) & (block < 8) & (row < 128 * block - 96)
        far_right = (block >= 8) & (block < 16) & (row >= 128 * (block - 8) + 224)
        masked = jnp.where(far_left | far_right, 1.0, masked)
        query_extra = jnp.where(lane == HD, 1.0, 0.0)
        value_extra = jnp.where((lane == HD) | (lane == HD + 1), 1.0, 0.0)
        for out_ref, w_ref, extra, scale in (
            (q_ref, wq_ref, query_extra, 0.125),
            (k_ref, wk_ref, masked, None),
            (v_ref, wv_ref, value_extra, None),
        ):
            full = dot(normed, w_ref[...], ((1,), (1,)))
            if scale is not None:
                full = full * scale
            pair = full[:, :PAD]
            last = jnp.concatenate([full[:, PAD:], jnp.zeros((rows, PAD - HD), F32)], axis=1)
            heads = (pair, pltpu.roll(pair, HD, 1), last)
            for head in range(HEADS):
                out_ref[here, head * PAD : (head + 1) * PAD] = jnp.where(lane < HD, heads[head], extra).astype(BF)
        return carry

    lax.fori_loop(0, x_ref.shape[0] // rows, block_of, 0)


def project(ids, *arrays):
    seq, width = arrays[0].shape
    outs = [shape((seq, width), BF)] + [shape((seq, HEADS * PAD), BF)] * 3
    return call(project_kernel, "project", ids, arrays, outs, mib=16, us=7)


def place(delta):
    magnitude = jnp.abs(delta)
    coarse = jnp.minimum(25 - lax.clz(delta * delta), 7)
    exact = magnitude < 8
    return jnp.where(exact, magnitude, coarse), exact, delta > 0


def look(table_ref, row, where):
    index, exact, after = where
    found = [jnp.take_along_axis(table_ref[row, part], index, axis=0) for part in range(4)]
    return jnp.where(after, jnp.where(exact, found[2], found[3]), jnp.where(exact, found[0], found[1]))


def tile_delta(tile):
    lane = lax.broadcasted_iota(I32, (8, 128), 1)
    sub = lax.broadcasted_iota(I32, (8, 128), 0)
    delta = 8 * (tile - 13) + sub - lane
    if tile == 0:
        delta = jnp.full_like(delta, -1000)
    if tile == TILES - 1:
        delta = jnp.full_like(delta, 1000)
    return delta


def attend_kernel(*refs, first, chunk):
    ids, q_ref, k_ref, v_ref, hor_ref, ver_ref = refs[:6]
    if first:
        hor_all, ver_all, rel_table, hor_table, ver_table, e_ref, att0, att1, inv_ref, out_ref = refs[6:16]
        rel_ref, t8_ref, hor_col, ver_col, s_ref = refs[16:]
    else:
        rel_ref, t8_ref, hor_col, ver_col, e_ref, att0, att1, inv_ref, out_ref, s_ref = refs[6:]
    seq = k_ref.shape[0]
    width = seq // 4
    lanes = width // 128

    if first:
        for all_ref, col_ref in ((hor_all, hor_col), (ver_all, ver_col)):
            for b in range(seq // 128):
                cols = slice(128 * b, 128 * b + 128)
                spread = jnp.broadcast_to(all_ref[:, cols].astype(F32), (128, 128))
                col_ref[cols, :] = spread.T.astype(I32)
        lane = lax.broadcasted_iota(I32, (8, 32), 1)
        sub = lax.broadcasted_iota(I32, (8, 32), 0)
        for axis, table_ref in enumerate((rel_table, hor_table, ver_table)):
            table = table_ref[...].astype(F32)
            for head in range(HEADS):
                row = jnp.broadcast_to(table[head : head + 1], (8, 32))
                for part in range(4):
                    entries = jnp.sum(jnp.where(lane == sub + 8 * part, row, 0.0), axis=1, keepdims=True)
                    t8_ref[axis * HEADS + head, part] = jnp.broadcast_to(entries, (8, 128))
        for tile in range(TILES):
            where = place(tile_delta(tile))
            for head in range(HEADS):
                rel_ref[head, tile] = look(t8_ref, head, where)

    def products(here):
        queries = q_ref[here, :]
        for head in range(HEADS):
            cols = slice(head * PAD, (head + 1) * PAD)
            s_ref[head] = dot(k_ref[:, cols], queries[:, cols], ((1,), (1,)))

    def biases(place_of, here):
        hor_row, ver_row = hor_ref[:, here], ver_ref[:, here]
        hor = [jnp.broadcast_to(hor_row[:, 128 * l : 128 * l + 128], (8, 128)) for l in range(lanes)]
        ver = [jnp.broadcast_to(ver_row[:, 128 * l : 128 * l + 128], (8, 128)) for l in range(lanes)]
        block = place_of * lanes

        def add_bias(c, tops):
            tops = list(tops)
            base = pl.multiple_of(c * chunk, chunk)
            for g in range(chunk // 8):
                rows = pl.ds(pl.multiple_of(base + 8 * g, 8), 8)
                hor_keys, ver_keys = hor_col[rows, :], ver_col[rows, :]
                for l in range(lanes):
                    cols = pl.ds(128 * l, 128)
                    hor_at, ver_at = place(hor_keys - hor[l]), place(ver_keys - ver[l])
                    tile = jnp.clip(c * (chunk // 8) + g - 16 * (block + l) + 13, 0, TILES - 1)
                    for head in range(HEADS):
                        s = s_ref[head, rows, cols] + rel_ref[head, tile]
                        s = s + (look(t8_ref, HEADS + head, hor_at) + look(t8_ref, 2 * HEADS + head, ver_at))
                        s_ref[head, rows, cols] = s
                        tops[head * lanes + l] = jnp.maximum(tops[head * lanes + l], s)
            return tuple(tops)

        tops = lax.fori_loop(
            0, seq // chunk, add_bias, tuple(jnp.full((8, 128), -1e30, F32) for _ in range(HEADS * lanes))
        )
        return [jnp.broadcast_to(jnp.max(top, axis=0, keepdims=True), (16, 128)) for top in tops]

    def attended(part, peaks):
        mine = quarter_of(part, width)
        for head in range(HEADS):
            for g in range(seq // 16):
                rows = slice(16 * g, 16 * g + 16)
                for l in range(lanes):
                    cols = slice(128 * l, 128 * l + 128)
                    into = pl.ds(pl.multiple_of(part * width + 128 * l, 128), 128)
                    e_ref[head, rows, into] = jnp.exp(s_ref[head, rows, cols] - peaks[head * lanes + l]).astype(BF)
            total = dot(v_ref[:, head * PAD : (head + 1) * PAD], e_ref[head, :, mine], ((0,), (0,)))
            inverse = 1.0 / total[HD : HD + 1, :]
            inv_ref[head : head + 1, mine] = inverse
            out_ref[head * HD : (head + 1) * HD, mine] = total[:HD] * inverse
        for at, att_ref in enumerate((att0, att1)):

            @pl.when(part == at)
            def _(att_ref=att_ref):
                att_ref[...] = out_ref[:, mine].astype(BF)

    def quarter(part, carry):
        place_of = ids[(0 if first else 2) + part]
        here = quarter_of(place_of, width)
        products(here)
        attended(part, biases(place_of, here))
        return carry

    lax.fori_loop(0, 2, quarter, 0)


def attend(ids, queries, keys, values, hor, ver, tables, lookups):
    seq = queries.shape[0]
    width = seq // 4
    first = lookups is None
    columns = HEADS * HD
    made = [
        shape((HEADS, TILES, 8, 128), F32), shape((3 * HEADS, 4, 8, 128), F32), shape((seq, 128), I32), shape((seq, 128), I32)
    ]
    extra = (hor, ver, *tables) if first else tuple(lookups)
    outs = [
        shape((HEADS, seq, 2 * width), BF), shape((columns, width), BF), shape((columns, width), BF),
        shape((HEADS, 2 * width), F32), shape((columns, 2 * width), F32),
    ]
    found = call(
        functools.partial(attend_kernel, first=first, chunk=128),
        "attend_first" if first else "attend_last",
        ids,
        (queries, keys, values, hor, ver, *extra),
        outs + made if first else outs,
        mib=14,
        us=14,
        scratch=[pltpu.VMEM((HEADS, seq, width), F32)],
    )
    return found[:5], found[5:]


def feed_kernel(
    ids, x_ref, page_ref, feat_ref, gain_ref, cot_ref, a0, a1, a2, a3, o0, o1, o2, o3, u0, u1, d0, d1,
    keep_ref, send_ref, mixed_ref, grad_ref, ffn_ref, *, slot,
):
    here = quarter_of(ids[slot], mixed_ref.shape[0])
    cotangent = cot_ref[here, :]
    mixed = hidden_rows(x_ref[here, :], page_ref[:, here], feat_ref[...])
    for a_ref, o_ref in ((a0, o0), (a1, o1), (a2, o2), (a3, o3)):
        mixed = mixed + dot(a_ref[...], o_ref[...], ((0,), (0,)))
    mixed_ref[...] = mixed
    unit, _ = unit_rows(mixed)
    normed = (unit * gain_ref[...].astype(F32).reshape(1, -1)).astype(BF)
    send_ref[2] = normed
    units = u0.shape[1]
    for u_ref, d_ref, goal in ((u0, d0, keep_ref), (u1, d1, send_ref)):
        for at in range(0, units, FEED_CHUNK):
            cols = slice(at, at + FEED_CHUNK)
            upward = dot(normed, u_ref[:, cols])
            square = upward * upward
            tanh = jnp.tanh(GELU_C * upward * (1.0 + 0.044715 * square))
            lifted = 0.5 * (1.0 + tanh)
            activated = (upward * lifted).astype(BF)
            slope = lifted + 0.5 * upward * (1.0 - tanh * tanh) * (GELU_C * (1.0 + 3 * 0.044715 * square))
            grad_up = (dot(cotangent, d_ref[cols, :], ((1,), (1,))) * slope).astype(BF)
            goal[0, :, cols] = activated
            goal[1, :, cols] = grad_up
    ffn = dot(keep_ref[0], d0[...]) + dot(send_ref[0], d1[...])
    ffn_ref[...] = ffn.astype(ffn_ref.dtype)
    grad = dot(keep_ref[1], u0[...], ((1,), (1,))) + dot(send_ref[1], u1[...], ((1,), (1,)))
    grad_ref[...] = grad.astype(grad_ref.dtype)


def feed(ids, own, inputs, onehot, feats, gain, cotangent, attended, w_outputs, ups, downs):
    seq, width = inputs.shape
    rows = seq // 4
    units = ups[0].shape[1]
    kept = F32 if own else BF
    outs = [
        shape((2, rows, units), BF), shape((3, rows, width), BF), shape((rows, width), F32),
        shape((rows, width), BF), shape((rows, width), kept),
    ]
    return call(
        functools.partial(feed_kernel, slot=0 if own else 2),
        "feed_own" if own else "feed_other",
        ids,
        (inputs, onehot, feats, gain, cotangent, *attended, *w_outputs, *ups, *downs),
        outs,
        mib=16,
        us=20 if own else 10,
    )


def add_kernel(ids, one_ref, two_ref, out_ref):
    out_ref[...] = one_ref[...].astype(F32) + two_ref[...].astype(F32)


def add(ids, one, two):
    return call(add_kernel, "add", ids, (one, two), shape(one.shape, F32), mib=8, us=20)


def mid_kernel(
    ids, own_grad, own_mixed, other_grad, other_got, other_mixed, cot_ref, gain_ref, o0, o1,
    grad_ref, own_ref, core_ref, low_own, low_other, part_ref,
):
    rows = own_grad.shape[0]
    other = other_grad[...].astype(F32) + other_got[...].astype(F32)
    for at, (grad_normed, mixed_ref) in enumerate(((own_grad[...], own_mixed), (other, other_mixed))):
        unit, factor = unit_rows(mixed_ref[...])
        scaled = grad_normed * gain_ref[...].astype(F32).reshape(1, -1)
        grad = factor * (scaled - unit * jnp.mean(scaled * unit, axis=-1, keepdims=True))
        grad = cot_ref[quarter_of(ids[2 * at], rows), :].astype(F32) + grad
        low = grad.astype(BF)
        (low_own, low_other)[at][...] = low
        if at == 0:
            grad_ref[...] = grad
            part_ref[...] = jnp.sum(grad_normed * unit, axis=0, keepdims=True)
        for o_ref, goal in ((o0, own_ref), (o1, core_ref)):
            goal[:, at * rows : (at + 1) * rows] = dot(o_ref[...], low, ((1,), (1,))).astype(BF)


def mid(ids, own, other, gain, cotangent, w_outputs):
    rows, width = own[0].shape
    columns = HEADS * HD
    outs = [
        shape((rows, width), F32), shape((columns, 2 * rows), BF), shape((columns, 2 * rows), BF), shape((rows, width), BF),
        shape((rows, width), BF), shape((1, width), F32),
    ]
    arrays = (*own, *other, cotangent, gain, *w_outputs)
    return call(mid_kernel, "mid", ids, arrays, outs, mib=16, us=0.01)


def back_kernel(*refs, first):
    ids, ea_ref, eb_ref, inv_a, inv_b, out_a, out_b, q_ref, k_ref, v_ref, grad_ref = refs[:11]
    refs = refs[11:]
    if first:
        ds_ref, dqa_ref, dqb_ref, key_ref, value_ref, near_ref, far_ref, x_ref = refs
    else:
        key_in, value_in, near_in, far_in, dqa_in, dqb_in = refs[:6]
        ds_ref, all_ref, near_ref, far_ref, x_ref = refs[6:]
    seq = k_ref.shape[0]
    width = seq // 4
    both = 2 * width
    lanes = width // 128
    base = 0 if first else 1
    sub = lax.broadcasted_iota(I32, (HD, both), 0)
    blocks = [ids[base + 2 * (l // lanes)] * lanes + l % lanes for l in range(2 * lanes)]
    mine = slice(base * width, (base + 1) * width)
    here = [quarter_of(ids[base + 2 * n], width) for n in range(2)]
    beside = lambda one, two: jnp.concatenate([one, two], axis=1)
    spot = lax.broadcasted_iota(I32, (8, 128), 0)

    def one_head(head, carry):
        cols = quarter_of(head, PAD)
        rows = pl.ds(pl.multiple_of(head * HD, HD), HD)
        grad = grad_ref[rows, :].astype(F32)
        grad = (grad * beside(inv_a[pl.ds(head, 1), mine], inv_b[pl.ds(head, 1), mine])).astype(BF).astype(F32)
        inner = jnp.sum(grad * beside(out_a[rows, mine], out_b[rows, mine]), axis=0, keepdims=True)
        high = inner.astype(BF).astype(F32)
        extra = jnp.where(sub == 0, -high, jnp.where(sub == 1, high - inner, 0.0))
        right = jnp.concatenate([grad, extra], axis=0).astype(BF)
        x_ref[...] = dot(v_ref[:, cols], right)
        value = dot(beside(ea_ref[head, :, mine], eb_ref[head, :, mine]), right, ((1,), (1,)))
        for c in range(seq // 16):
            at = slice(16 * c, 16 * c + 16)
            found = beside(ea_ref[head, at, mine], eb_ref[head, at, mine]).astype(F32)
            ds_ref[head, at, :] = (found * x_ref[at, :]).astype(BF)
        grad = ds_ref[head]
        key = dot(grad, jnp.concatenate([q_ref[at, cols] for at in here], axis=0))
        query = dot(k_ref[:, cols], grad, ((0,), (0,)))
        query_a = (query[:HD, :width] * 0.125).astype(BF)
        query_b = (query[:HD, width:] * 0.125).astype(BF)

        for g in range(NEAR // 2):
            total = None if first else near_in[head, 16 * g : 16 * g + 16]
            for l, block in enumerate(blocks):
                start = 128 * block - 96 + 16 * g
                inside = (start >= 0) & (start < seq)
                at = pl.ds(pl.multiple_of(jnp.clip(start, 0, seq - 16), 16), 16)
                found = ds_ref[head, at, 128 * l : 128 * l + 128].astype(F32)
                found = jnp.where(inside, found, 0.0)
                total = found if total is None else total + found
            near_ref[head, 16 * g : 16 * g + 16] = total
        for side in range(2):
            total = None if first else far_in[head, 8 * side : 8 * side + 8]
            for l, block in enumerate(blocks):
                marks = query[MARKS + 8 * side : MARKS + 8 * side + 8, 128 * l : 128 * l + 128]
                marks = jnp.where(spot == block, marks, 0.0)
                total = marks if total is None else total + marks
            far_ref[head, 8 * side : 8 * side + 8] = total

        if first:
            key_ref[:, cols] = key
            value_ref[:, cols] = value
            dqa_ref[rows, :] = query_a
            dqb_ref[rows, :] = query_b
        else:
            for k, found in enumerate((dqa_in[rows, :], query_a, dqb_in[rows, :], query_b)):
                all_ref[k, 0, rows, :] = found
            for part, acc in ((1, key_in[:, cols] + key), (2, value_in[:, cols] + value)):
                turned = acc.T[:HD].astype(BF)
                for q in range(4):
                    k = sum((jnp.where(ids[n] == q, n, 0) for n in range(1, 4)))
                    all_ref[k, part, rows, :] = turned[:, q * width : (q + 1) * width]
        return carry

    lax.fori_loop(0, HEADS, one_head, 0)


def back(ids, attended, queries, keys, values, grads, carried):
    seq, wide = queries.shape
    width = seq // 4
    first = carried is None
    columns = HEADS * HD
    queried = [shape((columns, width), BF)] * 2
    sums = [shape((seq, wide), F32)] * 2
    rel = [shape((HEADS, 8 * NEAR, 128), F32), shape((HEADS, 16, 128), F32)]
    outs = [shape((HEADS, seq, 2 * width), BF)]
    outs += queried + sums if first else [shape((4, 3, columns, width), BF)]
    outs += rel
    arrays = (*attended[0], *attended[1], *attended[2], queries, keys, values, grads, *(() if first else carried))
    return call(
        functools.partial(back_kernel, first=first),
        "back_first" if first else "back_last",
        ids,
        arrays,
        outs,
        mib=16,
        us=2 if first else 0.01,
        scratch=[pltpu.VMEM((seq, 2 * width), F32)],
    )


def places_kernel(ids, hor_ref, ver_ref, at_ref, both_ref):
    _, places, seq = at_ref.shape
    both_ref[0:1, :] = hor_ref[...]
    both_ref[1:2, :] = ver_ref[...]
    for axis, keys_ref in enumerate((hor_ref, ver_ref)):

        def block(b, carry, axis=axis, keys_ref=keys_ref):
            spot = lax.broadcasted_iota(I32, (128, seq), 0) + 128 * b
            at_ref[axis, quarter_of(b, 128), :] = jnp.where(spot == keys_ref[...], 1.0, 0.0).astype(BF)
            return carry

        lax.fori_loop(0, places // 128, block, 0)


def places_of(ids, hor, ver):
    seq = hor.shape[1]
    outs = [shape((2, PLACES, seq), BF), shape((2, seq), I32)]
    return call(places_kernel, "places", ids, (hor, ver), outs, mib=8, us=0.01)


def tables_kernel(ids, s_ref, e_ref, q_ref, *refs, base, axes):
    diagonals = refs[:-4]
    out_ref, left_ref, right_ref, found_ref = refs[-4:]
    width = s_ref.shape[2]
    groups = e_ref.shape[1] // 128

    def to_buckets(sums, delta):
        spot = lax.broadcasted_iota(I32, (32, sums.shape[1]), 0)
        return jnp.sum(jnp.where(bucket(delta) == spot, sums, 0.0), axis=1, keepdims=True)

    lane = lax.broadcasted_iota(I32, (1, 512), 1)
    spread = lax.broadcasted_iota(I32, (32, 128), 1)

    def heads_rows(column_of):
        return sum(jnp.where(spread == head, column_of(head), 0.0) for head in range(HEADS)).T[:8]

    def coordinate(axis, out_at):
        query = jnp.concatenate([q_ref[pl.ds(axis, 1), quarter_of(ids[base + n], width // 2)] for n in (0, 2)], axis=1)
        column = lax.broadcasted_iota(I32, (SPAN, width), 0)
        for b in range(groups):
            window = jnp.clip(128 * b + TOP - LOW - query, 0, TOP)
            right_ref[:, b * width : (b + 1) * width] = jnp.where(column == window, 1.0, 0.0).astype(BF)
        for head in range(HEADS):
            moved = dot(e_ref[axis], s_ref[head]).astype(BF)
            for b in range(groups):
                left_ref[head * 128 : head * 128 + 128, b * width : (b + 1) * width] = moved[128 * b : 128 * b + 128]
        found_ref[...] = dot(left_ref[...], right_ref[...], ((1,), (1,)))

        def column_of(head):
            grid = jnp.concatenate([found_ref[quarter_of(head, 128), :], jnp.zeros((128, 512 - SPAN), F32)], axis=1)
            grid = pltpu.roll(grid, 0, 1, stride=1, stride_axis=0)
            return to_buckets(jnp.sum(grid, axis=0, keepdims=True), lane + LOW - TOP)

        out_ref[out_at] = heads_rows(column_of)

    if len(axes) == 1:
        coordinate(axes[0], 0)
        return

    def one(axis, carry):
        coordinate(axis, axis)
        return carry

    lax.fori_loop(0, 2, one, 0)
    near_ref, far_ref = diagonals
    flip = 7 - lax.broadcasted_iota(I32, (8, 128), 0)
    spot = lax.broadcasted_iota(I32, (32, 1), 0)

    def near_column(head):
        near = [jnp.take_along_axis(near_ref[head, 8 * t : 8 * t + 8], flip, axis=0) for t in reversed(range(NEAR))]
        grid = jnp.concatenate(near, axis=0)
        grid = jnp.concatenate([grid, jnp.zeros((8 * NEAR, 384), F32)], axis=1)
        grid = pltpu.roll(grid, 0, 1, stride=1, stride_axis=0)
        near_sums = to_buckets(jnp.sum(grid, axis=0, keepdims=True), 8 * NEAR - 1 - 8 * 12 - lane)
        left = jnp.sum(jnp.sum(far_ref[head, :8], axis=0, keepdims=True), axis=1, keepdims=True)
        right = jnp.sum(jnp.sum(far_ref[head, 8:], axis=0, keepdims=True), axis=1, keepdims=True)
        return near_sums + jnp.where(spot == 15, left, 0.0) + jnp.where(spot == 31, right, 0.0)

    out_ref[2] = heads_rows(near_column)


def table_grads(ids, first, axes, scores, places, positions, sums=()):
    seq = positions.shape[1]
    wide = PLACES // 128 * seq // 2
    return call(
        functools.partial(tables_kernel, base=0 if first else 1, axes=axes),
        "table_grads",
        ids,
        (scores, places, positions, *sums),
        shape((3 if sums else 1, 8, 32), F32),
        mib=TABLES_MIB,
        us=0.01,
        scratch=[
            pltpu.VMEM((HEADS * 128, wide), BF), pltpu.VMEM((SPAN, wide), BF), pltpu.VMEM((HEADS * 128, SPAN), F32),
        ],
    )


def terms_of(grads, weights):
    total = None
    for part, w_ref in enumerate(weights):
        found = dot(grads[part], w_ref[...], ((0,), (0,)))
        total = found if total is None else total + found
    return total


def terms_send_kernel(ids, w0, w1, w2, grads_ref, *outs):
    for at, out_ref in enumerate(outs):
        out_ref[...] = terms_of(grads_ref[2 * at + 1], (w0, w1, w2)).astype(BF)


def terms_keep_kernel(ids, w0, w1, w2, grads_ref, got_own, got_other, own_ref, other_ref):
    other_ref[...] = (terms_of(grads_ref[2], (w0, w1, w2)) + got_other[...].astype(F32)).astype(BF)
    own_ref[...] = terms_of(grads_ref[0], (w0, w1, w2)) + got_own[...].astype(F32)


def terms_send(ids, weights, grads):
    outs = [shape((grads.shape[3], weights[0].shape[1]), BF)] * 2
    return call(terms_send_kernel, "terms_send", ids, (*weights, grads), outs, mib=16, us=0.01)


def terms_keep(ids, weights, grads, got):
    outs = [shape(got[0].shape, F32), shape(got[0].shape, BF)]
    return call(terms_keep_kernel, "terms_keep", ids, (*weights, grads, *got), outs, mib=16, us=0.01)


def last_kernel(
    ids, mine_ref, sent_ref, x_ref, page_ref, feat_ref, gain_ref, grad_ref, second_ref, mixed_ref, ffn_ref, got_ref,
    out_ref, part_ref,
):
    grad_normed = mine_ref[...] + sent_ref[...].astype(F32)
    here = quarter_of(ids[0], mine_ref.shape[0])
    unit, factor = unit_rows(hidden_rows(x_ref[here, :], page_ref[:, here], feat_ref[...]))
    scaled = grad_normed * gain_ref[...].astype(F32).reshape(1, -1)
    grad = factor * (scaled - unit * jnp.mean(scaled * unit, axis=-1, keepdims=True))
    rows, width = grad.shape
    out_ref[0, :rows] = (mixed_ref[...] + ffn_ref[...] + got_ref[...].astype(F32)).astype(BF)
    out_ref[1, :rows] = (grad_ref[...] + grad).astype(BF)
    part_ref[0:1] = jnp.sum(grad_normed * unit, axis=0, keepdims=True)
    part_ref[1:2] = second_ref[...]


def last(ids, mine, sent, inputs, onehot, feats, gain, grad_mixed, second, *ffn):
    rows, width = mine.shape
    arrays = (mine, sent, inputs, onehot, feats, gain, grad_mixed, second, *ffn)
    outs = [shape((2, rows, width), BF), shape((2, width), F32)]
    return call(last_kernel, "last", ids, arrays, outs, mib=16, us=0.01)


def pack_kernel(ids, gains_ref, got_ref, hor_a, ver_a, late, out_ref):
    gains = gains_ref[...] + got_ref[...]
    gains = [gains[slot : slot + 1] for slot in range(2)]
    parts = gains[0].shape[1] // 128
    for slot in range(2):
        gain = gains[slot]
        for part in range(parts):
            at = slot * parts + part
            out_ref[at : at + 1, :] = gain[:, part * 128 : part * 128 + 128]
    bins = hor_a.shape[2]
    at = 2 * parts
    out_ref[at:, :] = jnp.zeros((out_ref.shape[0] - at, 128), F32)
    for found in (late[2], hor_a[0] + late[0], ver_a[0] + late[1]):
        out_ref[at : at + HEADS, :bins] = found[:HEADS]
        at += HEADS


def pack(ids, gains, got, *sums):
    size = gains.shape[1] // 128 * 2 + 3 * HEADS
    size = -(-size // 8) * 8
    return call(pack_kernel, "pack", ids, (gains, got, *sums), shape((size, 128), F32), mib=8, us=0.1)


def join_kernel(ids, b0, b1, b2, b3, out_ref, *, slot):
    for k, b_ref in enumerate((b0, b1, b2, b3)):

        @pl.when(pl.program_id(0) == k)
        def _(b_ref=b_ref):
            out_ref[...] = b_ref[slot, : out_ref.shape[0]].astype(out_ref.dtype)


def join_feat_kernel(ids, b0, b1, b2, b3, page_ref, out_ref, feat_ref, all_ref, *, slot):
    step = pl.program_id(0)
    rows = out_ref.shape[0]
    for k, b_ref in enumerate((b0, b1, b2, b3)):

        @pl.when(step == k)
        def _(b_ref=b_ref, k=k):
            out_ref[...] = b_ref[slot, :rows].astype(out_ref.dtype)
            all_ref[pl.ds(pl.multiple_of(ids[k] * rows, rows), rows), :] = b_ref[slot, :rows]

    @pl.when(step == 3)
    def _():
        feat_ref[...] = dot(page_ref[...].astype(F32).astype(BF), all_ref[...])


def join(ids, blocks, slot, dtype, onehot=None):
    _, rows, width = blocks[0].shape
    specs = [VMEM] * 4
    outs, out_specs = [shape((4 * rows, width), dtype)], [pl.BlockSpec((rows, width), lambda i, s: (s[i], 0))]
    extra, scratch = (), []
    if onehot is not None:
        pages = onehot.shape[0]
        specs = specs + [VMEM]
        outs.append(shape((pages, width), F32))
        out_specs.append(whole((pages, width)))
        extra, scratch = (onehot,), [pltpu.VMEM((4 * rows, width), BF)]
    found = pl.pallas_call(
        functools.partial(join_kernel if onehot is None else join_feat_kernel, slot=slot),
        grid_spec=pltpu.PrefetchScalarGridSpec(
            num_scalar_prefetch=1, grid=(4,), in_specs=specs, out_specs=out_specs, scratch_shapes=scratch
        ),
        out_shape=outs,
        compiler_params=params(16),
        cost_estimate=cost(0.01),
        name="join_output" if onehot is None else "join_grads",
    )(ids, *blocks, *extra)
    return found[0] if onehot is None else found


def split_rows(ids, total, cols, keep_ref, send_ref, parity):
    groups, size = keep_ref.shape[0], keep_ref.shape[1]
    for g in range(groups):
        mine = pl.multiple_of((2 * g + parity) * size, 8)
        theirs = pl.multiple_of((2 * g + 1 - parity) * size, 8)
        keep_ref[g] = total[pl.ds(mine, size), cols].astype(keep_ref.dtype)
        send_ref[g] = total[pl.ds(theirs, size), cols].astype(BF)


def feed_grad_kernel(ids, k0, n0, k1, n1, c0, c1, cot_ref, *outs, fast):
    units = k0.shape[2]
    rows = lambda refs: jnp.concatenate(refs, axis=0)
    total = outs[-1]
    normed = rows([n0[2], c0[2], n1[2], c1[2]])
    total[:, :units] = dot(normed, rows([k0[1], c0[1], k1[1], c1[1]]), ((0,), (0,)))
    cotangent = rows([cot_ref[quarter_of(ids[n], k0.shape[1]), :] for n in range(4)])
    total[:, units:] = dot(cotangent, rows([k0[0], c0[0], k1[0], c1[0]]), ((0,), (0,)))
    if fast:
        split_rows(ids, total, slice(None), outs[0], outs[1], ids[9])
    else:
        outs[0][...] = total[...]


def feed_grad(ids, own, other, got_own, got_other, cotangent, fast):
    _, rows, units = own[0].shape
    width = cotangent.shape[1]
    if fast:
        outs = [shape((4, width // 8, 2 * units), F32), shape((4, width // 8, 2 * units), BF)]
    else:
        outs = [shape((width, 2 * units), F32)]
    return call(
        functools.partial(feed_grad_kernel, fast=fast),
        "feed_grad",
        ids,
        (*own, *other, got_own, got_other, cotangent),
        outs,
        mib=24,
        us=7,
        scratch=[pltpu.VMEM((width, 2 * units), F32)],
    )


def head_grad_kernel(ids, normed_ref, grads_ref, l0, l2, l1, l3, a0, a1, a2, a3, *outs, fast):
    total, turned = outs[-2:]
    n = a0.shape[0]
    normed = jnp.concatenate([normed_ref[quarter_of(ids[k], a0.shape[1]), :] for k in range(4)], axis=0)
    for part in range(3):
        left = jnp.concatenate([grads_ref[k, part] for k in range(4)], axis=1)
        total[part * n : (part + 1) * n, :] = dot(left, normed)
    low = jnp.concatenate([r[...] for r in (l0, l1, l2, l3)], axis=0)
    total[3 * n :, :] = dot(jnp.concatenate([r[...] for r in (a0, a1, a2, a3)], axis=1), low)
    turned[...] = total[...].T
    if fast:
        split_rows(ids, turned, slice(None), outs[0], outs[1], ids[9])
    else:
        outs[0][...] = turned[...]


def head_grad(ids, normed, grads, low, low_got, attended, fast):
    seq, width = normed.shape
    n = grads.shape[2]
    if fast:
        outs = [shape((4, width // 8, 4 * n), F32), shape((4, width // 8, 4 * n), BF)]
    else:
        outs = [shape((width, 4 * n), F32)]
    return call(
        functools.partial(head_grad_kernel, fast=fast),
        "head_grad",
        ids,
        (normed, grads, *low, *low_got, *attended),
        outs,
        mib=18,
        us=0.01,
        scratch=[pltpu.VMEM((4 * n, width), F32), pltpu.VMEM((width, 4 * n), F32)],
    )


def pair_kernel(ids, *refs):
    pairs, outs = refs[:-4], refs[-4:]
    for k, o_ref in enumerate(outs):
        at = ids[4 + k]
        start = 0
        for keep_ref, got_ref in zip(pairs[::2], pairs[1::2]):
            n = keep_ref.shape[2]
            o_ref[:, start : start + n] = (keep_ref[at] + got_ref[at].astype(F32)).astype(o_ref.dtype)
            start += n


def pair_sum(ids, *arrays):
    size = arrays[0].shape[1]
    n = sum(a.shape[2] for a in arrays[::2])
    outs = [shape((size, n), F32)] + [shape((size, n), BF)] * 3
    return call(pair_kernel, "pair_sum", ids, arrays, outs, mib=16, us=0.01)


def feed_final_kernel(a0, a1, a2, a3, up_ref, down_ref):
    total = a0[...] + a1[...].astype(F32) + a2[...].astype(F32) + a3[...].astype(F32)
    units = up_ref.shape[1]
    up_ref[...] = total[:, :units]
    down_ref[...] = total[:, units:]


def head_final_kernel(ids, a0, a1, a2, a3, one_ref, two_ref, q_ref, k_ref, v_ref, o_ref, *smalls):
    total = a0[...] + a1[...].astype(F32) + a2[...].astype(F32) + a3[...].astype(F32)
    n = q_ref.shape[1]
    for at, goal in enumerate((q_ref, k_ref, v_ref)):
        goal[...] = total[:, at * n : (at + 1) * n]
    o_ref[...] = total[:, 3 * n :].T
    *tables, gain_one, gain_two = smalls
    total = one_ref[...] + two_ref[...]
    size = gain_one.shape[1]
    width = 8 * size
    parts = width // 128
    mine = lax.rem(width - (2 * ids[4] + ids[9]) * size, width)
    for slot, goal in enumerate((gain_one, gain_two)):
        gain = jnp.concatenate([total[slot * parts + part : slot * parts + part + 1] for part in range(parts)], axis=1)
        goal[...] = pltpu.roll(jnp.broadcast_to(gain, (8, width)), mine, 1)[:1, :size]
    at, bins = 2 * parts, tables[0].shape[1]
    for goal in tables:
        goal[...] = total[at : at + HEADS, :bins]
        at += HEADS


def final(kernel, arrays, done, outs, *ids):
    arrays = [after(arrays[0], done)] + arrays[1:]
    return pl.pallas_call(
        kernel,
        grid=(1,),
        in_specs=[pl.BlockSpec(memory_space=pltpu.SMEM)] * len(ids) + [VMEM] * len(arrays),
        out_specs=jax.tree.map(lambda o: whole(o.shape), outs),
        out_shape=outs,
        compiler_params=params(16),
        cost_estimate=cost(5 if kernel is feed_final_kernel else 0.01),
        name=kernel.__name__[:-7],
    )(*ids, *arrays)


def swap(array, axis, size, bits):
    return lax.ppermute(array, axis, [(i, i ^ bits) for i in range(size)])


def after(array, *others):
    return lax.optimization_barrier((array, others))[0]


def local(
    inputs, page_feat, page_onehot, lengths, hor_pos, ver_pos, norm1_gain, w_query, w_key, w_value,
    rel_table, hor_table, ver_table, w_output, norm2_gain, w_up, w_down, cotangent, *, dp,
):
    seq, width = inputs.shape
    fast = dp == 8
    over = functools.partial(swap, axis="mp", size=4)
    m = lax.axis_index("mp").astype(I32)
    d = lax.axis_index("dp").astype(I32)
    k4 = jnp.arange(4, dtype=I32)
    spot = lambda who: (who & 1) * 2 + (who >> 1)
    ids = jnp.concatenate([
        spot(m ^ k4),
        (d >> 1) ^ k4,
        lengths[:1],
        (d & 1)[None],
    ])
    gain_one, gain_two = norm1_gain, norm2_gain
    feats = page_feat[0]
    hor, ver = hor_pos[None], ver_pos[None]
    tables = (rel_table, hor_table, ver_table)
    pages = page_onehot.T
    weights = [w_query.T, w_key.T, w_value.T]

    wo_y, wo_core = over(w_output, bits=2), over(w_output, bits=1)
    normed1, queries, keys, values = project(ids, inputs, pages, feats, gain_one, *weights)
    w_outputs = [w_output, wo_core, wo_y, over(after(wo_y, normed1), bits=1)]
    ups = [w_up, over(after(w_up, normed1), bits=1)]
    downs = [w_down, over(after(w_down, normed1), bits=1)]

    (e_a, att0, att1, inverse_a, out_a), lookups = attend(ids, queries, keys, values, hor, ver, tables, None)
    from_y, from_yc, own1 = over(att0, bits=2), over(att1, bits=3), over(att1, bits=1)
    ver_late = after(ver, att0, w_outputs[3], ups[1], downs[1])
    (e_b, att2, att3, inverse_b, out_b), _ = attend(ids, queries, keys, values, hor, ver_late, tables, lookups)
    attended = [att0, att1, att2, att3]
    for_other = [att2, over(att3, bits=1), from_y, from_yc]
    for_own = [att0, own1, over(att2, bits=2), over(att3, bits=3)]

    around = functools.partial(swap, axis="dp", size=dp)
    to_z = lambda parts: [parts[0]] + [around(part, bits=2 * k) for k, part in zip((1, 2, 3), parts[1:])]
    size = width // dp
    n = w_query.shape[1]
    units = w_up.shape[1]
    fixed = (inputs, pages, feats, gain_two, cotangent)
    x_keep, x_send, x_mixed, x_grad, x_ffn = feed(ids, False, *fixed, for_other, w_outputs, ups, downs)
    got_own, x_got = over(x_grad, bits=2), over(x_send, bits=1)
    for_own[0] = after(att0, x_ffn)
    m_keep, m_send, mixed, m_grad, m_ffn = feed(ids, True, *fixed, for_own, w_outputs, ups, downs)
    got_other, m_got = over(m_grad, bits=2), over(after(m_send, x_got), bits=1)
    own_grad = add(ids, m_grad, got_own)

    feed_grads = feed_grad(ids, (after(m_keep, own_grad), m_send), (x_keep, x_send), m_got, x_got, cotangent, fast)
    feed_got = around(feed_grads[1], bits=1) if fast else ids
    places_at, both = places_of(ids, after(hor, feed_grads[0]), ver)
    grad_mixed, ga, core_send, *low, gain_two_part = mid(
        ids, (after(own_grad, places_at), mixed), (x_grad, got_other, x_mixed), gain_two, cotangent, w_outputs[:2]
    )
    core_got = over(core_send, bits=1)
    sent_ffn = over(after(x_ffn, got_other, places_at), bits=2)

    halves = ((e_a, e_b), (inverse_a, inverse_b), (out_a, out_b))
    scores_a, dq0, dq2, key_sum, value_sum, near, far = back(ids, halves, queries, keys, values, ga, None)
    scores_b, grads, near, far = back(
        ids, halves, queries, keys, values, after(core_got, dq0), (key_sum, value_sum, near, far, dq0, dq2)
    )
    low_got = [over(part, bits=1) for part in low]
    to_core = terms_send(ids, weights, after(grads, sent_ffn))
    got_terms = [over(part, bits=1) for part in to_core]
    head_grads = head_grad(ids, normed1, after(grads, to_core[0]), low, low_got, attended, fast)
    own_terms, other_terms = terms_keep(ids, weights, after(grads, head_grads[0]), got_terms)
    sent_terms = over(other_terms, bits=2)

    hor_a = table_grads(ids, True, (0,), scores_a, places_at, after(both, own_terms))
    done = hor_a
    if fast:
        feed_parts = to_z(pair_sum(ids, after(feed_grads[0], done), feed_got))
        done = feed_parts[0]
    head_got = around(after(head_grads[1], done), bits=1) if fast else ids
    rows, gains = last(
        ids, after(own_terms, done), sent_terms, inputs, pages, feats, gain_one, grad_mixed, gain_two_part,
        mixed, m_ffn, sent_ffn,
    )
    rows_y, rows_core = over(rows, bits=2), over(rows, bits=1)
    ver_a = table_grads(ids, True, (1,), scores_a, places_at, after(both, rows))
    gains = after(gains, ver_a) + over(gains, bits=1)
    got_gains = over(gains, bits=2)
    late = table_grads(ids, False, (0, 1), scores_b, places_at, after(both, gains, head_got), (near, far))

    small = pack(ids, gains, got_gains, hor_a, ver_a, late)
    if fast:
        got = around(small, bits=1)
        grad_up, grad_down = final(feed_final_kernel, feed_parts, small, [shape((size, units), F32)] * 2)
        head_parts = to_z(pair_sum(ids, after(head_grads[0], grad_up), head_got))
        small = after(small, head_parts[0]) + got
        got = around(small, bits=2)
        quarters = [rows, rows_core, rows_y, over(after(rows_y, grad_up), bits=1)]
        outputs = join(ids, [after(rows, small)] + quarters[1:], 0, BF)
        grad_inputs, grad_feats = join(ids, [after(rows, outputs)] + quarters[1:], 1, F32, pages)
        small = after(small, grad_feats) + got
        bins = rel_table.shape[1]
        outs = [shape((size, n), F32)] * 3 + [shape((n, size), F32)] + [shape((HEADS, bins), F32)] * 3
        *found, first_gain, second_gain = final(
            head_final_kernel, head_parts + [small, around(small, bits=4)], grad_feats, outs + [shape((1, size), F32)] * 2, ids
        )
        grad_query, grad_key, grad_value, grad_output, grad_rel, grad_hor, grad_ver = found
    else:
        quarters = [rows, rows_core, rows_y, over(rows_y, bits=1)]
        outputs = join(ids, quarters, 0, BF)
        grad_inputs, grad_feats = join(ids, quarters, 1, F32, pages)
        small = lax.psum(small, "dp")
        scatter = lambda a: lax.psum_scatter(a[0], "dp", scatter_dimension=0, tiled=True)
        grad_feed, heads = scatter(feed_grads), scatter(head_grads)
        grad_up, grad_down = grad_feed[:, :units], grad_feed[:, units:]
        grad_query, grad_key, grad_value = heads[:, :n], heads[:, n : 2 * n], heads[:, 2 * n : 3 * n]
        grad_output = heads[:, 3 * n :].T
        gain_sums = lax.dynamic_slice(small[: width // 128 * 2].reshape(2, width), (0, d * size), (2, size))
        first_gain, second_gain = gain_sums[:1], gain_sums[1:]
        table_sums = small[width // 128 * 2 :, : rel_table.shape[1]]
        grad_rel, grad_hor, grad_ver = (table_sums[at : at + HEADS] for at in range(0, 3 * HEADS, HEADS))
    return (
        outputs, grad_inputs, grad_feats[None], first_gain[0], grad_query, grad_key, grad_value,
        grad_rel, grad_hor, grad_ver, grad_output, second_gain[0], grad_up, grad_down.T,
    )


def solution(mesh):
    return jax.shard_map(
        functools.partial(local, dp=mesh.shape["dp"]),
        mesh=mesh,
        in_specs=(
            P("dp", None),
            P("dp", None, None),
            P("dp", None),
            P("dp"),
            P("dp"),
            P("dp"),
            P(),
            P(None, "mp"),
            P(None, "mp"),
            P(None, "mp"),
            P("mp", None),
            P("mp", None),
            P("mp", None),
            P("mp", None),
            P(),
            P(None, "mp"),
            P("mp", None),
            P("dp", None),
        ),
        out_specs=(
            P("dp", None),
            P("dp", None),
            P("dp", None, None),
            P("dp"),
            P("dp", "mp"),
            P("dp", "mp"),
            P("dp", "mp"),
            P("mp", None),
            P("mp", None),
            P("mp", None),
            P("mp", "dp"),
            P("dp"),
            P("dp", "mp"),
            P("mp", "dp"),
        ),
        check_vma=False,
    )
```
